32 devices in a mesh: row: 4 (over z), col: 8 (over y, x, core).
Axes of the slice: x: 2, y: 2, z: 4, core: 2. Of those that a mesh axis runs over, the one named last changes fastest.
Arguments:
- hidden_in: bfloat16 [8192, 1536], P(('row', 'col')), may hold values from -6 to 6
- routes: int32 [2, 8192, 4], P(None, ('row', 'col')), may hold values from 0 to 31, all different within a row
- norm_attn: bfloat16 [2, 1536], replicated, may hold values from 0.099609375 to 1.8984375
- w_qkv: bfloat16 [2, 1536, 2048], P(None, 'row', 'col'), may hold values from -0.15625 to 0.15625
- w_out: bfloat16 [2, 1536, 1536], P(None, 'row', 'col'), may hold values from -2.5 to 2.5
- norm_moe: bfloat16 [2, 1536], replicated, may hold values from 0.099609375 to 1.8984375
- w_router: bfloat16 [2, 1536, 32], P(None, 'row'), may hold values from -0.078125 to 0.078125
- w_gate: bfloat16 [2, 32, 1536, 768], P(None, 'col', None, 'row'), may hold values from -0.15625 to 0.15625
- w_up: bfloat16 [2, 32, 1536, 768], P(None, 'col', None, 'row'), may hold values from -0.15625 to 0.15625
- w_down: bfloat16 [2, 32, 768, 1536], P(None, 'col', 'row'), may hold values from -0.4375 to 0.4375
- cotangent: bfloat16 [8192, 1536], P(('row', 'col')), may hold values from -6 to 6
Outputs:
- block_out: float32 [8192, 1536], P(('row', 'col'))
- grad_in: float32 [8192, 1536], P(('row', 'col'))
- grad_norm_attn: float32 [2, 1536], P(None, ('row', 'col'))
- grad_qkv: float32 [2, 1536, 2048], P(None, 'row', 'col')
- grad_out: float32 [2, 1536, 1536], P(None, 'row', 'col')
- grad_norm_moe: float32 [2, 1536], P(None, ('row', 'col'))
- grad_router: float32 [2, 1536, 32], P(None, ('row', 'col'))
- grad_gate: float32 [2, 32, 1536, 768], P(None, 'col', None, 'row')
- grad_up: float32 [2, 32, 1536, 768], P(None, 'col', None, 'row')
- grad_down: float32 [2, 32, 768, 1536], P(None, 'col', 'row')
The draws below stay inside these ranges and needn't reach their ends.
All inputs are finite; a program needn't handle non-finite values.
Results may differ from the reference program's by a relative error of at most 0.025.
Values may be sent and summed in bfloat16 or wider, within the bound.
A program may use at most 448 MiB of HBM per device.

```python
import jax
import jax.numpy as jnp
from jax import lax

D = 1536
QUERY_HEADS = 12
KEY_VALUE_HEADS = 2
HEAD_SIZE = 128
E = 32
TOPK = 4
F = 768
BLOCK = 256
LAYERS = 2
TOK_DEV = 256
SEQUENCE_TOKENS = 2048
TOKENS = 8192
QUERY_FEATURES = 1536
QKV = 2048
CAP = 36
N_ROW = 4
N_COL = 8


def levels(key, dims, cuts, low, high):
    level, own = 1.0, jax.random.fold_in(key, 6)
    for position, blocks in cuts:
        heights = jnp.exp(jax.random.uniform(jax.random.fold_in(own, position), (blocks,), jnp.float32, low / len(cuts), high / len(cuts)))
        level = level * jnp.repeat(heights, dims[position] // blocks).reshape([-1 if axis == position else 1 for axis in range(len(dims))])
    return level


def distinct(key, rows, number_of, top, lift):
    ranking = jax.random.permutation(jax.random.fold_in(key, 1), number_of)
    boost = ranking
    for power in range(3):
        boost = boost * boost // number_of
    boost = boost * lift // number_of
    tickets = jax.random.randint(jax.random.fold_in(key, 2), (rows, number_of), 0, 4096) + boost
    holders = jax.random.permutation(jax.random.fold_in(key, 3), rows)[jnp.arange(number_of) % rows]
    tickets = jnp.where(jnp.arange(rows)[:, None] == holders[None, :], 1 << 14, tickets)
    merit = tickets * number_of + jnp.arange(number_of)
    return lax.top_k(merit.astype(jnp.int32), top)[1].astype(jnp.int32)


def gaussian(stream_key, extent, deviation, most, split=(), kind=jnp.bfloat16):
    values = deviation * jax.random.normal(stream_key, extent, jnp.float32)
    if split:
        values = values * levels(stream_key, extent, split, -0.22, 0.18)
    return jnp.clip(values, -most, most).astype(kind)


def setup_inputs(seed: int = 0) -> dict:
    key_list = jax.random.split(jax.random.key(seed), 12)
    return {
        "hidden_in": gaussian(key_list[0], (TOKENS, D), 1.0, 6.0, ((0, 32),)),
        "routes": distinct(key_list[1], LAYERS * TOKENS, E, TOPK, 1024).reshape((LAYERS, TOKENS, TOPK)),
        "norm_attn": jnp.clip(1.0 + 0.18 * jax.random.normal(key_list[2], (LAYERS, D), jnp.float32), 0.099609375, 1.8984375).astype(jnp.bfloat16),
        "w_qkv": gaussian(key_list[3], (LAYERS, D, QKV), D ** -0.5, 0.15625, ((1, 4), (2, 8))),
        "w_out": gaussian(key_list[4], (LAYERS, QUERY_FEATURES, D), (max(QUERY_FEATURES // 256, 2)) ** -0.5, 2.5, ((1, 4), (2, 8))),
        "norm_moe": jnp.clip(1.0 + 0.18 * jax.random.normal(key_list[5], (LAYERS, D), jnp.float32), 0.099609375, 1.8984375).astype(jnp.bfloat16),
        "w_router": gaussian(key_list[6], (LAYERS, D, E), (4 * D) ** -0.5, 0.078125, ((1, 4),)),
        "w_gate": gaussian(key_list[7], (LAYERS, E, D, F), D ** -0.5, 0.15625, ((1, 8), (3, 4))),
        "w_up": gaussian(key_list[8], (LAYERS, E, D, F), D ** -0.5, 0.15625, ((1, 8), (3, 4))),
        "w_down": gaussian(key_list[9], (LAYERS, E, F, D), (F // 4) ** -0.5, 0.4375, ((1, 8), (2, 4))),
        "cotangent": gaussian(key_list[10], (TOKENS, D), 1.0, 6.0, ((0, 32),)),
    }


@jax.custom_vjp
def low(v):
    return lax.optimization_barrier(v.astype(jnp.bfloat16)).astype(jnp.float32)

@jax.custom_vjp
def low_back(v):
    return v

def low_keep(v):
    return (low(v), None)

def low_pass(kept, grad):
    return (grad,)

def back_keep(v):
    return (v, None)

def back_low(kept, grad):
    return (low(grad),)
low.defvjp(low_keep, low_pass)
low_back.defvjp(back_keep, back_low)
eps_norm = 1e-06
rope_base = 1000000.0
masked_score = -1e+30
highest = lax.Precision.HIGHEST

def rms_scale(values, gain_vec):
    return values * lax.rsqrt(lax.optimization_barrier(jnp.mean(values * values, axis=-1, keepdims=True)) + eps_norm) * gain_vec

def rope_angles(positions, half_dim):
    frequency = rope_base ** (-jnp.arange(half_dim, dtype=jnp.float32) / half_dim)
    angles = positions.astype(jnp.float32)[:, None] * frequency[None, :]
    return (jnp.cos(angles), jnp.sin(angles))

def rotate_heads(values, cosine_table, sine_table_rows, direction):
    half_dim = values.shape[-1] // 2
    first_half = values[..., :half_dim]
    second_half = values[..., half_dim:]
    cos_rows = cosine_table[:, None, :]
    sin_rows = direction * sine_table_rows[:, None, :]
    return jnp.concatenate([first_half * cos_rows - second_half * sin_rows, second_half * cos_rows + first_half * sin_rows], axis=-1)

def slot_table(route_rows):
    groups = route_rows.shape[0]
    onehot = (route_rows[..., None] == jnp.arange(E, dtype=jnp.int32)).astype(jnp.int32)
    flat_pairs = onehot.reshape(groups, -1, E)
    before = jnp.cumsum(flat_pairs, axis=1) - flat_pairs
    slot_number = lax.optimization_barrier(jnp.sum(before * flat_pairs, axis=-1)).reshape(route_rows.shape).astype(jnp.int32)
    usable = slot_number < CAP
    target = route_rows * CAP + jnp.minimum(slot_number, CAP - 1)
    return (target.astype(jnp.int32), usable)

def attend_block(query_rows, block_index, rotated_key_rows, value_row_block):
    query_group_width = QUERY_HEADS // KEY_VALUE_HEADS
    keys_wide = jnp.repeat(rotated_key_rows, query_group_width, axis=1)
    values_wide = jnp.repeat(value_row_block, query_group_width, axis=1)
    scores = jnp.einsum('qhd,khd->hqk', query_rows, keys_wide, precision=highest) * HEAD_SIZE ** (-0.5)
    scores = low_back(scores)
    query_block = (block_index * TOK_DEV + jnp.arange(TOK_DEV)) // BLOCK
    key_block = jnp.arange(SEQUENCE_TOKENS) // BLOCK
    allowed = key_block[None, :] <= query_block[:, None]
    scores = jnp.where(allowed[None], scores, masked_score)
    weights_soft = low(jax.nn.softmax(scores, axis=-1))
    result = jnp.einsum('hqk,khd->qhd', weights_soft, values_wide, precision=highest)
    return low(low_back(result))

def stack_forward(hidden, weights, seq_routes, tables):
    norm_attn, w_qkv, w_out, norm_moe, w_router, w_gate, w_up, w_down = weights
    positions = jnp.arange(SEQUENCE_TOKENS)
    cosine_table, sine_table_rows = rope_angles(positions, HEAD_SIZE // 2)
    key_value_width = KEY_VALUE_HEADS * HEAD_SIZE
    for layer_index in range(LAYERS):
        normed = low(rms_scale(hidden, norm_attn[layer_index]))
        projected_rows = low_back(jnp.dot(normed, w_qkv[layer_index], precision=highest))
        queries = projected_rows[:, :QUERY_FEATURES].reshape(SEQUENCE_TOKENS, QUERY_HEADS, HEAD_SIZE)
        rotated_key_rows = projected_rows[:, QUERY_FEATURES:QUERY_FEATURES + key_value_width].reshape(SEQUENCE_TOKENS, KEY_VALUE_HEADS, HEAD_SIZE)
        value_row_block = projected_rows[:, QUERY_FEATURES + key_value_width:].reshape(SEQUENCE_TOKENS, KEY_VALUE_HEADS, HEAD_SIZE)
        queries = low(low_back(rotate_heads(queries, cosine_table, sine_table_rows, 1.0)))
        rotated_key_rows = low(low_back(rotate_heads(rotated_key_rows, cosine_table, sine_table_rows, 1.0)))
        value_row_block = low(low_back(value_row_block))
        query_blocks = queries.reshape(N_COL, TOK_DEV, QUERY_HEADS, HEAD_SIZE)

        def attend_one(block_item, rotated_key_rows=rotated_key_rows, value_row_block=value_row_block):
            return attend_block(block_item[0], block_item[1], rotated_key_rows, value_row_block)
        attended = lax.map(jax.checkpoint(attend_one), (query_blocks, jnp.arange(N_COL)))
        attended = attended.reshape(SEQUENCE_TOKENS, QUERY_FEATURES)
        hidden = hidden + low_back(jnp.dot(attended, w_out[layer_index], precision=highest))
        normed_moe = low(rms_scale(hidden, norm_moe[layer_index]))
        logits = jnp.dot(normed_moe, w_router[layer_index], precision=highest)
        route_rows = seq_routes[layer_index]
        gate_weights = jax.nn.softmax(jnp.take_along_axis(logits, route_rows, axis=1), axis=-1)
        target, usable = tables[layer_index]
        slot_ids = jnp.arange(E * CAP)
        chosen = (target[..., None] == slot_ids) & usable[..., None]
        dispatch = jnp.any(chosen, axis=2).astype(jnp.float32)
        grouped = normed_moe.reshape(N_COL, TOK_DEV, D)
        slots_in = low_back(jnp.einsum('gts,gtd->gsd', dispatch, grouped, precision=highest)).reshape(N_COL, E, CAP, D)
        gate_val = low_back(jnp.einsum('gecd,edf->gecf', slots_in, w_gate[layer_index], precision=highest))
        up_val = low_back(jnp.einsum('gecd,edf->gecf', slots_in, w_up[layer_index], precision=highest))
        activated = low(jax.nn.silu(gate_val) * up_val)
        expert_res = low_back(low(jnp.einsum('gecf,efd->gecd', activated, w_down[layer_index], precision=highest)))
        expert_res = expert_res.reshape(N_COL, E * CAP, D)
        mixing = lax.optimization_barrier(jnp.sum(jnp.where(chosen, gate_weights.reshape(N_COL, TOK_DEV, TOPK)[..., None], 0.0), axis=2))
        hidden = hidden + jnp.einsum('gts,gsd->gtd', mixing, expert_res, precision=highest).reshape(SEQUENCE_TOKENS, D)
    return hidden

def reference(hidden_in, routes, norm_attn, w_qkv, w_out, norm_moe, w_router, w_gate, w_up, w_down, cotangent):
    params = (norm_attn.astype(jnp.float32), w_qkv.astype(jnp.float32), w_out.astype(jnp.float32), norm_moe.astype(jnp.float32), w_router.astype(jnp.float32), w_gate.astype(jnp.float32), w_up.astype(jnp.float32), w_down.astype(jnp.float32))
    inputs = hidden_in.astype(jnp.float32).reshape(N_ROW, SEQUENCE_TOKENS, D)
    cotangent_rows = cotangent.astype(jnp.float32).reshape(N_ROW, SEQUENCE_TOKENS, D)
    route_seqs = routes.reshape(LAYERS, N_ROW, SEQUENCE_TOKENS, TOPK).transpose(1, 0, 2, 3)

    def per_sequence(running, seq_item):
        seq_in, seq_cot, seq_routes = seq_item
        tables = [slot_table(seq_routes[layer_index].reshape(N_COL, TOK_DEV, TOPK)) for layer_index in range(LAYERS)]

        def forward(seq_hidden, *weights):
            return stack_forward(seq_hidden, weights, seq_routes, tables)
        result, pullback = jax.vjp(forward, seq_in, *params)
        grads = pullback(seq_cot)
        running = tuple((total + extra for total, extra in zip(running, grads[1:])))
        return (running, (result, grads[0]))
    zero_grads = tuple((jnp.zeros_like(param) for param in params))
    totals, (outputs, grad_rows) = lax.scan(per_sequence, zero_grads, (inputs, cotangent_rows, route_seqs))
    return (outputs.reshape(TOKENS, D), grad_rows.reshape(TOKENS, D), totals[0], totals[1], totals[2], totals[3], totals[4], totals[5], totals[6], totals[7])
```

```python
import functools

import jax
import jax.numpy as jnp
from jax import lax
from jax.experimental import pallas as pl
from jax.experimental.pallas import tpu as pltpu
from jax.sharding import PartitionSpec as P

QUERY_HEADS = 12
KEY_VALUE_HEADS = 2
HEAD_SIZE = 128
E = 32
TOPK = 4
BLOCK = 256
QUERY_FEATURES = 1536
CAP = 36


eps_norm = 1e-06
rope_base = 1000000.0
masked_score = -1e30
highest = lax.Precision.HIGHEST
wide_type = jnp.float32
narrow_type = jnp.bfloat16


def rms_parts(values, gain_vec):
    inverse = lax.rsqrt(jnp.mean(values * values, axis=-1, keepdims=True) + eps_norm)
    return (values * inverse * gain_vec, inverse)


def rms_backward(values, inverse, gain_vec, incoming):
    scaled = incoming * gain_vec
    inner_mean = jnp.mean(scaled * values, axis=-1, keepdims=True)
    grad_values = inverse * scaled - values * (inverse * inverse * inverse) * inner_mean
    grad_gain = jnp.sum(incoming * values * inverse, axis=0)
    return (grad_values, grad_gain)


def rope_angles(positions, half_dim):
    frequency = rope_base ** (-jnp.arange(half_dim, dtype=jnp.float32) / half_dim)
    angles = positions.astype(jnp.float32)[:, None] * frequency[None, :]
    return (jnp.cos(angles), jnp.sin(angles))


def rotate_heads(values, cosine_table, sine_table_rows, direction):
    half_dim = values.shape[-1] // 2
    first_half = values[..., :half_dim]
    second_half = values[..., half_dim:]
    cos_rows = cosine_table[:, None, :]
    sin_rows = direction * sine_table_rows[:, None, :]
    return jnp.concatenate(
        [
            first_half * cos_rows - second_half * sin_rows,
            second_half * cos_rows + first_half * sin_rows,
        ],
        axis=-1,
    )


def to_full(gathered, row_count, col_count):
    height = gathered.shape[1]
    breadth = gathered.shape[2]
    return (
        gathered.reshape(row_count, col_count, height, breadth)
        .transpose(0, 2, 1, 3)
        .reshape(row_count * height, col_count * breadth)
    )


def fetch_keys(kv_local):
    return lax.all_gather(kv_local, "col", axis=0, tiled=True)


def split_rows(total, most):
    best = 16
    for step in range(16, most + 1, 16):
        if total % step == 0:
            best = step
    return best


def over_blocks(total, block, step):
    def run(index, carry):
        step(pl.ds(pl.multiple_of(index * block, block), block))
        return carry

    lax.fori_loop(0, total // block, run, 0)


def over_chunks(chunks, width, step):
    def run(index, carry):
        step(index, pl.ds(pl.multiple_of(index * width, width), width))
        return carry

    lax.fori_loop(0, chunks, run, 0)


def dot_nt(left, right):
    return lax.dot_general(
        left, right, (((1,), (1,)), ((), ())), preferred_element_type=jnp.float32
    )


def dot_nn(left, right):
    return jnp.dot(left, right, preferred_element_type=jnp.float32)


class Peers:
    def __init__(self, count, place, device_of):
        self.count = count
        self.place = place
        self.device_of = device_of

    def ahead(self, step):
        return lax.rem(self.place + step, self.count)

    def behind(self, step):
        return lax.rem(self.place + self.count - step, self.count)


def expert_peers(col_count, copies, group_rows):
    row_index = lax.axis_index("row")
    share = lax.rem(row_index, copies)
    rows = Peers(
        group_rows, row_index // copies, lambda place: {"row": share + copies * place}
    )
    cols = Peers(col_count, lax.axis_index("col"), lambda place: {"col": place})
    return rows, cols


def greet(groups):
    barrier = pltpu.get_barrier_semaphore()
    total = 0
    for peers in groups:
        for step in range(1, peers.count):
            pl.semaphore_signal(
                barrier,
                inc=1,
                device_id=peers.device_of(peers.ahead(step)),
                device_id_type=pl.DeviceIdType.MESH,
            )
            total += 1
    pl.semaphore_wait(barrier, total)


class Exchange:
    def __init__(self, peers, send_sems, recv_sems, source, target):
        self.peers = peers
        self.send_sems = send_sems
        self.recv_sems = recv_sems
        self.source = source
        self.target = target

    def out(self, step, index, chunk):
        place = self.peers.ahead(step)
        return pltpu.make_async_remote_copy(
            src_ref=self.source(place, chunk),
            dst_ref=self.target(self.peers.place, step, chunk),
            send_sem=self.send_sems.at[index, step - 1],
            recv_sem=self.recv_sems.at[index, step - 1],
            device_id=self.peers.device_of(place),
            device_id_type=pl.DeviceIdType.MESH,
        )

    def start(self, index, chunk):
        for step in range(1, self.peers.count):
            self.out(step, index, chunk).start()

    def wait_send(self, index, chunk):
        for step in range(1, self.peers.count):
            self.out(step, index, chunk).wait_send()

    def wait_recv(self, index, chunk):
        for step in range(1, self.peers.count):
            landed = self.target(self.peers.behind(step), step, chunk)
            pltpu.make_async_remote_copy(
                src_ref=landed,
                dst_ref=landed,
                send_sem=self.send_sems.at[index, step - 1],
                recv_sem=self.recv_sems.at[index, step - 1],
                device_id=self.peers.device_of(self.peers.behind(step)),
                device_id_type=pl.DeviceIdType.MESH,
            ).wait_recv()


def slot_block(shape, slot_axis, slot_rows):
    slots = lax.broadcasted_iota(jnp.int32, shape, slot_axis)
    block = lax.broadcasted_iota(jnp.int32, shape, 1 - slot_axis)
    return (slots >= block * slot_rows) & (slots < (block + 1) * slot_rows)


def moe_forward_kernel(
    dims,
    own_ref,
    place_ref,
    place_t_ref,
    member_ref,
    router_ref,
    gate_ref,
    up_ref,
    down_ref,
    sum_ref,
    gates_ref,
    slots_out,
    returned_out,
    tokens,
    send,
    slots,
    gate_val,
    up_val,
    act,
    returned,
    mix_t,
    landed,
    row_send,
    row_recv,
    there_send,
    there_recv,
    back_send,
    back_recv,
    home_send,
    home_recv,
    local_sem,
):
    group_rows, col_count, copies, token_rows, slot_rows, chunks, width = dims
    all_tokens = group_rows * token_rows
    all_slots = col_count * slot_rows
    slot_step = split_rows(all_slots, 320)
    rows, cols = expert_peers(col_count, copies, group_rows)

    def token_part(place):
        return pl.ds(pl.multiple_of(place * token_rows, token_rows), token_rows)

    def slot_part(place):
        return pl.ds(pl.multiple_of(place * slot_rows, slot_rows), slot_rows)

    gather = Exchange(
        rows,
        row_send,
        row_recv,
        lambda place, chunk: own_ref.at[:, chunk],
        lambda place, step, chunk: tokens.at[token_part(place), chunk],
    )
    there = Exchange(
        cols,
        there_send,
        there_recv,
        lambda place, chunk: send.at[slot_part(place), chunk],
        lambda place, step, chunk: slots.at[slot_part(place), chunk],
    )
    back = Exchange(
        cols,
        back_send,
        back_recv,
        lambda place, chunk: send.at[slot_part(place), chunk],
        lambda place, step, chunk: returned.at[slot_part(place), chunk],
    )
    home = Exchange(
        rows,
        home_send,
        home_recv,
        lambda place, chunk: tokens.at[token_part(place), chunk],
        lambda place, step, chunk: landed.at[step - 1, :, chunk],
    )
    greet((rows, cols))
    over_chunks(chunks, width, gather.start)
    tokens[token_part(rows.place), :] = own_ref[...]

    def dispatch(index, chunk):
        gather.wait_recv(index, chunk)

        def rows_of(part):
            send[part, chunk] = dot_nn(place_ref[part, :], tokens[:, chunk]).astype(jnp.bfloat16)

        over_blocks(all_slots, slot_step, rows_of)
        there.start(index, chunk)
        slots[slot_part(cols.place), chunk] = send[slot_part(cols.place), chunk]

    over_chunks(chunks, width, dispatch)

    def gating(part):
        member = member_ref[part, :] > 0
        logits = jnp.where(member, dot_nt(tokens[part, :], router_ref[...]), masked_score)
        peak = jnp.max(logits, axis=-1, keepdims=True)
        exponent = jnp.where(member, jnp.exp(logits - peak), 0.0)
        gates = exponent / jnp.sum(exponent, axis=-1, keepdims=True)
        gates_ref[part, :] = gates
        pick = slot_block((gates.shape[1], all_slots), 1, slot_rows).astype(jnp.bfloat16)
        spread = dot_nn(gates.astype(jnp.bfloat16), pick)
        mix_t[part, :] = (place_t_ref[part, :].astype(jnp.float32) * spread).astype(jnp.bfloat16)

    over_blocks(all_tokens, token_rows, gating)

    def project(index, chunk):
        there.wait_recv(index, chunk)

        def rows_of(part):
            gate_part = dot_nt(slots[part, chunk], gate_ref[:, chunk])
            up_part = dot_nt(slots[part, chunk], up_ref[:, chunk])

            @pl.when(index == 0)
            def _():
                gate_val[part, :] = gate_part
                up_val[part, :] = up_part

            @pl.when(index > 0)
            def _():
                gate_val[part, :] += gate_part
                up_val[part, :] += up_part

        over_blocks(all_slots, slot_step, rows_of)

    over_chunks(chunks, width, project)
    keep_slots = pltpu.make_async_copy(slots, slots_out, local_sem.at[0])
    keep_slots.start()

    def activate(part):
        value = gate_val[part, :]
        act[part, :] = (value * jax.nn.sigmoid(value) * up_val[part, :]).astype(jnp.bfloat16)

    over_blocks(all_slots, slot_step, activate)

    def give_back(index, chunk):
        there.wait_send(index, chunk)

        def rows_of(part):
            send[part, chunk] = dot_nn(act[part, :], down_ref[:, chunk]).astype(jnp.bfloat16)

        over_blocks(all_slots, slot_step, rows_of)
        back.start(index, chunk)
        returned[slot_part(cols.place), chunk] = send[slot_part(cols.place), chunk]

    over_chunks(chunks, width, give_back)

    def combine(index, chunk):
        back.wait_recv(index, chunk)

        def rows_of(part):
            tokens[part, chunk] = dot_nn(mix_t[part, :], returned[:, chunk]).astype(jnp.bfloat16)

        over_blocks(all_tokens, token_rows, rows_of)
        home.start(index, chunk)

    over_chunks(chunks, width, combine)
    keep_returned = pltpu.make_async_copy(returned, returned_out, local_sem.at[1])
    keep_returned.start()

    def finish(index, chunk):
        home.wait_recv(index, chunk)
        total = tokens[token_part(rows.place), chunk].astype(jnp.float32)
        for step in range(1, group_rows):
            total = total + landed[step - 1, :, chunk].astype(jnp.float32)
        sum_ref[:, chunk] = total

    over_chunks(chunks, width, finish)

    def drain(index, chunk):
        gather.wait_send(index, chunk)
        back.wait_send(index, chunk)
        home.wait_send(index, chunk)

    over_chunks(chunks, width, drain)
    keep_slots.wait()
    keep_returned.wait()


def moe_backward_kernel(
    dims,
    own_ref,
    place_ref,
    place_t_ref,
    gates_ref,
    slots_ref,
    returned_ref,
    gate_ref,
    up_ref,
    down_ref,
    sum_ref,
    pair_ref,
    act_out,
    grad_gate_out,
    grad_up_out,
    received_out,
    tokens,
    send,
    slope,
    silu,
    act,
    weight,
    inner,
    received,
    grad_act,
    grad_gate,
    grad_up,
    returned,
    landed,
    pair_send,
    pair_landed,
    row_send,
    row_recv,
    there_send,
    there_recv,
    back_send,
    back_recv,
    home_send,
    home_recv,
    pair_send_sem,
    pair_recv_sem,
    local_sem,
):
    group_rows, col_count, copies, token_rows, slot_rows, chunks, width = dims
    all_tokens = group_rows * token_rows
    all_slots = col_count * slot_rows
    slot_step = split_rows(all_slots, 320)
    rows, cols = expert_peers(col_count, copies, group_rows)

    def token_part(place):
        return pl.ds(pl.multiple_of(place * token_rows, token_rows), token_rows)

    def slot_part(place):
        return pl.ds(pl.multiple_of(place * slot_rows, slot_rows), slot_rows)

    gather = Exchange(
        rows,
        row_send,
        row_recv,
        lambda place, chunk: own_ref.at[:, chunk],
        lambda place, step, chunk: tokens.at[token_part(place), chunk],
    )
    there = Exchange(
        cols,
        there_send,
        there_recv,
        lambda place, chunk: send.at[slot_part(place), chunk],
        lambda place, step, chunk: received.at[slot_part(place), chunk],
    )
    back = Exchange(
        cols,
        back_send,
        back_recv,
        lambda place, chunk: send.at[slot_part(place), chunk],
        lambda place, step, chunk: returned.at[slot_part(place), chunk],
    )
    home = Exchange(
        rows,
        home_send,
        home_recv,
        lambda place, chunk: tokens.at[token_part(place), chunk],
        lambda place, step, chunk: landed.at[step - 1, :, chunk],
    )
    pair = Exchange(
        rows,
        pair_send_sem,
        pair_recv_sem,
        lambda place, chunk: pair_send.at[token_part(place), :],
        lambda place, step, chunk: pair_landed.at[step - 1],
    )
    greet((rows, cols))
    over_chunks(chunks, width, gather.start)
    tokens[token_part(rows.place), :] = own_ref[...]

    def recompute(part):
        gate_val = dot_nt(slots_ref[part, :], gate_ref[...])
        up_val = dot_nt(slots_ref[part, :], up_ref[...])
        sigmoid = jax.nn.sigmoid(gate_val)
        value = gate_val * sigmoid
        act[part, :] = (value * up_val).astype(jnp.bfloat16)
        silu[part, :] = value
        slope[part, :] = up_val * sigmoid * (1.0 + gate_val * (1.0 - sigmoid))
        picked = dot_nn(place_ref[part, :], gates_ref[...].astype(jnp.bfloat16))
        block = lax.broadcasted_iota(jnp.int32, picked.shape, 1)
        slot = lax.broadcasted_iota(jnp.int32, picked.shape, 0) + part.start
        in_block = (slot >= block * slot_rows) & (slot < (block + 1) * slot_rows)
        weight[part, :] = jnp.sum(jnp.where(in_block, picked, 0.0), axis=1, keepdims=True)

    over_blocks(all_slots, slot_step, recompute)

    def dispatch(index, chunk):
        gather.wait_recv(index, chunk)

        def rows_of(part):
            grad = dot_nn(place_ref[part, :], tokens[:, chunk])
            share = jnp.sum(
                grad * returned_ref[part, chunk].astype(jnp.float32), axis=1, keepdims=True
            )
            send[part, chunk] = (weight[part, :] * grad).astype(jnp.bfloat16)

            @pl.when(index == 0)
            def _():
                inner[part, :] = share

            @pl.when(index > 0)
            def _():
                inner[part, :] += share

        over_blocks(all_slots, slot_step, rows_of)
        there.start(index, chunk)
        received[slot_part(cols.place), chunk] = send[slot_part(cols.place), chunk]

    over_chunks(chunks, width, dispatch)

    def pairs(part):
        picked = slot_block((all_slots, pair_send.shape[1]), 0, slot_rows)
        spread = jnp.where(picked, inner[...], 0.0)
        high = spread.astype(jnp.bfloat16)
        low = (spread - high.astype(jnp.float32)).astype(jnp.bfloat16)
        pair_send[part, :] = dot_nn(place_t_ref[part, :], high) + dot_nn(place_t_ref[part, :], low)

    over_blocks(all_tokens, token_rows, pairs)
    pair.start(0, None)

    def project(index, chunk):
        there.wait_recv(index, chunk)

        def rows_of(part):
            grad = dot_nt(received[part, chunk], down_ref[:, chunk])

            @pl.when(index == 0)
            def _():
                grad_act[part, :] = grad

            @pl.when(index > 0)
            def _():
                grad_act[part, :] += grad

        over_blocks(all_slots, slot_step, rows_of)

    over_chunks(chunks, width, project)

    def slopes(part):
        grad = grad_act[part, :]
        grad_gate[part, :] = (grad * slope[part, :]).astype(jnp.bfloat16)
        grad_up[part, :] = (grad * silu[part, :]).astype(jnp.bfloat16)

    over_blocks(all_slots, slot_step, slopes)
    kept = [
        pltpu.make_async_copy(source, target, local_sem.at[number])
        for number, (source, target) in enumerate(
            (
                (act, act_out),
                (grad_gate, grad_gate_out),
                (grad_up, grad_up_out),
                (received, received_out),
            )
        )
    ]
    for copy in kept:
        copy.start()

    def give_back(index, chunk):
        there.wait_send(index, chunk)

        def rows_of(part):
            send[part, chunk] = (
                dot_nn(grad_gate[part, :], gate_ref[:, chunk])
                + dot_nn(grad_up[part, :], up_ref[:, chunk])
            ).astype(jnp.bfloat16)

        over_blocks(all_slots, slot_step, rows_of)
        back.start(index, chunk)
        returned[slot_part(cols.place), chunk] = send[slot_part(cols.place), chunk]

    over_chunks(chunks, width, give_back)

    def combine(index, chunk):
        back.wait_recv(index, chunk)

        def rows_of(part):
            tokens[part, chunk] = dot_nn(place_t_ref[part, :], returned[:, chunk]).astype(
                jnp.bfloat16
            )

        over_blocks(all_tokens, token_rows, rows_of)
        home.start(index, chunk)

    over_chunks(chunks, width, combine)
    pair.wait_recv(0, None)
    pair_total = pair_send[token_part(rows.place), :]
    pair_ref[0] = pair_total
    for step in range(1, group_rows):
        pair_ref[step] = pair_landed[step - 1]

    def finish(index, chunk):
        home.wait_recv(index, chunk)
        total = tokens[token_part(rows.place), chunk].astype(jnp.float32)
        for step in range(1, group_rows):
            total = total + landed[step - 1, :, chunk].astype(jnp.float32)
        sum_ref[:, chunk] = total

    over_chunks(chunks, width, finish)

    def drain(index, chunk):
        gather.wait_send(index, chunk)
        back.wait_send(index, chunk)
        home.wait_send(index, chunk)

    over_chunks(chunks, width, drain)
    pair.wait_send(0, None)
    for copy in kept:
        copy.wait()


vmem_most = 60 * 1024 * 1024


def exchange_sems(chunks, count):
    return [pltpu.SemaphoreType.DMA((chunks, max(count - 1, 1))) for _ in range(2)]


def moe_forward(dims, own, place, place_t, member, router, gate, up, down):
    group_rows, col_count, copies, token_rows, slot_rows, chunks, width = dims
    all_tokens, all_slots = group_rows * token_rows, col_count * slot_rows
    model_width, hidden = own.shape[1], gate.shape[0]
    vmem = pl.BlockSpec(memory_space=pltpu.VMEM)
    outside = pl.BlockSpec(memory_space=pl.ANY)
    slot_array = pltpu.VMEM((all_slots, model_width), jnp.bfloat16)
    flops = 2 * all_slots * model_width * (3 * hidden + 2 * all_tokens)
    return pl.pallas_call(
        functools.partial(moe_forward_kernel, dims),
        out_shape=(
            jax.ShapeDtypeStruct((token_rows, model_width), jnp.float32),
            jax.ShapeDtypeStruct((all_tokens, member.shape[1]), jnp.float32),
            jax.ShapeDtypeStruct((all_slots, model_width), jnp.bfloat16),
            jax.ShapeDtypeStruct((all_slots, model_width), jnp.bfloat16),
        ),
        in_specs=[vmem] * 8,
        out_specs=(vmem, vmem, outside, outside),
        scratch_shapes=[
            pltpu.VMEM((all_tokens, model_width), jnp.bfloat16),
            slot_array,
            slot_array,
            pltpu.VMEM((all_slots, hidden), jnp.float32),
            pltpu.VMEM((all_slots, hidden), jnp.float32),
            pltpu.VMEM((all_slots, hidden), jnp.bfloat16),
            slot_array,
            pltpu.VMEM((all_tokens, all_slots), jnp.bfloat16),
            pltpu.VMEM((group_rows - 1, token_rows, model_width), jnp.bfloat16),
            *exchange_sems(chunks, group_rows),
            *exchange_sems(chunks, col_count),
            *exchange_sems(chunks, col_count),
            *exchange_sems(chunks, group_rows),
            pltpu.SemaphoreType.DMA((2,)),
        ],
        compiler_params=pltpu.CompilerParams(
            collective_id=1, has_side_effects=True, vmem_limit_bytes=vmem_most
        ),
        cost_estimate=pl.CostEstimate(
            flops=flops, bytes_accessed=40 * 1024 * 1024, transcendentals=all_slots * hidden
        ),
        name="moe_forward",
    )(own, place, place_t, member, router, gate, up, down)


def moe_backward(dims, own, place, place_t, gates, slots, returned, gate, up, down):
    group_rows, col_count, copies, token_rows, slot_rows, chunks, width = dims
    all_tokens, all_slots = group_rows * token_rows, col_count * slot_rows
    model_width, hidden = own.shape[1], gate.shape[0]
    vmem = pl.BlockSpec(memory_space=pltpu.VMEM)
    outside = pl.BlockSpec(memory_space=pl.ANY)
    slot_array = pltpu.VMEM((all_slots, model_width), jnp.bfloat16)
    hidden_wide = pltpu.VMEM((all_slots, hidden), jnp.float32)
    hidden_narrow = pltpu.VMEM((all_slots, hidden), jnp.bfloat16)
    flops = 2 * all_slots * model_width * (6 * hidden + 2 * all_tokens)
    return pl.pallas_call(
        functools.partial(moe_backward_kernel, dims),
        out_shape=(
            jax.ShapeDtypeStruct((token_rows, model_width), jnp.float32),
            jax.ShapeDtypeStruct((group_rows, token_rows, 128), jnp.float32),
            jax.ShapeDtypeStruct((all_slots, hidden), jnp.bfloat16),
            jax.ShapeDtypeStruct((all_slots, hidden), jnp.bfloat16),
            jax.ShapeDtypeStruct((all_slots, hidden), jnp.bfloat16),
            jax.ShapeDtypeStruct((all_slots, model_width), jnp.bfloat16),
        ),
        in_specs=[vmem] * 9,
        out_specs=(vmem, vmem, outside, outside, outside, outside),
        scratch_shapes=[
            pltpu.VMEM((all_tokens, model_width), jnp.bfloat16),
            slot_array,
            hidden_wide,
            hidden_wide,
            hidden_narrow,
            pltpu.VMEM((all_slots, 1), jnp.float32),
            pltpu.VMEM((all_slots, 1), jnp.float32),
            slot_array,
            hidden_wide,
            hidden_narrow,
            hidden_narrow,
            slot_array,
            pltpu.VMEM((group_rows - 1, token_rows, model_width), jnp.bfloat16),
            pltpu.VMEM((all_tokens, 128), jnp.float32),
            pltpu.VMEM((group_rows - 1, token_rows, 128), jnp.float32),
            *exchange_sems(chunks, group_rows),
            *exchange_sems(chunks, col_count),
            *exchange_sems(chunks, col_count),
            *exchange_sems(chunks, group_rows),
            *exchange_sems(1, group_rows),
            pltpu.SemaphoreType.DMA((4,)),
        ],
        compiler_params=pltpu.CompilerParams(
            collective_id=2, has_side_effects=True, vmem_limit_bytes=vmem_most
        ),
        cost_estimate=pl.CostEstimate(
            flops=flops, bytes_accessed=50 * 1024 * 1024, transcendentals=all_slots * hidden
        ),
        name="moe_backward",
    )(own, place, place_t, gates, slots, returned, gate, up, down)


def col_pairs():
    col_index = lax.axis_index("col")
    return col_index // 2, lax.rem(col_index, 2)


def send_to(source, target, sems, number, device):
    send_sems, recv_sems = sems
    return pltpu.make_async_remote_copy(
        src_ref=source,
        dst_ref=target,
        send_sem=send_sems.at[number],
        recv_sem=recv_sems.at[number],
        device_id=device,
        device_id_type=pl.DeviceIdType.MESH,
    )


def dense_peers(row_count, pair_count):
    row_index = lax.axis_index("row")
    pair, side = col_pairs()
    rows = Peers(row_count, row_index, lambda place: {"row": place})
    pairs = Peers(pair_count, pair, lambda place: {"col": place * 2 + side})
    sides = Peers(2, side, lambda place: {"col": pair * 2 + place})
    return rows, pairs, sides


def reduce_dense_kernel(
    dims,
    normed_ref,
    grad_proj_ref,
    grad_mid_ref,
    attended_ref,
    small_ref,
    qkv_ref,
    out_ref,
    small_out_ref,
    *scratch,
):
    row_count, pair_count = dims
    kinds = 3
    buffers = [scratch[6 * kind : 6 * kind + 6] for kind in range(kinds)]
    sems = scratch[6 * kinds :]
    side_sems = [(sems[6 * kind], sems[6 * kind + 1]) for kind in range(kinds)]
    pair_sems = [(sems[6 * kind + 2], sems[6 * kind + 3]) for kind in range(kinds)]
    row_sems = [(sems[6 * kind + 4], sems[6 * kind + 5]) for kind in range(kinds)]
    rows, pairs, sides = dense_peers(row_count, pair_count)
    other = 1 - sides.place

    def block(kind, row, pair, side):
        col = pair * 2 + side
        if kind == 0:
            return dot_nn(normed_ref[row], grad_proj_ref[col])
        if kind == 1:
            return dot_nn(grad_mid_ref[col], attended_ref[row])
        return small_ref[col, row].astype(jnp.float32)

    greet((rows, pairs, sides))
    outputs = (qkv_ref, out_ref, small_out_ref)

    def side_copy(kind, pair):
        side_send, side_recv = buffers[kind][0], buffers[kind][1]
        return send_to(
            side_send.at[pair],
            side_recv.at[pair],
            side_sems[kind],
            pair,
            sides.device_of(other),
        )

    def pair_copy(kind, step, row):
        place = pairs.ahead(step)
        half, pair_recv = buffers[kind][2], buffers[kind][3]
        return send_to(
            half.at[place, row],
            pair_recv.at[step - 1, row],
            pair_sems[kind],
            (step - 1) * row_count + row,
            pairs.device_of(place),
        )

    def row_copy(kind, step):
        place = rows.ahead(step)
        whole, row_recv = buffers[kind][4], buffers[kind][5]
        return send_to(
            whole.at[place],
            row_recv.at[step - 1],
            row_sems[kind],
            step - 1,
            rows.device_of(place),
        )

    def first(step, carry):
        pair = lax.rem(pairs.place + step, pair_count)
        for kind in range(kinds):
            for row in range(row_count):
                buffers[kind][0][pair, row] = block(kind, row, pair, other).astype(jnp.bfloat16)
            side_copy(kind, pair).start()
        return carry

    lax.fori_loop(1, pair_count + 1, first, 0)

    def second(step, carry):
        pair = lax.rem(pairs.place + step, pair_count)
        for kind in range(kinds):
            side_copy(kind, pair).wait_recv()
            side_recv, half = buffers[kind][1], buffers[kind][2]
            for row in range(row_count):
                total = block(kind, row, pair, sides.place)
                total = total + side_recv[pair, row].astype(jnp.float32)
                half[pair, row] = total.astype(jnp.bfloat16)

                @pl.when(step < pair_count)
                def _():
                    pair_copy(kind, step, row).start()

        return carry

    lax.fori_loop(1, pair_count + 1, second, 0)

    def third(step, carry):
        row = lax.rem(rows.place + step, row_count)
        for kind in range(kinds):
            half, pair_recv, whole = buffers[kind][2], buffers[kind][3], buffers[kind][4]
            total = half[pairs.place, row].astype(jnp.float32)
            for ahead in range(1, pair_count):
                pair_copy(kind, ahead, row).wait_recv()
                total = total + pair_recv[ahead - 1, row].astype(jnp.float32)

            whole[row] = total.astype(jnp.bfloat16)

            @pl.when(step < row_count)
            def _():
                row_copy(kind, step).start()

        return carry

    lax.fori_loop(1, row_count + 1, third, 0)
    for kind in range(kinds):
        whole, row_recv = buffers[kind][4], buffers[kind][5]
        total = whole[rows.place].astype(jnp.float32)
        for step in range(1, row_count):
            row_copy(kind, step).wait_recv()
            total = total + row_recv[step - 1].astype(jnp.float32)
        outputs[kind][...] = total

    def drain_sides(pair, carry):
        for kind in range(kinds):
            side_copy(kind, pair).wait_send()
        return carry

    lax.fori_loop(0, pair_count, drain_sides, 0)

    def drain_pairs(step, carry):
        for kind in range(kinds):
            for row in range(row_count):
                pair_copy(kind, step, row).wait_send()
        return carry

    lax.fori_loop(1, pair_count, drain_pairs, 0)
    for kind in range(kinds):
        for step in range(1, row_count):
            row_copy(kind, step).wait_send()


def reduce_dense(row_count, col_count, normed, grad_projected, grad_mid_b, attended, small):
    token_rows, model_width = normed.shape
    qkv_width, out_rows = grad_projected.shape[1], attended.shape[1]
    pair_count = col_count // 2
    shapes = (
        (model_width // row_count, qkv_width // col_count),
        (model_width // col_count, out_rows // row_count),
        small.shape[2:],
    )
    vmem = pl.BlockSpec(memory_space=pltpu.VMEM)
    scratch = []
    sems = []
    for height, breadth in shapes:
        for lead in (
            (pair_count, row_count),
            (pair_count, row_count),
            (pair_count, row_count),
            (max(pair_count - 1, 1), row_count),
            (row_count,),
            (max(row_count - 1, 1),),
        ):
            scratch.append(pltpu.VMEM((*lead, height, breadth), jnp.bfloat16))
        for count in (pair_count, max(pair_count - 1, 1) * row_count, max(row_count - 1, 1)):
            sems.extend([pltpu.SemaphoreType.DMA((count,))] * 2)
    return pl.pallas_call(
        functools.partial(reduce_dense_kernel, (row_count, pair_count)),
        out_shape=tuple(jax.ShapeDtypeStruct(shape, jnp.float32) for shape in shapes),
        in_specs=[vmem] * 5,
        out_specs=(vmem,) * 3,
        scratch_shapes=scratch + sems,
        compiler_params=pltpu.CompilerParams(
            collective_id=3, has_side_effects=True, vmem_limit_bytes=vmem_most
        ),
        cost_estimate=pl.CostEstimate(
            flops=2 * token_rows * model_width * (qkv_width + out_rows),
            bytes_accessed=8 * 1024 * 1024,
            transcendentals=0,
        ),
        name="reduce_dense",
    )(
        normed.T.reshape(row_count, -1, token_rows),
        grad_projected.reshape(token_rows, col_count, -1).transpose(1, 0, 2),
        grad_mid_b.T.reshape(col_count, -1, token_rows),
        attended.reshape(token_rows, row_count, -1).transpose(1, 0, 2),
        small,
    )


def gather_dense_kernel(dims, qkv_ref, out_ref, qkv_full, out_full, *sems):
    row_count, pair_count = dims
    rows, pairs, sides = dense_peers(row_count, pair_count)
    other = 1 - sides.place
    kinds = 2
    own_blocks = (qkv_ref, out_ref)
    height, breadth = qkv_ref.shape
    out_height = out_ref.shape[0]
    row_sems = [(sems[6 * kind], sems[6 * kind + 1]) for kind in range(kinds)]
    pair_sems = [(sems[6 * kind + 2], sems[6 * kind + 3]) for kind in range(kinds)]
    side_sems = [(sems[6 * kind + 4], sems[6 * kind + 5]) for kind in range(kinds)]
    local_sems = sems[6 * kinds]

    def spot(kind, row, pair, side):
        col = pair * 2 + side
        if kind == 0:
            return qkv_full.at[
                pl.ds(pl.multiple_of(row * height, height), height),
                pl.ds(pl.multiple_of(col * breadth, breadth), breadth),
            ]
        return out_full.at[row, pl.ds(pl.multiple_of(col * out_height, out_height), out_height), :]

    def row_copy(kind, step):
        target = spot(kind, rows.place, pairs.place, sides.place)
        return send_to(
            own_blocks[kind], target, row_sems[kind], step - 1, rows.device_of(rows.ahead(step))
        )

    def row_landed(kind, step):
        landed = spot(kind, rows.behind(step), pairs.place, sides.place)
        return send_to(
            landed, landed, row_sems[kind], step - 1, rows.device_of(rows.behind(step))
        )

    def pair_copy(kind, step, row, number):
        block = spot(kind, row, pairs.place, sides.place)
        return send_to(
            block if number else own_blocks[kind],
            block,
            pair_sems[kind],
            (step - 1) * row_count + number,
            pairs.device_of(pairs.ahead(step)),
        )

    def pair_landed(kind, step, number):
        row = rows.behind(number)
        landed = spot(kind, row, pairs.behind(step), sides.place)
        return send_to(
            landed,
            landed,
            pair_sems[kind],
            (step - 1) * row_count + number,
            pairs.device_of(pairs.behind(step)),
        )

    def side_copy(kind, step, number):
        block = spot(kind, rows.behind(number), pairs.behind(step), sides.place)
        source = own_blocks[kind] if step == 0 and number == 0 else block
        return send_to(
            source,
            block,
            side_sems[kind],
            step * row_count + number,
            sides.device_of(other),
        )

    def side_landed(kind, step, number):
        landed = spot(kind, rows.behind(number), pairs.behind(step), other)
        return send_to(
            landed,
            landed,
            side_sems[kind],
            step * row_count + number,
            sides.device_of(other),
        )

    greet((rows, pairs, sides))
    own_copies = []
    for kind in range(kinds):
        copy = pltpu.make_async_copy(
            own_blocks[kind],
            spot(kind, rows.place, pairs.place, sides.place),
            local_sems.at[kind],
        )
        copy.start()
        own_copies.append(copy)
    for kind in range(kinds):
        for step in range(1, row_count):
            row_copy(kind, step).start()
        for step in range(1, pair_count):
            pair_copy(kind, step, rows.place, 0).start()
        side_copy(kind, 0, 0).start()
    for kind in range(kinds):
        for number in range(1, row_count):
            row_landed(kind, number).wait_recv()
            for step in range(1, pair_count):
                pair_copy(kind, step, rows.behind(number), number).start()
            side_copy(kind, 0, number).start()
    for kind in range(kinds):
        for number in range(row_count):
            for step in range(1, pair_count):
                pair_landed(kind, step, number).wait_recv()
                side_copy(kind, step, number).start()
    for kind in range(kinds):
        for step in range(pair_count):
            for number in range(row_count):
                side_landed(kind, step, number).wait_recv()
    for kind in range(kinds):
        own_copies[kind].wait()
        for step in range(1, row_count):
            row_copy(kind, step).wait_send()
        for number in range(row_count):
            for step in range(1, pair_count):
                pair_copy(kind, step, rows.behind(number), number).wait_send()
            for step in range(pair_count):
                side_copy(kind, step, number).wait_send()


def gather_dense(row_count, col_count, qkv_block, out_block):
    height, breadth = qkv_block.shape
    out_height, out_breadth = out_block.shape
    pair_count = col_count // 2
    outside = pl.BlockSpec(memory_space=pl.ANY)
    sems = []
    for _ in range(2):
        for count in (
            max(row_count - 1, 1),
            max(pair_count - 1, 1) * row_count,
            pair_count * row_count,
        ):
            sems.extend([pltpu.SemaphoreType.DMA((count,))] * 2)
    return pl.pallas_call(
        functools.partial(gather_dense_kernel, (row_count, pair_count)),
        out_shape=(
            jax.ShapeDtypeStruct((row_count * height, col_count * breadth), qkv_block.dtype),
            jax.ShapeDtypeStruct((row_count, col_count * out_height, out_breadth), out_block.dtype),
        ),
        in_specs=[outside] * 2,
        out_specs=(outside,) * 2,
        scratch_shapes=sems + [pltpu.SemaphoreType.DMA((2,))],
        compiler_params=pltpu.CompilerParams(collective_id=4, has_side_effects=True),
        name="gather_dense",
    )(qkv_block, out_block)


def attend_forward_kernel(score_scale, q_ref, kv_ref, value_t_ref, out_ref, lse_ref):
    token_rows = q_ref.shape[0]
    group = QUERY_HEADS // KEY_VALUE_HEADS
    position = lax.axis_index("col") * token_rows + lax.broadcasted_iota(
        jnp.int32, (1, token_rows), 1
    )
    seen = (position // BLOCK + 1) * BLOCK

    def head(index, carry):
        kv_head = index // group
        lanes = pl.ds(pl.multiple_of(index * HEAD_SIZE, HEAD_SIZE), HEAD_SIZE)
        kv_lanes = pl.ds(pl.multiple_of(kv_head * HEAD_SIZE, HEAD_SIZE), HEAD_SIZE)
        scores = dot_nt(kv_ref[:, kv_lanes], q_ref[:, lanes]) * score_scale
        key = lax.broadcasted_iota(jnp.int32, scores.shape, 0)
        scores = jnp.where(key < seen, scores, masked_score)
        peak = jnp.max(scores, axis=0, keepdims=True)
        exponent = jnp.exp(scores - peak)
        total = jnp.sum(exponent, axis=0, keepdims=True)
        attended = dot_nn(value_t_ref[kv_lanes, :], exponent.astype(jnp.bfloat16)) / total
        out_ref[:, lanes] = attended.T.astype(jnp.bfloat16)
        lse_ref[index] = peak + jnp.log(total)
        return carry

    lax.fori_loop(0, QUERY_HEADS, head, 0)


def attend_forward(queries_b, key_value_full, value_t, score_scale):
    token_rows = queries_b.shape[0]
    seq_rows = key_value_full.shape[0]
    vmem = pl.BlockSpec(memory_space=pltpu.VMEM)
    return pl.pallas_call(
        functools.partial(attend_forward_kernel, score_scale),
        out_shape=(
            jax.ShapeDtypeStruct(queries_b.shape, jnp.bfloat16),
            jax.ShapeDtypeStruct((QUERY_HEADS, 1, token_rows), jnp.float32),
        ),
        in_specs=[vmem] * 3,
        out_specs=(vmem, vmem),
        compiler_params=pltpu.CompilerParams(vmem_limit_bytes=vmem_most),
        cost_estimate=pl.CostEstimate(
            flops=4 * token_rows * seq_rows * QUERY_FEATURES,
            bytes_accessed=6 * 1024 * 1024,
            transcendentals=token_rows * seq_rows * QUERY_HEADS,
        ),
        name="attend_forward",
    )(queries_b, key_value_full, value_t)


def attend_backward_kernel(
    score_scale,
    q_ref,
    kv_ref,
    key_t_ref,
    lse_ref,
    inner_ref,
    grad_ref,
    grad_q_ref,
    grad_kv_ref,
    key_sum,
    value_sum,
):
    token_rows = q_ref.shape[0]
    group = QUERY_HEADS // KEY_VALUE_HEADS
    position = lax.axis_index("col") * token_rows + lax.broadcasted_iota(
        jnp.int32, (1, token_rows), 1
    )
    seen = (position // BLOCK + 1) * BLOCK
    for kv_head in range(KEY_VALUE_HEADS):
        kv_lanes = slice(kv_head * HEAD_SIZE, (kv_head + 1) * HEAD_SIZE)
        value_lanes = slice(
            (KEY_VALUE_HEADS + kv_head) * HEAD_SIZE, (KEY_VALUE_HEADS + kv_head + 1) * HEAD_SIZE
        )
        key_sum[...] = jnp.zeros_like(key_sum)
        value_sum[...] = jnp.zeros_like(value_sum)

        def head(step, carry, kv_lanes=kv_lanes, value_lanes=value_lanes, kv_head=kv_head):
            index = kv_head * group + step
            lanes = pl.ds(pl.multiple_of(index * HEAD_SIZE, HEAD_SIZE), HEAD_SIZE)
            query = q_ref[:, lanes]
            grad = grad_ref[:, lanes]
            scores = dot_nt(kv_ref[:, kv_lanes], query) * score_scale
            key = lax.broadcasted_iota(jnp.int32, scores.shape, 0)
            soft = jnp.where(key < seen, jnp.exp(scores - lse_ref[index]), 0.0)
            grad_soft = dot_nt(kv_ref[:, value_lanes], grad)
            grad_scores = (soft * (grad_soft - inner_ref[index])).astype(jnp.bfloat16)
            value_sum[...] += dot_nn(soft.astype(jnp.bfloat16), grad)
            key_sum[...] += dot_nn(grad_scores, query)
            grad_q = dot_nn(key_t_ref[kv_lanes, :], grad_scores) * score_scale
            grad_q_ref[:, lanes] = grad_q.T.astype(jnp.bfloat16)
            return carry

        lax.fori_loop(0, group, head, 0)
        grad_kv_ref[:, kv_lanes] = (key_sum[...] * score_scale).astype(jnp.bfloat16)
        grad_kv_ref[:, value_lanes] = value_sum[...].astype(jnp.bfloat16)


def attend_backward(queries_b, key_value_full, key_t, score_scale, log_sums, inner, grad_out_b):
    token_rows = queries_b.shape[0]
    seq_rows = key_value_full.shape[0]
    vmem = pl.BlockSpec(memory_space=pltpu.VMEM)
    return pl.pallas_call(
        functools.partial(attend_backward_kernel, score_scale),
        out_shape=(
            jax.ShapeDtypeStruct(queries_b.shape, jnp.bfloat16),
            jax.ShapeDtypeStruct(key_value_full.shape, jnp.bfloat16),
        ),
        in_specs=[vmem] * 6,
        out_specs=(vmem, vmem),
        scratch_shapes=[pltpu.VMEM((seq_rows, HEAD_SIZE), jnp.float32)] * 2,
        compiler_params=pltpu.CompilerParams(vmem_limit_bytes=vmem_most),
        cost_estimate=pl.CostEstimate(
            flops=10 * token_rows * seq_rows * QUERY_FEATURES,
            bytes_accessed=10 * 1024 * 1024,
            transcendentals=token_rows * seq_rows * QUERY_HEADS,
        ),
        name="attend_backward",
    )(queries_b, key_value_full, key_t, log_sums, inner, grad_out_b)


def layer_routing(route_rows, dims, expert_pick):
    group_rows, col_count, copies, token_rows, slot_rows, chunks, width = dims
    expert_ids = jnp.arange(E, dtype=jnp.int32)
    member = jnp.any(route_rows[..., None] == expert_ids, axis=2)
    earlier = (
        jnp.arange(token_rows)[None, :] < jnp.arange(token_rows)[:, None]
    ).astype(narrow_type)
    before = jnp.einsum(
        "ts,gse->gte", earlier, member.astype(narrow_type), preferred_element_type=wide_type
    )
    slot_number = jnp.where(member, before, -1.0).reshape(group_rows * token_rows, E)
    slot_number = place_first(slot_number, group_rows, expert_pick)
    mine = slot_number[:, :col_count]
    token_group = jnp.arange(group_rows * token_rows, dtype=jnp.int32) // token_rows
    slot_group = jnp.arange(slot_rows, dtype=jnp.int32) // CAP
    slot_index = (jnp.arange(slot_rows, dtype=jnp.int32) % CAP).astype(wide_type)
    same_group = slot_group[:, None] == token_group[None, :]
    place = same_group[None] & (mine.T[:, None, :] == slot_index[None, :, None])
    place = place.astype(narrow_type).reshape(col_count * slot_rows, -1)
    return ((slot_number >= 0).astype(wide_type), place, place.T)


def place_first(values, group_rows, expert_pick):
    tokens = values.shape[0]
    rolled = jnp.roll(values.reshape(tokens, -1, group_rows), -expert_pick, axis=2)
    return rolled.transpose(0, 2, 1).reshape(tokens, E)


def place_back(values, group_rows, expert_pick):
    tokens = values.shape[0]
    rolled = values.reshape(tokens, group_rows, -1).transpose(0, 2, 1)
    return jnp.roll(rolled, expert_pick, axis=2).reshape(tokens, E)


def body(
    hidden_in, routes, norm_attn, w_qkv, w_out, norm_moe, w_router, w_gate, w_up, w_down, cotangent
):
    row_count = lax.axis_size("row")
    col_count = lax.axis_size("col")
    device_count = row_count * col_count
    row_index = lax.axis_index("row")
    col_index = lax.axis_index("col")
    layer_count = w_qkv.shape[0]
    token_rows = hidden_in.shape[0]
    model_width = hidden_in.shape[1]
    local_experts = w_gate.shape[1]
    slice_width = w_gate.shape[3]
    expert_width = slice_width * row_count
    copies = row_count // local_experts
    expert_pick = row_index // copies
    if copies > 1:
        token_rows_of = [[s + copies * i for i in range(local_experts)] for s in range(copies)]
    else:
        token_rows_of = None
    slot_rows = -(-local_experts * CAP // 16) * 16
    chunks = model_width // 384
    dims = (
        local_experts,
        col_count,
        copies,
        token_rows,
        slot_rows,
        chunks,
        model_width // chunks,
    )
    key_value_width = KEY_VALUE_HEADS * HEAD_SIZE
    positions = col_index * token_rows + jnp.arange(token_rows, dtype=jnp.int32)
    cosine_table, sine_table_rows = rope_angles(positions, HEAD_SIZE // 2)
    score_scale = HEAD_SIZE ** (-0.5)

    def own_tokens(rows):
        return lax.dynamic_slice_in_dim(rows, expert_pick * token_rows, token_rows, axis=0)

    def move_weights(block):
        spread = jnp.repeat(block, copies, axis=0) if copies > 1 else block
        return lax.all_to_all(spread, "row", split_axis=0, concat_axis=0, tiled=True).reshape(
            expert_width, model_width
        )

    def move_grads(full):
        spread = full.astype(narrow_type).reshape(row_count, slice_width, model_width)
        got = lax.all_to_all(spread, "row", split_axis=0, concat_axis=0, tiled=True)
        got = got.astype(wide_type)
        if copies > 1:
            got = jnp.sum(
                got.reshape(local_experts, copies, slice_width, model_width), axis=1
            )
        return got

    router_t = lax.all_gather(w_router.transpose(0, 2, 1), "row", axis=2, tiled=True)
    routers = [place_first(router_t[index].T, local_experts, expert_pick).T for index in range(layer_count)]
    routes_all = lax.all_gather(routes, "row", axis=0, axis_index_groups=token_rows_of)
    hidden = hidden_in.astype(wide_type)
    saved = []
    for layer_index in range(layer_count):
        layer_state = {}
        gain_attn = norm_attn[layer_index].astype(wide_type)
        gain_moe = norm_moe[layer_index].astype(wide_type)
        if layer_index == 0:
            qkv_full, out_full = gather_dense(
                row_count, col_count, w_qkv[layer_index], w_out[layer_index].T
            )
            out_full = out_full.transpose(0, 2, 1).reshape(QUERY_FEATURES, model_width)
        else:
            qkv_full = to_full(
                lax.all_gather(w_qkv[layer_index][None], ("row", "col"), axis=0, tiled=True),
                row_count,
                col_count,
            )
            out_full = to_full(
                lax.all_gather(w_out[layer_index][None], ("row", "col"), axis=0, tiled=True),
                row_count,
                col_count,
            )
        dense = (qkv_full, out_full)
        gate_full = move_weights(w_gate[layer_index].transpose(0, 2, 1))
        up_full = move_weights(w_up[layer_index].transpose(0, 2, 1))
        down_full = move_weights(w_down[layer_index])
        normed, inverse_attn = rms_parts(hidden, gain_attn)
        normed_b = normed.astype(narrow_type)
        projected_rows = jnp.dot(normed_b, dense[0], preferred_element_type=wide_type)
        queries_b = rotate_heads(
            projected_rows[:, :QUERY_FEATURES].reshape(token_rows, QUERY_HEADS, HEAD_SIZE),
            cosine_table,
            sine_table_rows,
            1.0,
        ).astype(narrow_type)
        keys_b = (
            rotate_heads(
                projected_rows[:, QUERY_FEATURES : QUERY_FEATURES + key_value_width].reshape(
                    token_rows, KEY_VALUE_HEADS, HEAD_SIZE
                ),
                cosine_table,
                sine_table_rows,
                1.0,
            )
            .reshape(token_rows, key_value_width)
            .astype(narrow_type)
        )
        kv_local = jnp.concatenate(
            [keys_b, projected_rows[:, QUERY_FEATURES + key_value_width :].astype(narrow_type)],
            axis=1,
        )
        key_value_full = fetch_keys(kv_local)
        key_value_t = key_value_full.T
        attended_b, log_sums = attend_forward(
            queries_b.reshape(token_rows, QUERY_FEATURES),
            key_value_full,
            key_value_t[key_value_width:],
            score_scale,
        )
        attn_proj = jnp.dot(attended_b, dense[1], preferred_element_type=wide_type)
        hidden_mid = hidden + attn_proj
        normed_moe, inverse_moe = rms_parts(hidden_mid, gain_moe)
        normed_moe_b = normed_moe.astype(narrow_type)
        member, place, place_t = layer_routing(routes_all[:, layer_index], dims, expert_pick)
        mixed, gates, slot_inputs, returned = moe_forward(
            dims,
            normed_moe_b,
            place,
            place_t,
            member,
            routers[layer_index],
            gate_full,
            up_full,
            down_full,
        )
        hidden_next = hidden_mid + mixed
        layer_state["dense"] = dense
        layer_state["experts"] = (gate_full, up_full, down_full)
        layer_state["hidden"] = hidden
        layer_state["normed"] = normed_b
        layer_state["inverse_attn"] = inverse_attn
        layer_state["queries"] = queries_b
        layer_state["key_value"] = (key_value_full, key_value_t[:key_value_width])
        layer_state["log_sums"] = log_sums
        layer_state["attended"] = attended_b
        layer_state["hidden_mid"] = hidden_mid
        layer_state["inverse_moe"] = inverse_moe
        layer_state["normed_moe"] = normed_moe_b
        layer_state["gates"] = gates
        layer_state["place"] = (place, place_t)
        layer_state["slot_inputs"] = slot_inputs
        layer_state["returned"] = returned
        saved.append(layer_state)
        hidden = hidden_next
    incoming = cotangent.astype(wide_type)
    dense_results = [None] * layer_count
    small_results = [None] * layer_count
    expert_results = [None] * layer_count
    for layer_index in reversed(range(layer_count)):
        layer_state = saved[layer_index]
        gain_attn = norm_attn[layer_index].astype(wide_type)
        gain_moe = norm_moe[layer_index].astype(wide_type)
        dense = layer_state["dense"]
        gate_full, up_full, down_full = layer_state["experts"]
        key_value_full, key_t = layer_state["key_value"]
        slot_inputs = layer_state["slot_inputs"]
        place, place_t = layer_state["place"]
        (
            grad_tokens,
            grad_pair,
            activated_b,
            grad_gate_b,
            grad_up_b,
            grad_received,
        ) = moe_backward(
            dims,
            incoming.astype(narrow_type),
            place,
            place_t,
            layer_state["gates"],
            slot_inputs,
            layer_state["returned"],
            gate_full,
            up_full,
            down_full,
        )
        gates = place_back(own_tokens(layer_state["gates"]), local_experts, expert_pick)
        places = (expert_pick - jnp.arange(local_experts)) % local_experts
        grad_pair = jnp.take(grad_pair[:, :, :col_count], places, axis=0)
        grad_pair = grad_pair.transpose(1, 2, 0).reshape(token_rows, E)
        expert_results[layer_index] = (
            move_grads(
                jnp.einsum(
                    "cf,cd->fd", grad_gate_b, slot_inputs, preferred_element_type=wide_type
                )
            ).transpose(0, 2, 1),
            move_grads(
                jnp.einsum("cf,cd->fd", grad_up_b, slot_inputs, preferred_element_type=wide_type)
            ).transpose(0, 2, 1),
            move_grads(
                jnp.einsum(
                    "cf,cd->fd", activated_b, grad_received, preferred_element_type=wide_type
                )
            ),
        )
        grad_logits = gates * (grad_pair - jnp.sum(gates * grad_pair, axis=-1, keepdims=True))
        grad_logits_high = grad_logits.astype(narrow_type)
        grad_normed_moe = grad_tokens + jnp.dot(
            grad_logits_high, router_t[layer_index], preferred_element_type=wide_type
        )
        grad_router = jnp.einsum(
            "td,te->de",
            layer_state["normed_moe"],
            grad_logits_high,
            preferred_element_type=wide_type,
        )
        grad_mid_norm, grad_gain_moe = rms_backward(
            layer_state["hidden_mid"], layer_state["inverse_moe"], gain_moe, grad_normed_moe
        )
        grad_mid = incoming + grad_mid_norm
        grad_attn_b = grad_mid.astype(narrow_type)
        grad_attended_b = jnp.einsum(
            "td,ad->ta", grad_attn_b, dense[1], preferred_element_type=wide_type
        ).astype(narrow_type)
        inner = jnp.sum(
            (grad_attended_b.astype(wide_type) * layer_state["attended"].astype(wide_type)).reshape(
                token_rows, QUERY_HEADS, HEAD_SIZE
            ),
            axis=-1,
        ).T[:, None, :]
        grad_queries, grad_kv_full = attend_backward(
            layer_state["queries"].reshape(token_rows, QUERY_FEATURES),
            key_value_full,
            key_t,
            score_scale,
            layer_state["log_sums"],
            inner,
            grad_attended_b,
        )
        grad_queries = grad_queries.reshape(token_rows, QUERY_HEADS, HEAD_SIZE).astype(wide_type)
        key_value_gradient = lax.psum_scatter(
            grad_kv_full, "col", scatter_dimension=0, tiled=True
        ).astype(wide_type)
        grad_queries = rotate_heads(grad_queries, cosine_table, sine_table_rows, -1.0).reshape(
            token_rows, QUERY_FEATURES
        )
        grad_keys = rotate_heads(
            key_value_gradient[:, :key_value_width].reshape(token_rows, KEY_VALUE_HEADS, HEAD_SIZE),
            cosine_table,
            sine_table_rows,
            -1.0,
        ).reshape(token_rows, key_value_width)
        grad_projected = jnp.concatenate(
            [grad_queries, grad_keys, key_value_gradient[:, key_value_width:]], axis=1
        ).astype(narrow_type)
        grad_normed = jnp.einsum(
            "tq,dq->td", grad_projected, dense[0], preferred_element_type=wide_type
        )
        grad_hidden_norm, grad_gain_attn = rms_backward(
            layer_state["hidden"], layer_state["inverse_attn"], gain_attn, grad_normed
        )
        incoming = grad_mid + grad_hidden_norm
        small = jnp.concatenate(
            [grad_router, grad_gain_attn[:, None], grad_gain_moe[:, None]], axis=1
        ).astype(narrow_type)
        small = small.reshape(device_count, -1)
        small_size = small.shape[1]
        small_rows = -(-small_size // 2048) * 16
        small = jnp.pad(small, ((0, 0), (0, small_rows * 128 - small_size)))
        small = small.reshape(row_count, col_count, small_rows, 128).transpose(1, 0, 2, 3)
        grad_qkv_block, grad_out_block, small = reduce_dense(
            row_count,
            col_count,
            layer_state["normed"],
            grad_projected,
            grad_attn_b,
            layer_state["attended"],
            small,
        )
        dense_results[layer_index] = (grad_qkv_block, grad_out_block.T)
        small_results[layer_index] = small.reshape(-1)[:small_size].reshape(-1, E + 2)
    small = jnp.stack(small_results)
    grad_router_all = small[:, :, :E]
    grad_norm_attn = small[:, :, E]
    grad_norm_moe = small[:, :, E + 1]
    grad_qkv = jnp.stack([dense_results[index][0] for index in range(layer_count)])
    grad_out = jnp.stack([dense_results[index][1] for index in range(layer_count)])
    grad_gate = jnp.stack([expert_results[index][0] for index in range(layer_count)])
    grad_up = jnp.stack([expert_results[index][1] for index in range(layer_count)])
    grad_down = jnp.stack([expert_results[index][2] for index in range(layer_count)])
    return (
        hidden,
        incoming,
        grad_norm_attn,
        grad_qkv,
        grad_out,
        grad_norm_moe,
        grad_router_all,
        grad_gate,
        grad_up,
        grad_down,
    )


def solution(mesh):
    in_specs = (
        P(("row", "col"), None),
        P(None, ("row", "col"), None),
        P(),
        P(None, "row", "col"),
        P(None, "row", "col"),
        P(),
        P(None, "row", None),
        P(None, "col", None, "row"),
        P(None, "col", None, "row"),
        P(None, "col", "row", None),
        P(("row", "col"), None),
    )
    out_specs = (
        P(("row", "col"), None),
        P(("row", "col"), None),
        P(None, ("row", "col")),
        P(None, "row", "col"),
        P(None, "row", "col"),
        P(None, ("row", "col")),
        P(None, ("row", "col"), None),
        P(None, "col", None, "row"),
        P(None, "col", None, "row"),
        P(None, "col", "row", None),
    )
    return jax.shard_map(body, mesh=mesh, in_specs=in_specs, out_specs=out_specs, check_vma=False)
```

```python
import functools

import jax
import jax.numpy as jnp
from jax import lax
from jax.experimental import pallas as pl
from jax.experimental.pallas import tpu as pltpu
from jax.sharding import PartitionSpec as P

QUERY_HEADS = 12
KEY_VALUE_HEADS = 2
HEAD_SIZE = 128
E = 32
TOPK = 4
BLOCK = 256
QUERY_FEATURES = 1536
CAP = 36


eps_norm = 1e-06
rope_base = 1000000.0
masked_score = -1e30
wide_type = jnp.float32
narrow_type = jnp.bfloat16


def rope_angles(positions, half_dim):
    frequency = rope_base ** (-jnp.arange(half_dim, dtype=jnp.float32) / half_dim)
    angles = positions.astype(jnp.float32)[:, None] * frequency[None, :]
    return (jnp.cos(angles), jnp.sin(angles))


def split_rows(total, most):
    best = 16
    for step in range(16, most + 1, 16):
        if total % step == 0:
            best = step
    return best


def over_blocks(total, block, step):
    def run(index, carry):
        step(pl.ds(pl.multiple_of(index * block, block), block))
        return carry

    lax.fori_loop(0, total // block, run, 0)


def over_chunks(chunks, width, step):
    def run(index, carry):
        step(index, pl.ds(pl.multiple_of(index * width, width), width))
        return carry

    lax.fori_loop(0, chunks, run, 0)


def dot_nt(left, right):
    return lax.dot_general(
        left, right, (((1,), (1,)), ((), ())), preferred_element_type=jnp.float32
    )


def dot_nn(left, right):
    return jnp.dot(left, right, preferred_element_type=jnp.float32)


class Peers:
    def __init__(self, count, place, device_of):
        self.count = count
        self.place = place
        self.device_of = device_of

    def ahead(self, step):
        return lax.rem(self.place + step, self.count)

    def behind(self, step):
        return lax.rem(self.place + self.count - step, self.count)


def expert_peers(col_count, copies, group_rows):
    row_index = lax.axis_index("row")
    share = lax.rem(row_index, copies)
    rows = Peers(group_rows, row_index // copies, lambda place: {"row": share + copies * place})
    return rows, col_peers(col_count)


def col_peers(col_count):
    return Peers(col_count, lax.axis_index("col"), lambda place: {"col": place})


def greet(groups):
    barrier = pltpu.get_barrier_semaphore()
    total = 0
    for peers in groups:
        for step in range(1, peers.count):
            pl.semaphore_signal(
                barrier,
                inc=1,
                device_id=peers.device_of(peers.ahead(step)),
                device_id_type=pl.DeviceIdType.MESH,
            )
            total += 1
    pl.semaphore_wait(barrier, total)


def send_to(source, target, sems, number, device):
    send_sems, recv_sems = sems
    return pltpu.make_async_remote_copy(
        src_ref=source,
        dst_ref=target,
        send_sem=send_sems.at[number],
        recv_sem=recv_sems.at[number],
        device_id=device,
        device_id_type=pl.DeviceIdType.MESH,
    )


class Exchange:
    def __init__(self, peers, send_sems, recv_sems, source, target):
        self.peers = peers
        self.sems = (send_sems, recv_sems)
        self.source = source
        self.target = target

    def out(self, step, index, chunk):
        place = self.peers.ahead(step)
        return send_to(
            self.source(place, chunk),
            self.target(self.peers.place, step, chunk),
            self.sems,
            (index, step - 1),
            self.peers.device_of(place),
        )

    def start(self, index, chunk):
        for step in range(1, self.peers.count):
            self.out(step, index, chunk).start()

    def wait_send(self, index, chunk):
        for step in range(1, self.peers.count):
            self.out(step, index, chunk).wait_send()

    def wait_recv(self, index, chunk):
        for step in range(1, self.peers.count):
            place = self.peers.behind(step)
            landed = self.target(place, step, chunk)
            send_to(
                landed, landed, self.sems, (index, step - 1), self.peers.device_of(place)
            ).wait_recv()


def exchange_sems(chunks, count):
    return [pltpu.SemaphoreType.DMA((chunks, max(count - 1, 1))) for _ in range(2)]


def iota(shape, axis):
    return lax.broadcasted_iota(jnp.int32, shape, axis)


def within(numbers, size, count):
    block = jnp.zeros_like(numbers)
    for index in range(1, count):
        block = block + (numbers >= index * size).astype(jnp.int32)
    return block, numbers - block * size


def slot_block(shape, slot_axis, slot_rows):
    slots = iota(shape, slot_axis)
    block = iota(shape, 1 - slot_axis)
    return (slots >= block * slot_rows) & (slots < (block + 1) * slot_rows)


def build_places(dims, rows, routes_ref, place, place_t, member):
    group_rows, col_count, copies, token_rows, slot_rows, chunks, width = dims
    all_slots = col_count * slot_rows
    number = iota((E, 1), 0)
    ahead, col = within(number, col_count, group_rows)
    owner = ahead + rows.place
    owner = jnp.where(owner >= group_rows, owner - group_rows, owner)
    expert = col * group_rows + owner
    earlier = (iota((token_rows, token_rows), 0) < iota((token_rows, token_rows), 1)).astype(
        jnp.bfloat16
    )
    pick = slot_block((E, all_slots), 1, slot_rows).astype(jnp.bfloat16)
    column = iota((slot_rows, 1), 0)
    lane = within(iota((1, all_slots), 1), slot_rows, col_count)[1]
    for group in range(group_rows):
        tokens = slice(group * token_rows, (group + 1) * token_rows)
        picked = routes_ref[group]
        has = picked[0:1, :] == expert
        for choice in range(1, TOPK):
            has = has | (picked[choice : choice + 1, :] == expert)
        before = dot_nn(has.astype(jnp.float32).astype(jnp.bfloat16), earlier)
        slot_number = jnp.where(has, before, -1.0)
        in_group = (column >= group * CAP) & (column < (group + 1) * CAP)
        wanted = jnp.where(in_group, column - group * CAP, -2).astype(jnp.float32)
        for index in range(col_count):
            slots = slice(index * slot_rows, (index + 1) * slot_rows)
            hit = slot_number[index : index + 1, :] == wanted
            place[slots, tokens] = jnp.where(hit, 1.0, 0.0).astype(jnp.bfloat16)
        turned = slot_number.T
        in_group = (lane >= group * CAP) & (lane < (group + 1) * CAP)
        wanted = jnp.where(in_group, lane - group * CAP, -2).astype(jnp.float32)
        hit = dot_nn(turned.astype(jnp.bfloat16), pick) == wanted
        place_t[tokens, :] = jnp.where(hit, 1.0, 0.0).astype(jnp.bfloat16)
        if member is not None:
            member[tokens, :] = turned


class WeightMove:
    def __init__(self, rows, copies, layer, shards, target, sems):
        self.rows = rows
        self.copies = copies
        self.layer = layer
        self.shards = shards
        self.target = target
        self.remote_sems = sems[:2]
        self.local_sem = sems[2]

    @staticmethod
    def sems(row_count):
        return [pltpu.SemaphoreType.DMA((max(row_count - 1, 1),))] * 2 + [pltpu.SemaphoreType.DMA]

    def shard(self, place):
        return self.shards.at[self.layer, place // self.copies]

    def own(self):
        return pltpu.make_async_copy(
            self.shard(self.rows.place), self.target.at[0], self.local_sem
        )

    def out(self, step):
        place = self.rows.ahead(step)
        return send_to(
            self.shard(place),
            self.target.at[step],
            self.remote_sems,
            step - 1,
            self.rows.device_of(place),
        )

    def start(self):
        for step in range(1, self.rows.count):
            self.out(step).start()
        self.own().start()

    def wait_recv(self):
        self.own().wait()
        for step in range(1, self.rows.count):
            landed = self.target.at[step]
            place = self.rows.behind(step)
            send_to(
                landed, landed, self.remote_sems, step - 1, self.rows.device_of(place)
            ).wait_recv()

    def wait_send(self):
        for step in range(1, self.rows.count):
            self.out(step).wait_send()


def all_rows(row_count):
    return Peers(row_count, lax.axis_index("row"), lambda place: {"row": place})


def moved_shape(row_count, shards):
    return jax.ShapeDtypeStruct((row_count, *shards.shape[2:]), shards.dtype)


vmem_most = 62 * 1024 * 1024
long_cost = pl.CostEstimate(flops=0, bytes_accessed=600 * 1024 * 1024, transcendentals=0)
no_cost = pl.CostEstimate(flops=0, bytes_accessed=0, transcendentals=0)


def moe_forward_kernel(dims, row_count, layer, moving, gather_dims, *refs):
    group_rows, col_count, copies, token_rows, slot_rows, chunks, width = dims
    own_ref, routes_ref, router_ref = refs[:3]
    weight_in = refs[3:6]
    refs = refs[6:]
    next_blocks = refs[: 2 if gather_dims else 0]
    refs = refs[len(next_blocks) :]
    sum_ref, gates_ref, slots_out, returned_out = refs[:4]
    refs = refs[4:]
    moved_out = refs[: len(moving)]
    refs = refs[len(moving) :]
    next_full = refs[: len(next_blocks)]
    refs = refs[len(next_blocks) :]
    dense = None
    if gather_dims:
        count = len(DenseGather.sems(gather_dims, 2))
        dense = DenseGather(gather_dims, next_blocks, next_full, refs[-count:])
        refs = refs[:-count]
    move_sems = refs[len(refs) - 3 * len(moving) :]
    refs = refs[: len(refs) - 3 * len(moving)]
    (
        place,
        place_t,
        member,
        gate,
        up,
        down,
        tokens,
        send,
        slots,
        gate_val,
        up_val,
        act,
        returned,
        landed,
        row_send,
        row_recv,
        there_send,
        there_recv,
        back_send,
        back_recv,
        home_send,
        home_recv,
        local_sem,
    ) = refs
    all_tokens = group_rows * token_rows
    all_slots = col_count * slot_rows
    slot_step = split_rows(all_slots, 320)
    rows, cols = expert_peers(col_count, copies, group_rows)

    def token_part(place):
        return pl.ds(pl.multiple_of(place * token_rows, token_rows), token_rows)

    def slot_part(place):
        return pl.ds(pl.multiple_of(place * slot_rows, slot_rows), slot_rows)

    gather = Exchange(
        rows,
        row_send,
        row_recv,
        lambda place, chunk: own_ref.at[:, chunk],
        lambda place, step, chunk: tokens.at[token_part(place), chunk],
    )
    there = Exchange(
        cols,
        there_send,
        there_recv,
        lambda place, chunk: send.at[slot_part(place), chunk],
        lambda place, step, chunk: slots.at[slot_part(place), chunk],
    )
    back = Exchange(
        cols,
        back_send,
        back_recv,
        lambda place, chunk: send.at[slot_part(place), chunk],
        lambda place, step, chunk: returned.at[slot_part(place), chunk],
    )
    home = Exchange(
        rows,
        home_send,
        home_recv,
        lambda place, chunk: tokens.at[token_part(place), chunk],
        lambda place, step, chunk: landed.at[step - 1, :, chunk],
    )
    weights = (gate, up, down)
    moves = {
        kind: WeightMove(
            all_rows(row_count),
            copies,
            layer,
            weight_in[kind],
            weights[kind],
            move_sems[3 * number : 3 * number + 3],
        )
        for number, kind in enumerate(moving)
    }
    loads = {
        kind: pltpu.make_async_copy(weight_in[kind], weights[kind], local_sem.at[2 + kind])
        for kind in range(3)
        if kind not in moving
    }
    keeps = []

    def weight_ready(kind):
        if kind in loads:
            loads[kind].wait()
        else:
            moves[kind].wait_recv()
            keep = pltpu.make_async_copy(
                weights[kind], moved_out[moving.index(kind)], local_sem.at[2 + kind]
            )
            keep.start()
            keeps.append(keep)

    def weight(kind, chunk):
        return weights[kind][:, :, chunk].reshape(-1, width)

    greet((all_rows(row_count), cols))
    over_chunks(chunks, width, gather.start)
    for kind in moving:
        moves[kind].start()
    if dense:
        for kind in dense.kinds:
            dense.start(kind)
    for copy in loads.values():
        copy.start()
    tokens[token_part(rows.place), :] = own_ref[...]
    build_places(dims, rows, routes_ref, place, place_t, member)

    def dispatch(index, chunk):
        gather.wait_recv(index, chunk)

        def rows_of(part):
            send[part, chunk] = dot_nn(place[part, :], tokens[:, chunk]).astype(jnp.bfloat16)

        over_blocks(all_slots, slot_step, rows_of)
        there.start(index, chunk)
        slots[slot_part(cols.place), chunk] = send[slot_part(cols.place), chunk]

    over_chunks(chunks, width, dispatch)

    def gating(part):
        chosen = member[part, :] >= 0
        logits = jnp.where(chosen, dot_nt(tokens[part, :], router_ref[...]), masked_score)
        peak = jnp.max(logits, axis=-1, keepdims=True)
        exponent = jnp.where(chosen, jnp.exp(logits - peak), 0.0)
        gates = exponent / jnp.sum(exponent, axis=-1, keepdims=True)
        gates_ref[part, :] = gates
        pick = slot_block((E, all_slots), 1, slot_rows).astype(jnp.bfloat16)
        spread = dot_nn(gates.astype(jnp.bfloat16), pick)
        place_t[part, :] = (place_t[part, :].astype(jnp.float32) * spread).astype(jnp.bfloat16)

    over_blocks(all_tokens, token_rows, gating)

    def project(kind, target, wait, index, chunk):
        if wait:
            there.wait_recv(index, chunk)

        def rows_of(part):
            value = dot_nt(slots[part, chunk], weight(kind, chunk))

            @pl.when(index == 0)
            def _():
                target[part, :] = value

            @pl.when(index > 0)
            def _():
                target[part, :] += value

        over_blocks(all_slots, slot_step, rows_of)

    weight_ready(0)
    over_chunks(chunks, width, functools.partial(project, 0, gate_val, True))
    weight_ready(1)
    over_chunks(chunks, width, functools.partial(project, 1, up_val, False))
    keep_slots = pltpu.make_async_copy(slots, slots_out, local_sem.at[0])
    keep_slots.start()

    def activate(part):
        value = gate_val[part, :]
        act[part, :] = (value * jax.nn.sigmoid(value) * up_val[part, :]).astype(jnp.bfloat16)

    over_blocks(all_slots, slot_step, activate)
    weight_ready(2)

    def give_back(index, chunk):
        there.wait_send(index, chunk)

        def rows_of(part):
            send[part, chunk] = dot_nn(act[part, :], weight(2, chunk)).astype(jnp.bfloat16)

        over_blocks(all_slots, slot_step, rows_of)
        back.start(index, chunk)
        returned[slot_part(cols.place), chunk] = send[slot_part(cols.place), chunk]

    over_chunks(chunks, width, give_back)

    def combine(index, chunk):
        back.wait_recv(index, chunk)

        def rows_of(part):
            tokens[part, chunk] = dot_nn(place_t[part, :], returned[:, chunk]).astype(jnp.bfloat16)

        over_blocks(all_tokens, token_rows, rows_of)
        home.start(index, chunk)

    over_chunks(chunks, width, combine)
    keep_returned = pltpu.make_async_copy(returned, returned_out, local_sem.at[1])
    keep_returned.start()
    if dense:
        for kind in dense.kinds:
            dense.pass_rows(kind)

    def finish(index, chunk):
        home.wait_recv(index, chunk)
        total = tokens[token_part(rows.place), chunk].astype(jnp.float32)
        for step in range(1, group_rows):
            total = total + landed[step - 1, :, chunk].astype(jnp.float32)
        sum_ref[:, chunk] = total

    over_chunks(chunks, width, finish)

    def drain(index, chunk):
        gather.wait_send(index, chunk)
        back.wait_send(index, chunk)
        home.wait_send(index, chunk)

    over_chunks(chunks, width, drain)
    if dense:
        for kind in dense.kinds:
            dense.pass_pairs(kind)
        for kind in dense.kinds:
            dense.finish(kind)
    for kind in moving:
        moves[kind].wait_send()
    keep_slots.wait()
    keep_returned.wait()
    for keep in keeps:
        keep.wait()


def moe_backward_kernel(dims, *refs):
    group_rows, col_count, copies, token_rows, slot_rows, chunks, width = dims
    own_ref, routes_ref, router_ref, gates_ref, normed_ref, slots_in, returned_in = refs[:7]
    weight_in = refs[7:10]
    sum_ref, router_grad_ref, grads_out = refs[10:13]
    (
        place,
        place_t,
        gate,
        up,
        down,
        tokens,
        send,
        slots,
        slope,
        silu,
        act,
        weight,
        inner,
        received,
        grad_act,
        grad_gate,
        grad_up,
        returned,
        turned,
        staged,
        landed,
        pair_send,
        pair_landed,
        row_send,
        row_recv,
        there_send,
        there_recv,
        back_send,
        back_recv,
        home_send,
        home_recv,
        pair_send_sem,
        pair_recv_sem,
        local_sem,
    ) = refs[13:]
    all_tokens = group_rows * token_rows
    all_slots = col_count * slot_rows
    slot_step = split_rows(all_slots, 320)
    block_count, slice_width = weight_in[0].shape[:2]
    rows, cols = expert_peers(col_count, copies, group_rows)

    def token_part(place):
        return pl.ds(pl.multiple_of(place * token_rows, token_rows), token_rows)

    def slot_part(place):
        return pl.ds(pl.multiple_of(place * slot_rows, slot_rows), slot_rows)

    gather = Exchange(
        rows,
        row_send,
        row_recv,
        lambda place, chunk: own_ref.at[:, chunk],
        lambda place, step, chunk: tokens.at[token_part(place), chunk],
    )
    there = Exchange(
        cols,
        there_send,
        there_recv,
        lambda place, chunk: send.at[slot_part(place), chunk],
        lambda place, step, chunk: received.at[slot_part(place), chunk],
    )
    back = Exchange(
        cols,
        back_send,
        back_recv,
        lambda place, chunk: send.at[slot_part(place), chunk],
        lambda place, step, chunk: returned.at[slot_part(place), chunk],
    )
    home = Exchange(
        rows,
        home_send,
        home_recv,
        lambda place, chunk: tokens.at[token_part(place), chunk],
        lambda place, step, chunk: landed.at[step - 1, :, chunk],
    )
    pair = Exchange(
        rows,
        pair_send_sem,
        pair_recv_sem,
        lambda place, chunk: pair_send.at[token_part(place), :],
        lambda place, step, chunk: pair_landed.at[step - 1],
    )
    greet((rows, cols))
    over_chunks(chunks, width, gather.start)
    load_slots = pltpu.make_async_copy(slots_in, slots, local_sem.at[0])
    load_slots.start()
    weights = (gate, up, down)
    loads = [
        pltpu.make_async_copy(weight_in[kind], weights[kind], local_sem.at[4 + kind])
        for kind in range(3)
    ]
    for copy in loads:
        copy.start()

    def weight_part(kind, chunk):
        return weights[kind][:, :, chunk].reshape(block_count * slice_width, width)

    load_returned = pltpu.make_async_copy(returned_in, returned, local_sem.at[1])
    load_returned.start()
    tokens[token_part(rows.place), :] = own_ref[...]
    build_places(dims, rows, routes_ref, place, place_t, None)
    load_slots.wait()
    for copy in loads:
        copy.wait()

    def recompute(part):
        gate_val = dot_nt(slots[part, :], gate[...].reshape(-1, gate.shape[2]))
        up_val = dot_nt(slots[part, :], up[...].reshape(-1, up.shape[2]))
        sigmoid = jax.nn.sigmoid(gate_val)
        value = gate_val * sigmoid
        act[part, :] = (value * up_val).astype(jnp.bfloat16)
        silu[part, :] = value.astype(jnp.bfloat16)
        slope[part, :] = (up_val * sigmoid * (1.0 + gate_val * (1.0 - sigmoid))).astype(
            jnp.bfloat16
        )
        picked = dot_nn(place[part, :], gates_ref[...].astype(jnp.bfloat16))
        block = iota(picked.shape, 1)
        slot = iota(picked.shape, 0) + part.start
        in_block = (slot >= block * slot_rows) & (slot < (block + 1) * slot_rows)
        weight[part, :] = jnp.sum(jnp.where(in_block, picked, 0.0), axis=1, keepdims=True)

    over_blocks(all_slots, slot_step, recompute)
    load_returned.wait()

    def dispatch(index, chunk):
        gather.wait_recv(index, chunk)

        def rows_of(part):
            grad = dot_nn(place[part, :], tokens[:, chunk])
            share = jnp.sum(
                grad * returned[part, chunk].astype(jnp.float32), axis=1, keepdims=True
            )
            send[part, chunk] = (weight[part, :] * grad).astype(jnp.bfloat16)

            @pl.when(index == 0)
            def _():
                inner[part, :] = share

            @pl.when(index > 0)
            def _():
                inner[part, :] += share

        over_blocks(all_slots, slot_step, rows_of)
        there.start(index, chunk)
        received[slot_part(cols.place), chunk] = send[slot_part(cols.place), chunk]

    over_chunks(chunks, width, dispatch)

    def pairs(part):
        picked = slot_block((all_slots, pair_send.shape[1]), 0, slot_rows)
        spread = jnp.where(picked, inner[...], 0.0)
        high = spread.astype(jnp.bfloat16)
        low = (spread - high.astype(jnp.float32)).astype(jnp.bfloat16)
        pair_send[part, :] = dot_nn(place_t[part, :], high) + dot_nn(place_t[part, :], low)

    over_blocks(all_tokens, token_rows, pairs)
    pair.start(0, None)

    def project(index, chunk):
        there.wait_recv(index, chunk)

        def rows_of(part):
            grad = dot_nt(received[part, chunk], weight_part(2, chunk))

            @pl.when(index == 0)
            def _():
                grad_act[part, :] = grad

            @pl.when(index > 0)
            def _():
                grad_act[part, :] += grad

        over_blocks(all_slots, slot_step, rows_of)

    over_chunks(chunks, width, project)

    def slopes(part):
        grad = grad_act[part, :]
        grad_gate[part, :] = (grad * slope[part, :].astype(jnp.float32)).astype(jnp.bfloat16)
        grad_up[part, :] = (grad * silu[part, :].astype(jnp.float32)).astype(jnp.bfloat16)

    over_blocks(all_slots, slot_step, slopes)

    def give_back(index, chunk):
        there.wait_send(index, chunk)

        def rows_of(part):
            send[part, chunk] = (
                dot_nn(grad_gate[part, :], weight_part(0, chunk))
                + dot_nn(grad_up[part, :], weight_part(1, chunk))
            ).astype(jnp.bfloat16)

        over_blocks(all_slots, slot_step, rows_of)
        back.start(index, chunk)

    over_chunks(chunks, width, give_back)

    def keep(kind, index):
        return pltpu.make_async_copy(
            staged.at[lax.rem(index, 2)],
            grads_out.at[index, kind],
            local_sem.at[2 + lax.rem(index, 2)],
        )

    for kind, (left, right) in enumerate(
        ((grad_gate, slots), (grad_up, slots), (act, received))
    ):
        turned[...] = left[...].T

        def one_slice(index, carry, kind=kind, right=right):
            @pl.when(index >= 2)
            def _():
                keep(kind, index - 2).wait()

            part = pl.ds(pl.multiple_of(index * slice_width, slice_width), slice_width)
            staged[lax.rem(index, 2)] = dot_nn(turned[part, :], right[...]).astype(jnp.bfloat16)
            keep(kind, index).start()
            return carry

        lax.fori_loop(0, block_count, one_slice, 0)
        for index in range(max(block_count - 2, 0), block_count):
            keep(kind, index).wait()

    returned[slot_part(cols.place), :] = send[slot_part(cols.place), :]

    def combine(index, chunk):
        back.wait_recv(index, chunk)

        def rows_of(part):
            tokens[part, chunk] = dot_nn(place_t[part, :], returned[:, chunk]).astype(jnp.bfloat16)

        over_blocks(all_tokens, token_rows, rows_of)
        home.start(index, chunk)

    over_chunks(chunks, width, combine)
    pair.wait_recv(0, None)
    grad_pair = pair_send[token_part(rows.place), :]
    for ahead in range(1, group_rows):
        shifted = pltpu.roll(pair_landed[group_rows - ahead - 1], ahead * col_count, 1)
        grad_pair = grad_pair + shifted
    grad_pair = grad_pair[:, :E]
    gates = gates_ref[token_part(rows.place), :]
    grad_logits = gates * (grad_pair - jnp.sum(gates * grad_pair, axis=-1, keepdims=True))
    grad_logits = grad_logits.astype(jnp.bfloat16)
    router_grad_ref[...] = dot_nn(grad_logits.astype(jnp.float32).T.astype(jnp.bfloat16), normed_ref[...])

    def finish(index, chunk):
        home.wait_recv(index, chunk)
        total = tokens[token_part(rows.place), chunk].astype(jnp.float32)
        for step in range(1, group_rows):
            total = total + landed[step - 1, :, chunk].astype(jnp.float32)
        sum_ref[:, chunk] = total + dot_nn(grad_logits, router_ref[:, chunk])

    over_chunks(chunks, width, finish)

    def drain(index, chunk):
        gather.wait_send(index, chunk)
        back.wait_send(index, chunk)
        home.wait_send(index, chunk)

    over_chunks(chunks, width, drain)
    pair.wait_send(0, None)


def moe_forward(dims, row_count, layer, own, routes, router, weights, moving, next_blocks):
    group_rows, col_count, copies, token_rows, slot_rows, chunks, width = dims
    all_tokens, all_slots = group_rows * token_rows, col_count * slot_rows
    model_width = own.shape[1]
    slice_width = weights[0].shape[-2]
    hidden = row_count * slice_width
    gather_dims = (row_count, col_count // 2) if next_blocks else None
    dense_sems = DenseGather.sems(gather_dims, 2) if next_blocks else []
    vmem = pl.BlockSpec(memory_space=pltpu.VMEM)
    outside = pl.BlockSpec(memory_space=pl.ANY)
    slot_array = pltpu.VMEM((all_slots, model_width), jnp.bfloat16)
    hidden_wide = pltpu.VMEM((all_slots, hidden), jnp.float32)
    weight_array = pltpu.VMEM((row_count, slice_width, model_width), jnp.bfloat16)
    return pl.pallas_call(
        functools.partial(
            moe_forward_kernel, dims, row_count, layer, moving, gather_dims
        ),
        out_shape=(
            jax.ShapeDtypeStruct((token_rows, model_width), jnp.float32),
            jax.ShapeDtypeStruct((all_tokens, E), jnp.float32),
            jax.ShapeDtypeStruct((all_slots, model_width), jnp.bfloat16),
            jax.ShapeDtypeStruct((all_slots, model_width), jnp.bfloat16),
            *(moved_shape(row_count, weights[kind]) for kind in moving),
            *(gathered_shapes(gather_dims, next_blocks) if next_blocks else ()),
        ),
        in_specs=[vmem] * 3 + [outside] * (3 + len(next_blocks)),
        out_specs=(vmem, vmem) + (outside,) * (2 + len(moving) + len(next_blocks)),
        scratch_shapes=[
            pltpu.VMEM((all_slots, all_tokens), jnp.bfloat16),
            pltpu.VMEM((all_tokens, all_slots), jnp.bfloat16),
            pltpu.VMEM((all_tokens, E), jnp.float32),
            weight_array,
            weight_array,
            weight_array,
            pltpu.VMEM((all_tokens, model_width), jnp.bfloat16),
            slot_array,
            slot_array,
            hidden_wide,
            hidden_wide,
            pltpu.VMEM((all_slots, hidden), jnp.bfloat16),
            slot_array,
            pltpu.VMEM((max(group_rows - 1, 1), token_rows, model_width), jnp.bfloat16),
            *exchange_sems(chunks, group_rows),
            *exchange_sems(chunks, col_count),
            *exchange_sems(chunks, col_count),
            *exchange_sems(chunks, group_rows),
            pltpu.SemaphoreType.DMA((5,)),
            *(WeightMove.sems(row_count) * len(moving)),
            *dense_sems,
        ],
        compiler_params=pltpu.CompilerParams(
            collective_id=1 + 7 * layer, has_side_effects=True, vmem_limit_bytes=vmem_most
        ),
        cost_estimate=long_cost,
        name="moe_forward",
    )(own, routes, router, *weights, *next_blocks)


def moe_backward(dims, own, routes, router, gates, normed, slots, returned, weights):
    group_rows, col_count, copies, token_rows, slot_rows, chunks, width = dims
    all_tokens, all_slots = group_rows * token_rows, col_count * slot_rows
    model_width = own.shape[1]
    block_count, slice_width = weights[0].shape[:2]
    hidden = block_count * slice_width
    vmem = pl.BlockSpec(memory_space=pltpu.VMEM)
    outside = pl.BlockSpec(memory_space=pl.ANY)
    slot_array = pltpu.VMEM((all_slots, model_width), jnp.bfloat16)
    hidden_narrow = pltpu.VMEM((all_slots, hidden), jnp.bfloat16)
    weight_array = pltpu.VMEM((block_count, slice_width, model_width), jnp.bfloat16)
    return pl.pallas_call(
        functools.partial(moe_backward_kernel, dims),
        out_shape=(
            jax.ShapeDtypeStruct((token_rows, model_width), jnp.float32),
            jax.ShapeDtypeStruct((E, model_width), jnp.float32),
            jax.ShapeDtypeStruct((block_count, 3, slice_width, model_width), jnp.bfloat16),
        ),
        in_specs=[vmem] * 5 + [outside] * 5,
        out_specs=(vmem, vmem, outside),
        scratch_shapes=[
            pltpu.VMEM((all_slots, all_tokens), jnp.bfloat16),
            pltpu.VMEM((all_tokens, all_slots), jnp.bfloat16),
            weight_array,
            weight_array,
            weight_array,
            pltpu.VMEM((all_tokens, model_width), jnp.bfloat16),
            slot_array,
            slot_array,
            hidden_narrow,
            hidden_narrow,
            hidden_narrow,
            pltpu.VMEM((all_slots, 1), jnp.float32),
            pltpu.VMEM((all_slots, 1), jnp.float32),
            slot_array,
            pltpu.VMEM((all_slots, hidden), jnp.float32),
            hidden_narrow,
            hidden_narrow,
            slot_array,
            pltpu.VMEM((hidden, all_slots), jnp.bfloat16),
            pltpu.VMEM((2, slice_width, model_width), jnp.bfloat16),
            pltpu.VMEM((max(group_rows - 1, 1), token_rows, model_width), jnp.bfloat16),
            pltpu.VMEM((all_tokens, 128), jnp.float32),
            pltpu.VMEM((max(group_rows - 1, 1), token_rows, 128), jnp.float32),
            *exchange_sems(chunks, group_rows),
            *exchange_sems(chunks, col_count),
            *exchange_sems(chunks, col_count),
            *exchange_sems(chunks, group_rows),
            *exchange_sems(1, group_rows),
            pltpu.SemaphoreType.DMA((7,)),
        ],
        compiler_params=pltpu.CompilerParams(
            collective_id=2, has_side_effects=True, vmem_limit_bytes=vmem_most
        ),
        cost_estimate=long_cost,
        name="moe_backward",
    )(own, routes, router, gates, normed, slots, returned, *weights)


def col_pairs():
    col_index = lax.axis_index("col")
    return col_index // 2, lax.rem(col_index, 2)


def dense_peers(row_count, pair_count):
    row_index = lax.axis_index("row")
    pair, side = col_pairs()
    rows = Peers(row_count, row_index, lambda place: {"row": place})
    pairs = Peers(pair_count, pair, lambda place: {"col": place * 2 + side})
    sides = Peers(2, side, lambda place: {"col": pair * 2 + place})
    return rows, pairs, sides


def reduce_dense_kernel(
    dims,
    normed_ref,
    grad_proj_ref,
    grad_mid_ref,
    attended_ref,
    small_ref,
    qkv_ref,
    out_ref,
    small_out_ref,
    *scratch,
):
    row_count, pair_count = dims
    kinds = 3
    buffers = [scratch[6 * kind : 6 * kind + 6] for kind in range(kinds)]
    sems = scratch[6 * kinds : 12 * kinds]
    normed_t, grad_proj, grad_mid_t, attended = scratch[12 * kinds :]
    side_sems = [(sems[6 * kind], sems[6 * kind + 1]) for kind in range(kinds)]
    pair_sems = [(sems[6 * kind + 2], sems[6 * kind + 3]) for kind in range(kinds)]
    row_sems = [(sems[6 * kind + 4], sems[6 * kind + 5]) for kind in range(kinds)]
    rows, pairs, sides = dense_peers(row_count, pair_count)
    other = 1 - sides.place

    def spread(target, source, turn):
        count = target.shape[0]
        size = source.shape[1] // count
        for index in range(count):
            part = source[:, index * size : (index + 1) * size]
            target[index] = part.T if turn else part

    spread(normed_t, normed_ref, True)
    spread(grad_proj, grad_proj_ref, False)
    spread(grad_mid_t, grad_mid_ref, True)
    spread(attended, attended_ref, False)

    def block(kind, row, pair, side):
        col = pair * 2 + side
        if kind == 0:
            return dot_nn(normed_t[row], grad_proj[col])
        if kind == 1:
            return dot_nn(grad_mid_t[col], attended[row])
        return small_ref[col, row].astype(jnp.float32)

    greet((rows, pairs, sides))
    outputs = (qkv_ref, out_ref, small_out_ref)

    def side_copy(kind, pair):
        side_send, side_recv = buffers[kind][0], buffers[kind][1]
        return send_to(
            side_send.at[pair],
            side_recv.at[pair],
            side_sems[kind],
            pair,
            sides.device_of(other),
        )

    def pair_copy(kind, step, row):
        place = pairs.ahead(step)
        half, pair_recv = buffers[kind][2], buffers[kind][3]
        return send_to(
            half.at[place, row],
            pair_recv.at[step - 1, row],
            pair_sems[kind],
            (step - 1) * row_count + row,
            pairs.device_of(place),
        )

    def row_copy(kind, step):
        place = rows.ahead(step)
        whole, row_recv = buffers[kind][4], buffers[kind][5]
        return send_to(
            whole.at[place],
            row_recv.at[step - 1],
            row_sems[kind],
            step - 1,
            rows.device_of(place),
        )

    def first(step, carry):
        pair = lax.rem(pairs.place + step, pair_count)
        for kind in range(kinds):
            for row in range(row_count):
                buffers[kind][0][pair, row] = block(kind, row, pair, other).astype(jnp.bfloat16)
            side_copy(kind, pair).start()
        return carry

    lax.fori_loop(1, pair_count + 1, first, 0)

    def second(step, carry):
        pair = lax.rem(pairs.place + step, pair_count)
        for kind in range(kinds):
            side_copy(kind, pair).wait_recv()
            side_recv, half = buffers[kind][1], buffers[kind][2]
            for row in range(row_count):
                total = block(kind, row, pair, sides.place)
                total = total + side_recv[pair, row].astype(jnp.float32)
                half[pair, row] = total.astype(jnp.bfloat16)

                @pl.when(step < pair_count)
                def _():
                    pair_copy(kind, step, row).start()

        return carry

    lax.fori_loop(1, pair_count + 1, second, 0)

    def third(step, carry):
        row = lax.rem(rows.place + step, row_count)
        for kind in range(kinds):
            half, pair_recv, whole = buffers[kind][2], buffers[kind][3], buffers[kind][4]
            total = half[pairs.place, row].astype(jnp.float32)
            for ahead in range(1, pair_count):
                pair_copy(kind, ahead, row).wait_recv()
                total = total + pair_recv[ahead - 1, row].astype(jnp.float32)

            whole[row] = total.astype(jnp.bfloat16)

            @pl.when(step < row_count)
            def _():
                row_copy(kind, step).start()

        return carry

    lax.fori_loop(1, row_count + 1, third, 0)
    for kind in range(kinds):
        whole, row_recv = buffers[kind][4], buffers[kind][5]
        total = whole[rows.place].astype(jnp.float32)
        for step in range(1, row_count):
            row_copy(kind, step).wait_recv()
            total = total + row_recv[step - 1].astype(jnp.float32)
        outputs[kind][...] = total

    def drain_sides(pair, carry):
        for kind in range(kinds):
            side_copy(kind, pair).wait_send()
        return carry

    lax.fori_loop(0, pair_count, drain_sides, 0)

    def drain_pairs(step, carry):
        for kind in range(kinds):
            for row in range(row_count):
                pair_copy(kind, step, row).wait_send()
        return carry

    lax.fori_loop(1, pair_count, drain_pairs, 0)
    for kind in range(kinds):
        for step in range(1, row_count):
            row_copy(kind, step).wait_send()


def reduce_dense(row_count, col_count, normed, grad_projected, grad_mid_b, attended, small):
    token_rows, model_width = normed.shape
    qkv_width, out_rows = grad_projected.shape[1], attended.shape[1]
    pair_count = col_count // 2
    shapes = (
        (model_width // row_count, qkv_width // col_count),
        (model_width // col_count, out_rows // row_count),
        small.shape[2:],
    )
    vmem = pl.BlockSpec(memory_space=pltpu.VMEM)
    scratch = []
    sems = []
    for height, breadth in shapes:
        for lead in (
            (pair_count, row_count),
            (pair_count, row_count),
            (pair_count, row_count),
            (max(pair_count - 1, 1), row_count),
            (row_count,),
            (max(row_count - 1, 1),),
        ):
            scratch.append(pltpu.VMEM((*lead, height, breadth), jnp.bfloat16))
        for count in (pair_count, max(pair_count - 1, 1) * row_count, max(row_count - 1, 1)):
            sems.extend([pltpu.SemaphoreType.DMA((count,))] * 2)
    operands = [
        pltpu.VMEM((row_count, shapes[0][0], token_rows), jnp.bfloat16),
        pltpu.VMEM((col_count, token_rows, shapes[0][1]), jnp.bfloat16),
        pltpu.VMEM((col_count, shapes[1][0], token_rows), jnp.bfloat16),
        pltpu.VMEM((row_count, token_rows, shapes[1][1]), jnp.bfloat16),
    ]
    return pl.pallas_call(
        functools.partial(reduce_dense_kernel, (row_count, pair_count)),
        out_shape=tuple(jax.ShapeDtypeStruct(shape, jnp.float32) for shape in shapes),
        in_specs=[vmem] * 5,
        out_specs=(vmem,) * 3,
        scratch_shapes=scratch + sems + operands,
        compiler_params=pltpu.CompilerParams(
            collective_id=3, has_side_effects=True, vmem_limit_bytes=vmem_most
        ),
        cost_estimate=no_cost,
        name="reduce_dense",
    )(normed, grad_projected, grad_mid_b, attended, small)


class DenseGather:
    def __init__(self, dims, own_blocks, fulls, sems):
        self.row_count, self.pair_count = dims
        self.rows, self.pairs, self.sides = dense_peers(*dims)
        self.own_blocks = own_blocks
        self.fulls = fulls
        self.kinds = range(len(own_blocks))
        self.row_sems = [sems[6 * kind : 6 * kind + 2] for kind in self.kinds]
        self.pair_sems = [sems[6 * kind + 2 : 6 * kind + 4] for kind in self.kinds]
        self.side_sems = [sems[6 * kind + 4 : 6 * kind + 6] for kind in self.kinds]
        self.local_sems = sems[6 * len(own_blocks)]

    @staticmethod
    def sems(dims, kinds):
        row_count, pair_count = dims
        sems = []
        for _ in range(kinds):
            for count in (
                max(row_count - 1, 1),
                max(pair_count - 1, 1) * row_count,
                pair_count * row_count,
            ):
                sems.extend([pltpu.SemaphoreType.DMA((count,))] * 2)
        return sems + [pltpu.SemaphoreType.DMA((kinds,))]

    def groups(self):
        return (self.rows, self.pairs, self.sides)

    def spot(self, kind, row, pair, side):
        col = pair * 2 + side
        height = self.own_blocks[kind].shape[0]
        return self.fulls[kind].at[row, pl.ds(pl.multiple_of(col * height, height), height), :]

    def own_spot(self, kind):
        return self.spot(kind, self.rows.place, self.pairs.place, self.sides.place)

    def own_copy(self, kind):
        return pltpu.make_async_copy(
            self.own_blocks[kind], self.own_spot(kind), self.local_sems.at[kind]
        )

    def row_copy(self, kind, step):
        return send_to(
            self.own_blocks[kind],
            self.own_spot(kind),
            self.row_sems[kind],
            step - 1,
            self.rows.device_of(self.rows.ahead(step)),
        )

    def row_landed(self, kind, step):
        place = self.rows.behind(step)
        landed = self.spot(kind, place, self.pairs.place, self.sides.place)
        return send_to(
            landed, landed, self.row_sems[kind], step - 1, self.rows.device_of(place)
        )

    def pair_copy(self, kind, step, number):
        block = self.spot(kind, self.rows.behind(number), self.pairs.place, self.sides.place)
        return send_to(
            block if number else self.own_blocks[kind],
            block,
            self.pair_sems[kind],
            (step - 1) * self.row_count + number,
            self.pairs.device_of(self.pairs.ahead(step)),
        )

    def pair_landed(self, kind, step, number):
        place = self.pairs.behind(step)
        landed = self.spot(kind, self.rows.behind(number), place, self.sides.place)
        return send_to(
            landed,
            landed,
            self.pair_sems[kind],
            (step - 1) * self.row_count + number,
            self.pairs.device_of(place),
        )

    def side_copy(self, kind, step, number):
        place = self.pairs.behind(step)
        block = self.spot(kind, self.rows.behind(number), place, self.sides.place)
        return send_to(
            block if step or number else self.own_blocks[kind],
            block,
            self.side_sems[kind],
            step * self.row_count + number,
            self.sides.device_of(1 - self.sides.place),
        )

    def side_landed(self, kind, step, number):
        place = self.pairs.behind(step)
        landed = self.spot(kind, self.rows.behind(number), place, 1 - self.sides.place)
        return send_to(
            landed,
            landed,
            self.side_sems[kind],
            step * self.row_count + number,
            self.sides.device_of(1 - self.sides.place),
        )

    def start(self, kind):
        self.own_copy(kind).start()
        for step in range(1, self.row_count):
            self.row_copy(kind, step).start()
        for step in range(1, self.pair_count):
            self.pair_copy(kind, step, 0).start()
        self.side_copy(kind, 0, 0).start()

    def pass_rows(self, kind):
        for number in range(1, self.row_count):
            self.row_landed(kind, number).wait_recv()
            for step in range(1, self.pair_count):
                self.pair_copy(kind, step, number).start()
            self.side_copy(kind, 0, number).start()

    def pass_pairs(self, kind):
        for number in range(self.row_count):
            for step in range(1, self.pair_count):
                self.pair_landed(kind, step, number).wait_recv()
                self.side_copy(kind, step, number).start()

    def finish(self, kind):
        self.own_copy(kind).wait()
        for step in range(self.pair_count):
            for number in range(self.row_count):
                self.side_landed(kind, step, number).wait_recv()
        for step in range(1, self.row_count):
            self.row_copy(kind, step).wait_send()
        for number in range(self.row_count):
            for step in range(1, self.pair_count):
                self.pair_copy(kind, step, number).wait_send()
            for step in range(self.pair_count):
                self.side_copy(kind, step, number).wait_send()


def gathered_shapes(dims, blocks):
    row_count, pair_count = dims
    return tuple(
        jax.ShapeDtypeStruct(
            (row_count, 2 * pair_count * block.shape[0], block.shape[1]), block.dtype
        )
        for block in blocks
    )


def gather_dense_kernel(
    dims,
    copies,
    qkv_ref,
    out_ref,
    routes_ref,
    router_ref,
    shards_ref,
    qkv_full,
    out_full,
    routes_all,
    router_all,
    moved,
    *sems,
):
    gather = DenseGather(dims, (qkv_ref, out_ref), (qkv_full, out_full), sems[:13])
    small_send, small_recv, local_sems = sems[13:16]
    rows = gather.rows
    move = WeightMove(rows, copies, 0, shards_ref, moved, sems[16:])
    small = [
        Exchange(
            rows,
            small_send,
            small_recv,
            lambda place, chunk, ref=ref: ref,
            lambda place, step, chunk, full=full: full.at[place],
        )
        for ref, full in ((routes_ref, routes_all), (router_ref, router_all))
    ]
    greet(gather.groups())
    own_copies = [
        pltpu.make_async_copy(ref, full.at[rows.place], local_sems.at[number])
        for number, (ref, full) in enumerate(((routes_ref, routes_all), (router_ref, router_all)))
    ]
    for kind in range(2):
        gather.start(kind)
        own_copies[kind].start()
        small[kind].start(kind, None)
    move.start()
    for kind in range(2):
        gather.pass_rows(kind)
    for kind in range(2):
        gather.pass_pairs(kind)
    for kind in range(2):
        small[kind].wait_recv(kind, None)
        gather.finish(kind)
        own_copies[kind].wait()
        small[kind].wait_send(kind, None)
    move.wait_recv()
    move.wait_send()


def gather_dense(row_count, col_count, copies, qkv_block, out_block, routes, router, shards):
    dims = (row_count, col_count // 2)
    outside = pl.BlockSpec(memory_space=pl.ANY)
    return pl.pallas_call(
        functools.partial(gather_dense_kernel, dims, copies),
        out_shape=gathered_shapes(dims, (qkv_block, out_block))
        + tuple(jax.ShapeDtypeStruct((row_count, *x.shape), x.dtype) for x in (routes, router))
        + (moved_shape(row_count, shards),),
        in_specs=[outside] * 5,
        out_specs=(outside,) * 5,
        scratch_shapes=DenseGather.sems(dims, 2)
        + [
            *exchange_sems(2, row_count),
            pltpu.SemaphoreType.DMA((2,)),
            *WeightMove.sems(row_count),
        ],
        compiler_params=pltpu.CompilerParams(collective_id=4, has_side_effects=True),
        cost_estimate=no_cost,
        name="gather_dense",
    )(qkv_block, out_block, routes, router, shards)


def order_grads_kernel(layer_count, block_count, *refs):
    blocks = refs[: layer_count * block_count]
    outputs = refs[layer_count * block_count : layer_count * block_count + 3]
    came, wide, in_sems, out_sems = refs[layer_count * block_count + 3 :]
    row_index = lax.axis_index("row")
    items = [
        (layer, step, kind)
        for layer in range(layer_count)
        for step in range(block_count)
        for kind in range(3)
    ]

    def load(number):
        layer, step, kind = items[number]
        return pltpu.make_async_copy(
            blocks[layer * block_count + step].at[kind],
            came.at[number % 4],
            in_sems.at[number % 4],
        )

    def store(number):
        layer, step, kind = items[number]
        expert = lax.rem(row_index + step, block_count)
        return pltpu.make_async_copy(
            wide.at[number % 4], outputs[kind].at[layer, expert], out_sems.at[number % 4]
        )

    count = len(items)
    for number in range(min(3, count)):
        load(number).start()
    for number in range(count):
        if number + 3 < count:
            load(number + 3).start()
        load(number).wait()
        if number >= 4:
            store(number - 4).wait()
        wide[number % 4] = came[number % 4].astype(jnp.float32)
        store(number).start()
    for number in range(max(count - 4, 0), count):
        store(number).wait()


def order_grads(layers):
    layer_count, block_count = len(layers), len(layers[0])
    _, slice_width, model_width = layers[0][0].shape
    outside = pl.BlockSpec(memory_space=pl.ANY)
    shape = jax.ShapeDtypeStruct((layer_count, block_count, slice_width, model_width), jnp.float32)
    return pl.pallas_call(
        functools.partial(order_grads_kernel, layer_count, block_count),
        out_shape=(shape,) * 3,
        in_specs=[outside] * (layer_count * block_count),
        out_specs=(outside,) * 3,
        scratch_shapes=[
            pltpu.VMEM((4, slice_width, model_width), jnp.bfloat16),
            pltpu.VMEM((4, slice_width, model_width), jnp.float32),
            pltpu.SemaphoreType.DMA((4,)),
            pltpu.SemaphoreType.DMA((4,)),
        ],
        compiler_params=pltpu.CompilerParams(vmem_limit_bytes=vmem_most),
        cost_estimate=no_cost,
        name="order_grads",
    )(*[block for blocks in layers for block in blocks])


def pieces_nt(left, weights_ref):
    pieces, _, size = weights_ref.shape
    total = None
    for index in range(pieces):
        part = dot_nt(left[:, index * size : (index + 1) * size], weights_ref[index])
        total = part if total is None else total + part
    return total


def rotate(values, cosine, sine):
    return values * cosine + pltpu.roll(values, HEAD_SIZE // 2, 1) * sine


def seen_keys(token_rows):
    position = lax.axis_index("col") * token_rows + iota((1, token_rows), 1)
    return (position // BLOCK + 1) * BLOCK


def attend_forward_kernel(
    dims,
    x_ref,
    gain_attn_ref,
    gain_moe_ref,
    cosine_ref,
    sine_ref,
    qkv_ref,
    out_w_ref,
    shards_ref,
    mid_ref,
    normed_ref,
    q_ref,
    kv_out,
    attended_ref,
    lse_ref,
    normed_moe_ref,
    moved,
    kv_all,
    value_t,
    proj,
    send_sem,
    recv_sem,
    local_sem,
    *move_sems,
):
    col_count, row_count, copies, layer, score_scale = dims
    token_rows = x_ref.shape[0]
    group = QUERY_HEADS // KEY_VALUE_HEADS
    kv_width = KEY_VALUE_HEADS * HEAD_SIZE
    cols = col_peers(col_count)

    def part(place):
        return pl.ds(pl.multiple_of(place * token_rows, token_rows), token_rows)

    share = Exchange(
        cols,
        send_sem,
        recv_sem,
        lambda place, chunk: kv_all.at[part(cols.place), :],
        lambda place, step, chunk: kv_all.at[part(place), :],
    )
    move = WeightMove(all_rows(row_count), copies, layer, shards_ref, moved, move_sems)
    greet((cols, move.rows))
    move.start()
    x = x_ref[...]
    inverse = lax.rsqrt(jnp.mean(x * x, axis=-1, keepdims=True) + eps_norm)
    normed_ref[...] = (x * inverse * gain_attn_ref[...]).astype(jnp.bfloat16)
    proj[...] = pieces_nt(normed_ref[...], qkv_ref)
    for head in range(KEY_VALUE_HEADS):
        lanes = slice(head * HEAD_SIZE, (head + 1) * HEAD_SIZE)
        start = QUERY_FEATURES + head * HEAD_SIZE
        turned = rotate(proj[:, start : start + HEAD_SIZE], cosine_ref[...], sine_ref[...])
        kv_all[part(cols.place), lanes] = turned.astype(jnp.bfloat16)
    kv_all[part(cols.place), kv_width:] = proj[:, QUERY_FEATURES + kv_width :].astype(jnp.bfloat16)
    share.start(0, None)
    for head in range(QUERY_HEADS):
        lanes = slice(head * HEAD_SIZE, (head + 1) * HEAD_SIZE)
        q_ref[:, lanes] = rotate(proj[:, lanes], cosine_ref[...], sine_ref[...]).astype(
            jnp.bfloat16
        )
    share.wait_recv(0, None)
    keep = pltpu.make_async_copy(kv_all, kv_out, local_sem)
    keep.start()
    value_t[...] = kv_all[:, kv_width:].T
    seen = seen_keys(token_rows)

    def head_step(index, carry):
        kv_head = index // group
        lanes = pl.ds(pl.multiple_of(index * HEAD_SIZE, HEAD_SIZE), HEAD_SIZE)
        kv_lanes = pl.ds(pl.multiple_of(kv_head * HEAD_SIZE, HEAD_SIZE), HEAD_SIZE)
        scores = dot_nt(kv_all[:, kv_lanes], q_ref[:, lanes]) * score_scale
        scores = jnp.where(iota(scores.shape, 0) < seen, scores, masked_score)
        peak = jnp.max(scores, axis=0, keepdims=True)
        exponent = jnp.exp(scores - peak)
        total = jnp.sum(exponent, axis=0, keepdims=True)
        attended = dot_nn(value_t[kv_lanes, :], exponent.astype(jnp.bfloat16)) / total
        attended_ref[:, lanes] = attended.T.astype(jnp.bfloat16)
        lse_ref[index] = peak + jnp.log(total)
        return carry

    lax.fori_loop(0, QUERY_HEADS, head_step, 0)
    mid = x_ref[...] + pieces_nt(attended_ref[...], out_w_ref)
    mid_ref[...] = mid
    inverse = lax.rsqrt(jnp.mean(mid * mid, axis=-1, keepdims=True) + eps_norm)
    normed_moe_ref[...] = (mid * inverse * gain_moe_ref[...]).astype(jnp.bfloat16)
    share.wait_send(0, None)
    keep.wait()
    move.wait_recv()
    move.wait_send()


def attend_forward(
    col_count,
    row_count,
    copies,
    layer,
    x,
    gain_attn,
    gain_moe,
    cosine,
    sine,
    qkv_full,
    out_full,
    shards,
):
    token_rows, model_width = x.shape
    seq_rows = col_count * token_rows
    kv_width = KEY_VALUE_HEADS * HEAD_SIZE
    vmem = pl.BlockSpec(memory_space=pltpu.VMEM)
    outside = pl.BlockSpec(memory_space=pl.ANY)
    rows_b = jax.ShapeDtypeStruct((token_rows, model_width), jnp.bfloat16)
    heads_b = jax.ShapeDtypeStruct((token_rows, QUERY_FEATURES), jnp.bfloat16)
    return pl.pallas_call(
        functools.partial(
            attend_forward_kernel, (col_count, row_count, copies, layer, HEAD_SIZE ** (-0.5))
        ),
        out_shape=(
            jax.ShapeDtypeStruct((token_rows, model_width), jnp.float32),
            rows_b,
            heads_b,
            jax.ShapeDtypeStruct((seq_rows, 2 * kv_width), jnp.bfloat16),
            heads_b,
            jax.ShapeDtypeStruct((QUERY_HEADS, 1, token_rows), jnp.float32),
            rows_b,
            moved_shape(row_count, shards),
        ),
        in_specs=[vmem] * 7 + [outside],
        out_specs=(vmem, vmem, vmem, outside, vmem, vmem, vmem, outside),
        scratch_shapes=[
            pltpu.VMEM((seq_rows, 2 * kv_width), jnp.bfloat16),
            pltpu.VMEM((kv_width, seq_rows), jnp.bfloat16),
            pltpu.VMEM((token_rows, QUERY_FEATURES + 2 * kv_width), jnp.float32),
            *exchange_sems(1, col_count),
            pltpu.SemaphoreType.DMA,
            *WeightMove.sems(row_count),
        ],
        compiler_params=pltpu.CompilerParams(
            collective_id=5 + 5 * layer, has_side_effects=True, vmem_limit_bytes=vmem_most
        ),
        cost_estimate=no_cost,
        name="attend_forward",
    )(x, gain_attn, gain_moe, cosine, sine, qkv_full, out_full, shards)


def norm_backward(values, gain, incoming):
    inverse = lax.rsqrt(jnp.mean(values * values, axis=-1, keepdims=True) + eps_norm)
    scaled = incoming * gain
    inner_mean = jnp.mean(scaled * values, axis=-1, keepdims=True)
    grad = inverse * scaled - values * (inverse * inverse * inverse) * inner_mean
    return grad, jnp.sum(incoming * values * inverse, axis=0, keepdims=True)


def attend_backward_kernel(
    dims,
    incoming_ref,
    grad_moe_ref,
    mid_ref,
    x_ref,
    gain_attn_ref,
    gain_moe_ref,
    cosine_ref,
    sine_ref,
    qkv_ref,
    out_w_ref,
    q_ref,
    kv_ref,
    attended_ref,
    lse_ref,
    grad_x_ref,
    grad_mid_ref,
    grad_proj_ref,
    grad_gain_attn_ref,
    grad_gain_moe_ref,
    grad_attended,
    key_t,
    key_sum,
    value_sum,
    grad_kv,
    landed,
    send_sem,
    recv_sem,
):
    col_count, score_scale = dims
    token_rows = x_ref.shape[0]
    group = QUERY_HEADS // KEY_VALUE_HEADS
    kv_width = KEY_VALUE_HEADS * HEAD_SIZE
    cols = col_peers(col_count)

    def part(place):
        return pl.ds(pl.multiple_of(place * token_rows, token_rows), token_rows)

    share = Exchange(
        cols,
        send_sem,
        recv_sem,
        lambda place, chunk: grad_kv.at[part(place), :],
        lambda place, step, chunk: landed.at[step - 1],
    )
    grad, gain_sum = norm_backward(mid_ref[...], gain_moe_ref[...], grad_moe_ref[...])
    grad_gain_moe_ref[...] = gain_sum
    grad_x_ref[...] = incoming_ref[...] + grad
    grad_mid_ref[...] = grad_x_ref[...].astype(jnp.bfloat16)
    pieces, _, size = out_w_ref.shape
    for index in range(pieces):
        lanes = slice(index * size, (index + 1) * size)
        grad_attended[:, lanes] = dot_nn(grad_mid_ref[...], out_w_ref[index]).astype(jnp.bfloat16)
    key_t[...] = kv_ref[:, :kv_width].T
    seen = seen_keys(token_rows)
    for kv_head in range(KEY_VALUE_HEADS):
        kv_lanes = slice(kv_head * HEAD_SIZE, (kv_head + 1) * HEAD_SIZE)
        value_lanes = slice(kv_width + kv_head * HEAD_SIZE, kv_width + (kv_head + 1) * HEAD_SIZE)
        key_sum[...] = jnp.zeros_like(key_sum)
        value_sum[...] = jnp.zeros_like(value_sum)

        def head_step(step, carry, kv_lanes=kv_lanes, value_lanes=value_lanes, kv_head=kv_head):
            index = kv_head * group + step
            lanes = pl.ds(pl.multiple_of(index * HEAD_SIZE, HEAD_SIZE), HEAD_SIZE)
            query = q_ref[:, lanes]
            grad_out = grad_attended[:, lanes]
            product = grad_out.astype(jnp.float32) * attended_ref[:, lanes].astype(jnp.float32)
            inner = jnp.sum(product.T, axis=0, keepdims=True)
            scores = dot_nt(kv_ref[:, kv_lanes], query) * score_scale
            soft = jnp.where(
                iota(scores.shape, 0) < seen, jnp.exp(scores - lse_ref[index]), 0.0
            )
            grad_soft = dot_nt(kv_ref[:, value_lanes], grad_out)
            grad_scores = (soft * (grad_soft - inner)).astype(jnp.bfloat16)
            value_sum[...] += dot_nn(soft.astype(jnp.bfloat16), grad_out)
            key_sum[...] += dot_nn(grad_scores, query)
            grad_q = (dot_nn(key_t[kv_lanes, :], grad_scores) * score_scale).T
            grad_q = rotate(grad_q, cosine_ref[...], -sine_ref[...])
            grad_proj_ref[:, lanes] = grad_q.astype(jnp.bfloat16)
            return carry

        lax.fori_loop(0, group, head_step, 0)
        grad_kv[:, kv_lanes] = (key_sum[...] * score_scale).astype(jnp.bfloat16)
        grad_kv[:, value_lanes] = value_sum[...].astype(jnp.bfloat16)
    greet((cols,))
    share.start(0, None)
    share.wait_recv(0, None)
    total = grad_kv[part(cols.place), :].astype(jnp.float32)
    for step in range(1, col_count):
        total = total + landed[step - 1].astype(jnp.float32)
    for head in range(KEY_VALUE_HEADS):
        start = QUERY_FEATURES + head * HEAD_SIZE
        grad_key = total[:, head * HEAD_SIZE : (head + 1) * HEAD_SIZE]
        grad_key = rotate(grad_key, cosine_ref[...], -sine_ref[...])
        grad_proj_ref[:, start : start + HEAD_SIZE] = grad_key.astype(jnp.bfloat16)
    grad_proj_ref[:, QUERY_FEATURES + kv_width :] = total[:, kv_width:].astype(jnp.bfloat16)
    pieces = qkv_ref.shape[0]
    grad_normed = [dot_nn(grad_proj_ref[...], qkv_ref[index]) for index in range(pieces)]
    grad_normed = jnp.concatenate(grad_normed, axis=1) if pieces > 1 else grad_normed[0]
    grad, gain_sum = norm_backward(x_ref[...], gain_attn_ref[...], grad_normed)
    grad_gain_attn_ref[...] = gain_sum
    grad_x_ref[...] += grad
    share.wait_send(0, None)


def attend_backward(
    col_count,
    incoming,
    grad_moe,
    mid,
    x,
    gain_attn,
    gain_moe,
    cosine,
    sine,
    qkv_full,
    out_full,
    queries,
    key_value,
    attended,
    log_sums,
):
    token_rows, model_width = x.shape
    seq_rows = col_count * token_rows
    kv_width = KEY_VALUE_HEADS * HEAD_SIZE
    vmem = pl.BlockSpec(memory_space=pltpu.VMEM)
    gain = jax.ShapeDtypeStruct((1, model_width), jnp.float32)
    return pl.pallas_call(
        functools.partial(attend_backward_kernel, (col_count, HEAD_SIZE ** (-0.5))),
        out_shape=(
            jax.ShapeDtypeStruct((token_rows, model_width), jnp.float32),
            jax.ShapeDtypeStruct((token_rows, model_width), jnp.bfloat16),
            jax.ShapeDtypeStruct((token_rows, QUERY_FEATURES + 2 * kv_width), jnp.bfloat16),
            gain,
            gain,
        ),
        in_specs=[vmem] * 14,
        out_specs=(vmem,) * 5,
        scratch_shapes=[
            pltpu.VMEM((token_rows, QUERY_FEATURES), jnp.bfloat16),
            pltpu.VMEM((kv_width, seq_rows), jnp.bfloat16),
            pltpu.VMEM((seq_rows, HEAD_SIZE), jnp.float32),
            pltpu.VMEM((seq_rows, HEAD_SIZE), jnp.float32),
            pltpu.VMEM((seq_rows, 2 * kv_width), jnp.bfloat16),
            pltpu.VMEM((max(col_count - 1, 1), token_rows, 2 * kv_width), jnp.bfloat16),
            *exchange_sems(1, col_count),
        ],
        compiler_params=pltpu.CompilerParams(
            collective_id=6, has_side_effects=True, vmem_limit_bytes=vmem_most
        ),
        cost_estimate=no_cost,
        name="attend_backward",
    )(
        incoming,
        grad_moe,
        mid,
        x,
        gain_attn,
        gain_moe,
        cosine,
        sine,
        qkv_full,
        out_full,
        queries,
        key_value,
        attended,
        log_sums,
    )


def place_first(values, group_rows, expert_pick):
    rolled = jnp.roll(values.reshape(-1, group_rows, values.shape[1]), -expert_pick, axis=1)
    return rolled.transpose(1, 0, 2).reshape(values.shape)


def place_back(values, group_rows, expert_pick):
    rolled = values.reshape(group_rows, -1, values.shape[1]).transpose(1, 0, 2)
    return jnp.roll(rolled, expert_pick, axis=1).reshape(values.shape)


def body(
    hidden_in, routes, norm_attn, w_qkv, w_out, norm_moe, w_router, w_gate, w_up, w_down, cotangent
):
    row_count = lax.axis_size("row")
    col_count = lax.axis_size("col")
    device_count = row_count * col_count
    row_index = lax.axis_index("row")
    col_index = lax.axis_index("col")
    layer_count = w_qkv.shape[0]
    token_rows = hidden_in.shape[0]
    model_width = hidden_in.shape[1]
    local_experts = w_gate.shape[1]
    slice_width = w_gate.shape[3]
    copies = row_count // local_experts
    expert_pick = row_index // copies
    slot_rows = -(-local_experts * CAP // 16) * 16
    chunks = model_width // 384
    dims = (
        local_experts,
        col_count,
        copies,
        token_rows,
        slot_rows,
        chunks,
        model_width // chunks,
    )
    positions = col_index * token_rows + jnp.arange(token_rows, dtype=jnp.int32)
    cosine, sine = rope_angles(positions, HEAD_SIZE // 2)
    cosine = jnp.concatenate([cosine, cosine], axis=1)
    sine = jnp.concatenate([-sine, sine], axis=1)

    def behind(step):
        return [(index, (index + step) % row_count) for index in range(row_count)]

    def move_grads(grads):
        blocks = [grads[0]]
        for step in range(1, row_count):
            blocks.append(lax.ppermute(grads[step], "row", behind(row_count - step)))
        return tuple(blocks)

    def own_grads(blocks):
        stacked = jnp.stack(blocks)
        ordered = [
            lax.dynamic_index_in_dim(
                stacked, (index - row_index) % row_count, axis=0, keepdims=False
            ).astype(wide_type)
            for index in range(row_count)
        ]
        return [
            functools.reduce(jnp.add, ordered[index * copies : (index + 1) * copies])
            for index in range(local_experts)
        ]

    def pieced(full):
        if full.shape[2] % 128 == 0:
            return full
        return full.transpose(1, 0, 2).reshape(1, full.shape[1], -1)

    def packed(values):
        return jnp.pad(values.reshape(-1), (0, -values.size % 2048)).reshape(-1, 128)

    shards = (w_gate.transpose(0, 1, 3, 2), w_up.transpose(0, 1, 3, 2), w_down)
    experts = []
    route_lines = routes.transpose(0, 2, 1)
    router_lines = w_router.transpose(0, 2, 1)
    qkv_full, out_full, routes_all, router_all, moved_gate = gather_dense(
        row_count,
        col_count,
        copies,
        w_qkv[0].T,
        w_out[0].T,
        packed(route_lines),
        packed(router_lines),
        shards[0],
    )
    dense = [(pieced(qkv_full), pieced(out_full))]
    routes_all = routes_all.reshape(row_count, -1)[:, : route_lines.size]
    routes_all = routes_all.reshape(row_count, *route_lines.shape)
    if copies > 1:
        routes_all = jnp.take(
            routes_all, row_index % copies + copies * jnp.arange(local_experts), axis=0
        )
    router_all = router_all.reshape(row_count, -1)[:, : router_lines.size]
    router_all = router_all.reshape(row_count, *router_lines.shape)
    router_all = router_all.transpose(1, 2, 0, 3).reshape(layer_count, E, model_width)
    routers = [
        place_first(router_all[index], local_experts, expert_pick) for index in range(layer_count)
    ]
    gains_attn = norm_attn.astype(wide_type)[:, None, :]
    gains_moe = norm_moe.astype(wide_type)[:, None, :]
    hidden = hidden_in.astype(wide_type)
    saved = []
    for layer_index in range(layer_count):
        early = 0 if layer_index else 1
        mid, normed, queries, key_value, attended, log_sums, normed_moe, moved = attend_forward(
            col_count,
            row_count,
            copies,
            layer_index,
            hidden,
            gains_attn[layer_index],
            gains_moe[layer_index],
            cosine,
            sine,
            *dense[layer_index],
            shards[early],
        )
        if layer_index == 0:
            weights, moving = [moved_gate, moved, shards[2]], (2,)
        else:
            weights, moving = [moved, shards[1], shards[2]], (1, 2)
        next_blocks = ()
        if layer_index + 1 < layer_count:
            next_blocks = (w_qkv[layer_index + 1].T, w_out[layer_index + 1].T)
        mixed, gates, slots, returned, *rest = moe_forward(
            dims,
            row_count,
            layer_index,
            normed_moe,
            routes_all[:, layer_index],
            routers[layer_index],
            weights,
            moving,
            next_blocks,
        )
        for kind, moved in zip(moving, rest):
            weights[kind] = moved
        experts.append(weights)
        if next_blocks:
            dense.append(tuple(pieced(full) for full in rest[len(moving) :]))
        saved.append(
            (hidden, mid, normed, queries, key_value, attended, log_sums, normed_moe)
            + (gates, slots, returned)
        )
        hidden = mid + mixed
    incoming = cotangent.astype(wide_type)
    dense_results = [None] * layer_count
    small_results = [None] * layer_count
    expert_results = [None] * layer_count
    for layer_index in reversed(range(layer_count)):
        x, mid, normed, queries, key_value, attended, log_sums, normed_moe = saved[layer_index][:8]
        gates, slots, returned = saved[layer_index][8:]
        grad_moe, grad_router, expert_grads = moe_backward(
            dims,
            incoming.astype(narrow_type),
            routes_all[:, layer_index],
            routers[layer_index],
            gates,
            normed_moe,
            slots,
            returned,
            experts[layer_index],
        )
        expert_results[layer_index] = move_grads(expert_grads)
        incoming, grad_mid, grad_projected, grad_gain_attn, grad_gain_moe = attend_backward(
            col_count,
            incoming,
            grad_moe,
            mid,
            x,
            gains_attn[layer_index],
            gains_moe[layer_index],
            cosine,
            sine,
            *dense[layer_index],
            queries,
            key_value,
            attended,
            log_sums,
        )
        small = jnp.concatenate(
            [
                place_back(grad_router, local_experts, expert_pick),
                grad_gain_attn,
                grad_gain_moe,
            ],
            axis=0,
        ).astype(narrow_type)
        small = small.reshape(E + 2, device_count, -1).transpose(1, 0, 2).reshape(device_count, -1)
        small_size = small.shape[1]
        small_rows = -(-small_size // 2048) * 16
        small = jnp.pad(small, ((0, 0), (0, small_rows * 128 - small_size)))
        small = small.reshape(row_count, col_count, small_rows, 128).transpose(1, 0, 2, 3)
        grad_qkv_block, grad_out_block, small = reduce_dense(
            row_count, col_count, normed, grad_projected, grad_mid, attended, small
        )
        dense_results[layer_index] = (grad_qkv_block, grad_out_block.T)
        small_results[layer_index] = small.reshape(-1)[:small_size].reshape(E + 2, -1).T
        if layer_index > 0:
            incoming, dense_results[layer_index], expert_results[layer_index] = (
                lax.optimization_barrier(
                    (incoming, dense_results[layer_index], expert_results[layer_index])
                )
            )
    small = jnp.stack(small_results)
    if copies == 1:
        grad_gate, grad_up, grad_down = order_grads(expert_results)
    else:
        expert_results = [own_grads(blocks) for blocks in expert_results]
        grad_gate, grad_up, grad_down = (
            jnp.stack([jnp.stack([got[kind] for got in layer]) for layer in expert_results])
            for kind in range(3)
        )
    grad_gate, grad_up = grad_gate.swapaxes(2, 3), grad_up.swapaxes(2, 3)
    return (
        hidden,
        incoming,
        small[:, :, E],
        jnp.stack([dense_results[index][0] for index in range(layer_count)]),
        jnp.stack([dense_results[index][1] for index in range(layer_count)]),
        small[:, :, E + 1],
        small[:, :, :E],
        grad_gate,
        grad_up,
        grad_down,
    )


def solution(mesh):
    in_specs = (
        P(("row", "col"), None),
        P(None, ("row", "col"), None),
        P(),
        P(None, "row", "col"),
        P(None, "row", "col"),
        P(),
        P(None, "row", None),
        P(None, "col", None, "row"),
        P(None, "col", None, "row"),
        P(None, "col", "row", None),
        P(("row", "col"), None),
    )
    out_specs = (
        P(("row", "col"), None),
        P(("row", "col"), None),
        P(None, ("row", "col")),
        P(None, "row", "col"),
        P(None, "row", "col"),
        P(None, ("row", "col")),
        P(None, ("row", "col"), None),
        P(None, "col", None, "row"),
        P(None, "col", None, "row"),
        P(None, "col", "row", None),
    )
    return jax.shard_map(body, mesh=mesh, in_specs=in_specs, out_specs=out_specs, check_vma=False)
```

```python
import functools

import jax
import jax.numpy as jnp
from jax import lax
from jax.experimental import pallas as pl
from jax.experimental.pallas import tpu as pltpu
from jax.sharding import PartitionSpec as P

QUERY_HEADS = 12
KEY_VALUE_HEADS = 2
HEAD_SIZE = 128
E = 32
TOPK = 4
BLOCK = 256
QUERY_FEATURES = 1536
CAP = 36


eps_norm = 1e-06
rope_base = 1000000.0
masked_score = -1e30
wide_type = jnp.float32
narrow_type = jnp.bfloat16


def rope_angles(positions, half_dim):
    frequency = rope_base ** (-jnp.arange(half_dim, dtype=jnp.float32) / half_dim)
    angles = positions.astype(jnp.float32)[:, None] * frequency[None, :]
    return (jnp.cos(angles), jnp.sin(angles))


def split_rows(total, most):
    best = 16
    for step in range(16, most + 1, 16):
        if total % step == 0:
            best = step
    return best


def over_blocks(total, block, step):
    def run(index, carry):
        step(pl.ds(pl.multiple_of(index * block, block), block))
        return carry

    lax.fori_loop(0, total // block, run, 0)


def over_chunks(chunks, width, step):
    def run(index, carry):
        step(index, pl.ds(pl.multiple_of(index * width, width), width))
        return carry

    lax.fori_loop(0, chunks, run, 0)


def dot_nt(left, right):
    return lax.dot_general(
        left, right, (((1,), (1,)), ((), ())), preferred_element_type=jnp.float32
    )


def dot_nn(left, right):
    return jnp.dot(left, right, preferred_element_type=jnp.float32)


class Peers:
    def __init__(self, count, place, device_of):
        self.count = count
        self.place = place
        self.device_of = device_of

    def ahead(self, step):
        return lax.rem(self.place + step, self.count)

    def behind(self, step):
        return lax.rem(self.place + self.count - step, self.count)


def expert_peers(col_count, copies, group_rows):
    row_index = lax.axis_index("row")
    share = lax.rem(row_index, copies)
    rows = Peers(group_rows, row_index // copies, lambda place: {"row": share + copies * place})
    return rows, col_peers(col_count)


def col_peers(col_count):
    return Peers(col_count, lax.axis_index("col"), lambda place: {"col": place})


def greet(groups):
    barrier = pltpu.get_barrier_semaphore()
    total = 0
    for peers in groups:
        for step in range(1, peers.count):
            pl.semaphore_signal(
                barrier,
                inc=1,
                device_id=peers.device_of(peers.ahead(step)),
                device_id_type=pl.DeviceIdType.MESH,
            )
            total += 1
    pl.semaphore_wait(barrier, total)


def send_to(source, target, sems, number, device):
    send_sems, recv_sems = sems
    return pltpu.make_async_remote_copy(
        src_ref=source,
        dst_ref=target,
        send_sem=send_sems.at[number],
        recv_sem=recv_sems.at[number],
        device_id=device,
        device_id_type=pl.DeviceIdType.MESH,
    )


class Exchange:
    def __init__(self, peers, send_sems, recv_sems, source, target):
        self.peers = peers
        self.sems = (send_sems, recv_sems)
        self.source = source
        self.target = target

    def out(self, step, index, chunk):
        place = self.peers.ahead(step)
        return send_to(
            self.source(place, chunk),
            self.target(self.peers.place, step, chunk),
            self.sems,
            (index, step - 1),
            self.peers.device_of(place),
        )

    def start(self, index, chunk):
        for step in range(1, self.peers.count):
            self.out(step, index, chunk).start()

    def wait_send(self, index, chunk):
        for step in range(1, self.peers.count):
            self.out(step, index, chunk).wait_send()

    def wait_recv(self, index, chunk):
        for step in range(1, self.peers.count):
            place = self.peers.behind(step)
            landed = self.target(place, step, chunk)
            send_to(
                landed, landed, self.sems, (index, step - 1), self.peers.device_of(place)
            ).wait_recv()


def exchange_sems(chunks, count):
    return [pltpu.SemaphoreType.DMA((chunks, max(count - 1, 1))) for _ in range(2)]


class LineGather:
    def __init__(self, rows, own, tokens, part, sems):
        self.rows = rows
        self.own = own
        self.tokens = tokens
        self.part = part
        self.own_send, self.pass_send, self.recv = sems

    @staticmethod
    def sems(chunks, count):
        return [
            pltpu.SemaphoreType.DMA((chunks, 2)),
            pltpu.SemaphoreType.DMA((chunks, count)),
            pltpu.SemaphoreType.DMA((chunks, count)),
        ]

    def copy(self, source, origin, index, chunk, sem, place):
        return pltpu.make_async_remote_copy(
            src_ref=source,
            dst_ref=self.tokens.at[self.part(origin), chunk],
            send_sem=sem,
            recv_sem=self.recv.at[index, origin],
            device_id=self.rows.device_of(place),
            device_id_type=pl.DeviceIdType.MESH,
        )

    def own_copies(self, index, chunk):
        me, last = self.rows.place, self.rows.count - 1
        for way, (there, place) in enumerate(((me < last, me + 1), (me > 0, me - 1))):
            yield there, self.copy(
                self.own.at[:, chunk], me, index, chunk, self.own_send.at[index, way], place
            )

    def passed(self, index, chunk):
        me, last = self.rows.place, self.rows.count - 1
        for distance in range(1, self.rows.count):
            for arrives, origin, goes_on, place in (
                (me >= distance, me - distance, me < last, me + 1),
                (me + distance <= last, me + distance, me > 0, me - 1),
            ):
                yield arrives, goes_on, self.copy(
                    self.tokens.at[self.part(origin), chunk],
                    origin,
                    index,
                    chunk,
                    self.pass_send.at[index, origin],
                    place,
                )

    def start_own(self, index, chunk):
        for there, copy in self.own_copies(index, chunk):
            pl.when(there)(copy.start)

    def arrive(self, index, chunk):
        for arrives, goes_on, copy in self.passed(index, chunk):

            @pl.when(arrives)
            def _():
                copy.wait_recv()
                pl.when(goes_on)(copy.start)

    def wait_send(self, index, chunk):
        for there, copy in self.own_copies(index, chunk):
            pl.when(there)(copy.wait_send)
        for arrives, goes_on, copy in self.passed(index, chunk):
            pl.when(arrives & goes_on)(copy.wait_send)


class LineSum:
    def __init__(self, rows, tokens, part, landed, sems):
        self.rows = rows
        self.tokens = tokens
        self.part = part
        self.landed = landed
        self.send, self.recv = sems

    @staticmethod
    def sems(chunks, count):
        return [
            pltpu.SemaphoreType.DMA((chunks, count)),
            pltpu.SemaphoreType.DMA((chunks, count + 1)),
        ]

    def copy(self, target, slot, index, chunk, place):
        return pltpu.make_async_remote_copy(
            src_ref=self.tokens.at[self.part(target), chunk],
            dst_ref=self.landed.at[slot, :, chunk],
            send_sem=self.send.at[index, target],
            recv_sem=self.recv.at[index, slot],
            device_id=self.rows.device_of(place),
            device_id_type=pl.DeviceIdType.MESH,
        )

    def passed(self, index, chunk):
        me, last = self.rows.place, self.rows.count - 1
        for number in range(self.rows.count):
            for goes, arrives, slot, target, place in (
                (me > number, me < last, number, number, me - 1),
                (me < last - number, me > 0, last - number + 1, last - number, me + 1),
            ):
                yield goes, arrives, slot, target, self.copy(target, slot, index, chunk, place)

    def pass_on(self, index, chunk):
        for goes, arrives, slot, target, copy in self.passed(index, chunk):

            @pl.when(goes)
            def _():
                @pl.when(arrives)
                def _():
                    copy.wait_recv()
                    total = self.tokens[self.part(target), chunk].astype(jnp.float32)
                    total = total + self.landed[slot, :, chunk].astype(jnp.float32)
                    self.tokens[self.part(target), chunk] = total.astype(jnp.bfloat16)

                copy.start()

    def is_middle(self):
        return (self.rows.place > 0) & (self.rows.place < self.rows.count - 1)

    def total(self, index, chunk, out):
        me, last = self.rows.place, self.rows.count - 1
        out[:, chunk] = self.tokens[self.part(me), chunk].astype(jnp.float32)
        for arrives, slot in ((me < last, me), (me > 0, me + 1)):

            @pl.when(arrives)
            def _():
                self.copy(me, slot, index, chunk, me).wait_recv()
                out[:, chunk] += self.landed[slot, :, chunk].astype(jnp.float32)

    def wait_send(self, index, chunk):
        for goes, _, _, _, copy in self.passed(index, chunk):
            pl.when(goes)(copy.wait_send)


def iota(shape, axis):
    return lax.broadcasted_iota(jnp.int32, shape, axis)


def within(numbers, size, count):
    block = jnp.zeros_like(numbers)
    for index in range(1, count):
        block = block + (numbers >= index * size).astype(jnp.int32)
    return block, numbers - block * size


def slot_block(shape, slot_axis, slot_rows):
    slots = iota(shape, slot_axis)
    block = iota(shape, 1 - slot_axis)
    return (slots >= block * slot_rows) & (slots < (block + 1) * slot_rows)


def build_places(dims, rows, routes_ref, place, place_t, member):
    group_rows, col_count, copies, token_rows, slot_rows, chunks, width = dims
    all_slots = col_count * slot_rows
    number = iota((E, 1), 0)
    ahead, col = within(number, col_count, group_rows)
    owner = ahead + rows.place
    owner = jnp.where(owner >= group_rows, owner - group_rows, owner)
    expert = col * group_rows + owner
    earlier = (iota((token_rows, token_rows), 0) < iota((token_rows, token_rows), 1)).astype(
        jnp.bfloat16
    )
    pick = slot_block((E, all_slots), 1, slot_rows).astype(jnp.bfloat16)
    column = iota((slot_rows, 1), 0)
    lane = within(iota((1, all_slots), 1), slot_rows, col_count)[1]
    for group in range(group_rows):
        tokens = slice(group * token_rows, (group + 1) * token_rows)
        picked = routes_ref[group]
        has = picked[0:1, :] == expert
        for choice in range(1, TOPK):
            has = has | (picked[choice : choice + 1, :] == expert)
        before = dot_nn(has.astype(jnp.float32).astype(jnp.bfloat16), earlier)
        slot_number = jnp.where(has, before, -1.0)
        in_group = (column >= group * CAP) & (column < (group + 1) * CAP)
        wanted = jnp.where(in_group, column - group * CAP, -2).astype(jnp.float32)
        for index in range(col_count):
            slots = slice(index * slot_rows, (index + 1) * slot_rows)
            hit = slot_number[index : index + 1, :] == wanted
            place[slots, tokens] = jnp.where(hit, 1.0, 0.0).astype(jnp.bfloat16)
        turned = slot_number.T
        in_group = (lane >= group * CAP) & (lane < (group + 1) * CAP)
        wanted = jnp.where(in_group, lane - group * CAP, -2).astype(jnp.float32)
        hit = dot_nn(turned.astype(jnp.bfloat16), pick) == wanted
        place_t[tokens, :] = jnp.where(hit, 1.0, 0.0).astype(jnp.bfloat16)
        if member is not None:
            member[tokens, :] = turned


def far_first(rows):
    for distance in range(rows.count - 1, 0, -1):
        for there, place in (
            (rows.place + distance < rows.count, rows.place + distance),
            (rows.place >= distance, rows.place - distance),
        ):
            yield there, place


class WeightMove:
    def __init__(self, rows, copies, layer, shards, target, sems):
        self.rows = rows
        self.copies = copies
        self.layer = layer
        self.shards = shards
        self.target = target
        self.remote_sems = sems[:2]
        self.local_sem = sems[2]

    @staticmethod
    def sems(row_count):
        return [pltpu.SemaphoreType.DMA((max(row_count - 1, 1),))] * 2 + [pltpu.SemaphoreType.DMA]

    def shard(self, place):
        return self.shards.at[self.layer, place // self.copies]

    def own(self):
        return pltpu.make_async_copy(
            self.shard(self.rows.place), self.target.at[0], self.local_sem
        )

    def out(self, step):
        place = self.rows.ahead(step)
        return send_to(
            self.shard(place),
            self.target.at[step],
            self.remote_sems,
            step - 1,
            self.rows.device_of(place),
        )

    def start(self):
        for there, place in far_first(self.rows):
            step = lax.rem(place - self.rows.place + self.rows.count, self.rows.count)

            @pl.when(there)
            def _():
                self.out(step).start()

        self.own().start()

    def wait_recv(self):
        self.own().wait()
        for step in range(1, self.rows.count):
            landed = self.target.at[step]
            place = self.rows.behind(step)
            send_to(
                landed, landed, self.remote_sems, step - 1, self.rows.device_of(place)
            ).wait_recv()

    def wait_send(self):
        for step in range(1, self.rows.count):
            self.out(step).wait_send()


def all_rows(row_count):
    return Peers(row_count, lax.axis_index("row"), lambda place: {"row": place})


def moved_shape(row_count, shards):
    return jax.ShapeDtypeStruct((row_count, *shards.shape[2:]), shards.dtype)


vmem_most = 62 * 1024 * 1024
long_cost = pl.CostEstimate(flops=0, bytes_accessed=600 * 1024 * 1024, transcendentals=0)
no_cost = pl.CostEstimate(flops=0, bytes_accessed=0, transcendentals=0)


def moe_forward_kernel(dims, row_count, layer, moving, gather_dims, closing, *refs):
    group_rows, col_count, copies, token_rows, slot_rows, chunks, width = dims
    own_ref, routes_ref, router_ref = refs[:3]
    weight_in = refs[3:6]
    refs = refs[6:]
    next_blocks = refs[: 2 if gather_dims else 0]
    refs = refs[len(next_blocks) :]
    closing_in = refs[: 1 if closing else 0]
    refs = refs[len(closing_in) :]
    sum_ref, gates_ref, slots_out, returned_out = refs[:4]
    refs = refs[4:]
    closing_out = refs[: len(closing_in)]
    refs = refs[len(closing_in) :]
    moved_out = refs[: len(moving)]
    refs = refs[len(moving) :]
    next_full = refs[: len(next_blocks)]
    refs = refs[len(next_blocks) :]
    dense = None
    if gather_dims:
        count = len(DenseGather.sems(gather_dims, 2))
        dense = DenseGather(gather_dims, next_blocks, next_full, refs[-count:])
        refs = refs[:-count]
    closing_sems = ()
    if closing:
        closing_sems = refs[-4:]
        refs = refs[:-4]
    move_sems = refs[len(refs) - 3 * len(moving) :]
    refs = refs[: len(refs) - 3 * len(moving)]
    (
        place,
        place_t,
        member,
        gate,
        up,
        down,
        tokens,
        send,
        slots,
        gate_val,
        up_val,
        act,
        returned,
        landed,
        own_send,
        pass_send,
        row_recv,
        there_send,
        there_recv,
        back_send,
        back_recv,
        home_send,
        home_recv,
        local_sem,
    ) = refs
    all_tokens = group_rows * token_rows
    all_slots = col_count * slot_rows
    slot_step = split_rows(all_slots, 320)
    rows, cols = expert_peers(col_count, copies, group_rows)

    def token_part(place):
        return pl.ds(pl.multiple_of(place * token_rows, token_rows), token_rows)

    def slot_part(place):
        return pl.ds(pl.multiple_of(place * slot_rows, slot_rows), slot_rows)

    gather = LineGather(rows, own_ref, tokens, token_part, (own_send, pass_send, row_recv))
    there = Exchange(
        cols,
        there_send,
        there_recv,
        lambda place, chunk: send.at[slot_part(place), chunk],
        lambda place, step, chunk: slots.at[slot_part(place), chunk],
    )
    back = Exchange(
        cols,
        back_send,
        back_recv,
        lambda place, chunk: send.at[slot_part(place), chunk],
        lambda place, step, chunk: returned.at[slot_part(place), chunk],
    )
    home = LineSum(rows, tokens, token_part, landed, (home_send, home_recv))
    ahead = None
    if closing:
        ahead = LineGather(rows, *closing_in, *closing_out, token_part, closing_sems[:3])
        ahead_own = pltpu.make_async_copy(
            closing_in[0], closing_out[0].at[token_part(rows.place), :], closing_sems[3]
        )
    weights = (gate, up, down)
    moves = {
        kind: WeightMove(
            all_rows(row_count),
            copies,
            layer,
            weight_in[kind],
            weights[kind],
            move_sems[3 * number : 3 * number + 3],
        )
        for number, kind in enumerate(moving)
    }
    loads = {
        kind: pltpu.make_async_copy(weight_in[kind], weights[kind], local_sem.at[2 + kind])
        for kind in range(3)
        if kind not in moving
    }
    keeps = []

    def weight_ready(kind):
        if kind in loads:
            loads[kind].wait()
        else:
            moves[kind].wait_recv()
            keep = pltpu.make_async_copy(
                weights[kind], moved_out[moving.index(kind)], local_sem.at[2 + kind]
            )
            keep.start()
            keeps.append(keep)

    def weight(kind, chunk):
        return weights[kind][:, :, chunk].reshape(-1, width)

    greet((all_rows(row_count), cols))
    for index in range(min(2, chunks)):
        gather.start_own(index, pl.ds(index * width, width))
    for copy in loads.values():
        copy.start()
    tokens[token_part(rows.place), :] = own_ref[...]
    build_places(dims, rows, routes_ref, place, place_t, member)

    def dispatch(index, chunk):
        gather.arrive(index, chunk)

        @pl.when(index + 2 < chunks)
        def _():
            later = pl.ds(pl.multiple_of((index + 2) * width, width), width)
            gather.start_own(index + 2, later)


        def rows_of(part):
            send[part, chunk] = dot_nn(place[part, :], tokens[:, chunk]).astype(jnp.bfloat16)

        over_blocks(all_slots, all_slots, rows_of)
        there.start(index, chunk)
        slots[slot_part(cols.place), chunk] = send[slot_part(cols.place), chunk]

    over_chunks(chunks, width, dispatch)
    if dense:
        for kind in dense.kinds:
            dense.start(kind)
    for kind in moving:
        moves[kind].start()

    def gating(part):
        chosen = member[part, :] >= 0
        logits = jnp.where(chosen, dot_nt(tokens[part, :], router_ref[...]), masked_score)
        peak = jnp.max(logits, axis=-1, keepdims=True)
        exponent = jnp.where(chosen, jnp.exp(logits - peak), 0.0)
        gates = exponent / jnp.sum(exponent, axis=-1, keepdims=True)
        gates_ref[part, :] = gates
        pick = slot_block((E, all_slots), 1, slot_rows).astype(jnp.bfloat16)
        spread = dot_nn(gates.astype(jnp.bfloat16), pick)
        place_t[part, :] = (place_t[part, :].astype(jnp.float32) * spread).astype(jnp.bfloat16)

    over_blocks(all_tokens, token_rows, gating)

    def project(kind, target, wait, index, chunk):
        if wait:
            there.wait_recv(index, chunk)

        def rows_of(part):
            value = dot_nt(slots[part, chunk], weight(kind, chunk))

            @pl.when(index == 0)
            def _():
                target[part, :] = value

            @pl.when(index > 0)
            def _():
                target[part, :] += value

        over_blocks(all_slots, all_slots, rows_of)

    weight_ready(0)
    over_chunks(chunks, width, functools.partial(project, 0, gate_val, True))
    weight_ready(1)
    over_chunks(chunks, width, functools.partial(project, 1, up_val, False))
    keep_slots = pltpu.make_async_copy(slots, slots_out, local_sem.at[0])
    keep_slots.start()

    def activate(part):
        value = gate_val[part, :]
        act[part, :] = (value * jax.nn.sigmoid(value) * up_val[part, :]).astype(jnp.bfloat16)

    over_blocks(all_slots, slot_step, activate)
    if dense:
        for kind in dense.kinds:
            dense.pass_rows(kind)
    weight_ready(2)
    if ahead:
        ahead_own.start()
        over_chunks(chunks, width, ahead.start_own)

    def give_back(index, chunk):
        there.wait_send(index, chunk)

        def rows_of(part):
            send[part, chunk] = dot_nn(act[part, :], weight(2, chunk)).astype(jnp.bfloat16)

        over_blocks(all_slots, all_slots, rows_of)
        back.start(index, chunk)
        returned[slot_part(cols.place), chunk] = send[slot_part(cols.place), chunk]

    over_chunks(chunks, width, give_back)

    over_chunks(chunks, width, gather.wait_send)

    def combine(index, chunk):
        back.wait_recv(index, chunk)

        def rows_of(part):
            tokens[part, chunk] = dot_nn(place_t[part, :], returned[:, chunk]).astype(jnp.bfloat16)

        over_blocks(all_tokens, token_rows, rows_of)
        if ahead:
            ahead.arrive(index, chunk)
            return
        pl.when(~home.is_middle())(functools.partial(home.pass_on, index, chunk))

        @pl.when(home.is_middle() & (index > 0))
        def _():
            before = pl.ds(pl.multiple_of((index - 1) * width, width), width)
            home.pass_on(index - 1, before)

    over_chunks(chunks, width, combine)
    if ahead:
        keep_mixed = pltpu.make_async_copy(tokens, sum_ref, local_sem.at[5])
        keep_mixed.start()
    else:
        last_chunk = pl.ds((chunks - 1) * width, width)
        pl.when(home.is_middle())(functools.partial(home.pass_on, chunks - 1, last_chunk))
    keep_returned = pltpu.make_async_copy(returned, returned_out, local_sem.at[1])
    keep_returned.start()
    if dense:
        for kind in dense.kinds:
            dense.pass_pairs(kind)

    def finish(index, chunk):
        home.total(index, chunk, sum_ref)

    if not ahead:
        over_chunks(chunks, width, finish)

    def drain(index, chunk):
        back.wait_send(index, chunk)
        (ahead or home).wait_send(index, chunk)

    over_chunks(chunks, width, drain)
    if dense:
        for kind in dense.kinds:
            dense.finish(kind)
    for kind in moving:
        moves[kind].wait_send()
    if ahead:
        ahead_own.wait()
        keep_mixed.wait()
    keep_slots.wait()
    keep_returned.wait()
    for keep in keeps:
        keep.wait()


def moe_backward_kernel(dims, opening, *refs):
    group_rows, col_count, copies, token_rows, slot_rows, chunks, width = dims
    own_ref, routes_ref, router_ref, gates_ref, normed_ref, slots_in, returned_in = refs[:7]
    weight_in = refs[7:10]
    refs = refs[10:]
    opening_in = refs[: 1 if opening else 0]
    refs = refs[len(opening_in) :]
    block_count, slice_width = weight_in[0].shape[:2]
    sum_ref, router_grad_ref, *grads_out = refs[: 2 + block_count]
    refs = refs[2 + block_count :]
    opening_out = refs[: len(opening_in)]
    refs = refs[len(opening_in) :]
    opening_scratch = ()
    if opening:
        opening_scratch = refs[-3:]
        refs = refs[:-3]
    (
        place,
        place_t,
        gate,
        up,
        down,
        tokens,
        send,
        slots,
        slope,
        silu,
        act,
        weight,
        inner,
        received,
        grad_act,
        grad_gate,
        grad_up,
        returned,
        turned,
        staged,
        landed,
        pair_send,
        pair_landed,
        own_send,
        pass_send,
        row_recv,
        there_send,
        there_recv,
        back_send,
        back_recv,
        home_send,
        home_recv,
        pair_send_sem,
        pair_recv_sem,
        local_sem,
    ) = refs
    all_tokens = group_rows * token_rows
    all_slots = col_count * slot_rows
    slot_step = split_rows(all_slots, 320)
    rows, cols = expert_peers(col_count, copies, group_rows)

    def token_part(place):
        return pl.ds(pl.multiple_of(place * token_rows, token_rows), token_rows)

    def slot_part(place):
        return pl.ds(pl.multiple_of(place * slot_rows, slot_rows), slot_rows)

    gather = LineGather(rows, own_ref, tokens, token_part, (own_send, pass_send, row_recv))
    there = Exchange(
        cols,
        there_send,
        there_recv,
        lambda place, chunk: send.at[slot_part(place), chunk],
        lambda place, step, chunk: received.at[slot_part(place), chunk],
    )
    back = Exchange(
        cols,
        back_send,
        back_recv,
        lambda place, chunk: send.at[slot_part(place), chunk],
        lambda place, step, chunk: returned.at[slot_part(place), chunk],
    )
    home = LineSum(rows, tokens, token_part, landed, (home_send, home_recv))
    before = None
    if opening:
        before = LineSum(rows, tokens, token_part, opening_scratch[0], opening_scratch[1:])
    pair = Exchange(
        rows,
        pair_send_sem,
        pair_recv_sem,
        lambda place, chunk: pair_send.at[token_part(place), :],
        lambda place, step, chunk: pair_landed.at[step - 1],
    )
    greet((all_rows(block_count), cols))
    if before:
        load_tokens = pltpu.make_async_copy(own_ref, tokens, local_sem.at[7])
        load_tokens.start()
    else:
        for index in range(min(2, chunks)):
            gather.start_own(index, pl.ds(index * width, width))
    load_returned = pltpu.make_async_copy(returned_in, returned, local_sem.at[1])
    load_returned.start()
    load_slots = pltpu.make_async_copy(slots_in, slots, local_sem.at[0])
    load_slots.start()
    weights = (gate, up, down)
    loads = [
        pltpu.make_async_copy(weight_in[kind], weights[kind], local_sem.at[4 + kind])
        for kind in range(3)
    ]
    for copy in loads:
        copy.start()

    def weight_part(kind, chunk):
        return weights[kind][:, :, chunk].reshape(block_count * slice_width, width)

    if not before:
        tokens[token_part(rows.place), :] = own_ref[...]
    build_places(dims, rows, routes_ref, place, place_t, None)

    def recompute(part):
        gate_val = dot_nt(slots[part, :], gate[...].reshape(-1, gate.shape[2]))
        up_val = dot_nt(slots[part, :], up[...].reshape(-1, up.shape[2]))
        sigmoid = jax.nn.sigmoid(gate_val)
        value = gate_val * sigmoid
        act[part, :] = (value * up_val).astype(jnp.bfloat16)
        silu[part, :] = value.astype(jnp.bfloat16)
        slope[part, :] = (up_val * sigmoid * (1.0 + gate_val * (1.0 - sigmoid))).astype(
            jnp.bfloat16
        )

    def slot_gates(part):
        picked = dot_nn(place[part, :], gates_ref[...].astype(jnp.bfloat16))
        block = iota(picked.shape, 1)
        slot = iota(picked.shape, 0) + part.start
        in_block = (slot >= block * slot_rows) & (slot < (block + 1) * slot_rows)
        weight[part, :] = jnp.sum(jnp.where(in_block, picked, 0.0), axis=1, keepdims=True)

    def recompute_all():
        load_slots.wait()
        for copy in loads:
            copy.wait()
        over_blocks(all_slots, slot_step, recompute)

    over_blocks(all_slots, slot_step, slot_gates)
    if before:
        load_tokens.wait()
    else:
        recompute_all()
    load_returned.wait()

    def dispatch(index, chunk):
        if not before:
            gather.arrive(index, chunk)

            @pl.when(index + 2 < chunks)
            def _():
                later = pl.ds(pl.multiple_of((index + 2) * width, width), width)
                gather.start_own(index + 2, later)


        def rows_of(part):
            grad = dot_nn(place[part, :], tokens[:, chunk])
            share = jnp.sum(
                grad * returned[part, chunk].astype(jnp.float32), axis=1, keepdims=True
            )
            send[part, chunk] = (weight[part, :] * grad).astype(jnp.bfloat16)

            @pl.when(index == 0)
            def _():
                inner[part, :] = share

            @pl.when(index > 0)
            def _():
                inner[part, :] += share

        over_blocks(all_slots, all_slots, rows_of)
        there.start(index, chunk)
        received[slot_part(cols.place), chunk] = send[slot_part(cols.place), chunk]

    over_chunks(chunks, width, dispatch)

    def pairs(part):
        picked = slot_block((all_slots, pair_send.shape[1]), 0, slot_rows)
        spread = jnp.where(picked, inner[...], 0.0)
        high = spread.astype(jnp.bfloat16)
        low = (spread - high.astype(jnp.float32)).astype(jnp.bfloat16)
        pair_send[part, :] = dot_nn(place_t[part, :], high) + dot_nn(place_t[part, :], low)

    if before:
        load_mixed = pltpu.make_async_copy(opening_in[0], tokens, local_sem.at[7])
        load_mixed.start()
    over_blocks(all_tokens, token_rows, pairs)
    pair.start(0, None)
    if before:
        load_mixed.wait()

        @pl.when(~before.is_middle())
        def _():
            over_chunks(chunks, width, before.pass_on)

        recompute_all()

    def project(index, chunk):
        if before:
            pl.when(before.is_middle())(functools.partial(before.pass_on, index, chunk))
        there.wait_recv(index, chunk)

        def rows_of(part):
            grad = dot_nt(received[part, chunk], weight_part(2, chunk))

            @pl.when(index == 0)
            def _():
                grad_act[part, :] = grad

            @pl.when(index > 0)
            def _():
                grad_act[part, :] += grad

        over_blocks(all_slots, all_slots, rows_of)

    over_chunks(chunks, width, project)

    def slopes(part):
        grad = grad_act[part, :]
        grad_gate[part, :] = (grad * slope[part, :].astype(jnp.float32)).astype(jnp.bfloat16)
        grad_up[part, :] = (grad * silu[part, :].astype(jnp.float32)).astype(jnp.bfloat16)

    over_blocks(all_slots, slot_step, slopes)

    def give_back(index, chunk):
        there.wait_send(index, chunk)

        def rows_of(part):
            send[part, chunk] = (
                dot_nn(grad_gate[part, :], weight_part(0, chunk))
                + dot_nn(grad_up[part, :], weight_part(1, chunk))
            ).astype(jnp.bfloat16)

        over_blocks(all_slots, all_slots, rows_of)
        back.start(index, chunk)

    over_chunks(chunks, width, give_back)

    returned[slot_part(cols.place), :] = send[slot_part(cols.place), :]
    if before:
        over_chunks(
            chunks, width, lambda index, chunk: before.total(index, chunk, opening_out[0])
        )
        over_chunks(chunks, width, before.wait_send)

    if not before:
        over_chunks(chunks, width, gather.wait_send)

    def combine(index, chunk):
        back.wait_recv(index, chunk)

        def rows_of(part):
            tokens[part, chunk] = dot_nn(place_t[part, :], returned[:, chunk]).astype(jnp.bfloat16)

        over_blocks(all_tokens, token_rows, rows_of)
        pl.when(~home.is_middle())(functools.partial(home.pass_on, index, chunk))

        @pl.when(home.is_middle() & (index > 0))
        def _():
            before = pl.ds(pl.multiple_of((index - 1) * width, width), width)
            home.pass_on(index - 1, before)

    over_chunks(chunks, width, combine)
    last_chunk = pl.ds((chunks - 1) * width, width)
    pl.when(home.is_middle())(functools.partial(home.pass_on, chunks - 1, last_chunk))
    def keep(kind, index):
        return pltpu.make_async_copy(
            staged.at[index % 2], grads_out[index].at[kind], local_sem.at[2 + index % 2]
        )

    for kind, (left, right) in enumerate(((grad_gate, slots), (grad_up, slots), (act, received))):
        turned[...] = left[...].T
        for index in range(block_count):
            if index >= 2:
                keep(kind, index - 2).wait()
            part = slice(index * slice_width, (index + 1) * slice_width)
            staged[index % 2] = dot_nn(turned[part, :], right[...]).astype(jnp.bfloat16)
            keep(kind, index).start()
        for index in range(max(block_count - 2, 0), block_count):
            keep(kind, index).wait()

    pair.wait_recv(0, None)
    grad_pair = pair_send[token_part(rows.place), :]
    for ahead in range(1, group_rows):
        shifted = pltpu.roll(pair_landed[group_rows - ahead - 1], ahead * col_count, 1)
        grad_pair = grad_pair + shifted
    grad_pair = grad_pair[:, :E]
    gates = gates_ref[token_part(rows.place), :]
    grad_logits = gates * (grad_pair - jnp.sum(gates * grad_pair, axis=-1, keepdims=True))
    grad_logits = grad_logits.astype(jnp.bfloat16)
    router_grad_ref[...] = dot_nn(grad_logits.astype(jnp.float32).T.astype(jnp.bfloat16), normed_ref[...])

    def finish(index, chunk):
        home.total(index, chunk, sum_ref)
        sum_ref[:, chunk] += dot_nn(grad_logits, router_ref[:, chunk])

    over_chunks(chunks, width, finish)

    def drain(index, chunk):
        back.wait_send(index, chunk)
        home.wait_send(index, chunk)

    over_chunks(chunks, width, drain)
    pair.wait_send(0, None)


def moe_forward(
    dims, row_count, layer, own, routes, router, weights, moving, next_blocks, closing
):
    group_rows, col_count, copies, token_rows, slot_rows, chunks, width = dims
    all_tokens, all_slots = group_rows * token_rows, col_count * slot_rows
    model_width = own.shape[1]
    slice_width = weights[0].shape[-2]
    hidden = row_count * slice_width
    gather_dims = (row_count, col_count // 2) if next_blocks else None
    dense_sems = DenseGather.sems(gather_dims, 2) if next_blocks else []
    vmem = pl.BlockSpec(memory_space=pltpu.VMEM)
    outside = pl.BlockSpec(memory_space=pl.ANY)
    every_row = jax.ShapeDtypeStruct((all_tokens, model_width), jnp.bfloat16)
    slot_array = pltpu.VMEM((all_slots, model_width), jnp.bfloat16)
    hidden_wide = pltpu.VMEM((all_slots, hidden), jnp.float32)
    weight_array = pltpu.VMEM((row_count, slice_width, model_width), jnp.bfloat16)
    return pl.pallas_call(
        functools.partial(
            moe_forward_kernel, dims, row_count, layer, moving, gather_dims, bool(closing)
        ),
        out_shape=(
            every_row if closing else jax.ShapeDtypeStruct((token_rows, model_width), jnp.float32),
            jax.ShapeDtypeStruct((all_tokens, E), jnp.float32),
            jax.ShapeDtypeStruct((all_slots, model_width), jnp.bfloat16),
            jax.ShapeDtypeStruct((all_slots, model_width), jnp.bfloat16),
            *([every_row] * len(closing)),
            *(moved_shape(row_count, weights[kind]) for kind in moving),
            *(gathered_shapes(gather_dims, next_blocks) if next_blocks else ()),
        ),
        in_specs=[vmem] * 3 + [outside] * (3 + len(next_blocks) + len(closing)),
        out_specs=(outside if closing else vmem, vmem)
        + (outside,) * (2 + len(closing) + len(moving) + len(next_blocks)),
        scratch_shapes=[
            pltpu.VMEM((all_slots, all_tokens), jnp.bfloat16),
            pltpu.VMEM((all_tokens, all_slots), jnp.bfloat16),
            pltpu.VMEM((all_tokens, E), jnp.float32),
            weight_array,
            weight_array,
            weight_array,
            pltpu.VMEM((all_tokens, model_width), jnp.bfloat16),
            slot_array,
            slot_array,
            hidden_wide,
            hidden_wide,
            pltpu.VMEM((all_slots, hidden), jnp.bfloat16),
            slot_array,
            pltpu.VMEM((group_rows + 1, token_rows, model_width), jnp.bfloat16),
            *LineGather.sems(chunks, group_rows),
            *exchange_sems(chunks, col_count),
            *exchange_sems(chunks, col_count),
            *LineSum.sems(chunks, group_rows),
            pltpu.SemaphoreType.DMA((6,)),
            *(WeightMove.sems(row_count) * len(moving)),
            *((*LineGather.sems(chunks, group_rows), pltpu.SemaphoreType.DMA) if closing else ()),
            *dense_sems,
        ],
        compiler_params=pltpu.CompilerParams(
            collective_id=1 + 7 * layer, has_side_effects=True, vmem_limit_bytes=vmem_most
        ),
        cost_estimate=long_cost,
        name="moe_forward",
    )(own, routes, router, *weights, *next_blocks, *closing)


def moe_backward(dims, own, routes, router, gates, normed, slots, returned, weights, opening):
    group_rows, col_count, copies, token_rows, slot_rows, chunks, width = dims
    all_tokens, all_slots = group_rows * token_rows, col_count * slot_rows
    model_width = own.shape[1]
    opened = len(opening)
    block_count, slice_width = weights[0].shape[:2]
    grads = jax.ShapeDtypeStruct((3, slice_width, model_width), jnp.bfloat16)
    hidden = block_count * slice_width
    vmem = pl.BlockSpec(memory_space=pltpu.VMEM)
    outside = pl.BlockSpec(memory_space=pl.ANY)
    slot_array = pltpu.VMEM((all_slots, model_width), jnp.bfloat16)
    hidden_narrow = pltpu.VMEM((all_slots, hidden), jnp.bfloat16)
    weight_array = pltpu.VMEM((block_count, slice_width, model_width), jnp.bfloat16)
    return pl.pallas_call(
        functools.partial(moe_backward_kernel, dims, bool(opening)),
        out_shape=(
            jax.ShapeDtypeStruct((token_rows, model_width), jnp.float32),
            jax.ShapeDtypeStruct((E, model_width), jnp.float32),
            *([grads] * block_count),
            *([jax.ShapeDtypeStruct((token_rows, model_width), jnp.float32)] * opened),
        ),
        in_specs=[outside if opening else vmem]
        + [vmem] * 4
        + [outside] * (5 + opened),
        out_specs=(vmem, vmem) + (outside,) * block_count + (vmem,) * opened,
        scratch_shapes=[
            pltpu.VMEM((all_slots, all_tokens), jnp.bfloat16),
            pltpu.VMEM((all_tokens, all_slots), jnp.bfloat16),
            weight_array,
            weight_array,
            weight_array,
            pltpu.VMEM((all_tokens, model_width), jnp.bfloat16),
            slot_array,
            slot_array,
            hidden_narrow,
            hidden_narrow,
            hidden_narrow,
            pltpu.VMEM((all_slots, 1), jnp.float32),
            pltpu.VMEM((all_slots, 1), jnp.float32),
            slot_array,
            pltpu.VMEM((all_slots, hidden), jnp.float32),
            hidden_narrow,
            hidden_narrow,
            slot_array,
            pltpu.VMEM((hidden, all_slots), jnp.bfloat16),
            pltpu.VMEM((2, slice_width, model_width), jnp.bfloat16),
            pltpu.VMEM((group_rows + 1, token_rows, model_width), jnp.bfloat16),
            pltpu.VMEM((all_tokens, 128), jnp.float32),
            pltpu.VMEM((max(group_rows - 1, 1), token_rows, 128), jnp.float32),
            *LineGather.sems(chunks, group_rows),
            *exchange_sems(chunks, col_count),
            *exchange_sems(chunks, col_count),
            *LineSum.sems(chunks, group_rows),
            *exchange_sems(1, group_rows),
            pltpu.SemaphoreType.DMA((8,)),
            *(
                (
                    pltpu.VMEM((group_rows + 1, token_rows, model_width), jnp.bfloat16),
                    *LineSum.sems(chunks, group_rows),
                )
                if opening
                else ()
            ),
        ],
        compiler_params=pltpu.CompilerParams(
            collective_id=9 if opening else 2, has_side_effects=True, vmem_limit_bytes=vmem_most
        ),
        cost_estimate=long_cost,
        name="moe_backward",
    )(own, routes, router, gates, normed, slots, returned, *weights, *opening)


def col_pairs():
    col_index = lax.axis_index("col")
    return col_index // 2, lax.rem(col_index, 2)


def dense_peers(row_count, pair_count):
    row_index = lax.axis_index("row")
    pair, side = col_pairs()
    rows = Peers(row_count, row_index, lambda place: {"row": place})
    pairs = Peers(pair_count, pair, lambda place: {"col": place * 2 + side})
    sides = Peers(2, side, lambda place: {"col": pair * 2 + place})
    return rows, pairs, sides


def reduce_dense_kernel(
    dims,
    normed_ref,
    grad_proj_ref,
    grad_mid_ref,
    attended_ref,
    small_ref,
    qkv_ref,
    out_ref,
    small_out_ref,
    *scratch,
):
    row_count, pair_count = dims
    kinds = 3
    buffers = [scratch[6 * kind : 6 * kind + 6] for kind in range(kinds)]
    sems = scratch[6 * kinds : 12 * kinds]
    normed_t, grad_proj, grad_mid_t, attended = scratch[12 * kinds :]
    side_sems = [(sems[6 * kind], sems[6 * kind + 1]) for kind in range(kinds)]
    pair_sems = [(sems[6 * kind + 2], sems[6 * kind + 3]) for kind in range(kinds)]
    row_sems = [(sems[6 * kind + 4], sems[6 * kind + 5]) for kind in range(kinds)]
    rows, pairs, sides = dense_peers(row_count, pair_count)
    other = 1 - sides.place

    def spread(target, source, turn):
        count = target.shape[0]
        size = source.shape[1] // count
        for index in range(count):
            part = source[:, index * size : (index + 1) * size]
            target[index] = part.T if turn else part

    spread(normed_t, normed_ref, True)
    spread(grad_proj, grad_proj_ref, False)
    spread(grad_mid_t, grad_mid_ref, True)
    spread(attended, attended_ref, False)

    def block(kind, row, pair, side):
        col = pair * 2 + side
        if kind == 0:
            return dot_nn(normed_t[row], grad_proj[col])
        if kind == 1:
            return dot_nn(grad_mid_t[col], attended[row])
        return small_ref[col, row].astype(jnp.float32)

    greet((rows, pairs, sides))
    outputs = (qkv_ref, out_ref, small_out_ref)

    def side_copy(kind, pair):
        side_send, side_recv = buffers[kind][0], buffers[kind][1]
        return send_to(
            side_send.at[pair],
            side_recv.at[pair],
            side_sems[kind],
            pair,
            sides.device_of(other),
        )

    def pair_copy(kind, step, row):
        place = pairs.ahead(step)
        half, pair_recv = buffers[kind][2], buffers[kind][3]
        return send_to(
            half.at[place, row],
            pair_recv.at[step - 1, row],
            pair_sems[kind],
            (step - 1) * row_count + row,
            pairs.device_of(place),
        )

    def row_copy(kind, step):
        place = rows.ahead(step)
        whole, row_recv = buffers[kind][4], buffers[kind][5]
        return send_to(
            whole.at[place],
            row_recv.at[step - 1],
            row_sems[kind],
            step - 1,
            rows.device_of(place),
        )

    def first(step, carry):
        pair = lax.rem(pairs.place + step, pair_count)
        for kind in range(kinds):
            for row in range(row_count):
                buffers[kind][0][pair, row] = block(kind, row, pair, other).astype(jnp.bfloat16)
            side_copy(kind, pair).start()
        return carry

    lax.fori_loop(1, pair_count + 1, first, 0)

    def second(step, carry):
        pair = lax.rem(pairs.place + step, pair_count)
        for kind in range(kinds):
            side_copy(kind, pair).wait_recv()
            side_recv, half = buffers[kind][1], buffers[kind][2]
            for row in range(row_count):
                total = block(kind, row, pair, sides.place)
                total = total + side_recv[pair, row].astype(jnp.float32)
                half[pair, row] = total.astype(jnp.bfloat16)

                @pl.when(step < pair_count)
                def _():
                    pair_copy(kind, step, row).start()

        return carry

    lax.fori_loop(1, pair_count + 1, second, 0)

    def third(step, carry):
        row = lax.rem(rows.place + step, row_count)
        for kind in range(kinds):
            half, pair_recv, whole = buffers[kind][2], buffers[kind][3], buffers[kind][4]
            total = half[pairs.place, row].astype(jnp.float32)
            for ahead in range(1, pair_count):
                pair_copy(kind, ahead, row).wait_recv()
                total = total + pair_recv[ahead - 1, row].astype(jnp.float32)

            whole[row] = total.astype(jnp.bfloat16)

            @pl.when(step < row_count)
            def _():
                row_copy(kind, step).start()

        return carry

    lax.fori_loop(1, row_count + 1, third, 0)
    for kind in range(kinds):
        whole, row_recv = buffers[kind][4], buffers[kind][5]
        total = whole[rows.place].astype(jnp.float32)
        for step in range(1, row_count):
            row_copy(kind, step).wait_recv()
            total = total + row_recv[step - 1].astype(jnp.float32)
        outputs[kind][...] = total

    def drain_sides(pair, carry):
        for kind in range(kinds):
            side_copy(kind, pair).wait_send()
        return carry

    lax.fori_loop(0, pair_count, drain_sides, 0)

    def drain_pairs(step, carry):
        for kind in range(kinds):
            for row in range(row_count):
                pair_copy(kind, step, row).wait_send()
        return carry

    lax.fori_loop(1, pair_count, drain_pairs, 0)
    for kind in range(kinds):
        for step in range(1, row_count):
            row_copy(kind, step).wait_send()


def reduce_dense(row_count, col_count, normed, grad_projected, grad_mid_b, attended, small):
    token_rows, model_width = normed.shape
    qkv_width, out_rows = grad_projected.shape[1], attended.shape[1]
    pair_count = col_count // 2
    shapes = (
        (model_width // row_count, qkv_width // col_count),
        (model_width // col_count, out_rows // row_count),
        small.shape[2:],
    )
    vmem = pl.BlockSpec(memory_space=pltpu.VMEM)
    scratch = []
    sems = []
    for height, breadth in shapes:
        for lead in (
            (pair_count, row_count),
            (pair_count, row_count),
            (pair_count, row_count),
            (max(pair_count - 1, 1), row_count),
            (row_count,),
            (max(row_count - 1, 1),),
        ):
            scratch.append(pltpu.VMEM((*lead, height, breadth), jnp.bfloat16))
        for count in (pair_count, max(pair_count - 1, 1) * row_count, max(row_count - 1, 1)):
            sems.extend([pltpu.SemaphoreType.DMA((count,))] * 2)
    operands = [
        pltpu.VMEM((row_count, shapes[0][0], token_rows), jnp.bfloat16),
        pltpu.VMEM((col_count, token_rows, shapes[0][1]), jnp.bfloat16),
        pltpu.VMEM((col_count, shapes[1][0], token_rows), jnp.bfloat16),
        pltpu.VMEM((row_count, token_rows, shapes[1][1]), jnp.bfloat16),
    ]
    return pl.pallas_call(
        functools.partial(reduce_dense_kernel, (row_count, pair_count)),
        out_shape=tuple(jax.ShapeDtypeStruct(shape, jnp.float32) for shape in shapes),
        in_specs=[vmem] * 5,
        out_specs=(vmem,) * 3,
        scratch_shapes=scratch + sems + operands,
        compiler_params=pltpu.CompilerParams(
            collective_id=3, has_side_effects=True, vmem_limit_bytes=vmem_most
        ),
        cost_estimate=no_cost,
        name="reduce_dense",
    )(normed, grad_projected, grad_mid_b, attended, small)


class DenseGather:
    def __init__(self, dims, own_blocks, fulls, sems):
        self.row_count, self.pair_count = dims
        self.rows, self.pairs, self.sides = dense_peers(*dims)
        self.own_blocks = own_blocks
        self.fulls = fulls
        self.kinds = range(len(own_blocks))
        self.row_sems = [sems[6 * kind : 6 * kind + 2] for kind in self.kinds]
        self.pair_sems = [sems[6 * kind + 2 : 6 * kind + 4] for kind in self.kinds]
        self.side_sems = [sems[6 * kind + 4 : 6 * kind + 6] for kind in self.kinds]
        self.local_sems = sems[6 * len(own_blocks)]

    @staticmethod
    def sems(dims, kinds):
        row_count, pair_count = dims
        sems = []
        for _ in range(kinds):
            for count in (
                max(row_count - 1, 1),
                max(pair_count - 1, 1) * row_count,
                pair_count * row_count,
            ):
                sems.extend([pltpu.SemaphoreType.DMA((count,))] * 2)
        return sems + [pltpu.SemaphoreType.DMA((kinds,))]

    def groups(self):
        return (self.rows, self.pairs, self.sides)

    def spot(self, kind, row, pair, side):
        col = pair * 2 + side
        height = self.own_blocks[kind].shape[0]
        return self.fulls[kind].at[row, pl.ds(pl.multiple_of(col * height, height), height), :]

    def own_spot(self, kind):
        return self.spot(kind, self.rows.place, self.pairs.place, self.sides.place)

    def own_copy(self, kind):
        return pltpu.make_async_copy(
            self.own_blocks[kind], self.own_spot(kind), self.local_sems.at[kind]
        )

    def row_copy(self, kind, step):
        return send_to(
            self.own_blocks[kind],
            self.own_spot(kind),
            self.row_sems[kind],
            step - 1,
            self.rows.device_of(self.rows.ahead(step)),
        )

    def row_landed(self, kind, step):
        place = self.rows.behind(step)
        landed = self.spot(kind, place, self.pairs.place, self.sides.place)
        return send_to(
            landed, landed, self.row_sems[kind], step - 1, self.rows.device_of(place)
        )

    def pair_copy(self, kind, step, number):
        block = self.spot(kind, self.rows.behind(number), self.pairs.place, self.sides.place)
        return send_to(
            block if number else self.own_blocks[kind],
            block,
            self.pair_sems[kind],
            (step - 1) * self.row_count + number,
            self.pairs.device_of(self.pairs.ahead(step)),
        )

    def pair_landed(self, kind, step, number):
        place = self.pairs.behind(step)
        landed = self.spot(kind, self.rows.behind(number), place, self.sides.place)
        return send_to(
            landed,
            landed,
            self.pair_sems[kind],
            (step - 1) * self.row_count + number,
            self.pairs.device_of(place),
        )

    def side_copy(self, kind, step, number):
        place = self.pairs.behind(step)
        block = self.spot(kind, self.rows.behind(number), place, self.sides.place)
        return send_to(
            block if step or number else self.own_blocks[kind],
            block,
            self.side_sems[kind],
            step * self.row_count + number,
            self.sides.device_of(1 - self.sides.place),
        )

    def side_landed(self, kind, step, number):
        place = self.pairs.behind(step)
        landed = self.spot(kind, self.rows.behind(number), place, 1 - self.sides.place)
        return send_to(
            landed,
            landed,
            self.side_sems[kind],
            step * self.row_count + number,
            self.sides.device_of(1 - self.sides.place),
        )

    def start(self, kind):
        self.own_copy(kind).start()
        for step in range(1, self.row_count):
            self.row_copy(kind, step).start()
        for step in range(1, self.pair_count):
            self.pair_copy(kind, step, 0).start()
        self.side_copy(kind, 0, 0).start()

    def pass_rows(self, kind):
        for number in range(1, self.row_count):
            self.row_landed(kind, number).wait_recv()
            for step in range(1, self.pair_count):
                self.pair_copy(kind, step, number).start()
            self.side_copy(kind, 0, number).start()

    def pass_pairs(self, kind):
        for number in range(self.row_count):
            for step in range(1, self.pair_count):
                self.pair_landed(kind, step, number).wait_recv()
                self.side_copy(kind, step, number).start()

    def finish(self, kind):
        self.own_copy(kind).wait()
        for step in range(self.pair_count):
            for number in range(self.row_count):
                self.side_landed(kind, step, number).wait_recv()
        for step in range(1, self.row_count):
            self.row_copy(kind, step).wait_send()
        for number in range(self.row_count):
            for step in range(1, self.pair_count):
                self.pair_copy(kind, step, number).wait_send()
            for step in range(self.pair_count):
                self.side_copy(kind, step, number).wait_send()


def gathered_shapes(dims, blocks):
    row_count, pair_count = dims
    return tuple(
        jax.ShapeDtypeStruct(
            (row_count, 2 * pair_count * block.shape[0], block.shape[1]), block.dtype
        )
        for block in blocks
    )


def gather_dense_kernel(
    dims,
    copies,
    qkv_ref,
    out_ref,
    routes_ref,
    router_ref,
    shards_ref,
    qkv_full,
    out_full,
    routes_all,
    router_all,
    moved,
    *sems,
):
    gather = DenseGather(dims, (qkv_ref, out_ref), (qkv_full, out_full), sems[:13])
    small_send, small_recv, local_sems = sems[13:16]
    rows = gather.rows
    move = WeightMove(rows, copies, 0, shards_ref, moved, sems[16:])
    small = [
        Exchange(
            rows,
            small_send,
            small_recv,
            lambda place, chunk, ref=ref: ref,
            lambda place, step, chunk, full=full: full.at[place],
        )
        for ref, full in ((routes_ref, routes_all), (router_ref, router_all))
    ]
    greet(gather.groups())
    own_copies = [
        pltpu.make_async_copy(ref, full.at[rows.place], local_sems.at[number])
        for number, (ref, full) in enumerate(((routes_ref, routes_all), (router_ref, router_all)))
    ]
    for kind in range(2):
        gather.start(kind)
        own_copies[kind].start()
        small[kind].start(kind, None)
    move.start()
    for kind in range(2):
        gather.pass_rows(kind)
    for kind in range(2):
        gather.pass_pairs(kind)
    for kind in range(2):
        small[kind].wait_recv(kind, None)
        gather.finish(kind)
        own_copies[kind].wait()
        small[kind].wait_send(kind, None)
    move.wait_recv()
    move.wait_send()


def gather_dense(row_count, col_count, copies, qkv_block, out_block, routes, router, shards):
    dims = (row_count, col_count // 2)
    outside = pl.BlockSpec(memory_space=pl.ANY)
    return pl.pallas_call(
        functools.partial(gather_dense_kernel, dims, copies),
        out_shape=gathered_shapes(dims, (qkv_block, out_block))
        + tuple(jax.ShapeDtypeStruct((row_count, *x.shape), x.dtype) for x in (routes, router))
        + (moved_shape(row_count, shards),),
        in_specs=[outside] * 5,
        out_specs=(outside,) * 5,
        scratch_shapes=DenseGather.sems(dims, 2)
        + [
            *exchange_sems(2, row_count),
            pltpu.SemaphoreType.DMA((2,)),
            *WeightMove.sems(row_count),
        ],
        compiler_params=pltpu.CompilerParams(collective_id=4, has_side_effects=True),
        cost_estimate=no_cost,
        name="gather_dense",
    )(qkv_block, out_block, routes, router, shards)


def order_grads_kernel(layer_count, block_count, *refs):
    blocks = refs[: layer_count * block_count]
    outputs = refs[layer_count * block_count : layer_count * block_count + 3]
    came, wide, in_sems, out_sems = refs[layer_count * block_count + 3 :]
    row_index = lax.axis_index("row")
    items = [
        (layer, step, kind)
        for layer in range(layer_count)
        for step in range(block_count)
        for kind in range(3)
    ]

    def load(number):
        layer, step, kind = items[number]
        return pltpu.make_async_copy(
            blocks[layer * block_count + step].at[kind],
            came.at[number % 4],
            in_sems.at[number % 4],
        )

    def store(number):
        layer, step, kind = items[number]
        expert = lax.rem(row_index + step, block_count)
        return pltpu.make_async_copy(
            wide.at[number % 4], outputs[kind].at[layer, expert], out_sems.at[number % 4]
        )

    count = len(items)
    for number in range(min(3, count)):
        load(number).start()
    for number in range(count):
        if number + 3 < count:
            load(number + 3).start()
        load(number).wait()
        if number >= 4:
            store(number - 4).wait()
        wide[number % 4] = came[number % 4].astype(jnp.float32)
        store(number).start()
    for number in range(max(count - 4, 0), count):
        store(number).wait()


def order_grads(layers):
    layer_count, block_count = len(layers), len(layers[0])
    _, slice_width, model_width = layers[0][0].shape
    outside = pl.BlockSpec(memory_space=pl.ANY)
    shape = jax.ShapeDtypeStruct((layer_count, block_count, slice_width, model_width), jnp.float32)
    return pl.pallas_call(
        functools.partial(order_grads_kernel, layer_count, block_count),
        out_shape=(shape,) * 3,
        in_specs=[outside] * (layer_count * block_count),
        out_specs=(outside,) * 3,
        scratch_shapes=[
            pltpu.VMEM((4, slice_width, model_width), jnp.bfloat16),
            pltpu.VMEM((4, slice_width, model_width), jnp.float32),
            pltpu.SemaphoreType.DMA((4,)),
            pltpu.SemaphoreType.DMA((4,)),
        ],
        compiler_params=pltpu.CompilerParams(vmem_limit_bytes=vmem_most),
        cost_estimate=no_cost,
        name="order_grads",
    )(*[block for blocks in layers for block in blocks])


def pieces_nt(left, weights_ref):
    pieces, _, size = weights_ref.shape
    total = None
    for index in range(pieces):
        part = dot_nt(left[:, index * size : (index + 1) * size], weights_ref[index])
        total = part if total is None else total + part
    return total


def rotate(values, cosine, sine):
    return values * cosine + pltpu.roll(values, HEAD_SIZE // 2, 1) * sine


def head_lanes(head):
    return slice(2 * head * HEAD_SIZE, 2 * (head + 1) * HEAD_SIZE)


def key_lanes(head):
    return slice(2 * head * HEAD_SIZE, (2 * head + 1) * HEAD_SIZE)


def value_lanes(head):
    return slice((2 * head + 1) * HEAD_SIZE, 2 * (head + 1) * HEAD_SIZE)


def seen_keys(token_rows):
    position = lax.axis_index("col") * token_rows + iota((1, token_rows), 1)
    return (position // BLOCK + 1) * BLOCK


def attend_forward_kernel(
    dims,
    x_ref,
    gain_attn_ref,
    gain_moe_ref,
    cosine_ref,
    sine_ref,
    qkv_ref,
    out_w_ref,
    shards_ref,
    mid_ref,
    normed_ref,
    q_ref,
    kv_out,
    attended_ref,
    lse_ref,
    normed_moe_ref,
    moved,
    kv_all,
    value_t,
    proj,
    send_sem,
    recv_sem,
    local_sem,
    *move_sems,
):
    col_count, row_count, copies, layer, score_scale = dims
    token_rows = x_ref.shape[0]
    group = QUERY_HEADS // KEY_VALUE_HEADS
    kv_width = KEY_VALUE_HEADS * HEAD_SIZE
    cols = col_peers(col_count)

    def part(place):
        return pl.ds(pl.multiple_of(place * token_rows, token_rows), token_rows)

    share = Exchange(
        cols,
        send_sem,
        recv_sem,
        lambda place, chunk: kv_all.at[part(cols.place), chunk],
        lambda place, step, chunk: kv_all.at[part(place), chunk],
    )
    move = WeightMove(all_rows(row_count), copies, layer, shards_ref, moved, move_sems)
    greet((cols, move.rows))
    move.start()
    x = x_ref[...]
    inverse = lax.rsqrt(jnp.mean(x * x, axis=-1, keepdims=True) + eps_norm)
    normed_ref[...] = (x * inverse * gain_attn_ref[...]).astype(jnp.bfloat16)
    proj[...] = pieces_nt(normed_ref[...], qkv_ref)
    own = part(cols.place)
    for head in range(KEY_VALUE_HEADS):
        start = QUERY_FEATURES + head * HEAD_SIZE
        turned = rotate(proj[:, start : start + HEAD_SIZE], cosine_ref[...], sine_ref[...])
        kv_all[own, key_lanes(head)] = turned.astype(jnp.bfloat16)
        start = start + kv_width
        kv_all[own, value_lanes(head)] = proj[:, start : start + HEAD_SIZE].astype(jnp.bfloat16)
        share.start(head, head_lanes(head))
    for head in range(QUERY_HEADS):
        lanes = slice(head * HEAD_SIZE, (head + 1) * HEAD_SIZE)
        q_ref[:, lanes] = rotate(proj[:, lanes], cosine_ref[...], sine_ref[...]).astype(
            jnp.bfloat16
        )
    seen = seen_keys(token_rows)
    for kv_head in range(KEY_VALUE_HEADS):
        share.wait_recv(kv_head, head_lanes(kv_head))
        value_t[...] = kv_all[:, value_lanes(kv_head)].T

        def head_step(step, carry, kv_head=kv_head):
            index = kv_head * group + step
            lanes = pl.ds(pl.multiple_of(index * HEAD_SIZE, HEAD_SIZE), HEAD_SIZE)
            scores = dot_nt(kv_all[:, key_lanes(kv_head)], q_ref[:, lanes]) * score_scale
            scores = jnp.where(iota(scores.shape, 0) < seen, scores, masked_score)
            peak = jnp.max(scores, axis=0, keepdims=True)
            exponent = jnp.exp(scores - peak)
            total = jnp.sum(exponent, axis=0, keepdims=True)
            attended = dot_nn(value_t[...], exponent.astype(jnp.bfloat16)) / total
            attended_ref[:, lanes] = attended.T.astype(jnp.bfloat16)
            lse_ref[index] = peak + jnp.log(total)
            return carry

        lax.fori_loop(0, group, head_step, 0)
    keep = pltpu.make_async_copy(kv_all, kv_out, local_sem)
    keep.start()
    mid = x_ref[...] + pieces_nt(attended_ref[...], out_w_ref)
    mid_ref[...] = mid
    inverse = lax.rsqrt(jnp.mean(mid * mid, axis=-1, keepdims=True) + eps_norm)
    normed_moe_ref[...] = (mid * inverse * gain_moe_ref[...]).astype(jnp.bfloat16)
    for head in range(KEY_VALUE_HEADS):
        share.wait_send(head, head_lanes(head))
    keep.wait()
    move.wait_recv()
    move.wait_send()


def attend_forward(
    col_count,
    row_count,
    copies,
    layer,
    x,
    gain_attn,
    gain_moe,
    cosine,
    sine,
    qkv_full,
    out_full,
    shards,
):
    token_rows, model_width = x.shape
    seq_rows = col_count * token_rows
    kv_width = KEY_VALUE_HEADS * HEAD_SIZE
    vmem = pl.BlockSpec(memory_space=pltpu.VMEM)
    outside = pl.BlockSpec(memory_space=pl.ANY)
    rows_b = jax.ShapeDtypeStruct((token_rows, model_width), jnp.bfloat16)
    heads_b = jax.ShapeDtypeStruct((token_rows, QUERY_FEATURES), jnp.bfloat16)
    return pl.pallas_call(
        functools.partial(
            attend_forward_kernel, (col_count, row_count, copies, layer, HEAD_SIZE ** (-0.5))
        ),
        out_shape=(
            jax.ShapeDtypeStruct((token_rows, model_width), jnp.float32),
            rows_b,
            heads_b,
            jax.ShapeDtypeStruct((seq_rows, 2 * kv_width), jnp.bfloat16),
            heads_b,
            jax.ShapeDtypeStruct((QUERY_HEADS, 1, token_rows), jnp.float32),
            rows_b,
            moved_shape(row_count, shards),
        ),
        in_specs=[vmem] * 7 + [outside],
        out_specs=(vmem, vmem, vmem, outside, vmem, vmem, vmem, outside),
        scratch_shapes=[
            pltpu.VMEM((seq_rows, 2 * kv_width), jnp.bfloat16),
            pltpu.VMEM((HEAD_SIZE, seq_rows), jnp.bfloat16),
            pltpu.VMEM((token_rows, QUERY_FEATURES + 2 * kv_width), jnp.float32),
            *exchange_sems(KEY_VALUE_HEADS, col_count),
            pltpu.SemaphoreType.DMA,
            *WeightMove.sems(row_count),
        ],
        compiler_params=pltpu.CompilerParams(
            collective_id=5 + 5 * layer, has_side_effects=True, vmem_limit_bytes=vmem_most
        ),
        cost_estimate=no_cost,
        name="attend_forward",
    )(x, gain_attn, gain_moe, cosine, sine, qkv_full, out_full, shards)


def norm_backward(values, gain, incoming):
    inverse = lax.rsqrt(jnp.mean(values * values, axis=-1, keepdims=True) + eps_norm)
    scaled = incoming * gain
    inner_mean = jnp.mean(scaled * values, axis=-1, keepdims=True)
    grad = inverse * scaled - values * (inverse * inverse * inverse) * inner_mean
    return grad, jnp.sum(incoming * values * inverse, axis=0, keepdims=True)


def attend_backward_kernel(
    dims,
    incoming_ref,
    grad_moe_ref,
    mid_ref,
    x_ref,
    gain_attn_ref,
    gain_moe_ref,
    cosine_ref,
    sine_ref,
    qkv_ref,
    out_w_ref,
    q_ref,
    kv_ref,
    attended_ref,
    lse_ref,
    grad_x_ref,
    grad_mid_ref,
    grad_proj_ref,
    grad_gain_attn_ref,
    grad_gain_moe_ref,
    grad_attended,
    key_t,
    key_sum,
    value_sum,
    grad_kv,
    landed,
    send_sem,
    recv_sem,
):
    col_count, score_scale = dims
    token_rows = x_ref.shape[0]
    group = QUERY_HEADS // KEY_VALUE_HEADS
    kv_width = KEY_VALUE_HEADS * HEAD_SIZE
    cols = col_peers(col_count)

    def part(place):
        return pl.ds(pl.multiple_of(place * token_rows, token_rows), token_rows)

    share = Exchange(
        cols,
        send_sem,
        recv_sem,
        lambda place, chunk: grad_kv.at[part(place), chunk],
        lambda place, step, chunk: landed.at[step - 1, :, chunk],
    )
    greet((cols,))
    grad, gain_sum = norm_backward(mid_ref[...], gain_moe_ref[...], grad_moe_ref[...])
    grad_gain_moe_ref[...] = gain_sum
    grad_x_ref[...] = incoming_ref[...] + grad
    grad_mid_ref[...] = grad_x_ref[...].astype(jnp.bfloat16)
    pieces, _, size = out_w_ref.shape
    for index in range(pieces):
        lanes = slice(index * size, (index + 1) * size)
        grad_attended[:, lanes] = dot_nn(grad_mid_ref[...], out_w_ref[index]).astype(jnp.bfloat16)
    seen = seen_keys(token_rows)
    for kv_head in range(KEY_VALUE_HEADS):
        key_t[...] = kv_ref[:, key_lanes(kv_head)].T
        key_sum[...] = jnp.zeros_like(key_sum)
        value_sum[...] = jnp.zeros_like(value_sum)

        def head_step(step, carry, kv_head=kv_head):
            index = kv_head * group + step
            lanes = pl.ds(pl.multiple_of(index * HEAD_SIZE, HEAD_SIZE), HEAD_SIZE)
            query = q_ref[:, lanes]
            grad_out = grad_attended[:, lanes]
            product = grad_out.astype(jnp.float32) * attended_ref[:, lanes].astype(jnp.float32)
            inner = jnp.sum(product.T, axis=0, keepdims=True)
            scores = dot_nt(kv_ref[:, key_lanes(kv_head)], query) * score_scale
            soft = jnp.where(
                iota(scores.shape, 0) < seen, jnp.exp(scores - lse_ref[index]), 0.0
            )
            grad_soft = dot_nt(kv_ref[:, value_lanes(kv_head)], grad_out)
            grad_scores = (soft * (grad_soft - inner)).astype(jnp.bfloat16)
            value_sum[...] += dot_nn(soft.astype(jnp.bfloat16), grad_out)
            key_sum[...] += dot_nn(grad_scores, query)
            grad_q = (dot_nn(key_t[...], grad_scores) * score_scale).T
            grad_q = rotate(grad_q, cosine_ref[...], -sine_ref[...])
            grad_proj_ref[:, lanes] = grad_q.astype(jnp.bfloat16)
            return carry

        lax.fori_loop(0, group, head_step, 0)
        grad_kv[:, key_lanes(kv_head)] = (key_sum[...] * score_scale).astype(jnp.bfloat16)
        grad_kv[:, value_lanes(kv_head)] = value_sum[...].astype(jnp.bfloat16)
        share.start(kv_head, head_lanes(kv_head))
    for head in range(KEY_VALUE_HEADS):
        share.wait_recv(head, head_lanes(head))
        total = grad_kv[part(cols.place), head_lanes(head)].astype(jnp.float32)
        for step in range(1, col_count):
            total = total + landed[step - 1, :, head_lanes(head)].astype(jnp.float32)
        start = QUERY_FEATURES + head * HEAD_SIZE
        grad_key = rotate(total[:, :HEAD_SIZE], cosine_ref[...], -sine_ref[...])
        grad_proj_ref[:, start : start + HEAD_SIZE] = grad_key.astype(jnp.bfloat16)
        start = start + kv_width
        grad_proj_ref[:, start : start + HEAD_SIZE] = total[:, HEAD_SIZE:].astype(jnp.bfloat16)
    pieces = qkv_ref.shape[0]
    grad_normed = [dot_nn(grad_proj_ref[...], qkv_ref[index]) for index in range(pieces)]
    grad_normed = jnp.concatenate(grad_normed, axis=1) if pieces > 1 else grad_normed[0]
    grad, gain_sum = norm_backward(x_ref[...], gain_attn_ref[...], grad_normed)
    grad_gain_attn_ref[...] = gain_sum
    grad_x_ref[...] += grad
    for head in range(KEY_VALUE_HEADS):
        share.wait_send(head, head_lanes(head))


def attend_backward(
    col_count,
    incoming,
    grad_moe,
    mid,
    x,
    gain_attn,
    gain_moe,
    cosine,
    sine,
    qkv_full,
    out_full,
    queries,
    key_value,
    attended,
    log_sums,
):
    token_rows, model_width = x.shape
    seq_rows = col_count * token_rows
    kv_width = KEY_VALUE_HEADS * HEAD_SIZE
    vmem = pl.BlockSpec(memory_space=pltpu.VMEM)
    gain = jax.ShapeDtypeStruct((1, model_width), jnp.float32)
    return pl.pallas_call(
        functools.partial(attend_backward_kernel, (col_count, HEAD_SIZE ** (-0.5))),
        out_shape=(
            jax.ShapeDtypeStruct((token_rows, model_width), jnp.float32),
            jax.ShapeDtypeStruct((token_rows, model_width), jnp.bfloat16),
            jax.ShapeDtypeStruct((token_rows, QUERY_FEATURES + 2 * kv_width), jnp.bfloat16),
            gain,
            gain,
        ),
        in_specs=[vmem] * 14,
        out_specs=(vmem,) * 5,
        scratch_shapes=[
            pltpu.VMEM((token_rows, QUERY_FEATURES), jnp.bfloat16),
            pltpu.VMEM((HEAD_SIZE, seq_rows), jnp.bfloat16),
            pltpu.VMEM((seq_rows, HEAD_SIZE), jnp.float32),
            pltpu.VMEM((seq_rows, HEAD_SIZE), jnp.float32),
            pltpu.VMEM((seq_rows, 2 * kv_width), jnp.bfloat16),
            pltpu.VMEM((max(col_count - 1, 1), token_rows, 2 * kv_width), jnp.bfloat16),
            *exchange_sems(KEY_VALUE_HEADS, col_count),
        ],
        compiler_params=pltpu.CompilerParams(
            collective_id=6, has_side_effects=True, vmem_limit_bytes=vmem_most
        ),
        cost_estimate=no_cost,
        name="attend_backward",
    )(
        incoming,
        grad_moe,
        mid,
        x,
        gain_attn,
        gain_moe,
        cosine,
        sine,
        qkv_full,
        out_full,
        queries,
        key_value,
        attended,
        log_sums,
    )


def place_first(values, group_rows, expert_pick):
    rolled = jnp.roll(values.reshape(-1, group_rows, values.shape[1]), -expert_pick, axis=1)
    return rolled.transpose(1, 0, 2).reshape(values.shape)


def place_back(values, group_rows, expert_pick):
    rolled = values.reshape(group_rows, -1, values.shape[1]).transpose(1, 0, 2)
    return jnp.roll(rolled, expert_pick, axis=1).reshape(values.shape)


def body(
    hidden_in, routes, norm_attn, w_qkv, w_out, norm_moe, w_router, w_gate, w_up, w_down, cotangent
):
    row_count = lax.axis_size("row")
    col_count = lax.axis_size("col")
    device_count = row_count * col_count
    row_index = lax.axis_index("row")
    col_index = lax.axis_index("col")
    layer_count = w_qkv.shape[0]
    token_rows = hidden_in.shape[0]
    model_width = hidden_in.shape[1]
    local_experts = w_gate.shape[1]
    slice_width = w_gate.shape[3]
    copies = row_count // local_experts
    expert_pick = row_index // copies
    slot_rows = -(-local_experts * CAP // 16) * 16
    chunks = model_width // 384
    dims = (
        local_experts,
        col_count,
        copies,
        token_rows,
        slot_rows,
        chunks,
        model_width // chunks,
    )
    positions = col_index * token_rows + jnp.arange(token_rows, dtype=jnp.int32)
    cosine, sine = rope_angles(positions, HEAD_SIZE // 2)
    cosine = jnp.concatenate([cosine, cosine], axis=1)
    sine = jnp.concatenate([-sine, sine], axis=1)

    def move_grads(grads):
        blocks = [grads[0]]
        for step in range(1, row_count):
            pairs = [(index, (index - step) % row_count) for index in range(row_count)]
            blocks.append(lax.ppermute(grads[step], "row", pairs))
        return tuple(blocks)

    def own_grads(blocks):
        ordered = jnp.roll(jnp.stack(blocks), row_index, axis=0).astype(wide_type)
        return jnp.sum(ordered.reshape(local_experts, copies, *blocks[0].shape), axis=1)

    def pieced(full):
        if full.shape[2] % 128 == 0:
            return full
        return full.transpose(1, 0, 2).reshape(1, full.shape[1], -1)

    def packed(values):
        return jnp.pad(values.reshape(-1), (0, -values.size % 2048)).reshape(-1, 128)

    shards = (w_gate.transpose(0, 1, 3, 2), w_up.transpose(0, 1, 3, 2), w_down)
    experts = []
    route_lines = routes.transpose(0, 2, 1)
    router_lines = w_router.transpose(0, 2, 1)
    qkv_full, out_full, routes_all, router_all, moved_gate = gather_dense(
        row_count,
        col_count,
        copies,
        w_qkv[0].T,
        w_out[0].T,
        packed(route_lines),
        packed(router_lines),
        shards[0],
    )
    dense = [(pieced(qkv_full), pieced(out_full))]
    routes_all = routes_all.reshape(row_count, -1)[:, : route_lines.size]
    routes_all = routes_all.reshape(row_count, *route_lines.shape)
    if copies > 1:
        routes_all = jnp.take(
            routes_all, row_index % copies + copies * jnp.arange(local_experts), axis=0
        )
    router_all = router_all.reshape(row_count, -1)[:, : router_lines.size]
    router_all = router_all.reshape(row_count, *router_lines.shape)
    router_all = router_all.transpose(1, 2, 0, 3).reshape(layer_count, E, model_width)
    routers = [
        place_first(router_all[index], local_experts, expert_pick) for index in range(layer_count)
    ]
    gains_attn = norm_attn.astype(wide_type)[:, None, :]
    gains_moe = norm_moe.astype(wide_type)[:, None, :]
    hidden = hidden_in.astype(wide_type)
    saved = []
    for layer_index in range(layer_count):
        early = 0 if layer_index else 1
        mid, normed, queries, key_value, attended, log_sums, normed_moe, moved = attend_forward(
            col_count,
            row_count,
            copies,
            layer_index,
            hidden,
            gains_attn[layer_index],
            gains_moe[layer_index],
            cosine,
            sine,
            *dense[layer_index],
            shards[early],
        )
        if layer_index == 0:
            weights, moving = [moved_gate, moved, shards[2]], (2,)
        else:
            weights, moving = [moved, shards[1], shards[2]], (1, 2)
        next_blocks = ()
        if layer_index + 1 < layer_count:
            next_blocks = (w_qkv[layer_index + 1].T, w_out[layer_index + 1].T)
        closing = (cotangent,) if layer_index + 1 == layer_count else ()
        mixed, gates, slots, returned, *rest = moe_forward(
            dims,
            row_count,
            layer_index,
            normed_moe,
            routes_all[:, layer_index],
            routers[layer_index],
            weights,
            moving,
            next_blocks,
            closing,
        )
        if closing:
            closing = (rest.pop(0), mixed)
        for kind, moved in zip(moving, rest):
            weights[kind] = moved
        experts.append(weights)
        if next_blocks:
            dense.append(tuple(pieced(full) for full in rest[len(moving) :]))
        saved.append(
            (hidden, mid, normed, queries, key_value, attended, log_sums, normed_moe)
            + (gates, slots, returned)
        )
        if not closing:
            hidden = mid + mixed
    incoming = cotangent.astype(wide_type)
    dense_results = [None] * layer_count
    small_results = [None] * layer_count
    expert_results = [None] * layer_count
    for layer_index in reversed(range(layer_count)):
        x, mid, normed, queries, key_value, attended, log_sums, normed_moe = saved[layer_index][:8]
        gates, slots, returned = saved[layer_index][8:]
        grad_moe, grad_router, *rest = moe_backward(
            dims,
            closing[0] if closing else incoming.astype(narrow_type),
            routes_all[:, layer_index],
            routers[layer_index],
            gates,
            normed_moe,
            slots,
            returned,
            experts[layer_index],
            closing[1:],
        )
        if closing:
            hidden = mid + rest.pop()
            closing = ()
        expert_results[layer_index] = move_grads(rest)
        incoming, grad_mid, grad_projected, grad_gain_attn, grad_gain_moe = attend_backward(
            col_count,
            incoming,
            grad_moe,
            mid,
            x,
            gains_attn[layer_index],
            gains_moe[layer_index],
            cosine,
            sine,
            *dense[layer_index],
            queries,
            key_value,
            attended,
            log_sums,
        )
        small = jnp.concatenate(
            [
                place_back(grad_router, local_experts, expert_pick),
                grad_gain_attn,
                grad_gain_moe,
            ],
            axis=0,
        ).astype(narrow_type)
        small = small.reshape(E + 2, device_count, -1).transpose(1, 0, 2).reshape(device_count, -1)
        small_size = small.shape[1]
        small_rows = -(-small_size // 2048) * 16
        small = jnp.pad(small, ((0, 0), (0, small_rows * 128 - small_size)))
        small = small.reshape(row_count, col_count, small_rows, 128).transpose(1, 0, 2, 3)
        grad_qkv_block, grad_out_block, small = reduce_dense(
            row_count, col_count, normed, grad_projected, grad_mid, attended, small
        )
        dense_results[layer_index] = (grad_qkv_block, grad_out_block.T)
        small_results[layer_index] = small.reshape(-1)[:small_size].reshape(E + 2, -1).T
        if layer_index > 0:
            incoming, dense_results[layer_index], expert_results[layer_index] = (
                lax.optimization_barrier(
                    (incoming, dense_results[layer_index], expert_results[layer_index])
                )
            )
    small = jnp.stack(small_results)
    if copies == 1:
        grad_gate, grad_up, grad_down = order_grads(expert_results)
    else:
        ordered = jnp.stack([own_grads(blocks) for blocks in expert_results])
        grad_gate, grad_up, grad_down = (ordered[:, :, kind] for kind in range(3))
    grad_gate, grad_up = grad_gate.swapaxes(2, 3), grad_up.swapaxes(2, 3)
    return (
        hidden,
        incoming,
        small[:, :, E],
        jnp.stack([dense_results[index][0] for index in range(layer_count)]),
        jnp.stack([dense_results[index][1] for index in range(layer_count)]),
        small[:, :, E + 1],
        small[:, :, :E],
        grad_gate,
        grad_up,
        grad_down,
    )


def solution(mesh):
    in_specs = (
        P(("row", "col"), None),
        P(None, ("row", "col"), None),
        P(),
        P(None, "row", "col"),
        P(None, "row", "col"),
        P(),
        P(None, "row", None),
        P(None, "col", None, "row"),
        P(None, "col", None, "row"),
        P(None, "col", "row", None),
        P(("row", "col"), None),
    )
    out_specs = (
        P(("row", "col"), None),
        P(("row", "col"), None),
        P(None, ("row", "col")),
        P(None, "row", "col"),
        P(None, "row", "col"),
        P(None, ("row", "col")),
        P(None, ("row", "col"), None),
        P(None, "col", None, "row"),
        P(None, "col", None, "row"),
        P(None, "col", "row", None),
    )
    return jax.shard_map(body, mesh=mesh, in_specs=in_specs, out_specs=out_specs, check_vma=False)
```

```python
import functools

import jax
import jax.numpy as jnp
from jax import lax
from jax.experimental import pallas as pl
from jax.experimental.pallas import tpu as pltpu
from jax.sharding import PartitionSpec as P

QUERY_HEADS = 12
KEY_VALUE_HEADS = 2
HEAD_SIZE = 128
E = 32
TOPK = 4
BLOCK = 256
QUERY_FEATURES = 1536
CAP = 36


eps_norm = 1e-06
rope_base = 1000000.0
masked_score = -1e30
wide_type = jnp.float32
narrow_type = jnp.bfloat16


def rope_angles(positions, half_dim):
    frequency = rope_base ** (-jnp.arange(half_dim, dtype=jnp.float32) / half_dim)
    angles = positions.astype(jnp.float32)[:, None] * frequency[None, :]
    return (jnp.cos(angles), jnp.sin(angles))


def split_rows(total, most):
    best = 16
    for step in range(16, most + 1, 16):
        if total % step == 0:
            best = step
    return best


def over_blocks(total, block, step):
    def run(index, carry):
        step(pl.ds(pl.multiple_of(index * block, block), block))
        return carry

    lax.fori_loop(0, total // block, run, 0)


def over_chunks(chunks, width, step):
    def run(index, carry):
        step(index, pl.ds(pl.multiple_of(index * width, width), width))
        return carry

    lax.fori_loop(0, chunks, run, 0)


def dot_nt(left, right):
    return lax.dot_general(
        left, right, (((1,), (1,)), ((), ())), preferred_element_type=jnp.float32
    )


def dot_nn(left, right):
    return jnp.dot(left, right, preferred_element_type=jnp.float32)


class Peers:
    def __init__(self, count, place, device_of):
        self.count = count
        self.place = place
        self.device_of = device_of

    def ahead(self, step):
        return lax.rem(self.place + step, self.count)

    def behind(self, step):
        return lax.rem(self.place + self.count - step, self.count)


def expert_peers(col_count, copies, group_rows):
    row_index = lax.axis_index("row")
    share = lax.rem(row_index, copies)
    rows = Peers(group_rows, row_index // copies, lambda place: {"row": share + copies * place})
    return rows, col_peers(col_count)


def col_peers(col_count):
    return Peers(col_count, lax.axis_index("col"), lambda place: {"col": place})


def greet(groups):
    barrier = pltpu.get_barrier_semaphore()
    total = 0
    for peers in groups:
        for step in range(1, peers.count):
            pl.semaphore_signal(
                barrier,
                inc=1,
                device_id=peers.device_of(peers.ahead(step)),
                device_id_type=pl.DeviceIdType.MESH,
            )
            total += 1
    pl.semaphore_wait(barrier, total)


def send_to(source, target, sems, number, device):
    send_sems, recv_sems = sems
    return pltpu.make_async_remote_copy(
        src_ref=source,
        dst_ref=target,
        send_sem=send_sems.at[number],
        recv_sem=recv_sems.at[number],
        device_id=device,
        device_id_type=pl.DeviceIdType.MESH,
    )


class Exchange:
    def __init__(self, peers, send_sems, recv_sems, source, target):
        self.peers = peers
        self.sems = (send_sems, recv_sems)
        self.source = source
        self.target = target

    def out(self, step, index, chunk):
        place = self.peers.ahead(step)
        return send_to(
            self.source(place, chunk),
            self.target(self.peers.place, step, chunk),
            self.sems,
            (index, step - 1),
            self.peers.device_of(place),
        )

    def start(self, index, chunk):
        for step in range(1, self.peers.count):
            self.out(step, index, chunk).start()

    def wait_send(self, index, chunk):
        for step in range(1, self.peers.count):
            self.out(step, index, chunk).wait_send()

    def wait_recv(self, index, chunk):
        for step in range(1, self.peers.count):
            place = self.peers.behind(step)
            landed = self.target(place, step, chunk)
            send_to(
                landed, landed, self.sems, (index, step - 1), self.peers.device_of(place)
            ).wait_recv()


def exchange_sems(chunks, count):
    return [pltpu.SemaphoreType.DMA((chunks, max(count - 1, 1))) for _ in range(2)]


class LineGather:
    def __init__(self, rows, own, tokens, part, sems):
        self.rows = rows
        self.own = own
        self.tokens = tokens
        self.part = part
        self.own_send, self.pass_send, self.recv = sems

    @staticmethod
    def sems(chunks, count):
        return [
            pltpu.SemaphoreType.DMA((chunks, 2)),
            pltpu.SemaphoreType.DMA((chunks, count)),
            pltpu.SemaphoreType.DMA((chunks, count)),
        ]

    def copy(self, source, origin, index, chunk, sem, place):
        return pltpu.make_async_remote_copy(
            src_ref=source,
            dst_ref=self.tokens.at[self.part(origin), chunk],
            send_sem=sem,
            recv_sem=self.recv.at[index, origin],
            device_id=self.rows.device_of(place),
            device_id_type=pl.DeviceIdType.MESH,
        )

    def own_copies(self, index, chunk):
        me, last = self.rows.place, self.rows.count - 1
        for way, (there, place) in enumerate(((me < last, me + 1), (me > 0, me - 1))):
            yield there, self.copy(
                self.own.at[:, chunk], me, index, chunk, self.own_send.at[index, way], place
            )

    def passed(self, index, chunk):
        me, last = self.rows.place, self.rows.count - 1
        for distance in range(1, self.rows.count):
            for arrives, origin, goes_on, place in (
                (me >= distance, me - distance, me < last, me + 1),
                (me + distance <= last, me + distance, me > 0, me - 1),
            ):
                yield arrives, goes_on, self.copy(
                    self.tokens.at[self.part(origin), chunk],
                    origin,
                    index,
                    chunk,
                    self.pass_send.at[index, origin],
                    place,
                )

    def start_own(self, index, chunk):
        for there, copy in self.own_copies(index, chunk):
            pl.when(there)(copy.start)

    def arrive(self, index, chunk):
        for arrives, goes_on, copy in self.passed(index, chunk):

            @pl.when(arrives)
            def _():
                copy.wait_recv()
                pl.when(goes_on)(copy.start)

    def wait_send(self, index, chunk):
        for there, copy in self.own_copies(index, chunk):
            pl.when(there)(copy.wait_send)
        for arrives, goes_on, copy in self.passed(index, chunk):
            pl.when(arrives & goes_on)(copy.wait_send)


class LineSum:
    def __init__(self, rows, tokens, part, landed, sems):
        self.rows = rows
        self.tokens = tokens
        self.part = part
        self.landed = landed
        self.send, self.recv = sems

    @staticmethod
    def sems(chunks, count):
        return [
            pltpu.SemaphoreType.DMA((chunks, count)),
            pltpu.SemaphoreType.DMA((chunks, count + 1)),
        ]

    def copy(self, target, slot, index, chunk, place):
        return pltpu.make_async_remote_copy(
            src_ref=self.tokens.at[self.part(target), chunk],
            dst_ref=self.landed.at[slot, :, chunk],
            send_sem=self.send.at[index, target],
            recv_sem=self.recv.at[index, slot],
            device_id=self.rows.device_of(place),
            device_id_type=pl.DeviceIdType.MESH,
        )

    def passed(self, index, chunk):
        me, last = self.rows.place, self.rows.count - 1
        for number in range(self.rows.count):
            for goes, arrives, slot, target, place in (
                (me > number, me < last, number, number, me - 1),
                (me < last - number, me > 0, last - number + 1, last - number, me + 1),
            ):
                yield goes, arrives, slot, target, self.copy(target, slot, index, chunk, place)

    def pass_on(self, index, chunk):
        for goes, arrives, slot, target, copy in self.passed(index, chunk):

            @pl.when(goes)
            def _():
                @pl.when(arrives)
                def _():
                    copy.wait_recv()
                    total = self.tokens[self.part(target), chunk].astype(jnp.float32)
                    total = total + self.landed[slot, :, chunk].astype(jnp.float32)
                    self.tokens[self.part(target), chunk] = total.astype(jnp.bfloat16)

                copy.start()

    def is_middle(self):
        return (self.rows.place > 0) & (self.rows.place < self.rows.count - 1)

    def total(self, index, chunk, out):
        me, last = self.rows.place, self.rows.count - 1
        out[:, chunk] = self.tokens[self.part(me), chunk].astype(jnp.float32)
        for arrives, slot in ((me < last, me), (me > 0, me + 1)):

            @pl.when(arrives)
            def _():
                self.copy(me, slot, index, chunk, me).wait_recv()
                out[:, chunk] += self.landed[slot, :, chunk].astype(jnp.float32)

    def wait_send(self, index, chunk):
        for goes, _, _, _, copy in self.passed(index, chunk):
            pl.when(goes)(copy.wait_send)


def iota(shape, axis):
    return lax.broadcasted_iota(jnp.int32, shape, axis)


def within(numbers, size, count):
    block = jnp.zeros_like(numbers)
    for index in range(1, count):
        block = block + (numbers >= index * size).astype(jnp.int32)
    return block, numbers - block * size


def slot_block(shape, slot_axis, slot_rows):
    slots = iota(shape, slot_axis)
    block = iota(shape, 1 - slot_axis)
    return (slots >= block * slot_rows) & (slots < (block + 1) * slot_rows)


def build_places(dims, rows, routes_ref, place, place_t, member):
    group_rows, col_count, copies, token_rows, slot_rows, chunks, width = dims
    all_slots = col_count * slot_rows
    number = iota((E, 1), 0)
    ahead, col = within(number, col_count, group_rows)
    owner = ahead + rows.place
    owner = jnp.where(owner >= group_rows, owner - group_rows, owner)
    expert = col * group_rows + owner
    earlier = (iota((token_rows, token_rows), 0) < iota((token_rows, token_rows), 1)).astype(
        jnp.bfloat16
    )
    pick = slot_block((E, all_slots), 1, slot_rows).astype(jnp.bfloat16)
    column = iota((slot_rows, 1), 0)
    lane = within(iota((1, all_slots), 1), slot_rows, col_count)[1]
    for group in range(group_rows):
        tokens = slice(group * token_rows, (group + 1) * token_rows)
        picked = routes_ref[group]
        has = picked[0:1, :] == expert
        for choice in range(1, TOPK):
            has = has | (picked[choice : choice + 1, :] == expert)
        before = dot_nn(has.astype(jnp.float32).astype(jnp.bfloat16), earlier)
        slot_number = jnp.where(has, before, -1.0)
        in_group = (column >= group * CAP) & (column < (group + 1) * CAP)
        wanted = jnp.where(in_group, column - group * CAP, -2).astype(jnp.float32)
        for index in range(col_count):
            slots = slice(index * slot_rows, (index + 1) * slot_rows)
            hit = slot_number[index : index + 1, :] == wanted
            place[slots, tokens] = jnp.where(hit, 1.0, 0.0).astype(jnp.bfloat16)
        turned = slot_number.T
        in_group = (lane >= group * CAP) & (lane < (group + 1) * CAP)
        wanted = jnp.where(in_group, lane - group * CAP, -2).astype(jnp.float32)
        hit = dot_nn(turned.astype(jnp.bfloat16), pick) == wanted
        place_t[tokens, :] = jnp.where(hit, 1.0, 0.0).astype(jnp.bfloat16)
        if member is not None:
            member[tokens, :] = turned


def far_first(rows):
    for distance in range(rows.count - 1, 0, -1):
        for there, place in (
            (rows.place + distance < rows.count, rows.place + distance),
            (rows.place >= distance, rows.place - distance),
        ):
            yield there, place


class WeightMove:
    def __init__(self, rows, copies, layer, shards, target, sems):
        self.rows = rows
        self.copies = copies
        self.layer = layer
        self.shards = shards
        self.target = target
        self.remote_sems = sems[:2]
        self.local_sem = sems[2]

    @staticmethod
    def sems(row_count):
        return [pltpu.SemaphoreType.DMA((max(row_count - 1, 1),))] * 2 + [pltpu.SemaphoreType.DMA]

    def shard(self, place):
        return self.shards.at[self.layer, place // self.copies]

    def own(self):
        return pltpu.make_async_copy(
            self.shard(self.rows.place), self.target.at[0], self.local_sem
        )

    def out(self, step):
        place = self.rows.ahead(step)
        return send_to(
            self.shard(place),
            self.target.at[step],
            self.remote_sems,
            step - 1,
            self.rows.device_of(place),
        )

    def start(self):
        for there, place in far_first(self.rows):
            step = lax.rem(place - self.rows.place + self.rows.count, self.rows.count)

            @pl.when(there)
            def _():
                self.out(step).start()

        self.own().start()

    def wait_recv(self):
        self.own().wait()
        for step in range(1, self.rows.count):
            landed = self.target.at[step]
            place = self.rows.behind(step)
            send_to(
                landed, landed, self.remote_sems, step - 1, self.rows.device_of(place)
            ).wait_recv()

    def wait_send(self):
        for step in range(1, self.rows.count):
            self.out(step).wait_send()


def all_rows(row_count):
    return Peers(row_count, lax.axis_index("row"), lambda place: {"row": place})


def moved_shape(row_count, shards):
    return jax.ShapeDtypeStruct((row_count, *shards.shape[2:]), shards.dtype)


vmem_most = 62 * 1024 * 1024
long_cost = pl.CostEstimate(flops=0, bytes_accessed=600 * 1024 * 1024, transcendentals=0)
no_cost = pl.CostEstimate(flops=0, bytes_accessed=0, transcendentals=0)


def moe_forward_kernel(dims, row_count, layer, moving, gather_dims, closing, *refs):
    group_rows, col_count, copies, token_rows, slot_rows, chunks, width = dims
    own_ref, routes_ref, router_ref = refs[:3]
    weight_in = refs[3:6]
    refs = refs[6:]
    next_blocks = refs[: 2 if gather_dims else 0]
    refs = refs[len(next_blocks) :]
    closing_in = refs[: 1 if closing else 0]
    refs = refs[len(closing_in) :]
    sum_ref, gates_ref, slots_out, returned_out = refs[:4]
    refs = refs[4:]
    closing_out = refs[: len(closing_in)]
    refs = refs[len(closing_in) :]
    moved_out = refs[: len(moving)]
    refs = refs[len(moving) :]
    next_full = refs[: len(next_blocks)]
    refs = refs[len(next_blocks) :]
    dense = None
    if gather_dims:
        count = len(DenseGather.sems(gather_dims, 2))
        dense = DenseGather(gather_dims, next_blocks, next_full, refs[-count:])
        refs = refs[:-count]
    closing_sems = ()
    if closing:
        closing_sems = refs[-4:]
        refs = refs[:-4]
    move_sems = refs[len(refs) - 3 * len(moving) :]
    refs = refs[: len(refs) - 3 * len(moving)]
    (
        place,
        place_t,
        member,
        gate,
        up,
        down,
        tokens,
        send,
        slots,
        gate_val,
        up_val,
        act,
        returned,
        landed,
        own_send,
        pass_send,
        row_recv,
        there_send,
        there_recv,
        back_send,
        back_recv,
        home_send,
        home_recv,
        local_sem,
    ) = refs
    all_tokens = group_rows * token_rows
    all_slots = col_count * slot_rows
    slot_step = split_rows(all_slots, 320)
    rows, cols = expert_peers(col_count, copies, group_rows)

    def token_part(place):
        return pl.ds(pl.multiple_of(place * token_rows, token_rows), token_rows)

    def slot_part(place):
        return pl.ds(pl.multiple_of(place * slot_rows, slot_rows), slot_rows)

    gather = LineGather(rows, own_ref, tokens, token_part, (own_send, pass_send, row_recv))
    there = Exchange(
        cols,
        there_send,
        there_recv,
        lambda place, chunk: send.at[slot_part(place), chunk],
        lambda place, step, chunk: slots.at[slot_part(place), chunk],
    )
    back = Exchange(
        cols,
        back_send,
        back_recv,
        lambda place, chunk: send.at[slot_part(place), chunk],
        lambda place, step, chunk: returned.at[slot_part(place), chunk],
    )
    home = LineSum(rows, tokens, token_part, landed, (home_send, home_recv))
    ahead = None
    if closing:
        ahead = LineGather(rows, *closing_in, *closing_out, token_part, closing_sems[:3])
        ahead_own = pltpu.make_async_copy(
            closing_in[0], closing_out[0].at[token_part(rows.place), :], closing_sems[3]
        )
    weights = (gate, up, down)
    moves = {
        kind: WeightMove(
            all_rows(row_count),
            copies,
            layer,
            weight_in[kind],
            weights[kind],
            move_sems[3 * number : 3 * number + 3],
        )
        for number, kind in enumerate(moving)
    }
    loads = {
        kind: pltpu.make_async_copy(weight_in[kind], weights[kind], local_sem.at[2 + kind])
        for kind in range(3)
        if kind not in moving
    }
    keeps = []

    def weight_ready(kind):
        if kind in loads:
            loads[kind].wait()
        else:
            moves[kind].wait_recv()
            keep = pltpu.make_async_copy(
                weights[kind], moved_out[moving.index(kind)], local_sem.at[2 + kind]
            )
            keep.start()
            keeps.append(keep)

    def weight(kind, chunk):
        return weights[kind][:, :, chunk].reshape(-1, width)

    greet((all_rows(row_count), cols))
    for index in range(min(2, chunks)):
        gather.start_own(index, pl.ds(index * width, width))
    for copy in loads.values():
        copy.start()
    tokens[token_part(rows.place), :] = own_ref[...]
    build_places(dims, rows, routes_ref, place, place_t, member)

    def dispatch(index, chunk):
        gather.arrive(index, chunk)

        @pl.when(index + 2 < chunks)
        def _():
            later = pl.ds(pl.multiple_of((index + 2) * width, width), width)
            gather.start_own(index + 2, later)


        def rows_of(part):
            send[part, chunk] = dot_nn(place[part, :], tokens[:, chunk]).astype(jnp.bfloat16)

        over_blocks(all_slots, all_slots, rows_of)
        there.start(index, chunk)
        slots[slot_part(cols.place), chunk] = send[slot_part(cols.place), chunk]

    over_chunks(chunks, width, dispatch)
    if dense:
        for kind in dense.kinds:
            dense.start(kind)
    for kind in moving:
        moves[kind].start()

    def gating(part):
        chosen = member[part, :] >= 0
        logits = jnp.where(chosen, dot_nt(tokens[part, :], router_ref[...]), masked_score)
        peak = jnp.max(logits, axis=-1, keepdims=True)
        exponent = jnp.where(chosen, jnp.exp(logits - peak), 0.0)
        gates = exponent / jnp.sum(exponent, axis=-1, keepdims=True)
        gates_ref[part, :] = gates
        pick = slot_block((E, all_slots), 1, slot_rows).astype(jnp.bfloat16)
        spread = dot_nn(gates.astype(jnp.bfloat16), pick)
        place_t[part, :] = (place_t[part, :].astype(jnp.float32) * spread).astype(jnp.bfloat16)

    over_blocks(all_tokens, token_rows, gating)

    def project(kind, target, wait, index, chunk):
        if wait:
            there.wait_recv(index, chunk)

        def rows_of(part):
            value = dot_nt(slots[part, chunk], weight(kind, chunk))

            @pl.when(index == 0)
            def _():
                target[part, :] = value

            @pl.when(index > 0)
            def _():
                target[part, :] += value

        over_blocks(all_slots, all_slots, rows_of)

    weight_ready(0)
    over_chunks(chunks, width, functools.partial(project, 0, gate_val, True))
    weight_ready(1)
    over_chunks(chunks, width, functools.partial(project, 1, up_val, False))
    keep_slots = pltpu.make_async_copy(slots, slots_out, local_sem.at[0])
    keep_slots.start()

    def activate(part):
        value = gate_val[part, :]
        act[part, :] = (value * jax.nn.sigmoid(value) * up_val[part, :]).astype(jnp.bfloat16)

    over_blocks(all_slots, slot_step, activate)
    if dense:
        for kind in dense.kinds:
            dense.pass_rows(kind)
    weight_ready(2)
    if ahead:
        ahead_own.start()
        over_chunks(chunks, width, ahead.start_own)

    def give_back(index, chunk):
        there.wait_send(index, chunk)

        def rows_of(part):
            send[part, chunk] = dot_nn(act[part, :], weight(2, chunk)).astype(jnp.bfloat16)

        over_blocks(all_slots, all_slots, rows_of)
        back.start(index, chunk)
        returned[slot_part(cols.place), chunk] = send[slot_part(cols.place), chunk]

    over_chunks(chunks, width, give_back)

    over_chunks(chunks, width, gather.wait_send)

    def combine(index, chunk):
        back.wait_recv(index, chunk)

        def rows_of(part):
            tokens[part, chunk] = dot_nn(place_t[part, :], returned[:, chunk]).astype(jnp.bfloat16)

        over_blocks(all_tokens, token_rows, rows_of)
        if ahead:
            ahead.arrive(index, chunk)
            return
        pl.when(~home.is_middle())(functools.partial(home.pass_on, index, chunk))

        @pl.when(home.is_middle() & (index > 0))
        def _():
            before = pl.ds(pl.multiple_of((index - 1) * width, width), width)
            home.pass_on(index - 1, before)

    over_chunks(chunks, width, combine)
    if ahead:
        keep_mixed = pltpu.make_async_copy(tokens, sum_ref, local_sem.at[5])
        keep_mixed.start()
    else:
        last_chunk = pl.ds((chunks - 1) * width, width)
        pl.when(home.is_middle())(functools.partial(home.pass_on, chunks - 1, last_chunk))
    keep_returned = pltpu.make_async_copy(returned, returned_out, local_sem.at[1])
    keep_returned.start()
    if dense:
        for kind in dense.kinds:
            dense.pass_pairs(kind)

    def finish(index, chunk):
        home.total(index, chunk, sum_ref)

    if not ahead:
        over_chunks(chunks, width, finish)

    def drain(index, chunk):
        back.wait_send(index, chunk)
        (ahead or home).wait_send(index, chunk)

    over_chunks(chunks, width, drain)
    if dense:
        for kind in dense.kinds:
            dense.finish(kind)
    for kind in moving:
        moves[kind].wait_send()
    if ahead:
        ahead_own.wait()
        keep_mixed.wait()
    keep_slots.wait()
    keep_returned.wait()
    for keep in keeps:
        keep.wait()


class RowTotal:
    def __init__(self, rows, blocks, landed, own, sems):
        self.rows = rows
        self.blocks = blocks
        self.landed = landed
        self.own = own
        self.remote_sems = sems[:2]
        self.local_sem = sems[2]

    def out(self, step):
        place = self.rows.ahead(step)
        return send_to(
            self.blocks.at[place],
            self.landed.at[step - 1],
            self.remote_sems,
            step - 1,
            self.rows.device_of(place),
        )

    def load(self):
        return pltpu.make_async_copy(self.blocks.at[self.rows.place], self.own, self.local_sem)

    def start(self):
        self.load().start()
        for step in range(1, self.rows.count):
            self.out(step).start()

    def finish(self, out):
        self.load().wait()
        total = self.own[...].astype(jnp.float32)
        for step in range(1, self.rows.count):
            self.out(step).wait_recv()
            total = total + self.landed[step - 1].astype(jnp.float32)
        out[...] = total
        for step in range(1, self.rows.count):
            self.out(step).wait_send()


def moe_backward_kernel(dims, opening, dense_count, *refs):
    group_rows, col_count, copies, token_rows, slot_rows, chunks, width = dims
    own_ref, routes_ref, router_ref, gates_ref, normed_ref, slots_in, returned_in = refs[:7]
    weight_in = refs[7:10]
    refs = refs[10:]
    opening_in = refs[: 1 if opening else 0]
    refs = refs[len(opening_in) :]
    block_count, slice_width = weight_in[0].shape[:2]
    dense_in = refs[:dense_count]
    refs = refs[dense_count:]
    sum_ref, router_grad_ref, *grads_out = refs[: 2 + block_count]
    refs = refs[2 + block_count :]
    dense_out = refs[:dense_count]
    refs = refs[dense_count:]
    dense_scratch = refs[len(refs) - 5 * dense_count :]
    refs = refs[: len(refs) - 5 * dense_count]
    totals = [
        RowTotal(all_rows(block_count), blocks, *dense_scratch[5 * n : 5 * n + 2], dense_scratch[5 * n + 2 : 5 * n + 5])
        for n, blocks in enumerate(dense_in)
    ]
    opening_out = refs[: len(opening_in)]
    refs = refs[len(opening_in) :]
    opening_scratch = ()
    if opening:
        opening_scratch = refs[-3:]
        refs = refs[:-3]
    (
        place,
        place_t,
        gate,
        up,
        down,
        tokens,
        send,
        slots,
        slope,
        silu,
        act,
        weight,
        inner,
        received,
        grad_act,
        grad_gate,
        grad_up,
        returned,
        turned,
        staged,
        landed,
        pair_send,
        pair_landed,
        own_send,
        pass_send,
        row_recv,
        there_send,
        there_recv,
        back_send,
        back_recv,
        home_send,
        home_recv,
        pair_send_sem,
        pair_recv_sem,
        local_sem,
    ) = refs
    all_tokens = group_rows * token_rows
    all_slots = col_count * slot_rows
    slot_step = split_rows(all_slots, 320)
    rows, cols = expert_peers(col_count, copies, group_rows)

    def token_part(place):
        return pl.ds(pl.multiple_of(place * token_rows, token_rows), token_rows)

    def slot_part(place):
        return pl.ds(pl.multiple_of(place * slot_rows, slot_rows), slot_rows)

    gather = LineGather(rows, own_ref, tokens, token_part, (own_send, pass_send, row_recv))
    there = Exchange(
        cols,
        there_send,
        there_recv,
        lambda place, chunk: send.at[slot_part(place), chunk],
        lambda place, step, chunk: received.at[slot_part(place), chunk],
    )
    back = Exchange(
        cols,
        back_send,
        back_recv,
        lambda place, chunk: send.at[slot_part(place), chunk],
        lambda place, step, chunk: returned.at[slot_part(place), chunk],
    )
    home = LineSum(rows, tokens, token_part, landed, (home_send, home_recv))
    before = None
    if opening:
        before = LineSum(rows, tokens, token_part, opening_scratch[0], opening_scratch[1:])
    pair = Exchange(
        rows,
        pair_send_sem,
        pair_recv_sem,
        lambda place, chunk: pair_send.at[token_part(place), :],
        lambda place, step, chunk: pair_landed.at[step - 1],
    )
    greet((all_rows(block_count), cols))
    if before:
        load_tokens = pltpu.make_async_copy(own_ref, tokens, local_sem.at[7])
        load_tokens.start()
    else:
        for index in range(min(2, chunks)):
            gather.start_own(index, pl.ds(index * width, width))
    load_returned = pltpu.make_async_copy(returned_in, returned, local_sem.at[1])
    load_returned.start()
    load_slots = pltpu.make_async_copy(slots_in, slots, local_sem.at[0])
    load_slots.start()
    weights = (gate, up, down)
    loads = [
        pltpu.make_async_copy(weight_in[kind], weights[kind], local_sem.at[4 + kind])
        for kind in range(3)
    ]
    for copy in loads:
        copy.start()

    def weight_part(kind, chunk):
        return weights[kind][:, :, chunk].reshape(block_count * slice_width, width)

    if not before:
        tokens[token_part(rows.place), :] = own_ref[...]
    build_places(dims, rows, routes_ref, place, place_t, None)

    def recompute(part):
        gate_val = dot_nt(slots[part, :], gate[...].reshape(-1, gate.shape[2]))
        up_val = dot_nt(slots[part, :], up[...].reshape(-1, up.shape[2]))
        sigmoid = jax.nn.sigmoid(gate_val)
        value = gate_val * sigmoid
        act[part, :] = (value * up_val).astype(jnp.bfloat16)
        silu[part, :] = value.astype(jnp.bfloat16)
        slope[part, :] = (up_val * sigmoid * (1.0 + gate_val * (1.0 - sigmoid))).astype(
            jnp.bfloat16
        )

    def slot_gates(part):
        picked = dot_nn(place[part, :], gates_ref[...].astype(jnp.bfloat16))
        block = iota(picked.shape, 1)
        slot = iota(picked.shape, 0) + part.start
        in_block = (slot >= block * slot_rows) & (slot < (block + 1) * slot_rows)
        weight[part, :] = jnp.sum(jnp.where(in_block, picked, 0.0), axis=1, keepdims=True)

    def recompute_all():
        load_slots.wait()
        for copy in loads:
            copy.wait()
        over_blocks(all_slots, slot_step, recompute)

    over_blocks(all_slots, slot_step, slot_gates)
    if before:
        load_tokens.wait()
    else:
        recompute_all()
    load_returned.wait()

    def dispatch(index, chunk):
        if not before:
            gather.arrive(index, chunk)

            @pl.when(index + 2 < chunks)
            def _():
                later = pl.ds(pl.multiple_of((index + 2) * width, width), width)
                gather.start_own(index + 2, later)


        def rows_of(part):
            grad = dot_nn(place[part, :], tokens[:, chunk])
            share = jnp.sum(
                grad * returned[part, chunk].astype(jnp.float32), axis=1, keepdims=True
            )
            send[part, chunk] = (weight[part, :] * grad).astype(jnp.bfloat16)

            @pl.when(index == 0)
            def _():
                inner[part, :] = share

            @pl.when(index > 0)
            def _():
                inner[part, :] += share

        over_blocks(all_slots, all_slots, rows_of)
        there.start(index, chunk)
        received[slot_part(cols.place), chunk] = send[slot_part(cols.place), chunk]

    over_chunks(chunks, width, dispatch)
    for total in totals:
        total.start()

    def pairs(part):
        picked = slot_block((all_slots, pair_send.shape[1]), 0, slot_rows)
        spread = jnp.where(picked, inner[...], 0.0)
        high = spread.astype(jnp.bfloat16)
        low = (spread - high.astype(jnp.float32)).astype(jnp.bfloat16)
        pair_send[part, :] = dot_nn(place_t[part, :], high) + dot_nn(place_t[part, :], low)

    if before:
        load_mixed = pltpu.make_async_copy(opening_in[0], tokens, local_sem.at[7])
        load_mixed.start()
    over_blocks(all_tokens, token_rows, pairs)
    pair.start(0, None)
    if before:
        load_mixed.wait()

        @pl.when(~before.is_middle())
        def _():
            over_chunks(chunks, width, before.pass_on)

        recompute_all()

    def project(index, chunk):
        if before:
            pl.when(before.is_middle())(functools.partial(before.pass_on, index, chunk))
        there.wait_recv(index, chunk)

        def rows_of(part):
            grad = dot_nt(received[part, chunk], weight_part(2, chunk))

            @pl.when(index == 0)
            def _():
                grad_act[part, :] = grad

            @pl.when(index > 0)
            def _():
                grad_act[part, :] += grad

        over_blocks(all_slots, all_slots, rows_of)

    over_chunks(chunks, width, project)

    def slopes(part):
        grad = grad_act[part, :]
        grad_gate[part, :] = (grad * slope[part, :].astype(jnp.float32)).astype(jnp.bfloat16)
        grad_up[part, :] = (grad * silu[part, :].astype(jnp.float32)).astype(jnp.bfloat16)

    over_blocks(all_slots, slot_step, slopes)

    def give_back(index, chunk):
        there.wait_send(index, chunk)

        def rows_of(part):
            send[part, chunk] = (
                dot_nn(grad_gate[part, :], weight_part(0, chunk))
                + dot_nn(grad_up[part, :], weight_part(1, chunk))
            ).astype(jnp.bfloat16)

        over_blocks(all_slots, all_slots, rows_of)
        back.start(index, chunk)

    over_chunks(chunks, width, give_back)

    returned[slot_part(cols.place), :] = send[slot_part(cols.place), :]
    if before:
        over_chunks(
            chunks, width, lambda index, chunk: before.total(index, chunk, opening_out[0])
        )
        over_chunks(chunks, width, before.wait_send)

    if not before:
        over_chunks(chunks, width, gather.wait_send)

    def combine(index, chunk):
        back.wait_recv(index, chunk)

        def rows_of(part):
            tokens[part, chunk] = dot_nn(place_t[part, :], returned[:, chunk]).astype(jnp.bfloat16)

        over_blocks(all_tokens, token_rows, rows_of)
        pl.when(~home.is_middle())(functools.partial(home.pass_on, index, chunk))

        @pl.when(home.is_middle() & (index > 0))
        def _():
            before = pl.ds(pl.multiple_of((index - 1) * width, width), width)
            home.pass_on(index - 1, before)

    over_chunks(chunks, width, combine)
    last_chunk = pl.ds((chunks - 1) * width, width)
    pl.when(home.is_middle())(functools.partial(home.pass_on, chunks - 1, last_chunk))
    def keep(kind, index):
        return pltpu.make_async_copy(
            staged.at[index % 2], grads_out[index].at[kind], local_sem.at[2 + index % 2]
        )

    for kind, (left, right) in enumerate(((grad_gate, slots), (grad_up, slots), (act, received))):
        turned[...] = left[...].T
        for index in range(block_count):
            if index >= 2:
                keep(kind, index - 2).wait()
            part = slice(index * slice_width, (index + 1) * slice_width)
            staged[index % 2] = dot_nn(turned[part, :], right[...]).astype(jnp.bfloat16)
            keep(kind, index).start()
        for index in range(max(block_count - 2, 0), block_count):
            keep(kind, index).wait()

    pair.wait_recv(0, None)
    grad_pair = pair_send[token_part(rows.place), :]
    for ahead in range(1, group_rows):
        shifted = pltpu.roll(pair_landed[group_rows - ahead - 1], ahead * col_count, 1)
        grad_pair = grad_pair + shifted
    grad_pair = grad_pair[:, :E]
    gates = gates_ref[token_part(rows.place), :]
    grad_logits = gates * (grad_pair - jnp.sum(gates * grad_pair, axis=-1, keepdims=True))
    grad_logits = grad_logits.astype(jnp.bfloat16)
    router_grad_ref[...] = dot_nn(grad_logits.astype(jnp.float32).T.astype(jnp.bfloat16), normed_ref[...])

    def finish(index, chunk):
        home.total(index, chunk, sum_ref)
        sum_ref[:, chunk] += dot_nn(grad_logits, router_ref[:, chunk])

    over_chunks(chunks, width, finish)

    def drain(index, chunk):
        back.wait_send(index, chunk)
        home.wait_send(index, chunk)

    over_chunks(chunks, width, drain)
    pair.wait_send(0, None)
    for total, out in zip(totals, dense_out):
        total.finish(out)


def moe_forward(
    dims, row_count, layer, own, routes, router, weights, moving, next_blocks, closing
):
    group_rows, col_count, copies, token_rows, slot_rows, chunks, width = dims
    all_tokens, all_slots = group_rows * token_rows, col_count * slot_rows
    model_width = own.shape[1]
    slice_width = weights[0].shape[-2]
    hidden = row_count * slice_width
    gather_dims = (row_count, col_count // 2) if next_blocks else None
    dense_sems = DenseGather.sems(gather_dims, 2) if next_blocks else []
    vmem = pl.BlockSpec(memory_space=pltpu.VMEM)
    outside = pl.BlockSpec(memory_space=pl.ANY)
    every_row = jax.ShapeDtypeStruct((all_tokens, model_width), jnp.bfloat16)
    slot_array = pltpu.VMEM((all_slots, model_width), jnp.bfloat16)
    hidden_wide = pltpu.VMEM((all_slots, hidden), jnp.float32)
    weight_array = pltpu.VMEM((row_count, slice_width, model_width), jnp.bfloat16)
    return pl.pallas_call(
        functools.partial(
            moe_forward_kernel, dims, row_count, layer, moving, gather_dims, bool(closing)
        ),
        out_shape=(
            every_row if closing else jax.ShapeDtypeStruct((token_rows, model_width), jnp.float32),
            jax.ShapeDtypeStruct((all_tokens, E), jnp.float32),
            jax.ShapeDtypeStruct((all_slots, model_width), jnp.bfloat16),
            jax.ShapeDtypeStruct((all_slots, model_width), jnp.bfloat16),
            *([every_row] * len(closing)),
            *(moved_shape(row_count, weights[kind]) for kind in moving),
            *(gathered_shapes(gather_dims, next_blocks) if next_blocks else ()),
        ),
        in_specs=[vmem] * 3 + [outside] * (3 + len(next_blocks) + len(closing)),
        out_specs=(outside if closing else vmem, vmem)
        + (outside,) * (2 + len(closing) + len(moving) + len(next_blocks)),
        scratch_shapes=[
            pltpu.VMEM((all_slots, all_tokens), jnp.bfloat16),
            pltpu.VMEM((all_tokens, all_slots), jnp.bfloat16),
            pltpu.VMEM((all_tokens, E), jnp.float32),
            weight_array,
            weight_array,
            weight_array,
            pltpu.VMEM((all_tokens, model_width), jnp.bfloat16),
            slot_array,
            slot_array,
            hidden_wide,
            hidden_wide,
            pltpu.VMEM((all_slots, hidden), jnp.bfloat16),
            slot_array,
            pltpu.VMEM((group_rows + 1, token_rows, model_width), jnp.bfloat16),
            *LineGather.sems(chunks, group_rows),
            *exchange_sems(chunks, col_count),
            *exchange_sems(chunks, col_count),
            *LineSum.sems(chunks, group_rows),
            pltpu.SemaphoreType.DMA((6,)),
            *(WeightMove.sems(row_count) * len(moving)),
            *((*LineGather.sems(chunks, group_rows), pltpu.SemaphoreType.DMA) if closing else ()),
            *dense_sems,
        ],
        compiler_params=pltpu.CompilerParams(
            collective_id=1 + 7 * layer, has_side_effects=True, vmem_limit_bytes=vmem_most
        ),
        cost_estimate=no_cost,
        name="moe_forward",
    )(own, routes, router, *weights, *next_blocks, *closing)


def moe_backward(dims, own, routes, router, gates, normed, slots, returned, weights, opening, dense):
    group_rows, col_count, copies, token_rows, slot_rows, chunks, width = dims
    all_tokens, all_slots = group_rows * token_rows, col_count * slot_rows
    model_width = own.shape[1]
    opened = len(opening)
    block_count, slice_width = weights[0].shape[:2]
    grads = jax.ShapeDtypeStruct((3, slice_width, model_width), jnp.bfloat16)
    hidden = block_count * slice_width
    vmem = pl.BlockSpec(memory_space=pltpu.VMEM)
    outside = pl.BlockSpec(memory_space=pl.ANY)
    slot_array = pltpu.VMEM((all_slots, model_width), jnp.bfloat16)
    hidden_narrow = pltpu.VMEM((all_slots, hidden), jnp.bfloat16)
    weight_array = pltpu.VMEM((block_count, slice_width, model_width), jnp.bfloat16)
    return pl.pallas_call(
        functools.partial(moe_backward_kernel, dims, bool(opening), len(dense)),
        out_shape=(
            jax.ShapeDtypeStruct((token_rows, model_width), jnp.float32),
            jax.ShapeDtypeStruct((E, model_width), jnp.float32),
            *([grads] * block_count),
            *(jax.ShapeDtypeStruct(block.shape[1:], jnp.float32) for block in dense),
            *([jax.ShapeDtypeStruct((token_rows, model_width), jnp.float32)] * opened),
        ),
        in_specs=[outside if opening else vmem]
        + [vmem] * 4
        + [outside] * (5 + opened + len(dense)),
        out_specs=(vmem, vmem)
        + (outside,) * block_count
        + (vmem,) * (len(dense) + opened),
        scratch_shapes=[
            pltpu.VMEM((all_slots, all_tokens), jnp.bfloat16),
            pltpu.VMEM((all_tokens, all_slots), jnp.bfloat16),
            weight_array,
            weight_array,
            weight_array,
            pltpu.VMEM((all_tokens, model_width), jnp.bfloat16),
            slot_array,
            slot_array,
            hidden_narrow,
            hidden_narrow,
            hidden_narrow,
            pltpu.VMEM((all_slots, 1), jnp.float32),
            pltpu.VMEM((all_slots, 1), jnp.float32),
            slot_array,
            pltpu.VMEM((all_slots, hidden), jnp.float32),
            hidden_narrow,
            hidden_narrow,
            slot_array,
            pltpu.VMEM((hidden, all_slots), jnp.bfloat16),
            pltpu.VMEM((2, slice_width, model_width), jnp.bfloat16),
            pltpu.VMEM((group_rows + 1, token_rows, model_width), jnp.bfloat16),
            pltpu.VMEM((all_tokens, 128), jnp.float32),
            pltpu.VMEM((max(group_rows - 1, 1), token_rows, 128), jnp.float32),
            *LineGather.sems(chunks, group_rows),
            *exchange_sems(chunks, col_count),
            *exchange_sems(chunks, col_count),
            *LineSum.sems(chunks, group_rows),
            *exchange_sems(1, group_rows),
            pltpu.SemaphoreType.DMA((8,)),
            *(
                (
                    pltpu.VMEM((group_rows + 1, token_rows, model_width), jnp.bfloat16),
                    *LineSum.sems(chunks, group_rows),
                )
                if opening
                else ()
            ),
            *(
                item
                for block in dense
                for item in (
                    pltpu.VMEM((max(block_count - 1, 1), *block.shape[1:]), jnp.bfloat16),
                    pltpu.VMEM(block.shape[1:], jnp.bfloat16),
                    *WeightMove.sems(block_count),
                )
            ),
        ],
        compiler_params=pltpu.CompilerParams(
            collective_id=(9 if opening else 2) + (10 if dense else 0), has_side_effects=True, vmem_limit_bytes=vmem_most
        ),
        cost_estimate=no_cost,
        name="moe_backward",
    )(own, routes, router, gates, normed, slots, returned, *weights, *opening, *dense)


def col_pairs():
    col_index = lax.axis_index("col")
    return col_index // 2, lax.rem(col_index, 2)


def dense_peers(row_count, pair_count):
    row_index = lax.axis_index("row")
    pair, side = col_pairs()
    rows = Peers(row_count, row_index, lambda place: {"row": place})
    pairs = Peers(pair_count, pair, lambda place: {"col": place * 2 + side})
    sides = Peers(2, side, lambda place: {"col": pair * 2 + place})
    return rows, pairs, sides


def reduce_dense_kernel(
    dims,
    normed_ref,
    grad_proj_ref,
    grad_mid_ref,
    attended_ref,
    small_ref,
    *refs,
):
    row_count, pair_count, to_rows = dims
    outputs = refs[:3]
    scratch = refs[3:]
    kinds = 3
    buffers = [scratch[6 * kind : 6 * kind + 6] for kind in range(kinds)]
    sems = scratch[6 * kinds : 12 * kinds]
    normed_t, grad_proj, grad_mid_t, attended = scratch[12 * kinds :]
    side_sems = [(sems[6 * kind], sems[6 * kind + 1]) for kind in range(kinds)]
    pair_sems = [(sems[6 * kind + 2], sems[6 * kind + 3]) for kind in range(kinds)]
    row_sems = [(sems[6 * kind + 4], sems[6 * kind + 5]) for kind in range(kinds)]
    rows, pairs, sides = dense_peers(row_count, pair_count)
    other = 1 - sides.place

    def spread(target, source, turn):
        count = target.shape[0]
        size = source.shape[1] // count
        for index in range(count):
            part = source[:, index * size : (index + 1) * size]
            target[index] = part.T if turn else part

    spread(normed_t, normed_ref, True)
    spread(grad_proj, grad_proj_ref, False)
    spread(grad_mid_t, grad_mid_ref, True)
    spread(attended, attended_ref, False)

    def block(kind, row, pair, side):
        col = pair * 2 + side
        if kind == 0:
            return dot_nn(normed_t[row], grad_proj[col])
        if kind == 1:
            return dot_nn(grad_mid_t[col], attended[row])
        return small_ref[col, row].astype(jnp.float32)

    greet((rows, pairs, sides) if to_rows else (pairs, sides))

    def side_copy(kind, pair):
        side_send, side_recv = buffers[kind][0], buffers[kind][1]
        return send_to(
            side_send.at[pair],
            side_recv.at[pair],
            side_sems[kind],
            pair,
            sides.device_of(other),
        )

    def pair_copy(kind, step, row):
        place = pairs.ahead(step)
        half, pair_recv = buffers[kind][2], buffers[kind][3]
        return send_to(
            half.at[place, row],
            pair_recv.at[step - 1, row],
            pair_sems[kind],
            (step - 1) * row_count + row,
            pairs.device_of(place),
        )

    def row_copy(kind, step):
        place = rows.ahead(step)
        whole, row_recv = buffers[kind][4], buffers[kind][5]
        return send_to(
            whole.at[place],
            row_recv.at[step - 1],
            row_sems[kind],
            step - 1,
            rows.device_of(place),
        )

    def first(step, carry):
        pair = lax.rem(pairs.place + step, pair_count)
        for kind in range(kinds):
            for row in range(row_count):
                buffers[kind][0][pair, row] = block(kind, row, pair, other).astype(jnp.bfloat16)
            side_copy(kind, pair).start()
        return carry

    lax.fori_loop(1, pair_count + 1, first, 0)

    def second(step, carry):
        pair = lax.rem(pairs.place + step, pair_count)
        for kind in range(kinds):
            side_copy(kind, pair).wait_recv()
            side_recv, half = buffers[kind][1], buffers[kind][2]
            for row in range(row_count):
                total = block(kind, row, pair, sides.place)
                total = total + side_recv[pair, row].astype(jnp.float32)
                half[pair, row] = total.astype(jnp.bfloat16)

                @pl.when(step < pair_count)
                def _():
                    pair_copy(kind, step, row).start()

        return carry

    lax.fori_loop(1, pair_count + 1, second, 0)

    def third(step, carry):
        row = lax.rem(rows.place + step, row_count)
        for kind in range(kinds):
            half, pair_recv, whole = buffers[kind][2], buffers[kind][3], buffers[kind][4]
            total = half[pairs.place, row].astype(jnp.float32)
            for ahead in range(1, pair_count):
                pair_copy(kind, ahead, row).wait_recv()
                total = total + pair_recv[ahead - 1, row].astype(jnp.float32)

            if not to_rows:
                outputs[kind][row] = total.astype(jnp.bfloat16)
                continue

            whole[row] = total.astype(jnp.bfloat16)

            @pl.when(step < row_count)
            def _():
                row_copy(kind, step).start()

        return carry

    lax.fori_loop(1, row_count + 1, third, 0)
    for kind in range(kinds if to_rows else 0):
        whole, row_recv = buffers[kind][4], buffers[kind][5]
        total = whole[rows.place].astype(jnp.float32)
        for step in range(1, row_count):
            row_copy(kind, step).wait_recv()
            total = total + row_recv[step - 1].astype(jnp.float32)
        outputs[kind][...] = total

    def drain_sides(pair, carry):
        for kind in range(kinds):
            side_copy(kind, pair).wait_send()
        return carry

    lax.fori_loop(0, pair_count, drain_sides, 0)

    def drain_pairs(step, carry):
        for kind in range(kinds):
            for row in range(row_count):
                pair_copy(kind, step, row).wait_send()
        return carry

    lax.fori_loop(1, pair_count, drain_pairs, 0)
    for kind in range(kinds if to_rows else 0):
        for step in range(1, row_count):
            row_copy(kind, step).wait_send()


def order_scratch(slice_width, model_width):
    return [
        pltpu.VMEM((4, slice_width, model_width), jnp.bfloat16),
        pltpu.VMEM((4, slice_width, model_width), jnp.float32),
        pltpu.SemaphoreType.DMA((4,)),
        pltpu.SemaphoreType.DMA((4,)),
    ]


def ordered_shapes(layer_count, blocks):
    _, slice_width, model_width = blocks[0].shape
    shape = (layer_count, len(blocks), slice_width, model_width)
    return (jax.ShapeDtypeStruct(shape, jnp.float32),) * 3


def reduce_dense(
    row_count, col_count, normed, grad_projected, grad_mid_b, attended, small, to_rows
):
    token_rows, model_width = normed.shape
    qkv_width, out_rows = grad_projected.shape[1], attended.shape[1]
    pair_count = col_count // 2
    shapes = (
        (model_width // row_count, qkv_width // col_count),
        (model_width // col_count, out_rows // row_count),
        small.shape[2:],
    )
    vmem = pl.BlockSpec(memory_space=pltpu.VMEM)
    scratch = []
    sems = []
    for height, breadth in shapes:
        for lead in (
            (pair_count, row_count),
            (pair_count, row_count),
            (pair_count, row_count),
            (max(pair_count - 1, 1), row_count),
            (row_count,),
            (max(row_count - 1, 1),),
        ):
            scratch.append(pltpu.VMEM((*lead, height, breadth), jnp.bfloat16))
        for count in (pair_count, max(pair_count - 1, 1) * row_count, max(row_count - 1, 1)):
            sems.extend([pltpu.SemaphoreType.DMA((count,))] * 2)
    operands = [
        pltpu.VMEM((row_count, shapes[0][0], token_rows), jnp.bfloat16),
        pltpu.VMEM((col_count, token_rows, shapes[0][1]), jnp.bfloat16),
        pltpu.VMEM((col_count, shapes[1][0], token_rows), jnp.bfloat16),
        pltpu.VMEM((row_count, token_rows, shapes[1][1]), jnp.bfloat16),
    ]
    return pl.pallas_call(
        functools.partial(
            reduce_dense_kernel,
            (row_count, pair_count, to_rows),
        ),
        out_shape=tuple(
            jax.ShapeDtypeStruct(shape, jnp.float32)
            if to_rows
            else jax.ShapeDtypeStruct((row_count, *shape), jnp.bfloat16)
            for shape in shapes
        ),
        in_specs=[vmem] * 5,
        out_specs=(vmem,) * 3,
        scratch_shapes=scratch + sems + operands,
        compiler_params=pltpu.CompilerParams(
            collective_id=3 if to_rows else 11, has_side_effects=True, vmem_limit_bytes=vmem_most
        ),
        cost_estimate=no_cost,
        name="reduce_dense",
    )(
        normed,
        grad_projected,
        grad_mid_b,
        attended,
        small,
    )


class DenseGather:
    def __init__(self, dims, own_blocks, fulls, sems):
        self.row_count, self.pair_count = dims
        self.rows, self.pairs, self.sides = dense_peers(*dims)
        self.own_blocks = own_blocks
        self.fulls = fulls
        self.kinds = range(len(own_blocks))
        self.row_sems = [sems[6 * kind : 6 * kind + 2] for kind in self.kinds]
        self.pair_sems = [sems[6 * kind + 2 : 6 * kind + 4] for kind in self.kinds]
        self.side_sems = [sems[6 * kind + 4 : 6 * kind + 6] for kind in self.kinds]
        self.local_sems = sems[6 * len(own_blocks)]

    @staticmethod
    def sems(dims, kinds):
        row_count, pair_count = dims
        sems = []
        for _ in range(kinds):
            for count in (
                max(row_count - 1, 1),
                max(pair_count - 1, 1) * row_count,
                pair_count * row_count,
            ):
                sems.extend([pltpu.SemaphoreType.DMA((count,))] * 2)
        return sems + [pltpu.SemaphoreType.DMA((kinds,))]

    def groups(self):
        return (self.rows, self.pairs, self.sides)

    def spot(self, kind, row, pair, side):
        col = pair * 2 + side
        height = self.own_blocks[kind].shape[0]
        return self.fulls[kind].at[row, pl.ds(pl.multiple_of(col * height, height), height), :]

    def own_spot(self, kind):
        return self.spot(kind, self.rows.place, self.pairs.place, self.sides.place)

    def own_copy(self, kind):
        return pltpu.make_async_copy(
            self.own_blocks[kind], self.own_spot(kind), self.local_sems.at[kind]
        )

    def row_copy(self, kind, step):
        return send_to(
            self.own_blocks[kind],
            self.own_spot(kind),
            self.row_sems[kind],
            step - 1,
            self.rows.device_of(self.rows.ahead(step)),
        )

    def row_landed(self, kind, step):
        place = self.rows.behind(step)
        landed = self.spot(kind, place, self.pairs.place, self.sides.place)
        return send_to(
            landed, landed, self.row_sems[kind], step - 1, self.rows.device_of(place)
        )

    def pair_copy(self, kind, step, number):
        block = self.spot(kind, self.rows.behind(number), self.pairs.place, self.sides.place)
        return send_to(
            block if number else self.own_blocks[kind],
            block,
            self.pair_sems[kind],
            (step - 1) * self.row_count + number,
            self.pairs.device_of(self.pairs.ahead(step)),
        )

    def pair_landed(self, kind, step, number):
        place = self.pairs.behind(step)
        landed = self.spot(kind, self.rows.behind(number), place, self.sides.place)
        return send_to(
            landed,
            landed,
            self.pair_sems[kind],
            (step - 1) * self.row_count + number,
            self.pairs.device_of(place),
        )

    def side_copy(self, kind, step, number):
        place = self.pairs.behind(step)
        block = self.spot(kind, self.rows.behind(number), place, self.sides.place)
        return send_to(
            block if step or number else self.own_blocks[kind],
            block,
            self.side_sems[kind],
            step * self.row_count + number,
            self.sides.device_of(1 - self.sides.place),
        )

    def side_landed(self, kind, step, number):
        place = self.pairs.behind(step)
        landed = self.spot(kind, self.rows.behind(number), place, 1 - self.sides.place)
        return send_to(
            landed,
            landed,
            self.side_sems[kind],
            step * self.row_count + number,
            self.sides.device_of(1 - self.sides.place),
        )

    def start(self, kind):
        self.own_copy(kind).start()
        for step in range(1, self.row_count):
            self.row_copy(kind, step).start()
        for step in range(1, self.pair_count):
            self.pair_copy(kind, step, 0).start()
        self.side_copy(kind, 0, 0).start()

    def pass_rows(self, kind):
        for number in range(1, self.row_count):
            self.row_landed(kind, number).wait_recv()
            for step in range(1, self.pair_count):
                self.pair_copy(kind, step, number).start()
            self.side_copy(kind, 0, number).start()

    def pass_pairs(self, kind):
        for number in range(self.row_count):
            for step in range(1, self.pair_count):
                self.pair_landed(kind, step, number).wait_recv()
                self.side_copy(kind, step, number).start()

    def finish(self, kind):
        self.own_copy(kind).wait()
        for step in range(self.pair_count):
            for number in range(self.row_count):
                self.side_landed(kind, step, number).wait_recv()
        for step in range(1, self.row_count):
            self.row_copy(kind, step).wait_send()
        for number in range(self.row_count):
            for step in range(1, self.pair_count):
                self.pair_copy(kind, step, number).wait_send()
            for step in range(self.pair_count):
                self.side_copy(kind, step, number).wait_send()


def gathered_shapes(dims, blocks):
    row_count, pair_count = dims
    return tuple(
        jax.ShapeDtypeStruct(
            (row_count, 2 * pair_count * block.shape[0], block.shape[1]), block.dtype
        )
        for block in blocks
    )


def gather_dense_kernel(
    dims,
    copies,
    qkv_ref,
    out_ref,
    routes_ref,
    router_ref,
    shards_ref,
    qkv_full,
    out_full,
    routes_all,
    router_all,
    moved,
    *sems,
):
    gather = DenseGather(dims, (qkv_ref, out_ref), (qkv_full, out_full), sems[:13])
    small_send, small_recv, local_sems = sems[13:16]
    rows = gather.rows
    move = WeightMove(rows, copies, 0, shards_ref, moved, sems[16:])
    small = [
        Exchange(
            rows,
            small_send,
            small_recv,
            lambda place, chunk, ref=ref: ref,
            lambda place, step, chunk, full=full: full.at[place],
        )
        for ref, full in ((routes_ref, routes_all), (router_ref, router_all))
    ]
    greet(gather.groups())
    own_copies = [
        pltpu.make_async_copy(ref, full.at[rows.place], local_sems.at[number])
        for number, (ref, full) in enumerate(((routes_ref, routes_all), (router_ref, router_all)))
    ]
    for kind in range(2):
        gather.start(kind)
        own_copies[kind].start()
        small[kind].start(kind, None)
    move.start()
    for kind in range(2):
        gather.pass_rows(kind)
    for kind in range(2):
        gather.pass_pairs(kind)
    for kind in range(2):
        small[kind].wait_recv(kind, None)
        gather.finish(kind)
        own_copies[kind].wait()
        small[kind].wait_send(kind, None)
    move.wait_recv()
    move.wait_send()


def gather_dense(row_count, col_count, copies, qkv_block, out_block, routes, router, shards):
    dims = (row_count, col_count // 2)
    outside = pl.BlockSpec(memory_space=pl.ANY)
    return pl.pallas_call(
        functools.partial(gather_dense_kernel, dims, copies),
        out_shape=gathered_shapes(dims, (qkv_block, out_block))
        + tuple(jax.ShapeDtypeStruct((row_count, *x.shape), x.dtype) for x in (routes, router))
        + (moved_shape(row_count, shards),),
        in_specs=[outside] * 5,
        out_specs=(outside,) * 5,
        scratch_shapes=DenseGather.sems(dims, 2)
        + [
            *exchange_sems(2, row_count),
            pltpu.SemaphoreType.DMA((2,)),
            *WeightMove.sems(row_count),
        ],
        compiler_params=pltpu.CompilerParams(collective_id=4, has_side_effects=True),
        cost_estimate=no_cost,
        name="gather_dense",
    )(qkv_block, out_block, routes, router, shards)


def order_layer(layer, blocks, outputs, came, wide, in_sems, out_sems):
    block_count = len(blocks)
    row_index = lax.axis_index("row")
    count = 3 * block_count

    def load(number):
        return pltpu.make_async_copy(
            blocks[number // 3].at[number % 3], came.at[number % 4], in_sems.at[number % 4]
        )

    def store(number):
        expert = lax.rem(row_index + number // 3, block_count)
        return pltpu.make_async_copy(
            wide.at[number % 4], outputs[number % 3].at[layer, expert], out_sems.at[number % 4]
        )

    for number in range(min(3, count)):
        load(number).start()
    for number in range(count):
        if number + 3 < count:
            load(number + 3).start()
        load(number).wait()
        if number >= 4:
            store(number - 4).wait()
        wide[number % 4] = came[number % 4].astype(jnp.float32)
        store(number).start()
    for number in range(max(count - 4, 0), count):
        store(number).wait()


def order_grads_kernel(block_count, layers, early, *refs):
    blocks = [refs[block_count * n : block_count * (n + 1)] for n in range(len(layers))]
    refs = refs[block_count * len(layers) + (3 if early else 0) :]
    for layer, group in zip(layers, blocks):
        order_layer(layer, group, refs[:3], *refs[3:])


def order_grads(layer_count, groups, early):
    blocks = [block for _, group in groups for block in group]
    block_count = len(groups[0][1])
    outside = pl.BlockSpec(memory_space=pl.ANY)
    return pl.pallas_call(
        functools.partial(
            order_grads_kernel, block_count, tuple(layer for layer, _ in groups), bool(early)
        ),
        out_shape=ordered_shapes(layer_count, groups[0][1]),
        in_specs=[outside] * (len(blocks) + len(early)),
        out_specs=(outside,) * 3,
        scratch_shapes=order_scratch(*blocks[0].shape[1:]),
        input_output_aliases={len(blocks) + n: n for n in range(len(early))},
        compiler_params=pltpu.CompilerParams(vmem_limit_bytes=vmem_most),
        cost_estimate=no_cost,
        name="order_grads",
    )(*blocks, *early)


def pieces_nt(left, weights_ref):
    pieces, _, size = weights_ref.shape
    total = None
    for index in range(pieces):
        part = dot_nt(left[:, index * size : (index + 1) * size], weights_ref[index])
        total = part if total is None else total + part
    return total


def rotate(values, cosine, sine):
    return values * cosine + pltpu.roll(values, HEAD_SIZE // 2, 1) * sine


def head_lanes(head):
    return slice(2 * head * HEAD_SIZE, 2 * (head + 1) * HEAD_SIZE)


def key_lanes(head):
    return slice(2 * head * HEAD_SIZE, (2 * head + 1) * HEAD_SIZE)


def value_lanes(head):
    return slice((2 * head + 1) * HEAD_SIZE, 2 * (head + 1) * HEAD_SIZE)


def seen_keys(token_rows):
    position = lax.axis_index("col") * token_rows + iota((1, token_rows), 1)
    return (position // BLOCK + 1) * BLOCK


def attend_forward_kernel(
    dims,
    x_ref,
    gain_attn_ref,
    gain_moe_ref,
    cosine_ref,
    sine_ref,
    qkv_ref,
    out_w_ref,
    shards_ref,
    mid_ref,
    normed_ref,
    q_ref,
    kv_out,
    attended_ref,
    lse_ref,
    normed_moe_ref,
    moved,
    kv_all,
    value_t,
    proj,
    send_sem,
    recv_sem,
    local_sem,
    *move_sems,
):
    col_count, row_count, copies, layer, score_scale = dims
    token_rows = x_ref.shape[0]
    group = QUERY_HEADS // KEY_VALUE_HEADS
    kv_width = KEY_VALUE_HEADS * HEAD_SIZE
    cols = col_peers(col_count)

    def part(place):
        return pl.ds(pl.multiple_of(place * token_rows, token_rows), token_rows)

    share = Exchange(
        cols,
        send_sem,
        recv_sem,
        lambda place, chunk: kv_all.at[part(cols.place), chunk],
        lambda place, step, chunk: kv_all.at[part(place), chunk],
    )
    move = WeightMove(all_rows(row_count), copies, layer, shards_ref, moved, move_sems)
    greet((cols, move.rows))
    move.start()
    x = x_ref[...]
    inverse = lax.rsqrt(jnp.mean(x * x, axis=-1, keepdims=True) + eps_norm)
    normed_ref[...] = (x * inverse * gain_attn_ref[...]).astype(jnp.bfloat16)
    proj[...] = pieces_nt(normed_ref[...], qkv_ref)
    own = part(cols.place)
    for head in range(KEY_VALUE_HEADS):
        start = QUERY_FEATURES + head * HEAD_SIZE
        turned = rotate(proj[:, start : start + HEAD_SIZE], cosine_ref[...], sine_ref[...])
        kv_all[own, key_lanes(head)] = turned.astype(jnp.bfloat16)
        start = start + kv_width
        kv_all[own, value_lanes(head)] = proj[:, start : start + HEAD_SIZE].astype(jnp.bfloat16)
        share.start(head, head_lanes(head))
    for head in range(QUERY_HEADS):
        lanes = slice(head * HEAD_SIZE, (head + 1) * HEAD_SIZE)
        q_ref[:, lanes] = rotate(proj[:, lanes], cosine_ref[...], sine_ref[...]).astype(
            jnp.bfloat16
        )
    seen = seen_keys(token_rows)
    for kv_head in range(KEY_VALUE_HEADS):
        share.wait_recv(kv_head, head_lanes(kv_head))
        value_t[...] = kv_all[:, value_lanes(kv_head)].T

        def head_step(step, carry, kv_head=kv_head):
            index = kv_head * group + step
            lanes = pl.ds(pl.multiple_of(index * HEAD_SIZE, HEAD_SIZE), HEAD_SIZE)
            scores = dot_nt(kv_all[:, key_lanes(kv_head)], q_ref[:, lanes]) * score_scale
            scores = jnp.where(iota(scores.shape, 0) < seen, scores, masked_score)
            peak = jnp.max(scores, axis=0, keepdims=True)
            exponent = jnp.exp(scores - peak)
            total = jnp.sum(exponent, axis=0, keepdims=True)
            attended = dot_nn(value_t[...], exponent.astype(jnp.bfloat16)) / total
            attended_ref[:, lanes] = attended.T.astype(jnp.bfloat16)
            lse_ref[index] = peak + jnp.log(total)
            return carry

        lax.fori_loop(0, group, head_step, 0)
    keep = pltpu.make_async_copy(kv_all, kv_out, local_sem)
    keep.start()
    mid = x_ref[...] + pieces_nt(attended_ref[...], out_w_ref)
    mid_ref[...] = mid
    inverse = lax.rsqrt(jnp.mean(mid * mid, axis=-1, keepdims=True) + eps_norm)
    normed_moe_ref[...] = (mid * inverse * gain_moe_ref[...]).astype(jnp.bfloat16)
    for head in range(KEY_VALUE_HEADS):
        share.wait_send(head, head_lanes(head))
    keep.wait()
    move.wait_recv()
    move.wait_send()


def attend_forward(
    col_count,
    row_count,
    copies,
    layer,
    x,
    gain_attn,
    gain_moe,
    cosine,
    sine,
    qkv_full,
    out_full,
    shards,
):
    token_rows, model_width = x.shape
    seq_rows = col_count * token_rows
    kv_width = KEY_VALUE_HEADS * HEAD_SIZE
    vmem = pl.BlockSpec(memory_space=pltpu.VMEM)
    outside = pl.BlockSpec(memory_space=pl.ANY)
    rows_b = jax.ShapeDtypeStruct((token_rows, model_width), jnp.bfloat16)
    heads_b = jax.ShapeDtypeStruct((token_rows, QUERY_FEATURES), jnp.bfloat16)
    return pl.pallas_call(
        functools.partial(
            attend_forward_kernel, (col_count, row_count, copies, layer, HEAD_SIZE ** (-0.5))
        ),
        out_shape=(
            jax.ShapeDtypeStruct((token_rows, model_width), jnp.float32),
            rows_b,
            heads_b,
            jax.ShapeDtypeStruct((seq_rows, 2 * kv_width), jnp.bfloat16),
            heads_b,
            jax.ShapeDtypeStruct((QUERY_HEADS, 1, token_rows), jnp.float32),
            rows_b,
            moved_shape(row_count, shards),
        ),
        in_specs=[vmem] * 7 + [outside],
        out_specs=(vmem, vmem, vmem, outside, vmem, vmem, vmem, outside),
        scratch_shapes=[
            pltpu.VMEM((seq_rows, 2 * kv_width), jnp.bfloat16),
            pltpu.VMEM((HEAD_SIZE, seq_rows), jnp.bfloat16),
            pltpu.VMEM((token_rows, QUERY_FEATURES + 2 * kv_width), jnp.float32),
            *exchange_sems(KEY_VALUE_HEADS, col_count),
            pltpu.SemaphoreType.DMA,
            *WeightMove.sems(row_count),
        ],
        compiler_params=pltpu.CompilerParams(
            collective_id=5 + 5 * layer, has_side_effects=True, vmem_limit_bytes=vmem_most
        ),
        cost_estimate=no_cost,
        name="attend_forward",
    )(x, gain_attn, gain_moe, cosine, sine, qkv_full, out_full, shards)


def norm_backward(values, gain, incoming):
    inverse = lax.rsqrt(jnp.mean(values * values, axis=-1, keepdims=True) + eps_norm)
    scaled = incoming * gain
    inner_mean = jnp.mean(scaled * values, axis=-1, keepdims=True)
    grad = inverse * scaled - values * (inverse * inverse * inverse) * inner_mean
    return grad, jnp.sum(incoming * values * inverse, axis=0, keepdims=True)


def attend_backward_kernel(
    dims,
    incoming_ref,
    grad_moe_ref,
    mid_ref,
    x_ref,
    gain_attn_ref,
    gain_moe_ref,
    cosine_ref,
    sine_ref,
    qkv_ref,
    out_w_ref,
    q_ref,
    kv_ref,
    attended_ref,
    lse_ref,
    grad_x_ref,
    grad_mid_ref,
    grad_proj_ref,
    grad_gain_attn_ref,
    grad_gain_moe_ref,
    grad_attended,
    key_t,
    key_sum,
    value_sum,
    grad_kv,
    landed,
    send_sem,
    recv_sem,
):
    col_count, score_scale = dims
    token_rows = x_ref.shape[0]
    group = QUERY_HEADS // KEY_VALUE_HEADS
    kv_width = KEY_VALUE_HEADS * HEAD_SIZE
    cols = col_peers(col_count)

    def part(place):
        return pl.ds(pl.multiple_of(place * token_rows, token_rows), token_rows)

    share = Exchange(
        cols,
        send_sem,
        recv_sem,
        lambda place, chunk: grad_kv.at[part(place), chunk],
        lambda place, step, chunk: landed.at[step - 1, :, chunk],
    )
    greet((cols,))
    grad, gain_sum = norm_backward(mid_ref[...], gain_moe_ref[...], grad_moe_ref[...])
    grad_gain_moe_ref[...] = gain_sum
    grad_x_ref[...] = incoming_ref[...] + grad
    grad_mid_ref[...] = grad_x_ref[...].astype(jnp.bfloat16)
    pieces, _, size = out_w_ref.shape
    for index in range(pieces):
        lanes = slice(index * size, (index + 1) * size)
        grad_attended[:, lanes] = dot_nn(grad_mid_ref[...], out_w_ref[index]).astype(jnp.bfloat16)
    seen = seen_keys(token_rows)
    for kv_head in range(KEY_VALUE_HEADS):
        key_t[...] = kv_ref[:, key_lanes(kv_head)].T
        key_sum[...] = jnp.zeros_like(key_sum)
        value_sum[...] = jnp.zeros_like(value_sum)

        def head_step(step, carry, kv_head=kv_head):
            index = kv_head * group + step
            lanes = pl.ds(pl.multiple_of(index * HEAD_SIZE, HEAD_SIZE), HEAD_SIZE)
            query = q_ref[:, lanes]
            grad_out = grad_attended[:, lanes]
            product = grad_out.astype(jnp.float32) * attended_ref[:, lanes].astype(jnp.float32)
            inner = jnp.sum(product.T, axis=0, keepdims=True)
            scores = dot_nt(kv_ref[:, key_lanes(kv_head)], query) * score_scale
            soft = jnp.where(
                iota(scores.shape, 0) < seen, jnp.exp(scores - lse_ref[index]), 0.0
            )
            grad_soft = dot_nt(kv_ref[:, value_lanes(kv_head)], grad_out)
            grad_scores = (soft * (grad_soft - inner)).astype(jnp.bfloat16)
            value_sum[...] += dot_nn(soft.astype(jnp.bfloat16), grad_out)
            key_sum[...] += dot_nn(grad_scores, query)
            grad_q = (dot_nn(key_t[...], grad_scores) * score_scale).T
            grad_q = rotate(grad_q, cosine_ref[...], -sine_ref[...])
            grad_proj_ref[:, lanes] = grad_q.astype(jnp.bfloat16)
            return carry

        lax.fori_loop(0, group, head_step, 0)
        grad_kv[:, key_lanes(kv_head)] = (key_sum[...] * score_scale).astype(jnp.bfloat16)
        grad_kv[:, value_lanes(kv_head)] = value_sum[...].astype(jnp.bfloat16)
        share.start(kv_head, head_lanes(kv_head))
    for head in range(KEY_VALUE_HEADS):
        share.wait_recv(head, head_lanes(head))
        total = grad_kv[part(cols.place), head_lanes(head)].astype(jnp.float32)
        for step in range(1, col_count):
            total = total + landed[step - 1, :, head_lanes(head)].astype(jnp.float32)
        start = QUERY_FEATURES + head * HEAD_SIZE
        grad_key = rotate(total[:, :HEAD_SIZE], cosine_ref[...], -sine_ref[...])
        grad_proj_ref[:, start : start + HEAD_SIZE] = grad_key.astype(jnp.bfloat16)
        start = start + kv_width
        grad_proj_ref[:, start : start + HEAD_SIZE] = total[:, HEAD_SIZE:].astype(jnp.bfloat16)
    pieces = qkv_ref.shape[0]
    grad_normed = [dot_nn(grad_proj_ref[...], qkv_ref[index]) for index in range(pieces)]
    grad_normed = jnp.concatenate(grad_normed, axis=1) if pieces > 1 else grad_normed[0]
    grad, gain_sum = norm_backward(x_ref[...], gain_attn_ref[...], grad_normed)
    grad_gain_attn_ref[...] = gain_sum
    grad_x_ref[...] += grad
    for head in range(KEY_VALUE_HEADS):
        share.wait_send(head, head_lanes(head))


def attend_backward(
    col_count,
    incoming,
    grad_moe,
    mid,
    x,
    gain_attn,
    gain_moe,
    cosine,
    sine,
    qkv_full,
    out_full,
    queries,
    key_value,
    attended,
    log_sums,
):
    token_rows, model_width = x.shape
    seq_rows = col_count * token_rows
    kv_width = KEY_VALUE_HEADS * HEAD_SIZE
    vmem = pl.BlockSpec(memory_space=pltpu.VMEM)
    gain = jax.ShapeDtypeStruct((1, model_width), jnp.float32)
    return pl.pallas_call(
        functools.partial(attend_backward_kernel, (col_count, HEAD_SIZE ** (-0.5))),
        out_shape=(
            jax.ShapeDtypeStruct((token_rows, model_width), jnp.float32),
            jax.ShapeDtypeStruct((token_rows, model_width), jnp.bfloat16),
            jax.ShapeDtypeStruct((token_rows, QUERY_FEATURES + 2 * kv_width), jnp.bfloat16),
            gain,
            gain,
        ),
        in_specs=[vmem] * 14,
        out_specs=(vmem,) * 5,
        scratch_shapes=[
            pltpu.VMEM((token_rows, QUERY_FEATURES), jnp.bfloat16),
            pltpu.VMEM((HEAD_SIZE, seq_rows), jnp.bfloat16),
            pltpu.VMEM((seq_rows, HEAD_SIZE), jnp.float32),
            pltpu.VMEM((seq_rows, HEAD_SIZE), jnp.float32),
            pltpu.VMEM((seq_rows, 2 * kv_width), jnp.bfloat16),
            pltpu.VMEM((max(col_count - 1, 1), token_rows, 2 * kv_width), jnp.bfloat16),
            *exchange_sems(KEY_VALUE_HEADS, col_count),
        ],
        compiler_params=pltpu.CompilerParams(
            collective_id=6, has_side_effects=True, vmem_limit_bytes=vmem_most
        ),
        cost_estimate=no_cost,
        name="attend_backward",
    )(
        incoming,
        grad_moe,
        mid,
        x,
        gain_attn,
        gain_moe,
        cosine,
        sine,
        qkv_full,
        out_full,
        queries,
        key_value,
        attended,
        log_sums,
    )


def place_first(values, group_rows, expert_pick):
    rolled = jnp.roll(values.reshape(-1, group_rows, values.shape[1]), -expert_pick, axis=1)
    return rolled.transpose(1, 0, 2).reshape(values.shape)


def place_back(values, group_rows, expert_pick):
    rolled = values.reshape(group_rows, -1, values.shape[1]).transpose(1, 0, 2)
    return jnp.roll(rolled, expert_pick, axis=1).reshape(values.shape)


def body(
    hidden_in, routes, norm_attn, w_qkv, w_out, norm_moe, w_router, w_gate, w_up, w_down, cotangent
):
    row_count = lax.axis_size("row")
    col_count = lax.axis_size("col")
    device_count = row_count * col_count
    row_index = lax.axis_index("row")
    col_index = lax.axis_index("col")
    layer_count = w_qkv.shape[0]
    token_rows = hidden_in.shape[0]
    model_width = hidden_in.shape[1]
    local_experts = w_gate.shape[1]
    slice_width = w_gate.shape[3]
    copies = row_count // local_experts
    expert_pick = row_index // copies
    slot_rows = -(-local_experts * CAP // 16) * 16
    chunks = model_width // 384
    dims = (
        local_experts,
        col_count,
        copies,
        token_rows,
        slot_rows,
        chunks,
        model_width // chunks,
    )
    positions = col_index * token_rows + jnp.arange(token_rows, dtype=jnp.int32)
    cosine, sine = rope_angles(positions, HEAD_SIZE // 2)
    cosine = jnp.concatenate([cosine, cosine], axis=1)
    sine = jnp.concatenate([-sine, sine], axis=1)

    def move_grads(grads):
        blocks = [grads[0]]
        for step in range(1, row_count):
            pairs = [(index, (index - step) % row_count) for index in range(row_count)]
            blocks.append(lax.ppermute(grads[step], "row", pairs))
        return tuple(blocks)

    def own_grads(blocks):
        ordered = jnp.roll(jnp.stack(blocks), row_index, axis=0).astype(wide_type)
        return jnp.sum(ordered.reshape(local_experts, copies, *blocks[0].shape), axis=1)

    def pieced(full):
        if full.shape[2] % 128 == 0:
            return full
        return full.transpose(1, 0, 2).reshape(1, full.shape[1], -1)

    def packed(values):
        return jnp.pad(values.reshape(-1), (0, -values.size % 2048)).reshape(-1, 128)

    shards = (w_gate.transpose(0, 1, 3, 2), w_up.transpose(0, 1, 3, 2), w_down)
    experts = []
    route_lines = routes.transpose(0, 2, 1)
    router_lines = w_router.transpose(0, 2, 1)
    qkv_full, out_full, routes_all, router_all, moved_gate = gather_dense(
        row_count,
        col_count,
        copies,
        w_qkv[0].T,
        w_out[0].T,
        packed(route_lines),
        packed(router_lines),
        shards[0],
    )
    dense = [(pieced(qkv_full), pieced(out_full))]
    routes_all = routes_all.reshape(row_count, -1)[:, : route_lines.size]
    routes_all = routes_all.reshape(row_count, *route_lines.shape)
    if copies > 1:
        routes_all = jnp.take(
            routes_all, row_index % copies + copies * jnp.arange(local_experts), axis=0
        )
    router_all = router_all.reshape(row_count, -1)[:, : router_lines.size]
    router_all = router_all.reshape(row_count, *router_lines.shape)
    router_all = router_all.transpose(1, 2, 0, 3).reshape(layer_count, E, model_width)
    routers = [
        place_first(router_all[index], local_experts, expert_pick) for index in range(layer_count)
    ]
    gains_attn = norm_attn.astype(wide_type)[:, None, :]
    gains_moe = norm_moe.astype(wide_type)[:, None, :]
    hidden = hidden_in.astype(wide_type)
    saved = []
    for layer_index in range(layer_count):
        early = 0 if layer_index else 1
        mid, normed, queries, key_value, attended, log_sums, normed_moe, moved = attend_forward(
            col_count,
            row_count,
            copies,
            layer_index,
            hidden,
            gains_attn[layer_index],
            gains_moe[layer_index],
            cosine,
            sine,
            *dense[layer_index],
            shards[early],
        )
        if layer_index == 0:
            weights, moving = [moved_gate, moved, shards[2]], (2,)
        else:
            weights, moving = [moved, shards[1], shards[2]], (1, 2)
        next_blocks = ()
        if layer_index + 1 < layer_count:
            next_blocks = (w_qkv[layer_index + 1].T, w_out[layer_index + 1].T)
        closing = (cotangent,) if layer_index + 1 == layer_count else ()
        mixed, gates, slots, returned, *rest = moe_forward(
            dims,
            row_count,
            layer_index,
            normed_moe,
            routes_all[:, layer_index],
            routers[layer_index],
            weights,
            moving,
            next_blocks,
            closing,
        )
        if closing:
            closing = (rest.pop(0), mixed)
        for kind, moved in zip(moving, rest):
            weights[kind] = moved
        experts.append(weights)
        if next_blocks:
            dense.append(tuple(pieced(full) for full in rest[len(moving) :]))
        saved.append(
            (hidden, mid, normed, queries, key_value, attended, log_sums, normed_moe)
            + (gates, slots, returned)
        )
        if not closing:
            hidden = mid + mixed
    incoming = cotangent.astype(wide_type)
    dense_results = [None] * layer_count
    expert_results = [None] * layer_count
    part_sums = ()
    ordered = ()
    for layer_index in reversed(range(layer_count)):
        x, mid, normed, queries, key_value, attended, log_sums, normed_moe = saved[layer_index][:8]
        gates, slots, returned = saved[layer_index][8:]
        grad_moe, grad_router, *rest = moe_backward(
            dims,
            closing[0] if closing else incoming.astype(narrow_type),
            routes_all[:, layer_index],
            routers[layer_index],
            gates,
            normed_moe,
            slots,
            returned,
            experts[layer_index],
            closing[1:],
            part_sums,
        )
        if part_sums:
            dense_results[layer_index + 1] = rest[row_count : row_count + 3]
            del rest[row_count : row_count + 3]
        if closing:
            hidden = mid + rest.pop()
            closing = ()
        if layer_index + 1 < layer_count:
            grad_moe, expert_results[layer_index + 1] = lax.optimization_barrier(
                (grad_moe, expert_results[layer_index + 1])
            )
        expert_results[layer_index] = move_grads(rest)
        incoming, grad_mid, grad_projected, grad_gain_attn, grad_gain_moe = attend_backward(
            col_count,
            incoming,
            grad_moe,
            mid,
            x,
            gains_attn[layer_index],
            gains_moe[layer_index],
            cosine,
            sine,
            *dense[layer_index],
            queries,
            key_value,
            attended,
            log_sums,
        )
        small = jnp.concatenate(
            [
                place_back(grad_router, local_experts, expert_pick),
                grad_gain_attn,
                grad_gain_moe,
            ],
            axis=0,
        ).astype(narrow_type)
        small = small.reshape(E + 2, device_count, -1).transpose(1, 0, 2).reshape(device_count, -1)
        small_size = small.shape[1]
        small_rows = -(-small_size // 2048) * 16
        small = jnp.pad(small, ((0, 0), (0, small_rows * 128 - small_size)))
        small = small.reshape(row_count, col_count, small_rows, 128).transpose(1, 0, 2, 3)
        if layer_index == 0 and copies == 1 and layer_count > 1:
            groups = tuple((above, expert_results[above]) for above in range(1, layer_count))
            grad_mid, ordered = lax.optimization_barrier(
                (grad_mid, order_grads(layer_count, groups, ()))
            )
        part_sums = reduce_dense(
            row_count,
            col_count,
            normed,
            grad_projected,
            grad_mid,
            attended,
            small,
            layer_index == 0,
        )
        if layer_index > 0:
            incoming, part_sums = lax.optimization_barrier((incoming, part_sums))
        else:
            dense_results[0] = part_sums
    small_results = [
        small.reshape(-1)[:small_size].reshape(E + 2, -1).T for _, _, small in dense_results
    ]
    dense_results = [(qkv, out.T) for qkv, out, _ in dense_results]
    small = jnp.stack(small_results)
    if copies == 1:
        grad_gate, grad_up, grad_down = order_grads(
            layer_count, ((0, expert_results[0]),), ordered
        )
    else:
        ordered = jnp.stack([own_grads(blocks) for blocks in expert_results])
        grad_gate, grad_up, grad_down = (ordered[:, :, kind] for kind in range(3))
    grad_gate, grad_up = grad_gate.swapaxes(2, 3), grad_up.swapaxes(2, 3)
    return (
        hidden,
        incoming,
        small[:, :, E],
        jnp.stack([dense_results[index][0] for index in range(layer_count)]),
        jnp.stack([dense_results[index][1] for index in range(layer_count)]),
        small[:, :, E + 1],
        small[:, :, :E],
        grad_gate,
        grad_up,
        grad_down,
    )


def solution(mesh):
    in_specs = (
        P(("row", "col"), None),
        P(None, ("row", "col"), None),
        P(),
        P(None, "row", "col"),
        P(None, "row", "col"),
        P(),
        P(None, "row", None),
        P(None, "col", None, "row"),
        P(None, "col", None, "row"),
        P(None, "col", "row", None),
        P(("row", "col"), None),
    )
    out_specs = (
        P(("row", "col"), None),
        P(("row", "col"), None),
        P(None, ("row", "col")),
        P(None, "row", "col"),
        P(None, "row", "col"),
        P(None, ("row", "col")),
        P(None, ("row", "col"), None),
        P(None, "col", None, "row"),
        P(None, "col", None, "row"),
        P(None, "col", "row", None),
    )
    return jax.shard_map(body, mesh=mesh, in_specs=in_specs, out_specs=out_specs, check_vma=False)
```

```python
import functools

import jax
import jax.numpy as jnp
from jax import lax
from jax.experimental import pallas as pl
from jax.experimental.pallas import tpu as pltpu
from jax.sharding import PartitionSpec as P

QUERY_HEADS = 12
KEY_VALUE_HEADS = 2
HEAD_SIZE = 128
E = 32
TOPK = 4
BLOCK = 256
QUERY_FEATURES = 1536
CAP = 36


eps_norm = 1e-06
rope_base = 1000000.0
masked_score = -1e30
wide_type = jnp.float32
narrow_type = jnp.bfloat16


def rope_angles(positions, half_dim):
    frequency = rope_base ** (-jnp.arange(half_dim, dtype=jnp.float32) / half_dim)
    angles = positions.astype(jnp.float32)[:, None] * frequency[None, :]
    return (jnp.cos(angles), jnp.sin(angles))


def split_rows(total, most):
    best = 16
    for step in range(16, most + 1, 16):
        if total % step == 0:
            best = step
    return best


def over_blocks(total, block, step):
    def run(index, carry):
        step(pl.ds(pl.multiple_of(index * block, block), block))
        return carry

    lax.fori_loop(0, total // block, run, 0)


def over_chunks(chunks, width, step):
    def run(index, carry):
        step(index, pl.ds(pl.multiple_of(index * width, width), width))
        return carry

    lax.fori_loop(0, chunks, run, 0)


def dot_nt(left, right):
    return lax.dot_general(
        left, right, (((1,), (1,)), ((), ())), preferred_element_type=jnp.float32
    )


def dot_nn(left, right):
    return jnp.dot(left, right, preferred_element_type=jnp.float32)


class Peers:
    def __init__(self, count, place, device_of):
        self.count = count
        self.place = place
        self.device_of = device_of

    def ahead(self, step):
        return lax.rem(self.place + step, self.count)

    def behind(self, step):
        return lax.rem(self.place + self.count - step, self.count)


def expert_peers(col_count, copies, group_rows):
    row_index = lax.axis_index("row")
    share = lax.rem(row_index, copies)
    rows = Peers(group_rows, row_index // copies, lambda place: {"row": share + copies * place})
    return rows, col_peers(col_count)


def col_peers(col_count):
    return Peers(col_count, lax.axis_index("col"), lambda place: {"col": place})


def greet(groups):
    barrier = pltpu.get_barrier_semaphore()
    total = 0
    for peers in groups:
        for step in range(1, peers.count):
            pl.semaphore_signal(
                barrier,
                inc=1,
                device_id=peers.device_of(peers.ahead(step)),
                device_id_type=pl.DeviceIdType.MESH,
            )
            total += 1
    pl.semaphore_wait(barrier, total)


def send_to(source, target, sems, number, device):
    send_sems, recv_sems = sems
    return pltpu.make_async_remote_copy(
        src_ref=source,
        dst_ref=target,
        send_sem=send_sems.at[number],
        recv_sem=recv_sems.at[number],
        device_id=device,
        device_id_type=pl.DeviceIdType.MESH,
    )


class Exchange:
    def __init__(self, peers, send_sems, recv_sems, source, target):
        self.peers = peers
        self.sems = (send_sems, recv_sems)
        self.source = source
        self.target = target

    def out(self, step, index, chunk):
        place = self.peers.ahead(step)
        return send_to(
            self.source(place, chunk),
            self.target(self.peers.place, step, chunk),
            self.sems,
            (index, step - 1),
            self.peers.device_of(place),
        )

    def start(self, index, chunk):
        for step in range(1, self.peers.count):
            self.out(step, index, chunk).start()

    def wait_send(self, index, chunk):
        for step in range(1, self.peers.count):
            self.out(step, index, chunk).wait_send()

    def wait_recv(self, index, chunk):
        for step in range(1, self.peers.count):
            place = self.peers.behind(step)
            landed = self.target(place, step, chunk)
            send_to(
                landed, landed, self.sems, (index, step - 1), self.peers.device_of(place)
            ).wait_recv()


def exchange_sems(chunks, count):
    return [pltpu.SemaphoreType.DMA((chunks, max(count - 1, 1))) for _ in range(2)]


class LineGather:
    def __init__(self, rows, own, tokens, part, sems):
        self.rows = rows
        self.own = own
        self.tokens = tokens
        self.part = part
        self.own_send, self.pass_send, self.recv = sems

    @staticmethod
    def sems(chunks, count):
        return [
            pltpu.SemaphoreType.DMA((chunks, 2)),
            pltpu.SemaphoreType.DMA((chunks, count)),
            pltpu.SemaphoreType.DMA((chunks, count)),
        ]

    def copy(self, source, origin, index, chunk, sem, place):
        return pltpu.make_async_remote_copy(
            src_ref=source,
            dst_ref=self.tokens.at[self.part(origin), chunk],
            send_sem=sem,
            recv_sem=self.recv.at[index, origin],
            device_id=self.rows.device_of(place),
            device_id_type=pl.DeviceIdType.MESH,
        )

    def own_copies(self, index, chunk):
        me, last = self.rows.place, self.rows.count - 1
        for way, (there, place) in enumerate(((me < last, me + 1), (me > 0, me - 1))):
            yield there, self.copy(
                self.own.at[:, chunk], me, index, chunk, self.own_send.at[index, way], place
            )

    def passed(self, index, chunk):
        me, last = self.rows.place, self.rows.count - 1
        for distance in range(1, self.rows.count):
            for arrives, origin, goes_on, place in (
                (me >= distance, me - distance, me < last, me + 1),
                (me + distance <= last, me + distance, me > 0, me - 1),
            ):
                yield arrives, goes_on, self.copy(
                    self.tokens.at[self.part(origin), chunk],
                    origin,
                    index,
                    chunk,
                    self.pass_send.at[index, origin],
                    place,
                )

    def start_own(self, index, chunk):
        for there, copy in self.own_copies(index, chunk):
            pl.when(there)(copy.start)

    def arrive(self, index, chunk):
        for arrives, goes_on, copy in self.passed(index, chunk):

            @pl.when(arrives)
            def _():
                copy.wait_recv()
                pl.when(goes_on)(copy.start)

    def wait_send(self, index, chunk):
        for there, copy in self.own_copies(index, chunk):
            pl.when(there)(copy.wait_send)
        for arrives, goes_on, copy in self.passed(index, chunk):
            pl.when(arrives & goes_on)(copy.wait_send)


class LineSum:
    def __init__(self, rows, tokens, part, landed, sems):
        self.rows = rows
        self.tokens = tokens
        self.part = part
        self.landed = landed
        self.send, self.recv = sems

    @staticmethod
    def sems(chunks, count):
        return [
            pltpu.SemaphoreType.DMA((chunks, count)),
            pltpu.SemaphoreType.DMA((chunks, count + 1)),
        ]

    def copy(self, target, slot, index, chunk, place):
        return pltpu.make_async_remote_copy(
            src_ref=self.tokens.at[self.part(target), chunk],
            dst_ref=self.landed.at[slot, :, chunk],
            send_sem=self.send.at[index, target],
            recv_sem=self.recv.at[index, slot],
            device_id=self.rows.device_of(place),
            device_id_type=pl.DeviceIdType.MESH,
        )

    def passed(self, index, chunk):
        me, last = self.rows.place, self.rows.count - 1
        for number in range(self.rows.count):
            for goes, arrives, slot, target, place in (
                (me > number, me < last, number, number, me - 1),
                (me < last - number, me > 0, last - number + 1, last - number, me + 1),
            ):
                yield goes, arrives, slot, target, self.copy(target, slot, index, chunk, place)

    def pass_on(self, index, chunk):
        for goes, arrives, slot, target, copy in self.passed(index, chunk):

            @pl.when(goes)
            def _():
                @pl.when(arrives)
                def _():
                    copy.wait_recv()
                    total = self.tokens[self.part(target), chunk].astype(jnp.float32)
                    total = total + self.landed[slot, :, chunk].astype(jnp.float32)
                    self.tokens[self.part(target), chunk] = total.astype(jnp.bfloat16)

                copy.start()

    def is_middle(self):
        return (self.rows.place > 0) & (self.rows.place < self.rows.count - 1)

    def total(self, index, chunk, out):
        me, last = self.rows.place, self.rows.count - 1
        out[:, chunk] = self.tokens[self.part(me), chunk].astype(jnp.float32)
        for arrives, slot in ((me < last, me), (me > 0, me + 1)):

            @pl.when(arrives)
            def _():
                self.copy(me, slot, index, chunk, me).wait_recv()
                out[:, chunk] += self.landed[slot, :, chunk].astype(jnp.float32)

    def wait_send(self, index, chunk):
        for goes, _, _, _, copy in self.passed(index, chunk):
            pl.when(goes)(copy.wait_send)


def iota(shape, axis):
    return lax.broadcasted_iota(jnp.int32, shape, axis)


def within(numbers, size, count):
    block = jnp.zeros_like(numbers)
    for index in range(1, count):
        block = block + (numbers >= index * size).astype(jnp.int32)
    return block, numbers - block * size


def slot_block(shape, slot_axis, slot_rows):
    slots = iota(shape, slot_axis)
    block = iota(shape, 1 - slot_axis)
    return (slots >= block * slot_rows) & (slots < (block + 1) * slot_rows)


def build_places(dims, rows, routes_ref, place, place_t, member):
    group_rows, col_count, copies, token_rows, slot_rows, chunks, width = dims
    all_slots = col_count * slot_rows
    number = iota((E, 1), 0)
    ahead, col = within(number, col_count, group_rows)
    owner = ahead + rows.place
    owner = jnp.where(owner >= group_rows, owner - group_rows, owner)
    expert = col * group_rows + owner
    earlier = (iota((token_rows, token_rows), 0) < iota((token_rows, token_rows), 1)).astype(
        jnp.bfloat16
    )
    pick = slot_block((E, all_slots), 1, slot_rows).astype(jnp.bfloat16)
    column = iota((slot_rows, 1), 0)
    lane = within(iota((1, all_slots), 1), slot_rows, col_count)[1]
    for group in range(group_rows):
        tokens = slice(group * token_rows, (group + 1) * token_rows)
        picked = routes_ref[group]
        has = picked[0:1, :] == expert
        for choice in range(1, TOPK):
            has = has | (picked[choice : choice + 1, :] == expert)
        before = dot_nn(has.astype(jnp.float32).astype(jnp.bfloat16), earlier)
        slot_number = jnp.where(has, before, -1.0)
        in_group = (column >= group * CAP) & (column < (group + 1) * CAP)
        wanted = jnp.where(in_group, column - group * CAP, -2).astype(jnp.float32)
        for index in range(col_count):
            slots = slice(index * slot_rows, (index + 1) * slot_rows)
            hit = slot_number[index : index + 1, :] == wanted
            place[slots, tokens] = jnp.where(hit, 1.0, 0.0).astype(jnp.bfloat16)
        turned = slot_number.T
        in_group = (lane >= group * CAP) & (lane < (group + 1) * CAP)
        wanted = jnp.where(in_group, lane - group * CAP, -2).astype(jnp.float32)
        hit = dot_nn(turned.astype(jnp.bfloat16), pick) == wanted
        place_t[tokens, :] = jnp.where(hit, 1.0, 0.0).astype(jnp.bfloat16)
        if member is not None:
            member[tokens, :] = turned


def far_first(rows):
    for distance in range(rows.count - 1, 0, -1):
        for there, place in (
            (rows.place + distance < rows.count, rows.place + distance),
            (rows.place >= distance, rows.place - distance),
        ):
            yield there, place


class WeightMove:
    def __init__(self, rows, copies, layer, shards, target, sems, parts=1):
        self.rows = rows
        self.copies = copies
        self.layer = layer
        self.shards = shards
        self.target = target
        self.remote_sems = sems[:2]
        self.local_sem = sems[2]
        self.parts = parts
        self.width = target.shape[2] // parts

    @staticmethod
    def sems(row_count, parts=1):
        return [pltpu.SemaphoreType.DMA((parts, max(row_count - 1, 1)))] * 2 + [
            pltpu.SemaphoreType.DMA
        ]

    def own(self):
        return pltpu.make_async_copy(
            self.shards.at[self.layer, self.rows.place // self.copies],
            self.target.at[0],
            self.local_sem,
        )

    def lanes(self, part):
        return pl.ds(pl.multiple_of(part * self.width, self.width), self.width)

    def out(self, step, part):
        place = self.rows.ahead(step)
        return send_to(
            self.shards.at[self.layer, place // self.copies, :, self.lanes(part)],
            self.target.at[step, :, self.lanes(part)],
            self.remote_sems,
            (part, step - 1),
            self.rows.device_of(place),
        )

    def start(self):
        self.own().start()

        def one_part(part, carry):
            for there, place in far_first(self.rows):
                step = lax.rem(place - self.rows.place + self.rows.count, self.rows.count)

                @pl.when(there)
                def _():
                    self.out(step, part).start()

            return carry

        lax.fori_loop(0, self.parts, one_part, 0)

    def wait_part(self, part):
        for step in range(1, self.rows.count):
            landed = self.target.at[step, :, self.lanes(part)]
            place = self.rows.behind(step)
            send_to(
                landed, landed, self.remote_sems, (part, step - 1), self.rows.device_of(place)
            ).wait_recv()

    def wait_recv(self):
        self.own().wait()
        for part in range(self.parts):
            self.wait_part(part)

    def wait_send(self):
        for part in range(self.parts):
            for step in range(1, self.rows.count):
                self.out(step, part).wait_send()


def line_sems(row_count):
    return [pltpu.SemaphoreType.DMA((max(row_count - 1, 1),))] * 2 + [pltpu.SemaphoreType.DMA]


def all_rows(row_count):
    return Peers(row_count, lax.axis_index("row"), lambda place: {"row": place})


def moved_shape(row_count, shards):
    return jax.ShapeDtypeStruct((row_count, *shards.shape[2:]), shards.dtype)


vmem_most = 62 * 1024 * 1024
long_cost = pl.CostEstimate(flops=0, bytes_accessed=600 * 1024 * 1024, transcendentals=0)
no_cost = pl.CostEstimate(flops=0, bytes_accessed=0, transcendentals=0)


def moe_forward_kernel(dims, row_count, layer, moving, gather_dims, closing, *refs):
    group_rows, col_count, copies, token_rows, slot_rows, chunks, width = dims
    own_ref, routes_ref, router_ref = refs[:3]
    weight_in = refs[3:6]
    refs = refs[6:]
    next_blocks = refs[: 2 if gather_dims else 0]
    refs = refs[len(next_blocks) :]
    sum_ref, gates_ref, slots_out, returned_out = refs[:4]
    refs = refs[4:]
    moved_out = refs[: len(moving)]
    refs = refs[len(moving) :]
    next_full = refs[: len(next_blocks)]
    refs = refs[len(next_blocks) :]
    dense = None
    if gather_dims:
        count = len(DenseGather.sems(gather_dims, 2))
        dense = DenseGather(gather_dims, next_blocks, next_full, refs[-count:])
        refs = refs[:-count]
    move_sems = refs[len(refs) - 3 * len(moving) :]
    refs = refs[: len(refs) - 3 * len(moving)]
    (
        place,
        place_t,
        member,
        gate,
        up,
        down,
        tokens,
        send,
        slots,
        gate_val,
        up_val,
        act,
        returned,
        landed,
        own_send,
        pass_send,
        row_recv,
        there_send,
        there_recv,
        back_send,
        back_recv,
        home_send,
        home_recv,
        local_sem,
    ) = refs
    all_tokens = group_rows * token_rows
    all_slots = col_count * slot_rows
    slot_step = split_rows(all_slots, 320)
    rows, cols = expert_peers(col_count, copies, group_rows)

    def token_part(place):
        return pl.ds(pl.multiple_of(place * token_rows, token_rows), token_rows)

    def slot_part(place):
        return pl.ds(pl.multiple_of(place * slot_rows, slot_rows), slot_rows)

    gather = LineGather(rows, own_ref, tokens, token_part, (own_send, pass_send, row_recv))
    there = Exchange(
        cols,
        there_send,
        there_recv,
        lambda place, chunk: send.at[slot_part(place), chunk],
        lambda place, step, chunk: slots.at[slot_part(place), chunk],
    )
    back = Exchange(
        cols,
        back_send,
        back_recv,
        lambda place, chunk: send.at[slot_part(place), chunk],
        lambda place, step, chunk: returned.at[slot_part(place), chunk],
    )
    home = LineSum(rows, tokens, token_part, landed, (home_send, home_recv))
    weights = (gate, up, down)
    moves = {
        kind: WeightMove(
            all_rows(row_count),
            copies,
            layer,
            weight_in[kind],
            weights[kind],
            move_sems[3 * number : 3 * number + 3],
            chunks if kind == 2 else 1,
        )
        for number, kind in enumerate(moving)
    }
    loads = {
        kind: pltpu.make_async_copy(weight_in[kind], weights[kind], local_sem.at[2 + kind])
        for kind in range(3)
        if kind not in moving
    }
    keeps = []

    def keep_weight(kind):
        keep = pltpu.make_async_copy(
            weights[kind], moved_out[moving.index(kind)], local_sem.at[2 + kind]
        )
        keep.start()
        keeps.append(keep)

    def weight_ready(kind):
        if kind in loads:
            loads[kind].wait()
        elif kind == 2:
            moves[kind].own().wait()
        else:
            moves[kind].wait_recv()
            keep_weight(kind)

    def weight(kind, chunk):
        return weights[kind][:, :, chunk].reshape(-1, width)

    greet((all_rows(row_count), cols))
    for index in range(min(2, chunks)):
        gather.start_own(index, pl.ds(index * width, width))
    for copy in loads.values():
        copy.start()
    tokens[token_part(rows.place), :] = own_ref[...]
    build_places(dims, rows, routes_ref, place, place_t, member)

    def dispatch(index, chunk):
        gather.arrive(index, chunk)

        @pl.when(index + 2 < chunks)
        def _():
            later = pl.ds(pl.multiple_of((index + 2) * width, width), width)
            gather.start_own(index + 2, later)


        def rows_of(part):
            send[part, chunk] = dot_nn(place[part, :], tokens[:, chunk]).astype(jnp.bfloat16)

        over_blocks(all_slots, all_slots, rows_of)
        there.start(index, chunk)
        slots[slot_part(cols.place), chunk] = send[slot_part(cols.place), chunk]

    over_chunks(chunks, width, dispatch)
    if dense:
        for kind in dense.kinds:
            dense.start(kind)
    for kind in moving:
        moves[kind].start()

    def gating(part):
        chosen = member[part, :] >= 0
        logits = jnp.where(chosen, dot_nt(tokens[part, :], router_ref[...]), masked_score)
        peak = jnp.max(logits, axis=-1, keepdims=True)
        exponent = jnp.where(chosen, jnp.exp(logits - peak), 0.0)
        gates = exponent / jnp.sum(exponent, axis=-1, keepdims=True)
        gates_ref[part, :] = gates
        pick = slot_block((E, all_slots), 1, slot_rows).astype(jnp.bfloat16)
        spread = dot_nn(gates.astype(jnp.bfloat16), pick)
        place_t[part, :] = (place_t[part, :].astype(jnp.float32) * spread).astype(jnp.bfloat16)

    over_blocks(all_tokens, token_rows, gating)

    def project(kind, target, wait, index, chunk):
        if wait:
            there.wait_recv(index, chunk)

        def rows_of(part):
            value = dot_nt(slots[part, chunk], weight(kind, chunk))

            @pl.when(index == 0)
            def _():
                target[part, :] = value

            @pl.when(index > 0)
            def _():
                target[part, :] += value

        over_blocks(all_slots, all_slots, rows_of)

    weight_ready(0)
    over_chunks(chunks, width, functools.partial(project, 0, gate_val, True))
    weight_ready(1)
    over_chunks(chunks, width, functools.partial(project, 1, up_val, False))
    keep_slots = pltpu.make_async_copy(slots, slots_out, local_sem.at[0])
    keep_slots.start()

    def activate(part):
        value = gate_val[part, :]
        act[part, :] = (value * jax.nn.sigmoid(value) * up_val[part, :]).astype(jnp.bfloat16)

    over_blocks(all_slots, slot_step, activate)
    if dense:
        for kind in dense.kinds:
            dense.pass_rows(kind)
    weight_ready(2)
    def give_back(index, chunk):
        if 2 in moves:
            moves[2].wait_part(index)
        there.wait_send(index, chunk)

        def rows_of(part):
            send[part, chunk] = dot_nn(act[part, :], weight(2, chunk)).astype(jnp.bfloat16)

        over_blocks(all_slots, all_slots, rows_of)
        back.start(index, chunk)
        returned[slot_part(cols.place), chunk] = send[slot_part(cols.place), chunk]

    over_chunks(chunks, width, give_back)
    if 2 in moves:
        keep_weight(2)

    over_chunks(chunks, width, gather.wait_send)

    def combine(index, chunk):
        back.wait_recv(index, chunk)

        def rows_of(part):
            tokens[part, chunk] = dot_nn(place_t[part, :], returned[:, chunk]).astype(jnp.bfloat16)

        over_blocks(all_tokens, token_rows, rows_of)
        if closing:
            return
        pl.when(~home.is_middle())(functools.partial(home.pass_on, index, chunk))

        @pl.when(home.is_middle() & (index > 0))
        def _():
            before = pl.ds(pl.multiple_of((index - 1) * width, width), width)
            home.pass_on(index - 1, before)

    over_chunks(chunks, width, combine)
    if closing:
        keep_mixed = pltpu.make_async_copy(tokens, sum_ref, local_sem.at[5])
        keep_mixed.start()
    else:
        last_chunk = pl.ds((chunks - 1) * width, width)
        pl.when(home.is_middle())(functools.partial(home.pass_on, chunks - 1, last_chunk))
    keep_returned = pltpu.make_async_copy(returned, returned_out, local_sem.at[1])
    keep_returned.start()
    if dense:
        for kind in dense.kinds:
            dense.pass_pairs(kind)

    def finish(index, chunk):
        home.total(index, chunk, sum_ref)

    if not closing:
        over_chunks(chunks, width, finish)

    def drain(index, chunk):
        back.wait_send(index, chunk)
        if not closing:
            home.wait_send(index, chunk)

    over_chunks(chunks, width, drain)
    if dense:
        for kind in dense.kinds:
            dense.finish(kind)
    for kind in moving:
        moves[kind].wait_send()
    if closing:
        keep_mixed.wait()
    keep_slots.wait()
    keep_returned.wait()
    for keep in keeps:
        keep.wait()


class RowTotal:
    def __init__(self, rows, blocks, landed, own, sems):
        self.rows = rows
        self.blocks = blocks
        self.landed = landed
        self.own = own
        self.remote_sems = sems[:2]
        self.local_sem = sems[2]

    def out(self, step):
        place = self.rows.ahead(step)
        return send_to(
            self.blocks.at[place],
            self.landed.at[step - 1],
            self.remote_sems,
            step - 1,
            self.rows.device_of(place),
        )

    def load(self):
        return pltpu.make_async_copy(self.blocks.at[self.rows.place], self.own, self.local_sem)

    def start(self):
        self.load().start()
        for step in range(1, self.rows.count):
            self.out(step).start()

    def finish(self, out):
        self.load().wait()
        total = self.own[...].astype(jnp.float32)
        for step in range(1, self.rows.count):
            self.out(step).wait_recv()
            total = total + self.landed[step - 1].astype(jnp.float32)
        out[...] = total
        for step in range(1, self.rows.count):
            self.out(step).wait_send()


def moe_backward_kernel(dims, opening, dense_count, *refs):
    group_rows, col_count, copies, token_rows, slot_rows, chunks, width = dims
    own_ref, routes_ref, router_ref, gates_ref, normed_ref, slots_in, returned_in = refs[:7]
    weight_in = refs[7:10]
    refs = refs[10:]
    opening_in = refs[: 1 if opening else 0]
    refs = refs[len(opening_in) :]
    block_count, slice_width = weight_in[0].shape[:2]
    dense_in = refs[:dense_count]
    refs = refs[dense_count:]
    sum_ref, router_grad_ref, *grads_out = refs[: 2 + block_count]
    refs = refs[2 + block_count :]
    dense_out = refs[:dense_count]
    refs = refs[dense_count:]
    dense_scratch = refs[len(refs) - 5 * dense_count :]
    refs = refs[: len(refs) - 5 * dense_count]
    totals = [
        RowTotal(all_rows(block_count), blocks, *dense_scratch[5 * n : 5 * n + 2], dense_scratch[5 * n + 2 : 5 * n + 5])
        for n, blocks in enumerate(dense_in)
    ]
    opening_out = refs[: len(opening_in)]
    refs = refs[len(opening_in) :]
    opening_scratch = ()
    if opening:
        opening_scratch = refs[-3:]
        refs = refs[:-3]
    (
        place,
        place_t,
        gate,
        up,
        down,
        tokens,
        send,
        slots,
        slope,
        silu,
        act,
        weight,
        inner,
        received,
        grad_act,
        grad_gate,
        grad_up,
        returned,
        turned,
        staged,
        landed,
        pair_send,
        pair_landed,
        own_send,
        pass_send,
        row_recv,
        there_send,
        there_recv,
        back_send,
        back_recv,
        home_send,
        home_recv,
        pair_send_sem,
        pair_recv_sem,
        local_sem,
    ) = refs
    all_tokens = group_rows * token_rows
    all_slots = col_count * slot_rows
    slot_step = split_rows(all_slots, 320)
    rows, cols = expert_peers(col_count, copies, group_rows)

    def token_part(place):
        return pl.ds(pl.multiple_of(place * token_rows, token_rows), token_rows)

    def slot_part(place):
        return pl.ds(pl.multiple_of(place * slot_rows, slot_rows), slot_rows)

    gather = LineGather(rows, own_ref, tokens, token_part, (own_send, pass_send, row_recv))
    there = Exchange(
        cols,
        there_send,
        there_recv,
        lambda place, chunk: send.at[slot_part(place), chunk],
        lambda place, step, chunk: received.at[slot_part(place), chunk],
    )
    back = Exchange(
        cols,
        back_send,
        back_recv,
        lambda place, chunk: send.at[slot_part(place), chunk],
        lambda place, step, chunk: returned.at[slot_part(place), chunk],
    )
    home = LineSum(rows, tokens, token_part, landed, (home_send, home_recv))
    before = None
    if opening:
        before = LineSum(rows, tokens, token_part, opening_scratch[0], opening_scratch[1:])
    pair = Exchange(
        rows,
        pair_send_sem,
        pair_recv_sem,
        lambda place, chunk: pair_send.at[token_part(place), :],
        lambda place, step, chunk: pair_landed.at[step - 1],
    )
    greet((all_rows(block_count), cols))
    for index in range(min(2, chunks)):
        gather.start_own(index, pl.ds(index * width, width))
    load_returned = pltpu.make_async_copy(returned_in, returned, local_sem.at[1])
    load_returned.start()
    load_slots = pltpu.make_async_copy(slots_in, slots, local_sem.at[0])
    load_slots.start()
    weights = (gate, up, down)
    loads = [
        pltpu.make_async_copy(weight_in[kind], weights[kind], local_sem.at[4 + kind])
        for kind in range(3)
    ]
    for copy in loads:
        copy.start()

    def weight_part(kind, chunk):
        return weights[kind][:, :, chunk].reshape(block_count * slice_width, width)

    tokens[token_part(rows.place), :] = own_ref[...]
    build_places(dims, rows, routes_ref, place, place_t, None)

    def recompute(part):
        gate_val = dot_nt(slots[part, :], gate[...].reshape(-1, gate.shape[2]))
        up_val = dot_nt(slots[part, :], up[...].reshape(-1, up.shape[2]))
        sigmoid = jax.nn.sigmoid(gate_val)
        value = gate_val * sigmoid
        act[part, :] = (value * up_val).astype(jnp.bfloat16)
        silu[part, :] = value.astype(jnp.bfloat16)
        slope[part, :] = (up_val * sigmoid * (1.0 + gate_val * (1.0 - sigmoid))).astype(
            jnp.bfloat16
        )

    def slot_gates(part):
        picked = dot_nn(place[part, :], gates_ref[...].astype(jnp.bfloat16))
        block = iota(picked.shape, 1)
        slot = iota(picked.shape, 0) + part.start
        in_block = (slot >= block * slot_rows) & (slot < (block + 1) * slot_rows)
        weight[part, :] = jnp.sum(jnp.where(in_block, picked, 0.0), axis=1, keepdims=True)

    def recompute_all():
        load_slots.wait()
        for copy in loads:
            copy.wait()
        over_blocks(all_slots, slot_step, recompute)

    over_blocks(all_slots, slot_step, slot_gates)
    recompute_all()
    load_returned.wait()

    def dispatch(index, chunk):
        gather.arrive(index, chunk)

        @pl.when(index + 2 < chunks)
        def _():
            later = pl.ds(pl.multiple_of((index + 2) * width, width), width)
            gather.start_own(index + 2, later)


        def rows_of(part):
            grad = dot_nn(place[part, :], tokens[:, chunk])
            share = jnp.sum(
                grad * returned[part, chunk].astype(jnp.float32), axis=1, keepdims=True
            )
            send[part, chunk] = (weight[part, :] * grad).astype(jnp.bfloat16)

            @pl.when(index == 0)
            def _():
                inner[part, :] = share

            @pl.when(index > 0)
            def _():
                inner[part, :] += share

        over_blocks(all_slots, all_slots, rows_of)
        there.start(index, chunk)
        received[slot_part(cols.place), chunk] = send[slot_part(cols.place), chunk]

    over_chunks(chunks, width, dispatch)
    for total in totals:
        total.start()

    def pairs(part):
        picked = slot_block((all_slots, pair_send.shape[1]), 0, slot_rows)
        spread = jnp.where(picked, inner[...], 0.0)
        high = spread.astype(jnp.bfloat16)
        low = (spread - high.astype(jnp.float32)).astype(jnp.bfloat16)
        pair_send[part, :] = dot_nn(place_t[part, :], high) + dot_nn(place_t[part, :], low)

    over_chunks(chunks, width, gather.wait_send)
    if before:
        load_mixed = pltpu.make_async_copy(opening_in[0], tokens, local_sem.at[7])
        load_mixed.start()
    over_blocks(all_tokens, token_rows, pairs)
    pair.start(0, None)
    if before:
        load_mixed.wait()

        @pl.when(~before.is_middle())
        def _():
            over_chunks(chunks, width, before.pass_on)


    def project(index, chunk):
        there.wait_recv(index, chunk)

        def rows_of(part):
            grad = dot_nt(received[part, chunk], weight_part(2, chunk))

            @pl.when(index == 0)
            def _():
                grad_act[part, :] = grad

            @pl.when(index > 0)
            def _():
                grad_act[part, :] += grad

        over_blocks(all_slots, all_slots, rows_of)

    over_chunks(chunks, width, project)

    def slopes(part):
        grad = grad_act[part, :]
        grad_gate[part, :] = (grad * slope[part, :].astype(jnp.float32)).astype(jnp.bfloat16)
        grad_up[part, :] = (grad * silu[part, :].astype(jnp.float32)).astype(jnp.bfloat16)

    over_blocks(all_slots, slot_step, slopes)

    def give_back(index, chunk):
        there.wait_send(index, chunk)

        def rows_of(part):
            send[part, chunk] = (
                dot_nn(grad_gate[part, :], weight_part(0, chunk))
                + dot_nn(grad_up[part, :], weight_part(1, chunk))
            ).astype(jnp.bfloat16)

        over_blocks(all_slots, all_slots, rows_of)
        back.start(index, chunk)

    over_chunks(chunks, width, give_back)

    returned[slot_part(cols.place), :] = send[slot_part(cols.place), :]
    if before:

        @pl.when(before.is_middle())
        def _():
            over_chunks(chunks, width, before.pass_on)

        over_chunks(
            chunks, width, lambda index, chunk: before.total(index, chunk, opening_out[0])
        )
        over_chunks(chunks, width, before.wait_send)

    def combine(index, chunk):
        back.wait_recv(index, chunk)

        def rows_of(part):
            tokens[part, chunk] = dot_nn(place_t[part, :], returned[:, chunk]).astype(jnp.bfloat16)

        over_blocks(all_tokens, token_rows, rows_of)
        pl.when(~home.is_middle())(functools.partial(home.pass_on, index, chunk))

        @pl.when(home.is_middle() & (index > 0))
        def _():
            before = pl.ds(pl.multiple_of((index - 1) * width, width), width)
            home.pass_on(index - 1, before)

    over_chunks(chunks, width, combine)
    last_chunk = pl.ds((chunks - 1) * width, width)
    pl.when(home.is_middle())(functools.partial(home.pass_on, chunks - 1, last_chunk))
    def keep(kind, index):
        return pltpu.make_async_copy(
            staged.at[index % 2], grads_out[index].at[kind], local_sem.at[2 + index % 2]
        )

    for kind, (left, right) in enumerate(((grad_gate, slots), (grad_up, slots), (act, received))):
        turned[...] = left[...].T
        for index in range(block_count):
            if index >= 2:
                keep(kind, index - 2).wait()
            part = slice(index * slice_width, (index + 1) * slice_width)
            staged[index % 2] = dot_nn(turned[part, :], right[...]).astype(jnp.bfloat16)
            keep(kind, index).start()
        for index in range(max(block_count - 2, 0), block_count):
            keep(kind, index).wait()

    pair.wait_recv(0, None)
    grad_pair = pair_send[token_part(rows.place), :]
    for ahead in range(1, group_rows):
        shifted = pltpu.roll(pair_landed[group_rows - ahead - 1], ahead * col_count, 1)
        grad_pair = grad_pair + shifted
    grad_pair = grad_pair[:, :E]
    gates = gates_ref[token_part(rows.place), :]
    grad_logits = gates * (grad_pair - jnp.sum(gates * grad_pair, axis=-1, keepdims=True))
    grad_logits = grad_logits.astype(jnp.bfloat16)
    router_grad_ref[...] = dot_nn(grad_logits.astype(jnp.float32).T.astype(jnp.bfloat16), normed_ref[...])

    def finish(index, chunk):
        home.total(index, chunk, sum_ref)
        sum_ref[:, chunk] += dot_nn(grad_logits, router_ref[:, chunk])

    over_chunks(chunks, width, finish)

    def drain(index, chunk):
        back.wait_send(index, chunk)
        home.wait_send(index, chunk)

    over_chunks(chunks, width, drain)
    pair.wait_send(0, None)
    for total, out in zip(totals, dense_out):
        total.finish(out)


def moe_forward(
    dims, row_count, layer, own, routes, router, weights, moving, next_blocks, closing
):
    group_rows, col_count, copies, token_rows, slot_rows, chunks, width = dims
    all_tokens, all_slots = group_rows * token_rows, col_count * slot_rows
    model_width = own.shape[1]
    slice_width = weights[0].shape[-2]
    hidden = row_count * slice_width
    gather_dims = (row_count, col_count // 2) if next_blocks else None
    dense_sems = DenseGather.sems(gather_dims, 2) if next_blocks else []
    vmem = pl.BlockSpec(memory_space=pltpu.VMEM)
    outside = pl.BlockSpec(memory_space=pl.ANY)
    every_row = jax.ShapeDtypeStruct((all_tokens, model_width), jnp.bfloat16)
    slot_array = pltpu.VMEM((all_slots, model_width), jnp.bfloat16)
    hidden_wide = pltpu.VMEM((all_slots, hidden), jnp.float32)
    weight_array = pltpu.VMEM((row_count, slice_width, model_width), jnp.bfloat16)
    return pl.pallas_call(
        functools.partial(
            moe_forward_kernel, dims, row_count, layer, moving, gather_dims, closing
        ),
        out_shape=(
            every_row if closing else jax.ShapeDtypeStruct((token_rows, model_width), jnp.float32),
            jax.ShapeDtypeStruct((all_tokens, E), jnp.float32),
            jax.ShapeDtypeStruct((all_slots, model_width), jnp.bfloat16),
            jax.ShapeDtypeStruct((all_slots, model_width), jnp.bfloat16),
            *(moved_shape(row_count, weights[kind]) for kind in moving),
            *(gathered_shapes(gather_dims, next_blocks) if next_blocks else ()),
        ),
        in_specs=[vmem] * 3 + [outside] * (3 + len(next_blocks)),
        out_specs=(outside if closing else vmem, vmem)
        + (outside,) * (2 + len(moving) + len(next_blocks)),
        scratch_shapes=[
            pltpu.VMEM((all_slots, all_tokens), jnp.bfloat16),
            pltpu.VMEM((all_tokens, all_slots), jnp.bfloat16),
            pltpu.VMEM((all_tokens, E), jnp.float32),
            weight_array,
            weight_array,
            weight_array,
            pltpu.VMEM((all_tokens, model_width), jnp.bfloat16),
            slot_array,
            slot_array,
            hidden_wide,
            hidden_wide,
            pltpu.VMEM((all_slots, hidden), jnp.bfloat16),
            slot_array,
            pltpu.VMEM((group_rows + 1, token_rows, model_width), jnp.bfloat16),
            *LineGather.sems(chunks, group_rows),
            *exchange_sems(chunks, col_count),
            *exchange_sems(chunks, col_count),
            *LineSum.sems(chunks, group_rows),
            pltpu.SemaphoreType.DMA((6,)),
            *(
                sem
                for kind in moving
                for sem in WeightMove.sems(row_count, chunks if kind == 2 else 1)
            ),
            *dense_sems,
        ],
        compiler_params=pltpu.CompilerParams(
            collective_id=1 + 7 * layer, has_side_effects=True, vmem_limit_bytes=vmem_most
        ),
        cost_estimate=no_cost,
        name="moe_forward",
    )(own, routes, router, *weights, *next_blocks)


def moe_backward(dims, own, routes, router, gates, normed, slots, returned, weights, opening, dense):
    group_rows, col_count, copies, token_rows, slot_rows, chunks, width = dims
    all_tokens, all_slots = group_rows * token_rows, col_count * slot_rows
    model_width = own.shape[1]
    opened = len(opening)
    block_count, slice_width = weights[0].shape[:2]
    grads = jax.ShapeDtypeStruct((3, slice_width, model_width), jnp.bfloat16)
    hidden = block_count * slice_width
    vmem = pl.BlockSpec(memory_space=pltpu.VMEM)
    outside = pl.BlockSpec(memory_space=pl.ANY)
    slot_array = pltpu.VMEM((all_slots, model_width), jnp.bfloat16)
    hidden_narrow = pltpu.VMEM((all_slots, hidden), jnp.bfloat16)
    weight_array = pltpu.VMEM((block_count, slice_width, model_width), jnp.bfloat16)
    return pl.pallas_call(
        functools.partial(moe_backward_kernel, dims, bool(opening), len(dense)),
        out_shape=(
            jax.ShapeDtypeStruct((token_rows, model_width), jnp.float32),
            jax.ShapeDtypeStruct((E, model_width), jnp.float32),
            *([grads] * block_count),
            *(jax.ShapeDtypeStruct(block.shape[1:], jnp.float32) for block in dense),
            *([jax.ShapeDtypeStruct((token_rows, model_width), jnp.float32)] * opened),
        ),
        in_specs=[vmem] * 5
        + [outside] * (5 + opened + len(dense)),
        out_specs=(vmem, vmem)
        + (outside,) * block_count
        + (vmem,) * (len(dense) + opened),
        scratch_shapes=[
            pltpu.VMEM((all_slots, all_tokens), jnp.bfloat16),
            pltpu.VMEM((all_tokens, all_slots), jnp.bfloat16),
            weight_array,
            weight_array,
            weight_array,
            pltpu.VMEM((all_tokens, model_width), jnp.bfloat16),
            slot_array,
            slot_array,
            hidden_narrow,
            hidden_narrow,
            hidden_narrow,
            pltpu.VMEM((all_slots, 1), jnp.float32),
            pltpu.VMEM((all_slots, 1), jnp.float32),
            slot_array,
            pltpu.VMEM((all_slots, hidden), jnp.float32),
            hidden_narrow,
            hidden_narrow,
            slot_array,
            pltpu.VMEM((hidden, all_slots), jnp.bfloat16),
            pltpu.VMEM((2, slice_width, model_width), jnp.bfloat16),
            pltpu.VMEM((group_rows + 1, token_rows, model_width), jnp.bfloat16),
            pltpu.VMEM((all_tokens, 128), jnp.float32),
            pltpu.VMEM((max(group_rows - 1, 1), token_rows, 128), jnp.float32),
            *LineGather.sems(chunks, group_rows),
            *exchange_sems(chunks, col_count),
            *exchange_sems(chunks, col_count),
            *LineSum.sems(chunks, group_rows),
            *exchange_sems(1, group_rows),
            pltpu.SemaphoreType.DMA((8,)),
            *(
                (
                    pltpu.VMEM((group_rows + 1, token_rows, model_width), jnp.bfloat16),
                    *LineSum.sems(chunks, group_rows),
                )
                if opening
                else ()
            ),
            *(
                item
                for block in dense
                for item in (
                    pltpu.VMEM((max(block_count - 1, 1), *block.shape[1:]), jnp.bfloat16),
                    pltpu.VMEM(block.shape[1:], jnp.bfloat16),
                    *line_sems(block_count),
                )
            ),
        ],
        compiler_params=pltpu.CompilerParams(
            collective_id=(9 if opening else 2) + (10 if dense else 0), has_side_effects=True, vmem_limit_bytes=vmem_most
        ),
        cost_estimate=no_cost,
        name="moe_backward",
    )(own, routes, router, gates, normed, slots, returned, *weights, *opening, *dense)


def col_pairs():
    col_index = lax.axis_index("col")
    return col_index // 2, lax.rem(col_index, 2)


def dense_peers(row_count, pair_count):
    row_index = lax.axis_index("row")
    pair, side = col_pairs()
    rows = Peers(row_count, row_index, lambda place: {"row": place})
    pairs = Peers(pair_count, pair, lambda place: {"col": place * 2 + side})
    sides = Peers(2, side, lambda place: {"col": pair * 2 + place})
    return rows, pairs, sides


def reduce_dense_kernel(
    dims,
    normed_ref,
    grad_proj_ref,
    grad_mid_ref,
    attended_ref,
    small_ref,
    *refs,
):
    row_count, pair_count, to_rows = dims
    outputs = refs[:3]
    scratch = refs[3:]
    kinds = 3
    buffers = [scratch[6 * kind : 6 * kind + 6] for kind in range(kinds)]
    sems = scratch[6 * kinds : 12 * kinds]
    normed_t, grad_proj, grad_mid_t, attended = scratch[12 * kinds :]
    side_sems = [(sems[6 * kind], sems[6 * kind + 1]) for kind in range(kinds)]
    pair_sems = [(sems[6 * kind + 2], sems[6 * kind + 3]) for kind in range(kinds)]
    row_sems = [(sems[6 * kind + 4], sems[6 * kind + 5]) for kind in range(kinds)]
    rows, pairs, sides = dense_peers(row_count, pair_count)
    other = 1 - sides.place

    def spread(target, source, turn):
        count = target.shape[0]
        size = source.shape[1] // count
        for index in range(count):
            part = source[:, index * size : (index + 1) * size]
            target[index] = part.T if turn else part

    spread(normed_t, normed_ref, True)
    spread(grad_proj, grad_proj_ref, False)
    spread(grad_mid_t, grad_mid_ref, True)
    spread(attended, attended_ref, False)

    def block(kind, row, pair, side):
        col = pair * 2 + side
        if kind == 0:
            return dot_nn(normed_t[row], grad_proj[col])
        if kind == 1:
            return dot_nn(grad_mid_t[col], attended[row])
        return small_ref[col, row].astype(jnp.float32)

    greet((rows, pairs, sides) if to_rows else (pairs, sides))

    def side_copy(kind, pair):
        side_send, side_recv = buffers[kind][0], buffers[kind][1]
        return send_to(
            side_send.at[pair],
            side_recv.at[pair],
            side_sems[kind],
            pair,
            sides.device_of(other),
        )

    def pair_copy(kind, step, row):
        place = pairs.ahead(step)
        half, pair_recv = buffers[kind][2], buffers[kind][3]
        return send_to(
            half.at[place, row],
            pair_recv.at[step - 1, row],
            pair_sems[kind],
            (step - 1) * row_count + row,
            pairs.device_of(place),
        )

    def row_copy(kind, step):
        place = rows.ahead(step)
        whole, row_recv = buffers[kind][4], buffers[kind][5]
        return send_to(
            whole.at[place],
            row_recv.at[step - 1],
            row_sems[kind],
            step - 1,
            rows.device_of(place),
        )

    def first(step, carry):
        pair = lax.rem(pairs.place + step, pair_count)
        for kind in range(kinds):
            for row in range(row_count):
                buffers[kind][0][pair, row] = block(kind, row, pair, other).astype(jnp.bfloat16)
            side_copy(kind, pair).start()
        return carry

    lax.fori_loop(1, pair_count + 1, first, 0)

    def second(step, carry):
        pair = lax.rem(pairs.place + step, pair_count)
        for kind in range(kinds):
            side_copy(kind, pair).wait_recv()
            side_recv, half = buffers[kind][1], buffers[kind][2]
            for row in range(row_count):
                total = block(kind, row, pair, sides.place)
                total = total + side_recv[pair, row].astype(jnp.float32)
                half[pair, row] = total.astype(jnp.bfloat16)

                @pl.when(step < pair_count)
                def _():
                    pair_copy(kind, step, row).start()

        return carry

    lax.fori_loop(1, pair_count + 1, second, 0)

    def third(step, carry):
        row = lax.rem(rows.place + step, row_count)
        for kind in range(kinds):
            half, pair_recv, whole = buffers[kind][2], buffers[kind][3], buffers[kind][4]
            total = half[pairs.place, row].astype(jnp.float32)
            for ahead in range(1, pair_count):
                pair_copy(kind, ahead, row).wait_recv()
                total = total + pair_recv[ahead - 1, row].astype(jnp.float32)

            if not to_rows:
                outputs[kind][row] = total.astype(jnp.bfloat16)
                continue

            whole[row] = total.astype(jnp.bfloat16)

            @pl.when(step < row_count)
            def _():
                row_copy(kind, step).start()

        return carry

    lax.fori_loop(1, row_count + 1, third, 0)
    for kind in range(kinds if to_rows else 0):
        whole, row_recv = buffers[kind][4], buffers[kind][5]
        total = whole[rows.place].astype(jnp.float32)
        for step in range(1, row_count):
            row_copy(kind, step).wait_recv()
            total = total + row_recv[step - 1].astype(jnp.float32)
        outputs[kind][...] = total

    def drain_sides(pair, carry):
        for kind in range(kinds):
            side_copy(kind, pair).wait_send()
        return carry

    lax.fori_loop(0, pair_count, drain_sides, 0)

    def drain_pairs(step, carry):
        for kind in range(kinds):
            for row in range(row_count):
                pair_copy(kind, step, row).wait_send()
        return carry

    lax.fori_loop(1, pair_count, drain_pairs, 0)
    for kind in range(kinds if to_rows else 0):
        for step in range(1, row_count):
            row_copy(kind, step).wait_send()


def order_scratch(slice_width, model_width):
    return [
        pltpu.VMEM((4, slice_width, model_width), jnp.bfloat16),
        pltpu.VMEM((4, slice_width, model_width), jnp.float32),
        pltpu.SemaphoreType.DMA((4,)),
        pltpu.SemaphoreType.DMA((4,)),
    ]


def ordered_shapes(layer_count, blocks):
    _, slice_width, model_width = blocks[0].shape
    shape = (layer_count, len(blocks), slice_width, model_width)
    return (jax.ShapeDtypeStruct(shape, jnp.float32),) * 3


def reduce_dense(
    row_count, col_count, normed, grad_projected, grad_mid_b, attended, small, to_rows
):
    token_rows, model_width = normed.shape
    qkv_width, out_rows = grad_projected.shape[1], attended.shape[1]
    pair_count = col_count // 2
    shapes = (
        (model_width // row_count, qkv_width // col_count),
        (model_width // col_count, out_rows // row_count),
        small.shape[2:],
    )
    vmem = pl.BlockSpec(memory_space=pltpu.VMEM)
    scratch = []
    sems = []
    for height, breadth in shapes:
        for lead in (
            (pair_count, row_count),
            (pair_count, row_count),
            (pair_count, row_count),
            (max(pair_count - 1, 1), row_count),
            (row_count,),
            (max(row_count - 1, 1),),
        ):
            scratch.append(pltpu.VMEM((*lead, height, breadth), jnp.bfloat16))
        for count in (pair_count, max(pair_count - 1, 1) * row_count, max(row_count - 1, 1)):
            sems.extend([pltpu.SemaphoreType.DMA((count,))] * 2)
    operands = [
        pltpu.VMEM((row_count, shapes[0][0], token_rows), jnp.bfloat16),
        pltpu.VMEM((col_count, token_rows, shapes[0][1]), jnp.bfloat16),
        pltpu.VMEM((col_count, shapes[1][0], token_rows), jnp.bfloat16),
        pltpu.VMEM((row_count, token_rows, shapes[1][1]), jnp.bfloat16),
    ]
    return pl.pallas_call(
        functools.partial(
            reduce_dense_kernel,
            (row_count, pair_count, to_rows),
        ),
        out_shape=tuple(
            jax.ShapeDtypeStruct(shape, jnp.float32)
            if to_rows
            else jax.ShapeDtypeStruct((row_count, *shape), jnp.bfloat16)
            for shape in shapes
        ),
        in_specs=[vmem] * 5,
        out_specs=(vmem,) * 3,
        scratch_shapes=scratch + sems + operands,
        compiler_params=pltpu.CompilerParams(
            collective_id=3 if to_rows else 11, has_side_effects=True, vmem_limit_bytes=vmem_most
        ),
        cost_estimate=no_cost,
        name="reduce_dense",
    )(
        normed,
        grad_projected,
        grad_mid_b,
        attended,
        small,
    )


class DenseGather:
    def __init__(self, dims, own_blocks, fulls, sems):
        self.row_count, self.pair_count = dims
        self.rows, self.pairs, self.sides = dense_peers(*dims)
        self.own_blocks = own_blocks
        self.fulls = fulls
        self.kinds = range(len(own_blocks))
        self.row_sems = [sems[6 * kind : 6 * kind + 2] for kind in self.kinds]
        self.pair_sems = [sems[6 * kind + 2 : 6 * kind + 4] for kind in self.kinds]
        self.side_sems = [sems[6 * kind + 4 : 6 * kind + 6] for kind in self.kinds]
        self.local_sems = sems[6 * len(own_blocks)]

    @staticmethod
    def sems(dims, kinds):
        row_count, pair_count = dims
        sems = []
        for _ in range(kinds):
            for count in (
                max(row_count - 1, 1),
                max(pair_count - 1, 1) * row_count,
                pair_count * row_count,
            ):
                sems.extend([pltpu.SemaphoreType.DMA((count,))] * 2)
        return sems + [pltpu.SemaphoreType.DMA((kinds,))]

    def groups(self):
        return (self.rows, self.pairs, self.sides)

    def spot(self, kind, row, pair, side):
        col = pair * 2 + side
        height = self.own_blocks[kind].shape[0]
        return self.fulls[kind].at[row, pl.ds(pl.multiple_of(col * height, height), height), :]

    def own_spot(self, kind):
        return self.spot(kind, self.rows.place, self.pairs.place, self.sides.place)

    def own_copy(self, kind):
        return pltpu.make_async_copy(
            self.own_blocks[kind], self.own_spot(kind), self.local_sems.at[kind]
        )

    def row_copy(self, kind, step):
        return send_to(
            self.own_blocks[kind],
            self.own_spot(kind),
            self.row_sems[kind],
            step - 1,
            self.rows.device_of(self.rows.ahead(step)),
        )

    def row_landed(self, kind, step):
        place = self.rows.behind(step)
        landed = self.spot(kind, place, self.pairs.place, self.sides.place)
        return send_to(
            landed, landed, self.row_sems[kind], step - 1, self.rows.device_of(place)
        )

    def pair_copy(self, kind, step, number):
        block = self.spot(kind, self.rows.behind(number), self.pairs.place, self.sides.place)
        return send_to(
            block if number else self.own_blocks[kind],
            block,
            self.pair_sems[kind],
            (step - 1) * self.row_count + number,
            self.pairs.device_of(self.pairs.ahead(step)),
        )

    def pair_landed(self, kind, step, number):
        place = self.pairs.behind(step)
        landed = self.spot(kind, self.rows.behind(number), place, self.sides.place)
        return send_to(
            landed,
            landed,
            self.pair_sems[kind],
            (step - 1) * self.row_count + number,
            self.pairs.device_of(place),
        )

    def side_copy(self, kind, step, number):
        place = self.pairs.behind(step)
        block = self.spot(kind, self.rows.behind(number), place, self.sides.place)
        return send_to(
            block if step or number else self.own_blocks[kind],
            block,
            self.side_sems[kind],
            step * self.row_count + number,
            self.sides.device_of(1 - self.sides.place),
        )

    def side_landed(self, kind, step, number):
        place = self.pairs.behind(step)
        landed = self.spot(kind, self.rows.behind(number), place, 1 - self.sides.place)
        return send_to(
            landed,
            landed,
            self.side_sems[kind],
            step * self.row_count + number,
            self.sides.device_of(1 - self.sides.place),
        )

    def start(self, kind):
        self.own_copy(kind).start()
        for step in range(1, self.row_count):
            self.row_copy(kind, step).start()
        for step in range(1, self.pair_count):
            self.pair_copy(kind, step, 0).start()
        self.side_copy(kind, 0, 0).start()

    def pass_rows(self, kind):
        for number in range(1, self.row_count):
            self.row_landed(kind, number).wait_recv()
            for step in range(1, self.pair_count):
                self.pair_copy(kind, step, number).start()
            self.side_copy(kind, 0, number).start()

    def pass_pairs(self, kind):
        for number in range(self.row_count):
            for step in range(1, self.pair_count):
                self.pair_landed(kind, step, number).wait_recv()
                self.side_copy(kind, step, number).start()

    def finish(self, kind):
        self.own_copy(kind).wait()
        for step in range(self.pair_count):
            for number in range(self.row_count):
                self.side_landed(kind, step, number).wait_recv()
        for step in range(1, self.row_count):
            self.row_copy(kind, step).wait_send()
        for number in range(self.row_count):
            for step in range(1, self.pair_count):
                self.pair_copy(kind, step, number).wait_send()
            for step in range(self.pair_count):
                self.side_copy(kind, step, number).wait_send()


def gathered_shapes(dims, blocks):
    row_count, pair_count = dims
    return tuple(
        jax.ShapeDtypeStruct(
            (row_count, 2 * pair_count * block.shape[0], block.shape[1]), block.dtype
        )
        for block in blocks
    )


def gather_dense_kernel(
    dims,
    copies,
    qkv_ref,
    out_ref,
    routes_ref,
    router_ref,
    shards_ref,
    qkv_full,
    out_full,
    routes_all,
    router_all,
    moved,
    *sems,
):
    gather = DenseGather(dims, (qkv_ref, out_ref), (qkv_full, out_full), sems[:13])
    small_send, small_recv, local_sems = sems[13:16]
    rows = gather.rows
    move = WeightMove(rows, copies, 0, shards_ref, moved, sems[16:])
    small = [
        Exchange(
            rows,
            small_send,
            small_recv,
            lambda place, chunk, ref=ref: ref,
            lambda place, step, chunk, full=full: full.at[place],
        )
        for ref, full in ((routes_ref, routes_all), (router_ref, router_all))
    ]
    greet(gather.groups())
    own_copies = [
        pltpu.make_async_copy(ref, full.at[rows.place], local_sems.at[number])
        for number, (ref, full) in enumerate(((routes_ref, routes_all), (router_ref, router_all)))
    ]
    for kind in range(2):
        gather.start(kind)
        own_copies[kind].start()
        small[kind].start(kind, None)
    move.start()
    for kind in range(2):
        gather.pass_rows(kind)
    for kind in range(2):
        gather.pass_pairs(kind)
    for kind in range(2):
        small[kind].wait_recv(kind, None)
        gather.finish(kind)
        own_copies[kind].wait()
        small[kind].wait_send(kind, None)
    move.wait_recv()
    move.wait_send()


def gather_dense(row_count, col_count, copies, qkv_block, out_block, routes, router, shards):
    dims = (row_count, col_count // 2)
    outside = pl.BlockSpec(memory_space=pl.ANY)
    return pl.pallas_call(
        functools.partial(gather_dense_kernel, dims, copies),
        out_shape=gathered_shapes(dims, (qkv_block, out_block))
        + tuple(jax.ShapeDtypeStruct((row_count, *x.shape), x.dtype) for x in (routes, router))
        + (moved_shape(row_count, shards),),
        in_specs=[outside] * 5,
        out_specs=(outside,) * 5,
        scratch_shapes=DenseGather.sems(dims, 2)
        + [
            *exchange_sems(2, row_count),
            pltpu.SemaphoreType.DMA((2,)),
            *WeightMove.sems(row_count),
        ],
        compiler_params=pltpu.CompilerParams(collective_id=4, has_side_effects=True),
        cost_estimate=no_cost,
        name="gather_dense",
    )(qkv_block, out_block, routes, router, shards)


def order_layer(layer, blocks, outputs, came, wide, in_sems, out_sems):
    block_count = len(blocks)
    row_index = lax.axis_index("row")
    count = 3 * block_count

    def load(number):
        return pltpu.make_async_copy(
            blocks[number // 3].at[number % 3], came.at[number % 4], in_sems.at[number % 4]
        )

    def store(number):
        expert = lax.rem(row_index + number // 3, block_count)
        return pltpu.make_async_copy(
            wide.at[number % 4], outputs[number % 3].at[layer, expert], out_sems.at[number % 4]
        )

    for number in range(min(3, count)):
        load(number).start()
    for number in range(count):
        if number + 3 < count:
            load(number + 3).start()
        load(number).wait()
        if number >= 4:
            store(number - 4).wait()
        wide[number % 4] = came[number % 4].astype(jnp.float32)
        store(number).start()
    for number in range(max(count - 4, 0), count):
        store(number).wait()


def order_grads_kernel(block_count, layers, early, *refs):
    blocks = [refs[block_count * n : block_count * (n + 1)] for n in range(len(layers))]
    refs = refs[block_count * len(layers) + (3 if early else 0) :]
    for layer, group in zip(layers, blocks):
        order_layer(layer, group, refs[:3], *refs[3:])


def order_grads(layer_count, groups, early):
    blocks = [block for _, group in groups for block in group]
    block_count = len(groups[0][1])
    outside = pl.BlockSpec(memory_space=pl.ANY)
    return pl.pallas_call(
        functools.partial(
            order_grads_kernel, block_count, tuple(layer for layer, _ in groups), bool(early)
        ),
        out_shape=ordered_shapes(layer_count, groups[0][1]),
        in_specs=[outside] * (len(blocks) + len(early)),
        out_specs=(outside,) * 3,
        scratch_shapes=order_scratch(*blocks[0].shape[1:]),
        input_output_aliases={len(blocks) + n: n for n in range(len(early))},
        compiler_params=pltpu.CompilerParams(vmem_limit_bytes=vmem_most),
        cost_estimate=no_cost,
        name="order_grads",
    )(*blocks, *early)


def pieces_nt(left, weights_ref):
    pieces, _, size = weights_ref.shape
    total = None
    for index in range(pieces):
        part = dot_nt(left[:, index * size : (index + 1) * size], weights_ref[index])
        total = part if total is None else total + part
    return total


def rotate(values, cosine, sine):
    return values * cosine + pltpu.roll(values, HEAD_SIZE // 2, 1) * sine


def head_lanes(head):
    return slice(2 * head * HEAD_SIZE, 2 * (head + 1) * HEAD_SIZE)


def key_lanes(head):
    return slice(2 * head * HEAD_SIZE, (2 * head + 1) * HEAD_SIZE)


def value_lanes(head):
    return slice((2 * head + 1) * HEAD_SIZE, 2 * (head + 1) * HEAD_SIZE)


def seen_keys(token_rows):
    position = lax.axis_index("col") * token_rows + iota((1, token_rows), 1)
    return (position // BLOCK + 1) * BLOCK


def attend_forward_kernel(
    dims,
    x_ref,
    gain_attn_ref,
    gain_moe_ref,
    cosine_ref,
    sine_ref,
    qkv_ref,
    out_w_ref,
    shards_ref,
    mid_ref,
    normed_ref,
    q_ref,
    kv_out,
    attended_ref,
    lse_ref,
    normed_moe_ref,
    moved,
    kv_all,
    value_t,
    proj,
    send_sem,
    recv_sem,
    local_sem,
    *move_sems,
):
    col_count, row_count, copies, layer, score_scale = dims
    token_rows = x_ref.shape[0]
    group = QUERY_HEADS // KEY_VALUE_HEADS
    kv_width = KEY_VALUE_HEADS * HEAD_SIZE
    cols = col_peers(col_count)

    def part(place):
        return pl.ds(pl.multiple_of(place * token_rows, token_rows), token_rows)

    share = Exchange(
        cols,
        send_sem,
        recv_sem,
        lambda place, chunk: kv_all.at[part(cols.place), chunk],
        lambda place, step, chunk: kv_all.at[part(place), chunk],
    )
    move = WeightMove(all_rows(row_count), copies, layer, shards_ref, moved, move_sems)
    greet((cols, move.rows))
    move.start()
    x = x_ref[...]
    inverse = lax.rsqrt(jnp.mean(x * x, axis=-1, keepdims=True) + eps_norm)
    normed_ref[...] = (x * inverse * gain_attn_ref[...]).astype(jnp.bfloat16)
    proj[...] = pieces_nt(normed_ref[...], qkv_ref)
    own = part(cols.place)
    for head in range(KEY_VALUE_HEADS):
        start = QUERY_FEATURES + head * HEAD_SIZE
        turned = rotate(proj[:, start : start + HEAD_SIZE], cosine_ref[...], sine_ref[...])
        kv_all[own, key_lanes(head)] = turned.astype(jnp.bfloat16)
        start = start + kv_width
        kv_all[own, value_lanes(head)] = proj[:, start : start + HEAD_SIZE].astype(jnp.bfloat16)
        share.start(head, head_lanes(head))
    for head in range(QUERY_HEADS):
        lanes = slice(head * HEAD_SIZE, (head + 1) * HEAD_SIZE)
        q_ref[:, lanes] = rotate(proj[:, lanes], cosine_ref[...], sine_ref[...]).astype(
            jnp.bfloat16
        )
    seen = seen_keys(token_rows)
    for kv_head in range(KEY_VALUE_HEADS):
        share.wait_recv(kv_head, head_lanes(kv_head))
        value_t[...] = kv_all[:, value_lanes(kv_head)].T

        def head_step(step, carry, kv_head=kv_head):
            index = kv_head * group + step
            lanes = pl.ds(pl.multiple_of(index * HEAD_SIZE, HEAD_SIZE), HEAD_SIZE)
            scores = dot_nt(kv_all[:, key_lanes(kv_head)], q_ref[:, lanes]) * score_scale
            scores = jnp.where(iota(scores.shape, 0) < seen, scores, masked_score)
            peak = jnp.max(scores, axis=0, keepdims=True)
            exponent = jnp.exp(scores - peak)
            total = jnp.sum(exponent, axis=0, keepdims=True)
            attended = dot_nn(value_t[...], exponent.astype(jnp.bfloat16)) / total
            attended_ref[:, lanes] = attended.T.astype(jnp.bfloat16)
            lse_ref[index] = peak + jnp.log(total)
            return carry

        lax.fori_loop(0, group, head_step, 0)
    keep = pltpu.make_async_copy(kv_all, kv_out, local_sem)
    keep.start()
    mid = x_ref[...] + pieces_nt(attended_ref[...], out_w_ref)
    mid_ref[...] = mid
    inverse = lax.rsqrt(jnp.mean(mid * mid, axis=-1, keepdims=True) + eps_norm)
    normed_moe_ref[...] = (mid * inverse * gain_moe_ref[...]).astype(jnp.bfloat16)
    for head in range(KEY_VALUE_HEADS):
        share.wait_send(head, head_lanes(head))
    keep.wait()
    move.wait_recv()
    move.wait_send()


def attend_forward(
    col_count,
    row_count,
    copies,
    layer,
    x,
    gain_attn,
    gain_moe,
    cosine,
    sine,
    qkv_full,
    out_full,
    shards,
):
    token_rows, model_width = x.shape
    seq_rows = col_count * token_rows
    kv_width = KEY_VALUE_HEADS * HEAD_SIZE
    vmem = pl.BlockSpec(memory_space=pltpu.VMEM)
    outside = pl.BlockSpec(memory_space=pl.ANY)
    rows_b = jax.ShapeDtypeStruct((token_rows, model_width), jnp.bfloat16)
    heads_b = jax.ShapeDtypeStruct((token_rows, QUERY_FEATURES), jnp.bfloat16)
    return pl.pallas_call(
        functools.partial(
            attend_forward_kernel, (col_count, row_count, copies, layer, HEAD_SIZE ** (-0.5))
        ),
        out_shape=(
            jax.ShapeDtypeStruct((token_rows, model_width), jnp.float32),
            rows_b,
            heads_b,
            jax.ShapeDtypeStruct((seq_rows, 2 * kv_width), jnp.bfloat16),
            heads_b,
            jax.ShapeDtypeStruct((QUERY_HEADS, 1, token_rows), jnp.float32),
            rows_b,
            moved_shape(row_count, shards),
        ),
        in_specs=[vmem] * 7 + [outside],
        out_specs=(vmem, vmem, vmem, outside, vmem, vmem, vmem, outside),
        scratch_shapes=[
            pltpu.VMEM((seq_rows, 2 * kv_width), jnp.bfloat16),
            pltpu.VMEM((HEAD_SIZE, seq_rows), jnp.bfloat16),
            pltpu.VMEM((token_rows, QUERY_FEATURES + 2 * kv_width), jnp.float32),
            *exchange_sems(KEY_VALUE_HEADS, col_count),
            pltpu.SemaphoreType.DMA,
            *WeightMove.sems(row_count),
        ],
        compiler_params=pltpu.CompilerParams(
            collective_id=5 + 5 * layer, has_side_effects=True, vmem_limit_bytes=vmem_most
        ),
        cost_estimate=no_cost,
        name="attend_forward",
    )(x, gain_attn, gain_moe, cosine, sine, qkv_full, out_full, shards)


def norm_backward(values, gain, incoming):
    inverse = lax.rsqrt(jnp.mean(values * values, axis=-1, keepdims=True) + eps_norm)
    scaled = incoming * gain
    inner_mean = jnp.mean(scaled * values, axis=-1, keepdims=True)
    grad = inverse * scaled - values * (inverse * inverse * inverse) * inner_mean
    return grad, jnp.sum(incoming * values * inverse, axis=0, keepdims=True)


def attend_backward_kernel(
    dims,
    incoming_ref,
    grad_moe_ref,
    mid_ref,
    x_ref,
    gain_attn_ref,
    gain_moe_ref,
    cosine_ref,
    sine_ref,
    qkv_ref,
    out_w_ref,
    q_ref,
    kv_ref,
    attended_ref,
    lse_ref,
    grad_x_ref,
    grad_mid_ref,
    grad_proj_ref,
    grad_gain_attn_ref,
    grad_gain_moe_ref,
    grad_attended,
    key_t,
    key_sum,
    value_sum,
    grad_kv,
    landed,
    send_sem,
    recv_sem,
):
    col_count, score_scale = dims
    token_rows = x_ref.shape[0]
    group = QUERY_HEADS // KEY_VALUE_HEADS
    kv_width = KEY_VALUE_HEADS * HEAD_SIZE
    cols = col_peers(col_count)

    def part(place):
        return pl.ds(pl.multiple_of(place * token_rows, token_rows), token_rows)

    share = Exchange(
        cols,
        send_sem,
        recv_sem,
        lambda place, chunk: grad_kv.at[part(place), chunk],
        lambda place, step, chunk: landed.at[step - 1, :, chunk],
    )
    greet((cols,))
    grad, gain_sum = norm_backward(mid_ref[...], gain_moe_ref[...], grad_moe_ref[...])
    grad_gain_moe_ref[...] = gain_sum
    grad_x_ref[...] = incoming_ref[...] + grad
    grad_mid_ref[...] = grad_x_ref[...].astype(jnp.bfloat16)
    pieces, _, size = out_w_ref.shape
    for index in range(pieces):
        lanes = slice(index * size, (index + 1) * size)
        grad_attended[:, lanes] = dot_nn(grad_mid_ref[...], out_w_ref[index]).astype(jnp.bfloat16)
    seen = seen_keys(token_rows)
    for kv_head in range(KEY_VALUE_HEADS):
        key_t[...] = kv_ref[:, key_lanes(kv_head)].T
        key_sum[...] = jnp.zeros_like(key_sum)
        value_sum[...] = jnp.zeros_like(value_sum)

        def head_step(step, carry, kv_head=kv_head):
            index = kv_head * group + step
            lanes = pl.ds(pl.multiple_of(index * HEAD_SIZE, HEAD_SIZE), HEAD_SIZE)
            query = q_ref[:, lanes]
            grad_out = grad_attended[:, lanes]
            product = grad_out.astype(jnp.float32) * attended_ref[:, lanes].astype(jnp.float32)
            inner = jnp.sum(product.T, axis=0, keepdims=True)
            scores = dot_nt(kv_ref[:, key_lanes(kv_head)], query) * score_scale
            soft = jnp.where(
                iota(scores.shape, 0) < seen, jnp.exp(scores - lse_ref[index]), 0.0
            )
            grad_soft = dot_nt(kv_ref[:, value_lanes(kv_head)], grad_out)
            grad_scores = (soft * (grad_soft - inner)).astype(jnp.bfloat16)
            value_sum[...] += dot_nn(soft.astype(jnp.bfloat16), grad_out)
            key_sum[...] += dot_nn(grad_scores, query)
            grad_q = (dot_nn(key_t[...], grad_scores) * score_scale).T
            grad_q = rotate(grad_q, cosine_ref[...], -sine_ref[...])
            grad_proj_ref[:, lanes] = grad_q.astype(jnp.bfloat16)
            return carry

        lax.fori_loop(0, group, head_step, 0)
        grad_kv[:, key_lanes(kv_head)] = (key_sum[...] * score_scale).astype(jnp.bfloat16)
        grad_kv[:, value_lanes(kv_head)] = value_sum[...].astype(jnp.bfloat16)
        share.start(kv_head, head_lanes(kv_head))
    for head in range(KEY_VALUE_HEADS):
        share.wait_recv(head, head_lanes(head))
        total = grad_kv[part(cols.place), head_lanes(head)].astype(jnp.float32)
        for step in range(1, col_count):
            total = total + landed[step - 1, :, head_lanes(head)].astype(jnp.float32)
        start = QUERY_FEATURES + head * HEAD_SIZE
        grad_key = rotate(total[:, :HEAD_SIZE], cosine_ref[...], -sine_ref[...])
        grad_proj_ref[:, start : start + HEAD_SIZE] = grad_key.astype(jnp.bfloat16)
        start = start + kv_width
        grad_proj_ref[:, start : start + HEAD_SIZE] = total[:, HEAD_SIZE:].astype(jnp.bfloat16)
    pieces = qkv_ref.shape[0]
    grad_normed = [dot_nn(grad_proj_ref[...], qkv_ref[index]) for index in range(pieces)]
    grad_normed = jnp.concatenate(grad_normed, axis=1) if pieces > 1 else grad_normed[0]
    grad, gain_sum = norm_backward(x_ref[...], gain_attn_ref[...], grad_normed)
    grad_gain_attn_ref[...] = gain_sum
    grad_x_ref[...] += grad
    for head in range(KEY_VALUE_HEADS):
        share.wait_send(head, head_lanes(head))


def attend_backward(
    col_count,
    incoming,
    grad_moe,
    mid,
    x,
    gain_attn,
    gain_moe,
    cosine,
    sine,
    qkv_full,
    out_full,
    queries,
    key_value,
    attended,
    log_sums,
):
    token_rows, model_width = x.shape
    seq_rows = col_count * token_rows
    kv_width = KEY_VALUE_HEADS * HEAD_SIZE
    vmem = pl.BlockSpec(memory_space=pltpu.VMEM)
    gain = jax.ShapeDtypeStruct((1, model_width), jnp.float32)
    return pl.pallas_call(
        functools.partial(attend_backward_kernel, (col_count, HEAD_SIZE ** (-0.5))),
        out_shape=(
            jax.ShapeDtypeStruct((token_rows, model_width), jnp.float32),
            jax.ShapeDtypeStruct((token_rows, model_width), jnp.bfloat16),
            jax.ShapeDtypeStruct((token_rows, QUERY_FEATURES + 2 * kv_width), jnp.bfloat16),
            gain,
            gain,
        ),
        in_specs=[vmem] * 14,
        out_specs=(vmem,) * 5,
        scratch_shapes=[
            pltpu.VMEM((token_rows, QUERY_FEATURES), jnp.bfloat16),
            pltpu.VMEM((HEAD_SIZE, seq_rows), jnp.bfloat16),
            pltpu.VMEM((seq_rows, HEAD_SIZE), jnp.float32),
            pltpu.VMEM((seq_rows, HEAD_SIZE), jnp.float32),
            pltpu.VMEM((seq_rows, 2 * kv_width), jnp.bfloat16),
            pltpu.VMEM((max(col_count - 1, 1), token_rows, 2 * kv_width), jnp.bfloat16),
            *exchange_sems(KEY_VALUE_HEADS, col_count),
        ],
        compiler_params=pltpu.CompilerParams(
            collective_id=6, has_side_effects=True, vmem_limit_bytes=vmem_most
        ),
        cost_estimate=no_cost,
        name="attend_backward",
    )(
        incoming,
        grad_moe,
        mid,
        x,
        gain_attn,
        gain_moe,
        cosine,
        sine,
        qkv_full,
        out_full,
        queries,
        key_value,
        attended,
        log_sums,
    )


def place_first(values, group_rows, expert_pick):
    rolled = jnp.roll(values.reshape(-1, group_rows, values.shape[1]), -expert_pick, axis=1)
    return rolled.transpose(1, 0, 2).reshape(values.shape)


def place_back(values, group_rows, expert_pick):
    rolled = values.reshape(group_rows, -1, values.shape[1]).transpose(1, 0, 2)
    return jnp.roll(rolled, expert_pick, axis=1).reshape(values.shape)


def body(
    hidden_in, routes, norm_attn, w_qkv, w_out, norm_moe, w_router, w_gate, w_up, w_down, cotangent
):
    row_count = lax.axis_size("row")
    col_count = lax.axis_size("col")
    device_count = row_count * col_count
    row_index = lax.axis_index("row")
    col_index = lax.axis_index("col")
    layer_count = w_qkv.shape[0]
    token_rows = hidden_in.shape[0]
    model_width = hidden_in.shape[1]
    local_experts = w_gate.shape[1]
    slice_width = w_gate.shape[3]
    copies = row_count // local_experts
    expert_pick = row_index // copies
    slot_rows = -(-local_experts * CAP // 16) * 16
    chunks = model_width // 384
    dims = (
        local_experts,
        col_count,
        copies,
        token_rows,
        slot_rows,
        chunks,
        model_width // chunks,
    )
    positions = col_index * token_rows + jnp.arange(token_rows, dtype=jnp.int32)
    cosine, sine = rope_angles(positions, HEAD_SIZE // 2)
    cosine = jnp.concatenate([cosine, cosine], axis=1)
    sine = jnp.concatenate([-sine, sine], axis=1)

    def move_grads(grads):
        blocks = [grads[0]]
        for step in range(1, row_count):
            pairs = [(index, (index - step) % row_count) for index in range(row_count)]
            blocks.append(lax.ppermute(grads[step], "row", pairs))
        return tuple(blocks)

    def own_grads(blocks):
        ordered = jnp.roll(jnp.stack(blocks), row_index, axis=0).astype(wide_type)
        return jnp.sum(ordered.reshape(local_experts, copies, *blocks[0].shape), axis=1)

    def pieced(full):
        if full.shape[2] % 128 == 0:
            return full
        return full.transpose(1, 0, 2).reshape(1, full.shape[1], -1)

    def packed(values):
        return jnp.pad(values.reshape(-1), (0, -values.size % 2048)).reshape(-1, 128)

    shards = (w_gate.transpose(0, 1, 3, 2), w_up.transpose(0, 1, 3, 2), w_down)
    experts = []
    route_lines = routes.transpose(0, 2, 1)
    router_lines = w_router.transpose(0, 2, 1)
    qkv_full, out_full, routes_all, router_all, moved_gate = gather_dense(
        row_count,
        col_count,
        copies,
        w_qkv[0].T,
        w_out[0].T,
        packed(route_lines),
        packed(router_lines),
        shards[0],
    )
    dense = [(pieced(qkv_full), pieced(out_full))]
    routes_all = routes_all.reshape(row_count, -1)[:, : route_lines.size]
    routes_all = routes_all.reshape(row_count, *route_lines.shape)
    if copies > 1:
        routes_all = jnp.take(
            routes_all, row_index % copies + copies * jnp.arange(local_experts), axis=0
        )
    router_all = router_all.reshape(row_count, -1)[:, : router_lines.size]
    router_all = router_all.reshape(row_count, *router_lines.shape)
    router_all = router_all.transpose(1, 2, 0, 3).reshape(layer_count, E, model_width)
    routers = [
        place_first(router_all[index], local_experts, expert_pick) for index in range(layer_count)
    ]
    gains_attn = norm_attn.astype(wide_type)[:, None, :]
    gains_moe = norm_moe.astype(wide_type)[:, None, :]
    hidden = hidden_in.astype(wide_type)
    saved = []
    for layer_index in range(layer_count):
        early = 0 if layer_index else 1
        mid, normed, queries, key_value, attended, log_sums, normed_moe, moved = attend_forward(
            col_count,
            row_count,
            copies,
            layer_index,
            hidden,
            gains_attn[layer_index],
            gains_moe[layer_index],
            cosine,
            sine,
            *dense[layer_index],
            shards[early],
        )
        if layer_index == 0:
            weights, moving = [moved_gate, moved, shards[2]], (2,)
        else:
            weights, moving = [moved, shards[1], shards[2]], (1, 2)
        next_blocks = ()
        if layer_index + 1 < layer_count:
            next_blocks = (w_qkv[layer_index + 1].T, w_out[layer_index + 1].T)
        closing = layer_index + 1 == layer_count
        mixed, gates, slots, returned, *rest = moe_forward(
            dims,
            row_count,
            layer_index,
            normed_moe,
            routes_all[:, layer_index],
            routers[layer_index],
            weights,
            moving,
            next_blocks,
            closing,
        )
        if closing:
            left_sum = (mixed,)
        for kind, moved in zip(moving, rest):
            weights[kind] = moved
        experts.append(weights)
        if next_blocks:
            dense.append(tuple(pieced(full) for full in rest[len(moving) :]))
        saved.append(
            (hidden, mid, normed, queries, key_value, attended, log_sums, normed_moe)
            + (gates, slots, returned)
        )
        if not closing:
            hidden = mid + mixed
    incoming = cotangent.astype(wide_type)
    dense_results = [None] * layer_count
    expert_results = [None] * layer_count
    part_sums = ()
    ordered = ()
    for layer_index in reversed(range(layer_count)):
        x, mid, normed, queries, key_value, attended, log_sums, normed_moe = saved[layer_index][:8]
        gates, slots, returned = saved[layer_index][8:]
        grad_moe, grad_router, *rest = moe_backward(
            dims,
            incoming.astype(narrow_type),
            routes_all[:, layer_index],
            routers[layer_index],
            gates,
            normed_moe,
            slots,
            returned,
            experts[layer_index],
            left_sum,
            part_sums,
        )
        if part_sums:
            dense_results[layer_index + 1] = rest[row_count : row_count + 3]
            del rest[row_count : row_count + 3]
        if left_sum:
            hidden = mid + rest.pop()
            left_sum = ()
        if layer_index + 1 < layer_count:
            grad_moe, expert_results[layer_index + 1] = lax.optimization_barrier(
                (grad_moe, expert_results[layer_index + 1])
            )
        expert_results[layer_index] = move_grads(rest)
        incoming, grad_mid, grad_projected, grad_gain_attn, grad_gain_moe = attend_backward(
            col_count,
            incoming,
            grad_moe,
            mid,
            x,
            gains_attn[layer_index],
            gains_moe[layer_index],
            cosine,
            sine,
            *dense[layer_index],
            queries,
            key_value,
            attended,
            log_sums,
        )
        small = jnp.concatenate(
            [
                place_back(grad_router, local_experts, expert_pick),
                grad_gain_attn,
                grad_gain_moe,
            ],
            axis=0,
        ).astype(narrow_type)
        small = small.reshape(E + 2, device_count, -1).transpose(1, 0, 2).reshape(device_count, -1)
        small_size = small.shape[1]
        small_rows = -(-small_size // 2048) * 16
        small = jnp.pad(small, ((0, 0), (0, small_rows * 128 - small_size)))
        small = small.reshape(row_count, col_count, small_rows, 128).transpose(1, 0, 2, 3)
        if layer_index == 0 and copies == 1 and layer_count > 1:
            groups = tuple((above, expert_results[above]) for above in range(1, layer_count))
            grad_mid, ordered = lax.optimization_barrier(
                (grad_mid, order_grads(layer_count, groups, ()))
            )
        part_sums = reduce_dense(
            row_count,
            col_count,
            normed,
            grad_projected,
            grad_mid,
            attended,
            small,
            layer_index == 0,
        )
        if layer_index > 0:
            incoming, part_sums = lax.optimization_barrier((incoming, part_sums))
        else:
            dense_results[0] = part_sums
    small_results = [
        small.reshape(-1)[:small_size].reshape(E + 2, -1).T for _, _, small in dense_results
    ]
    dense_results = [(qkv, out.T) for qkv, out, _ in dense_results]
    small = jnp.stack(small_results)
    if copies == 1:
        grad_gate, grad_up, grad_down = order_grads(
            layer_count, ((0, expert_results[0]),), ordered
        )
    else:
        ordered = jnp.stack([own_grads(blocks) for blocks in expert_results])
        grad_gate, grad_up, grad_down = (ordered[:, :, kind] for kind in range(3))
    grad_gate, grad_up = grad_gate.swapaxes(2, 3), grad_up.swapaxes(2, 3)
    return (
        hidden,
        incoming,
        small[:, :, E],
        jnp.stack([dense_results[index][0] for index in range(layer_count)]),
        jnp.stack([dense_results[index][1] for index in range(layer_count)]),
        small[:, :, E + 1],
        small[:, :, :E],
        grad_gate,
        grad_up,
        grad_down,
    )


def solution(mesh):
    in_specs = (
        P(("row", "col"), None),
        P(None, ("row", "col"), None),
        P(),
        P(None, "row", "col"),
        P(None, "row", "col"),
        P(),
        P(None, "row", None),
        P(None, "col", None, "row"),
        P(None, "col", None, "row"),
        P(None, "col", "row", None),
        P(("row", "col"), None),
    )
    out_specs = (
        P(("row", "col"), None),
        P(("row", "col"), None),
        P(None, ("row", "col")),
        P(None, "row", "col"),
        P(None, "row", "col"),
        P(None, ("row", "col")),
        P(None, ("row", "col"), None),
        P(None, "col", None, "row"),
        P(None, "col", None, "row"),
        P(None, "col", "row", None),
    )
    return jax.shard_map(body, mesh=mesh, in_specs=in_specs, out_specs=out_specs, check_vma=False)
```

```python
import functools

import jax
import jax.numpy as jnp
from jax import lax
from jax.experimental import pallas as pl
from jax.experimental.pallas import tpu as pltpu
from jax.sharding import PartitionSpec as P

QUERY_HEADS = 12
KEY_VALUE_HEADS = 2
HEAD_SIZE = 128
E = 32
TOPK = 4
BLOCK = 256
QUERY_FEATURES = 1536
CAP = 36


eps_norm = 1e-06
rope_base = 1000000.0
masked_score = -1e30
wide_type = jnp.float32
narrow_type = jnp.bfloat16


def rope_angles(positions, half_dim):
    frequency = rope_base ** (-jnp.arange(half_dim, dtype=jnp.float32) / half_dim)
    angles = positions.astype(jnp.float32)[:, None] * frequency[None, :]
    return (jnp.cos(angles), jnp.sin(angles))


def split_rows(total, most):
    best = 16
    for step in range(16, most + 1, 16):
        if total % step == 0:
            best = step
    return best


def over_blocks(total, block, step):
    def run(index, carry):
        step(pl.ds(pl.multiple_of(index * block, block), block))
        return carry

    lax.fori_loop(0, total // block, run, 0)


def over_chunks(chunks, width, step):
    def run(index, carry):
        step(index, pl.ds(pl.multiple_of(index * width, width), width))
        return carry

    lax.fori_loop(0, chunks, run, 0)


def dot_nt(left, right):
    return lax.dot_general(
        left, right, (((1,), (1,)), ((), ())), preferred_element_type=jnp.float32
    )


def dot_nn(left, right):
    return jnp.dot(left, right, preferred_element_type=jnp.float32)


class Peers:
    def __init__(self, count, place, device_of):
        self.count = count
        self.place = place
        self.device_of = device_of

    def ahead(self, step):
        return lax.rem(self.place + step, self.count)

    def behind(self, step):
        return lax.rem(self.place + self.count - step, self.count)


def expert_peers(col_count, copies, group_rows):
    row_index = lax.axis_index("row")
    share = lax.rem(row_index, copies)
    rows = Peers(group_rows, row_index // copies, lambda place: {"row": share + copies * place})
    return rows, col_peers(col_count)


def col_peers(col_count):
    return Peers(col_count, lax.axis_index("col"), lambda place: {"col": place})


def greet(groups):
    barrier = pltpu.get_barrier_semaphore()
    total = 0
    for peers in groups:
        for step in range(1, peers.count):
            pl.semaphore_signal(
                barrier,
                inc=1,
                device_id=peers.device_of(peers.ahead(step)),
                device_id_type=pl.DeviceIdType.MESH,
            )
            total += 1
    pl.semaphore_wait(barrier, total)


def send_to(source, target, sems, number, device):
    send_sems, recv_sems = sems
    return pltpu.make_async_remote_copy(
        src_ref=source,
        dst_ref=target,
        send_sem=send_sems.at[number],
        recv_sem=recv_sems.at[number],
        device_id=device,
        device_id_type=pl.DeviceIdType.MESH,
    )


class Exchange:
    def __init__(self, peers, send_sems, recv_sems, source, target):
        self.peers = peers
        self.sems = (send_sems, recv_sems)
        self.source = source
        self.target = target

    def out(self, step, index, chunk):
        place = self.peers.ahead(step)
        return send_to(
            self.source(place, chunk),
            self.target(self.peers.place, step, chunk),
            self.sems,
            (index, step - 1),
            self.peers.device_of(place),
        )

    def start(self, index, chunk):
        for step in range(1, self.peers.count):
            self.out(step, index, chunk).start()

    def wait_send(self, index, chunk):
        for step in range(1, self.peers.count):
            self.out(step, index, chunk).wait_send()

    def wait_recv(self, index, chunk):
        for step in range(1, self.peers.count):
            place = self.peers.behind(step)
            landed = self.target(place, step, chunk)
            send_to(
                landed, landed, self.sems, (index, step - 1), self.peers.device_of(place)
            ).wait_recv()


def exchange_sems(chunks, count):
    return [pltpu.SemaphoreType.DMA((chunks, max(count - 1, 1))) for _ in range(2)]


class LineGather:
    def __init__(self, rows, own, tokens, part, sems):
        self.rows = rows
        self.own = own
        self.tokens = tokens
        self.part = part
        self.own_send, self.pass_send, self.recv = sems

    @staticmethod
    def sems(chunks, count):
        return [
            pltpu.SemaphoreType.DMA((chunks, 2)),
            pltpu.SemaphoreType.DMA((chunks, count)),
            pltpu.SemaphoreType.DMA((chunks, count)),
        ]

    def copy(self, source, origin, index, chunk, sem, place):
        return pltpu.make_async_remote_copy(
            src_ref=source,
            dst_ref=self.tokens.at[self.part(origin), chunk],
            send_sem=sem,
            recv_sem=self.recv.at[index, origin],
            device_id=self.rows.device_of(place),
            device_id_type=pl.DeviceIdType.MESH,
        )

    def own_copies(self, index, chunk):
        me, last = self.rows.place, self.rows.count - 1
        for way, (there, place) in enumerate(((me < last, me + 1), (me > 0, me - 1))):
            yield there, self.copy(
                self.own.at[:, chunk], me, index, chunk, self.own_send.at[index, way], place
            )

    def passed(self, index, chunk):
        me, last = self.rows.place, self.rows.count - 1
        for distance in range(1, self.rows.count):
            for arrives, origin, goes_on, place in (
                (me >= distance, me - distance, me < last, me + 1),
                (me + distance <= last, me + distance, me > 0, me - 1),
            ):
                yield arrives, goes_on, self.copy(
                    self.tokens.at[self.part(origin), chunk],
                    origin,
                    index,
                    chunk,
                    self.pass_send.at[index, origin],
                    place,
                )

    def start_own(self, index, chunk):
        for there, copy in self.own_copies(index, chunk):
            pl.when(there)(copy.start)

    def arrive(self, index, chunk):
        for arrives, goes_on, copy in self.passed(index, chunk):

            @pl.when(arrives)
            def _():
                copy.wait_recv()
                pl.when(goes_on)(copy.start)

    def wait_send(self, index, chunk):
        for there, copy in self.own_copies(index, chunk):
            pl.when(there)(copy.wait_send)
        for arrives, goes_on, copy in self.passed(index, chunk):
            pl.when(arrives & goes_on)(copy.wait_send)


class LineSum:
    def __init__(self, rows, tokens, part, landed, sems):
        self.rows = rows
        self.tokens = tokens
        self.part = part
        self.landed = landed
        self.send, self.recv = sems

    @staticmethod
    def sems(chunks, count):
        return [
            pltpu.SemaphoreType.DMA((chunks, count)),
            pltpu.SemaphoreType.DMA((chunks, count + 1)),
        ]

    def copy(self, target, slot, index, chunk, place):
        return pltpu.make_async_remote_copy(
            src_ref=self.tokens.at[self.part(target), chunk],
            dst_ref=self.landed.at[slot, :, chunk],
            send_sem=self.send.at[index, target],
            recv_sem=self.recv.at[index, slot],
            device_id=self.rows.device_of(place),
            device_id_type=pl.DeviceIdType.MESH,
        )

    def passed(self, index, chunk):
        me, last = self.rows.place, self.rows.count - 1
        for number in range(self.rows.count):
            for goes, arrives, slot, target, place in (
                (me > number, me < last, number, number, me - 1),
                (me < last - number, me > 0, last - number + 1, last - number, me + 1),
            ):
                yield goes, arrives, slot, target, self.copy(target, slot, index, chunk, place)

    def pass_on(self, index, chunk):
        for goes, arrives, slot, target, copy in self.passed(index, chunk):

            @pl.when(goes)
            def _():
                @pl.when(arrives)
                def _():
                    copy.wait_recv()
                    total = self.tokens[self.part(target), chunk].astype(jnp.float32)
                    total = total + self.landed[slot, :, chunk].astype(jnp.float32)
                    self.tokens[self.part(target), chunk] = total.astype(jnp.bfloat16)

                copy.start()

    def is_middle(self):
        return (self.rows.place > 0) & (self.rows.place < self.rows.count - 1)

    def total(self, index, chunk, out):
        me, last = self.rows.place, self.rows.count - 1
        out[:, chunk] = self.tokens[self.part(me), chunk].astype(jnp.float32)
        for arrives, slot in ((me < last, me), (me > 0, me + 1)):

            @pl.when(arrives)
            def _():
                self.copy(me, slot, index, chunk, me).wait_recv()
                out[:, chunk] += self.landed[slot, :, chunk].astype(jnp.float32)

    def wait_send(self, index, chunk):
        for goes, _, _, _, copy in self.passed(index, chunk):
            pl.when(goes)(copy.wait_send)


def iota(shape, axis):
    return lax.broadcasted_iota(jnp.int32, shape, axis)


def within(numbers, size, count):
    block = jnp.zeros_like(numbers)
    for index in range(1, count):
        block = block + (numbers >= index * size).astype(jnp.int32)
    return block, numbers - block * size


def slot_block(shape, slot_axis, slot_rows):
    slots = iota(shape, slot_axis)
    block = iota(shape, 1 - slot_axis)
    return (slots >= block * slot_rows) & (slots < (block + 1) * slot_rows)


def build_places(dims, rows, routes_ref, place, place_t, member):
    group_rows, col_count, copies, token_rows, slot_rows, chunks, width = dims
    all_slots = col_count * slot_rows
    number = iota((E, 1), 0)
    ahead, col = within(number, col_count, group_rows)
    owner = ahead + rows.place
    owner = jnp.where(owner >= group_rows, owner - group_rows, owner)
    expert = col * group_rows + owner
    earlier = (iota((token_rows, token_rows), 0) < iota((token_rows, token_rows), 1)).astype(
        jnp.bfloat16
    )
    pick = slot_block((E, all_slots), 1, slot_rows).astype(jnp.bfloat16)
    column = iota((slot_rows, 1), 0)
    lane = within(iota((1, all_slots), 1), slot_rows, col_count)[1]
    for group in range(group_rows):
        tokens = slice(group * token_rows, (group + 1) * token_rows)
        picked = routes_ref[group]
        has = picked[0:1, :] == expert
        for choice in range(1, TOPK):
            has = has | (picked[choice : choice + 1, :] == expert)
        before = dot_nn(has.astype(jnp.float32).astype(jnp.bfloat16), earlier)
        slot_number = jnp.where(has, before, -1.0)
        in_group = (column >= group * CAP) & (column < (group + 1) * CAP)
        wanted = jnp.where(in_group, column - group * CAP, -2).astype(jnp.float32)
        for index in range(col_count):
            slots = slice(index * slot_rows, (index + 1) * slot_rows)
            hit = slot_number[index : index + 1, :] == wanted
            place[slots, tokens] = jnp.where(hit, 1.0, 0.0).astype(jnp.bfloat16)
        turned = slot_number.T
        in_group = (lane >= group * CAP) & (lane < (group + 1) * CAP)
        wanted = jnp.where(in_group, lane - group * CAP, -2).astype(jnp.float32)
        hit = dot_nn(turned.astype(jnp.bfloat16), pick) == wanted
        place_t[tokens, :] = jnp.where(hit, 1.0, 0.0).astype(jnp.bfloat16)
        if member is not None:
            member[tokens, :] = turned


def far_first(rows):
    for distance in range(rows.count - 1, 0, -1):
        for there, place in (
            (rows.place + distance < rows.count, rows.place + distance),
            (rows.place >= distance, rows.place - distance),
        ):
            yield there, place


class WeightMove:
    def __init__(self, rows, copies, layer, shards, target, sems, parts=1):
        self.rows = rows
        self.copies = copies
        self.layer = layer
        self.shards = shards
        self.target = target
        self.remote_sems = sems[:2]
        self.local_sem = sems[2]
        self.parts = parts
        self.width = target.shape[2] // parts

    @staticmethod
    def sems(row_count, parts=1):
        return [pltpu.SemaphoreType.DMA((parts, max(row_count - 1, 1)))] * 2 + [
            pltpu.SemaphoreType.DMA
        ]

    def own(self):
        return pltpu.make_async_copy(
            self.shards.at[self.layer, self.rows.place // self.copies],
            self.target.at[0],
            self.local_sem,
        )

    def lanes(self, part):
        return pl.ds(pl.multiple_of(part * self.width, self.width), self.width)

    def out(self, step, part):
        place = self.rows.ahead(step)
        return send_to(
            self.shards.at[self.layer, place // self.copies, :, self.lanes(part)],
            self.target.at[step, :, self.lanes(part)],
            self.remote_sems,
            (part, step - 1),
            self.rows.device_of(place),
        )

    def start(self):
        self.own().start()

        def one_part(part, carry):
            for there, place in far_first(self.rows):
                step = lax.rem(place - self.rows.place + self.rows.count, self.rows.count)

                @pl.when(there)
                def _():
                    self.out(step, part).start()

            return carry

        lax.fori_loop(0, self.parts, one_part, 0)

    def wait_part(self, part):
        for step in range(1, self.rows.count):
            landed = self.target.at[step, :, self.lanes(part)]
            place = self.rows.behind(step)
            send_to(
                landed, landed, self.remote_sems, (part, step - 1), self.rows.device_of(place)
            ).wait_recv()

    def wait_recv(self):
        self.own().wait()
        for part in range(self.parts):
            self.wait_part(part)

    def wait_send(self):
        for part in range(self.parts):
            for step in range(1, self.rows.count):
                self.out(step, part).wait_send()


def line_sems(row_count):
    return [pltpu.SemaphoreType.DMA((max(row_count - 1, 1),))] * 2 + [pltpu.SemaphoreType.DMA]


def all_rows(row_count):
    return Peers(row_count, lax.axis_index("row"), lambda place: {"row": place})


def moved_shape(row_count, shards):
    return jax.ShapeDtypeStruct((row_count, *shards.shape[2:]), shards.dtype)


vmem_most = 62 * 1024 * 1024
long_cost = pl.CostEstimate(flops=0, bytes_accessed=600 * 1024 * 1024, transcendentals=0)
no_cost = pl.CostEstimate(flops=0, bytes_accessed=0, transcendentals=0)


def moe_forward_kernel(dims, row_count, layer, moving, gather_dims, closing, *refs):
    group_rows, col_count, copies, token_rows, slot_rows, chunks, width = dims
    own_ref, routes_ref, router_ref = refs[:3]
    weight_in = refs[3:6]
    refs = refs[6:]
    mid_in = refs[: 0 if closing else 1]
    refs = refs[len(mid_in) :]
    next_blocks = refs[: 2 if gather_dims else 0]
    refs = refs[len(next_blocks) :]
    sum_ref, gates_ref, slots_out, returned_out = refs[:4]
    refs = refs[4:]
    moved_out = refs[: len(moving)]
    refs = refs[len(moving) :]
    next_full = refs[: len(next_blocks)]
    refs = refs[len(next_blocks) :]
    dense = None
    if gather_dims:
        count = len(DenseGather.sems(gather_dims, 2))
        dense = DenseGather(gather_dims, next_blocks, next_full, refs[-count:])
        refs = refs[:-count]
    move_sems = refs[len(refs) - 3 * len(moving) :]
    refs = refs[: len(refs) - 3 * len(moving)]
    (
        place,
        place_t,
        member,
        gate,
        up,
        down,
        tokens,
        send,
        slots,
        gate_val,
        up_val,
        act,
        returned,
        landed,
        own_send,
        pass_send,
        row_recv,
        there_send,
        there_recv,
        back_send,
        back_recv,
        home_send,
        home_recv,
        local_sem,
    ) = refs
    all_tokens = group_rows * token_rows
    all_slots = col_count * slot_rows
    slot_step = split_rows(all_slots, 320)
    rows, cols = expert_peers(col_count, copies, group_rows)

    def token_part(place):
        return pl.ds(pl.multiple_of(place * token_rows, token_rows), token_rows)

    def slot_part(place):
        return pl.ds(pl.multiple_of(place * slot_rows, slot_rows), slot_rows)

    gather = LineGather(rows, own_ref, tokens, token_part, (own_send, pass_send, row_recv))
    there = Exchange(
        cols,
        there_send,
        there_recv,
        lambda place, chunk: send.at[slot_part(place), chunk],
        lambda place, step, chunk: slots.at[slot_part(place), chunk],
    )
    back = Exchange(
        cols,
        back_send,
        back_recv,
        lambda place, chunk: send.at[slot_part(place), chunk],
        lambda place, step, chunk: returned.at[slot_part(place), chunk],
    )
    home = LineSum(rows, tokens, token_part, landed, (home_send, home_recv))
    weights = (gate, up, down)
    moves = {
        kind: WeightMove(
            all_rows(row_count),
            copies,
            layer,
            weight_in[kind],
            weights[kind],
            move_sems[3 * number : 3 * number + 3],
            chunks if kind == 2 else 1,
        )
        for number, kind in enumerate(moving)
    }
    loads = {
        kind: pltpu.make_async_copy(weight_in[kind], weights[kind], local_sem.at[2 + kind])
        for kind in range(3)
        if kind not in moving
    }
    keeps = []

    def keep_weight(kind):
        keep = pltpu.make_async_copy(
            weights[kind], moved_out[moving.index(kind)], local_sem.at[2 + kind]
        )
        keep.start()
        keeps.append(keep)

    def weight_ready(kind):
        if kind in loads:
            loads[kind].wait()
        elif kind == 2:
            moves[kind].own().wait()
        else:
            moves[kind].wait_recv()
            keep_weight(kind)

    def weight(kind, chunk):
        return weights[kind][:, :, chunk].reshape(-1, width)

    greet((all_rows(row_count), cols))
    for index in range(min(2, chunks)):
        gather.start_own(index, pl.ds(index * width, width))
    for copy in loads.values():
        copy.start()
    tokens[token_part(rows.place), :] = own_ref[...]
    build_places(dims, rows, routes_ref, place, place_t, member)

    def dispatch(index, chunk):
        gather.arrive(index, chunk)

        @pl.when(index + 2 < chunks)
        def _():
            later = pl.ds(pl.multiple_of((index + 2) * width, width), width)
            gather.start_own(index + 2, later)


        def rows_of(part):
            send[part, chunk] = dot_nn(place[part, :], tokens[:, chunk]).astype(jnp.bfloat16)

        over_blocks(all_slots, all_slots, rows_of)
        there.start(index, chunk)
        slots[slot_part(cols.place), chunk] = send[slot_part(cols.place), chunk]

    over_chunks(chunks, width, dispatch)
    if dense:
        for kind in dense.kinds:
            dense.start(kind)
    for kind in moving:
        moves[kind].start()

    def gating(part):
        chosen = member[part, :] >= 0
        logits = jnp.where(chosen, dot_nt(tokens[part, :], router_ref[...]), masked_score)
        peak = jnp.max(logits, axis=-1, keepdims=True)
        exponent = jnp.where(chosen, jnp.exp(logits - peak), 0.0)
        gates = exponent / jnp.sum(exponent, axis=-1, keepdims=True)
        gates_ref[part, :] = gates
        pick = slot_block((E, all_slots), 1, slot_rows).astype(jnp.bfloat16)
        spread = dot_nn(gates.astype(jnp.bfloat16), pick)
        place_t[part, :] = (place_t[part, :].astype(jnp.float32) * spread).astype(jnp.bfloat16)

    over_blocks(all_tokens, token_rows, gating)

    def project(kind, target, wait, index, chunk):
        if wait:
            there.wait_recv(index, chunk)

        def rows_of(part):
            value = dot_nt(slots[part, chunk], weight(kind, chunk))

            @pl.when(index == 0)
            def _():
                target[part, :] = value

            @pl.when(index > 0)
            def _():
                target[part, :] += value

        over_blocks(all_slots, all_slots, rows_of)

    weight_ready(0)
    over_chunks(chunks, width, functools.partial(project, 0, gate_val, True))
    weight_ready(1)
    over_chunks(chunks, width, functools.partial(project, 1, up_val, False))
    keep_slots = pltpu.make_async_copy(slots, slots_out, local_sem.at[0])
    keep_slots.start()

    def activate(part):
        value = gate_val[part, :]
        act[part, :] = (value * jax.nn.sigmoid(value) * up_val[part, :]).astype(jnp.bfloat16)

    over_blocks(all_slots, slot_step, activate)
    if dense:
        for kind in dense.kinds:
            dense.pass_rows(kind)
    weight_ready(2)
    def give_back(index, chunk):
        if 2 in moves:
            moves[2].wait_part(index)
        there.wait_send(index, chunk)

        def rows_of(part):
            send[part, chunk] = dot_nn(act[part, :], weight(2, chunk)).astype(jnp.bfloat16)

        over_blocks(all_slots, all_slots, rows_of)
        back.start(index, chunk)
        returned[slot_part(cols.place), chunk] = send[slot_part(cols.place), chunk]

    over_chunks(chunks, width, give_back)
    if 2 in moves:
        keep_weight(2)

    over_chunks(chunks, width, gather.wait_send)

    def combine(index, chunk):
        back.wait_recv(index, chunk)

        def rows_of(part):
            tokens[part, chunk] = dot_nn(place_t[part, :], returned[:, chunk]).astype(jnp.bfloat16)

        over_blocks(all_tokens, token_rows, rows_of)
        if closing:
            return
        pl.when(~home.is_middle())(functools.partial(home.pass_on, index, chunk))

        @pl.when(home.is_middle() & (index > 0))
        def _():
            before = pl.ds(pl.multiple_of((index - 1) * width, width), width)
            home.pass_on(index - 1, before)

    over_chunks(chunks, width, combine)
    if closing:
        keep_mixed = pltpu.make_async_copy(tokens, sum_ref, local_sem.at[5])
        keep_mixed.start()
    else:
        last_chunk = pl.ds((chunks - 1) * width, width)
        pl.when(home.is_middle())(functools.partial(home.pass_on, chunks - 1, last_chunk))
    keep_returned = pltpu.make_async_copy(returned, returned_out, local_sem.at[1])
    keep_returned.start()
    if dense:
        for kind in dense.kinds:
            dense.pass_pairs(kind)

    def finish(index, chunk):
        home.total(index, chunk, sum_ref)
        sum_ref[:, chunk] += mid_in[0][:, chunk]

    if not closing:
        over_chunks(chunks, width, finish)

    def drain(index, chunk):
        back.wait_send(index, chunk)
        if not closing:
            home.wait_send(index, chunk)

    over_chunks(chunks, width, drain)
    if dense:
        for kind in dense.kinds:
            dense.finish(kind)
    for kind in moving:
        moves[kind].wait_send()
    if closing:
        keep_mixed.wait()
    keep_slots.wait()
    keep_returned.wait()
    for keep in keeps:
        keep.wait()


class RowTotal:
    def __init__(self, rows, blocks, landed, own, sems):
        self.rows = rows
        self.blocks = blocks
        self.landed = landed
        self.own = own
        self.remote_sems = sems[:2]
        self.local_sem = sems[2]

    def out(self, step):
        place = self.rows.ahead(step)
        return send_to(
            self.blocks.at[place],
            self.landed.at[step - 1],
            self.remote_sems,
            step - 1,
            self.rows.device_of(place),
        )

    def load(self):
        return pltpu.make_async_copy(self.blocks.at[self.rows.place], self.own, self.local_sem)

    def start(self):
        self.load().start()
        for step in range(1, self.rows.count):
            self.out(step).start()

    def finish(self, out):
        self.load().wait()
        total = self.own[...].astype(jnp.float32)
        for step in range(1, self.rows.count):
            self.out(step).wait_recv()
            total = total + self.landed[step - 1].astype(jnp.float32)
        out[...] = total
        for step in range(1, self.rows.count):
            self.out(step).wait_send()


def moe_backward_kernel(dims, opening, dense_count, *refs):
    group_rows, col_count, copies, token_rows, slot_rows, chunks, width = dims
    own_ref, routes_ref, router_ref, gates_ref, normed_ref, slots_in, returned_in = refs[:7]
    weight_in = refs[7:10]
    refs = refs[10:]
    opening_in = refs[: 1 if opening else 0]
    refs = refs[len(opening_in) :]
    block_count, slice_width = weight_in[0].shape[:2]
    dense_in = refs[:dense_count]
    refs = refs[dense_count:]
    sum_ref, router_grad_ref, *grads_out = refs[: 2 + block_count]
    refs = refs[2 + block_count :]
    dense_out = refs[:dense_count]
    refs = refs[dense_count:]
    dense_scratch = refs[len(refs) - 5 * dense_count :]
    refs = refs[: len(refs) - 5 * dense_count]
    totals = [
        RowTotal(all_rows(block_count), blocks, *dense_scratch[5 * n : 5 * n + 2], dense_scratch[5 * n + 2 : 5 * n + 5])
        for n, blocks in enumerate(dense_in)
    ]
    opening_out = refs[: len(opening_in)]
    refs = refs[len(opening_in) :]
    opening_scratch = ()
    if opening:
        opening_scratch = refs[-4:]
        refs = refs[:-4]
    (
        place,
        place_t,
        gate,
        up,
        down,
        tokens,
        send,
        slope,
        silu,
        act,
        weight,
        inner,
        received,
        grad_act,
        grad_gate,
        grad_up,
        returned,
        turned,
        staged,
        landed,
        pair_send,
        pair_landed,
        own_send,
        pass_send,
        row_recv,
        there_send,
        there_recv,
        back_send,
        back_recv,
        home_send,
        home_recv,
        pair_send_sem,
        pair_recv_sem,
        local_sem,
    ) = refs
    all_tokens = group_rows * token_rows
    all_slots = col_count * slot_rows
    slot_step = split_rows(all_slots, 320)
    rows, cols = expert_peers(col_count, copies, group_rows)

    def token_part(place):
        return pl.ds(pl.multiple_of(place * token_rows, token_rows), token_rows)

    def slot_part(place):
        return pl.ds(pl.multiple_of(place * slot_rows, slot_rows), slot_rows)

    gather = LineGather(rows, own_ref, tokens, token_part, (own_send, pass_send, row_recv))
    there = Exchange(
        cols,
        there_send,
        there_recv,
        lambda place, chunk: send.at[slot_part(place), chunk],
        lambda place, step, chunk: received.at[slot_part(place), chunk],
    )
    back = Exchange(
        cols,
        back_send,
        back_recv,
        lambda place, chunk: send.at[slot_part(place), chunk],
        lambda place, step, chunk: returned.at[slot_part(place), chunk],
    )
    home = LineSum(rows, tokens, token_part, landed, (home_send, home_recv))
    before = None
    if opening:
        before = LineSum(rows, opening_scratch[0], token_part, opening_scratch[1], opening_scratch[2:])
        load_mixed = pltpu.make_async_copy(opening_in[0], opening_scratch[0], local_sem.at[7])
    pair = Exchange(
        rows,
        pair_send_sem,
        pair_recv_sem,
        lambda place, chunk: pair_send.at[token_part(place), :],
        lambda place, step, chunk: pair_landed.at[step - 1],
    )
    greet((all_rows(block_count), cols))
    for index in range(min(2, chunks)):
        gather.start_own(index, pl.ds(index * width, width))
    load_returned = pltpu.make_async_copy(returned_in, returned, local_sem.at[1])
    load_returned.start()
    load_slots = pltpu.make_async_copy(slots_in, send, local_sem.at[0])
    load_slots.start()
    if before:
        load_mixed.start()
    weights = (gate, up, down)
    loads = [
        pltpu.make_async_copy(weight_in[kind], weights[kind], local_sem.at[4 + kind])
        for kind in range(3)
    ]
    for copy in loads:
        copy.start()

    def weight_part(kind, chunk):
        return weights[kind][:, :, chunk].reshape(block_count * slice_width, width)

    tokens[token_part(rows.place), :] = own_ref[...]
    build_places(dims, rows, routes_ref, place, place_t, None)

    def recompute(part):
        gate_val = dot_nt(send[part, :], gate[...].reshape(-1, gate.shape[2]))
        up_val = dot_nt(send[part, :], up[...].reshape(-1, up.shape[2]))
        sigmoid = jax.nn.sigmoid(gate_val)
        value = gate_val * sigmoid
        act[part, :] = (value * up_val).astype(jnp.bfloat16)
        silu[part, :] = value.astype(jnp.bfloat16)
        slope[part, :] = (up_val * sigmoid * (1.0 + gate_val * (1.0 - sigmoid))).astype(
            jnp.bfloat16
        )

    def slot_gates(part):
        picked = dot_nn(place[part, :], gates_ref[...].astype(jnp.bfloat16))
        block = iota(picked.shape, 1)
        slot = iota(picked.shape, 0) + part.start
        in_block = (slot >= block * slot_rows) & (slot < (block + 1) * slot_rows)
        weight[part, :] = jnp.sum(jnp.where(in_block, picked, 0.0), axis=1, keepdims=True)

    def recompute_all():
        load_slots.wait()
        for copy in loads:
            copy.wait()
        over_blocks(all_slots, slot_step, recompute)

    over_blocks(all_slots, slot_step, slot_gates)
    recompute_all()
    load_returned.wait()

    def dispatch(index, chunk):
        gather.arrive(index, chunk)

        @pl.when(index + 2 < chunks)
        def _():
            later = pl.ds(pl.multiple_of((index + 2) * width, width), width)
            gather.start_own(index + 2, later)


        def rows_of(part):
            grad = dot_nn(place[part, :], tokens[:, chunk])
            share = jnp.sum(
                grad * returned[part, chunk].astype(jnp.float32), axis=1, keepdims=True
            )
            send[part, chunk] = (weight[part, :] * grad).astype(jnp.bfloat16)

            @pl.when(index == 0)
            def _():
                inner[part, :] = share

            @pl.when(index > 0)
            def _():
                inner[part, :] += share

        over_blocks(all_slots, all_slots, rows_of)
        there.start(index, chunk)
        received[slot_part(cols.place), chunk] = send[slot_part(cols.place), chunk]

    over_chunks(chunks, width, dispatch)
    for total in totals:
        total.start()

    def pairs(part):
        picked = slot_block((all_slots, pair_send.shape[1]), 0, slot_rows)
        spread = jnp.where(picked, inner[...], 0.0)
        high = spread.astype(jnp.bfloat16)
        low = (spread - high.astype(jnp.float32)).astype(jnp.bfloat16)
        pair_send[part, :] = dot_nn(place_t[part, :], high) + dot_nn(place_t[part, :], low)

    over_chunks(chunks, width, gather.wait_send)
    over_blocks(all_tokens, token_rows, pairs)
    pair.start(0, None)
    if before:
        load_mixed.wait()

        @pl.when(~before.is_middle())
        def _():
            over_chunks(chunks, width, before.pass_on)


    def project(index, chunk):
        there.wait_recv(index, chunk)

        def rows_of(part):
            grad = dot_nt(received[part, chunk], weight_part(2, chunk))

            @pl.when(index == 0)
            def _():
                grad_act[part, :] = grad

            @pl.when(index > 0)
            def _():
                grad_act[part, :] += grad

        over_blocks(all_slots, all_slots, rows_of)

    over_chunks(chunks, width, project)

    def slopes(part):
        grad = grad_act[part, :]
        grad_gate[part, :] = (grad * slope[part, :].astype(jnp.float32)).astype(jnp.bfloat16)
        grad_up[part, :] = (grad * silu[part, :].astype(jnp.float32)).astype(jnp.bfloat16)

    over_blocks(all_slots, slot_step, slopes)

    def give_back(index, chunk):
        there.wait_send(index, chunk)

        def rows_of(part):
            send[part, chunk] = (
                dot_nn(grad_gate[part, :], weight_part(0, chunk))
                + dot_nn(grad_up[part, :], weight_part(1, chunk))
            ).astype(jnp.bfloat16)

        over_blocks(all_slots, all_slots, rows_of)
        back.start(index, chunk)

    over_chunks(chunks, width, give_back)

    returned[slot_part(cols.place), :] = send[slot_part(cols.place), :]

    if before:

        @pl.when(before.is_middle())
        def _():
            over_chunks(chunks, width, before.pass_on)

    def combine(index, chunk):
        back.wait_recv(index, chunk)

        def rows_of(part):
            tokens[part, chunk] = dot_nn(place_t[part, :], returned[:, chunk]).astype(jnp.bfloat16)

        over_blocks(all_tokens, token_rows, rows_of)
        pl.when(~home.is_middle())(functools.partial(home.pass_on, index, chunk))

        @pl.when(home.is_middle() & (index > 0))
        def _():
            before = pl.ds(pl.multiple_of((index - 1) * width, width), width)
            home.pass_on(index - 1, before)

    over_chunks(chunks, width, combine)
    last_chunk = pl.ds((chunks - 1) * width, width)
    pl.when(home.is_middle())(functools.partial(home.pass_on, chunks - 1, last_chunk))
    over_chunks(chunks, width, back.wait_send)
    load_slots = pltpu.make_async_copy(slots_in, send, local_sem.at[0])
    load_slots.start()
    load_slots.wait()

    def keep(kind, index):
        return pltpu.make_async_copy(
            staged.at[index % 2], grads_out[index].at[kind], local_sem.at[2 + index % 2]
        )

    for kind, (left, right) in enumerate(((grad_gate, send), (grad_up, send), (act, received))):
        turned[...] = left[...].T
        for index in range(block_count):
            if index >= 2:
                keep(kind, index - 2).wait()
            part = slice(index * slice_width, (index + 1) * slice_width)
            staged[index % 2] = dot_nn(turned[part, :], right[...]).astype(jnp.bfloat16)
            keep(kind, index).start()
        for index in range(max(block_count - 2, 0), block_count):
            keep(kind, index).wait()

    pair.wait_recv(0, None)
    grad_pair = pair_send[token_part(rows.place), :]
    for ahead in range(1, group_rows):
        shifted = pltpu.roll(pair_landed[group_rows - ahead - 1], ahead * col_count, 1)
        grad_pair = grad_pair + shifted
    grad_pair = grad_pair[:, :E]
    gates = gates_ref[token_part(rows.place), :]
    grad_logits = gates * (grad_pair - jnp.sum(gates * grad_pair, axis=-1, keepdims=True))
    grad_logits = grad_logits.astype(jnp.bfloat16)
    router_grad_ref[...] = dot_nn(grad_logits.astype(jnp.float32).T.astype(jnp.bfloat16), normed_ref[...])

    def finish(index, chunk):
        home.total(index, chunk, sum_ref)
        sum_ref[:, chunk] += dot_nn(grad_logits, router_ref[:, chunk])

    over_chunks(chunks, width, finish)
    if before:
        over_chunks(
            chunks, width, lambda index, chunk: before.total(index, chunk, opening_out[0])
        )
        over_chunks(chunks, width, before.wait_send)

    def drain(index, chunk):
        home.wait_send(index, chunk)

    over_chunks(chunks, width, drain)
    pair.wait_send(0, None)
    for total, out in zip(totals, dense_out):
        total.finish(out)


def moe_forward(
    dims, row_count, layer, own, routes, router, weights, moving, next_blocks, closing, mid
):
    group_rows, col_count, copies, token_rows, slot_rows, chunks, width = dims
    all_tokens, all_slots = group_rows * token_rows, col_count * slot_rows
    model_width = own.shape[1]
    slice_width = weights[0].shape[-2]
    hidden = row_count * slice_width
    gather_dims = (row_count, col_count // 2) if next_blocks else None
    dense_sems = DenseGather.sems(gather_dims, 2) if next_blocks else []
    vmem = pl.BlockSpec(memory_space=pltpu.VMEM)
    outside = pl.BlockSpec(memory_space=pl.ANY)
    every_row = jax.ShapeDtypeStruct((all_tokens, model_width), jnp.bfloat16)
    slot_array = pltpu.VMEM((all_slots, model_width), jnp.bfloat16)
    hidden_wide = pltpu.VMEM((all_slots, hidden), jnp.float32)
    weight_array = pltpu.VMEM((row_count, slice_width, model_width), jnp.bfloat16)
    return pl.pallas_call(
        functools.partial(
            moe_forward_kernel, dims, row_count, layer, moving, gather_dims, closing
        ),
        out_shape=(
            every_row if closing else jax.ShapeDtypeStruct((token_rows, model_width), jnp.float32),
            jax.ShapeDtypeStruct((all_tokens, E), jnp.float32),
            jax.ShapeDtypeStruct((all_slots, model_width), jnp.bfloat16),
            jax.ShapeDtypeStruct((all_slots, model_width), jnp.bfloat16),
            *(moved_shape(row_count, weights[kind]) for kind in moving),
            *(gathered_shapes(gather_dims, next_blocks) if next_blocks else ()),
        ),
        in_specs=[vmem] * 3 + [outside] * 3 + [vmem] * len(mid) + [outside] * len(next_blocks),
        out_specs=(outside if closing else vmem, vmem)
        + (outside,) * (2 + len(moving) + len(next_blocks)),
        scratch_shapes=[
            pltpu.VMEM((all_slots, all_tokens), jnp.bfloat16),
            pltpu.VMEM((all_tokens, all_slots), jnp.bfloat16),
            pltpu.VMEM((all_tokens, E), jnp.float32),
            weight_array,
            weight_array,
            weight_array,
            pltpu.VMEM((all_tokens, model_width), jnp.bfloat16),
            slot_array,
            slot_array,
            hidden_wide,
            hidden_wide,
            pltpu.VMEM((all_slots, hidden), jnp.bfloat16),
            slot_array,
            pltpu.VMEM((group_rows + 1, token_rows, model_width), jnp.bfloat16),
            *LineGather.sems(chunks, group_rows),
            *exchange_sems(chunks, col_count),
            *exchange_sems(chunks, col_count),
            *LineSum.sems(chunks, group_rows),
            pltpu.SemaphoreType.DMA((6,)),
            *(
                sem
                for kind in moving
                for sem in WeightMove.sems(row_count, chunks if kind == 2 else 1)
            ),
            *dense_sems,
        ],
        compiler_params=pltpu.CompilerParams(
            collective_id=1 + 7 * layer, has_side_effects=True, vmem_limit_bytes=vmem_most
        ),
        cost_estimate=no_cost,
        name="moe_forward",
    )(own, routes, router, *weights, *mid, *next_blocks)


def moe_backward(dims, own, routes, router, gates, normed, slots, returned, weights, opening, dense):
    group_rows, col_count, copies, token_rows, slot_rows, chunks, width = dims
    all_tokens, all_slots = group_rows * token_rows, col_count * slot_rows
    model_width = own.shape[1]
    opened = len(opening)
    block_count, slice_width = weights[0].shape[:2]
    grads = jax.ShapeDtypeStruct((3, slice_width, model_width), jnp.bfloat16)
    hidden = block_count * slice_width
    vmem = pl.BlockSpec(memory_space=pltpu.VMEM)
    outside = pl.BlockSpec(memory_space=pl.ANY)
    slot_array = pltpu.VMEM((all_slots, model_width), jnp.bfloat16)
    hidden_narrow = pltpu.VMEM((all_slots, hidden), jnp.bfloat16)
    weight_array = pltpu.VMEM((block_count, slice_width, model_width), jnp.bfloat16)
    return pl.pallas_call(
        functools.partial(moe_backward_kernel, dims, bool(opening), len(dense)),
        out_shape=(
            jax.ShapeDtypeStruct((token_rows, model_width), jnp.float32),
            jax.ShapeDtypeStruct((E, model_width), jnp.float32),
            *([grads] * block_count),
            *(jax.ShapeDtypeStruct(block.shape[1:], jnp.float32) for block in dense),
            *([jax.ShapeDtypeStruct((token_rows, model_width), jnp.float32)] * opened),
        ),
        in_specs=[vmem] * 5
        + [outside] * (5 + opened + len(dense)),
        out_specs=(vmem, vmem)
        + (outside,) * block_count
        + (vmem,) * (len(dense) + opened),
        scratch_shapes=[
            pltpu.VMEM((all_slots, all_tokens), jnp.bfloat16),
            pltpu.VMEM((all_tokens, all_slots), jnp.bfloat16),
            weight_array,
            weight_array,
            weight_array,
            pltpu.VMEM((all_tokens, model_width), jnp.bfloat16),
            slot_array,
            hidden_narrow,
            hidden_narrow,
            hidden_narrow,
            pltpu.VMEM((all_slots, 1), jnp.float32),
            pltpu.VMEM((all_slots, 1), jnp.float32),
            slot_array,
            pltpu.VMEM((all_slots, hidden), jnp.float32),
            hidden_narrow,
            hidden_narrow,
            slot_array,
            pltpu.VMEM((hidden, all_slots), jnp.bfloat16),
            pltpu.VMEM((2, slice_width, model_width), jnp.bfloat16),
            pltpu.VMEM((group_rows + 1, token_rows, model_width), jnp.bfloat16),
            pltpu.VMEM((all_tokens, 128), jnp.float32),
            pltpu.VMEM((max(group_rows - 1, 1), token_rows, 128), jnp.float32),
            *LineGather.sems(chunks, group_rows),
            *exchange_sems(chunks, col_count),
            *exchange_sems(chunks, col_count),
            *LineSum.sems(chunks, group_rows),
            *exchange_sems(1, group_rows),
            pltpu.SemaphoreType.DMA((8,)),
            *(
                (
                    pltpu.VMEM((all_tokens, model_width), jnp.bfloat16),
                    pltpu.VMEM((group_rows + 1, token_rows, model_width), jnp.bfloat16),
                    *LineSum.sems(chunks, group_rows),
                )
                if opening
                else ()
            ),
            *(
                item
                for block in dense
                for item in (
                    pltpu.VMEM((max(block_count - 1, 1), *block.shape[1:]), jnp.bfloat16),
                    pltpu.VMEM(block.shape[1:], jnp.bfloat16),
                    *line_sems(block_count),
                )
            ),
        ],
        compiler_params=pltpu.CompilerParams(
            collective_id=(9 if opening else 2) + (10 if dense else 0), has_side_effects=True, vmem_limit_bytes=vmem_most
        ),
        cost_estimate=no_cost,
        name="moe_backward",
    )(own, routes, router, gates, normed, slots, returned, *weights, *opening, *dense)


def col_pairs():
    col_index = lax.axis_index("col")
    return col_index // 2, lax.rem(col_index, 2)


def dense_peers(row_count, pair_count):
    row_index = lax.axis_index("row")
    pair, side = col_pairs()
    rows = Peers(row_count, row_index, lambda place: {"row": place})
    pairs = Peers(pair_count, pair, lambda place: {"col": place * 2 + side})
    sides = Peers(2, side, lambda place: {"col": pair * 2 + place})
    return rows, pairs, sides


def reduce_dense_kernel(
    dims,
    normed_ref,
    grad_proj_ref,
    grad_mid_ref,
    attended_ref,
    small_ref,
    *refs,
):
    row_count, pair_count, to_rows = dims
    outputs = refs[:3]
    scratch = refs[3:]
    kinds = 3
    buffers = [scratch[6 * kind : 6 * kind + 6] for kind in range(kinds)]
    sems = scratch[6 * kinds : 12 * kinds]
    normed_t, grad_proj, grad_mid_t, attended = scratch[12 * kinds :]
    side_sems = [(sems[6 * kind], sems[6 * kind + 1]) for kind in range(kinds)]
    pair_sems = [(sems[6 * kind + 2], sems[6 * kind + 3]) for kind in range(kinds)]
    row_sems = [(sems[6 * kind + 4], sems[6 * kind + 5]) for kind in range(kinds)]
    rows, pairs, sides = dense_peers(row_count, pair_count)
    other = 1 - sides.place

    def spread(target, source, turn):
        count = target.shape[0]
        size = source.shape[1] // count
        for index in range(count):
            part = source[:, index * size : (index + 1) * size]
            target[index] = part.T if turn else part

    spread(normed_t, normed_ref, True)
    spread(grad_proj, grad_proj_ref, False)
    spread(grad_mid_t, grad_mid_ref, True)
    spread(attended, attended_ref, False)

    def block(kind, row, pair, side):
        col = pair * 2 + side
        if kind == 0:
            return dot_nn(normed_t[row], grad_proj[col])
        if kind == 1:
            return dot_nn(grad_mid_t[col], attended[row])
        return small_ref[col, row].astype(jnp.float32)

    greet((rows, pairs, sides) if to_rows else (pairs, sides))

    def side_copy(kind, pair):
        side_send, side_recv = buffers[kind][0], buffers[kind][1]
        return send_to(
            side_send.at[pair],
            side_recv.at[pair],
            side_sems[kind],
            pair,
            sides.device_of(other),
        )

    def pair_copy(kind, step, row):
        place = pairs.ahead(step)
        half, pair_recv = buffers[kind][2], buffers[kind][3]
        return send_to(
            half.at[place, row],
            pair_recv.at[step - 1, row],
            pair_sems[kind],
            (step - 1) * row_count + row,
            pairs.device_of(place),
        )

    def row_copy(kind, step):
        place = rows.ahead(step)
        whole, row_recv = buffers[kind][4], buffers[kind][5]
        return send_to(
            whole.at[place],
            row_recv.at[step - 1],
            row_sems[kind],
            step - 1,
            rows.device_of(place),
        )

    def first(step, carry):
        pair = lax.rem(pairs.place + step, pair_count)
        for kind in range(kinds):
            for row in range(row_count):
                buffers[kind][0][pair, row] = block(kind, row, pair, other).astype(jnp.bfloat16)
            side_copy(kind, pair).start()
        return carry

    lax.fori_loop(1, pair_count + 1, first, 0)

    def second(step, carry):
        pair = lax.rem(pairs.place + step, pair_count)
        for kind in range(kinds):
            side_copy(kind, pair).wait_recv()
            side_recv, half = buffers[kind][1], buffers[kind][2]
            for row in range(row_count):
                total = block(kind, row, pair, sides.place)
                total = total + side_recv[pair, row].astype(jnp.float32)
                half[pair, row] = total.astype(jnp.bfloat16)

                @pl.when(step < pair_count)
                def _():
                    pair_copy(kind, step, row).start()

        return carry

    lax.fori_loop(1, pair_count + 1, second, 0)

    def third(step, carry):
        row = lax.rem(rows.place + step, row_count)
        for kind in range(kinds):
            half, pair_recv, whole = buffers[kind][2], buffers[kind][3], buffers[kind][4]
            total = half[pairs.place, row].astype(jnp.float32)
            for ahead in range(1, pair_count):
                pair_copy(kind, ahead, row).wait_recv()
                total = total + pair_recv[ahead - 1, row].astype(jnp.float32)

            if not to_rows:
                outputs[kind][row] = total.astype(jnp.bfloat16)
                continue

            whole[row] = total.astype(jnp.bfloat16)

            @pl.when(step < row_count)
            def _():
                row_copy(kind, step).start()

        return carry

    lax.fori_loop(1, row_count + 1, third, 0)
    for kind in range(kinds if to_rows else 0):
        whole, row_recv = buffers[kind][4], buffers[kind][5]
        total = whole[rows.place].astype(jnp.float32)
        for step in range(1, row_count):
            row_copy(kind, step).wait_recv()
            total = total + row_recv[step - 1].astype(jnp.float32)
        outputs[kind][...] = total

    def drain_sides(pair, carry):
        for kind in range(kinds):
            side_copy(kind, pair).wait_send()
        return carry

    lax.fori_loop(0, pair_count, drain_sides, 0)

    def drain_pairs(step, carry):
        for kind in range(kinds):
            for row in range(row_count):
                pair_copy(kind, step, row).wait_send()
        return carry

    lax.fori_loop(1, pair_count, drain_pairs, 0)
    for kind in range(kinds if to_rows else 0):
        for step in range(1, row_count):
            row_copy(kind, step).wait_send()


def order_scratch(slice_width, model_width):
    return [
        pltpu.VMEM((4, slice_width, model_width), jnp.bfloat16),
        pltpu.VMEM((4, slice_width, model_width), jnp.float32),
        pltpu.SemaphoreType.DMA((4,)),
        pltpu.SemaphoreType.DMA((4,)),
    ]


def ordered_shapes(layer_count, blocks):
    _, slice_width, model_width = blocks[0].shape
    shape = (layer_count, len(blocks), slice_width, model_width)
    return (jax.ShapeDtypeStruct(shape, jnp.float32),) * 3


def reduce_dense(
    row_count, col_count, normed, grad_projected, grad_mid_b, attended, small, to_rows
):
    token_rows, model_width = normed.shape
    qkv_width, out_rows = grad_projected.shape[1], attended.shape[1]
    pair_count = col_count // 2
    shapes = (
        (model_width // row_count, qkv_width // col_count),
        (model_width // col_count, out_rows // row_count),
        small.shape[2:],
    )
    vmem = pl.BlockSpec(memory_space=pltpu.VMEM)
    scratch = []
    sems = []
    for height, breadth in shapes:
        for lead in (
            (pair_count, row_count),
            (pair_count, row_count),
            (pair_count, row_count),
            (max(pair_count - 1, 1), row_count),
            (row_count,),
            (max(row_count - 1, 1),),
        ):
            scratch.append(pltpu.VMEM((*lead, height, breadth), jnp.bfloat16))
        for count in (pair_count, max(pair_count - 1, 1) * row_count, max(row_count - 1, 1)):
            sems.extend([pltpu.SemaphoreType.DMA((count,))] * 2)
    operands = [
        pltpu.VMEM((row_count, shapes[0][0], token_rows), jnp.bfloat16),
        pltpu.VMEM((col_count, token_rows, shapes[0][1]), jnp.bfloat16),
        pltpu.VMEM((col_count, shapes[1][0], token_rows), jnp.bfloat16),
        pltpu.VMEM((row_count, token_rows, shapes[1][1]), jnp.bfloat16),
    ]
    return pl.pallas_call(
        functools.partial(
            reduce_dense_kernel,
            (row_count, pair_count, to_rows),
        ),
        out_shape=tuple(
            jax.ShapeDtypeStruct(shape, jnp.float32)
            if to_rows
            else jax.ShapeDtypeStruct((row_count, *shape), jnp.bfloat16)
            for shape in shapes
        ),
        in_specs=[vmem] * 5,
        out_specs=(vmem,) * 3,
        scratch_shapes=scratch + sems + operands,
        compiler_params=pltpu.CompilerParams(
            collective_id=3 if to_rows else 11, has_side_effects=True, vmem_limit_bytes=vmem_most
        ),
        cost_estimate=no_cost,
        name="reduce_dense",
    )(
        normed,
        grad_projected,
        grad_mid_b,
        attended,
        small,
    )


class DenseGather:
    def __init__(self, dims, own_blocks, fulls, sems):
        self.row_count, self.pair_count = dims
        self.rows, self.pairs, self.sides = dense_peers(*dims)
        self.own_blocks = own_blocks
        self.fulls = fulls
        self.kinds = range(len(own_blocks))
        self.row_sems = [sems[6 * kind : 6 * kind + 2] for kind in self.kinds]
        self.pair_sems = [sems[6 * kind + 2 : 6 * kind + 4] for kind in self.kinds]
        self.side_sems = [sems[6 * kind + 4 : 6 * kind + 6] for kind in self.kinds]
        self.local_sems = sems[6 * len(own_blocks)]

    @staticmethod
    def sems(dims, kinds):
        row_count, pair_count = dims
        sems = []
        for _ in range(kinds):
            for count in (
                max(row_count - 1, 1),
                max(pair_count - 1, 1) * row_count,
                pair_count * row_count,
            ):
                sems.extend([pltpu.SemaphoreType.DMA((count,))] * 2)
        return sems + [pltpu.SemaphoreType.DMA((kinds,))]

    def groups(self):
        return (self.rows, self.pairs, self.sides)

    def spot(self, kind, row, pair, side):
        col = pair * 2 + side
        height = self.own_blocks[kind].shape[0]
        return self.fulls[kind].at[row, pl.ds(pl.multiple_of(col * height, height), height), :]

    def own_spot(self, kind):
        return self.spot(kind, self.rows.place, self.pairs.place, self.sides.place)

    def own_copy(self, kind):
        return pltpu.make_async_copy(
            self.own_blocks[kind], self.own_spot(kind), self.local_sems.at[kind]
        )

    def row_copy(self, kind, step):
        return send_to(
            self.own_blocks[kind],
            self.own_spot(kind),
            self.row_sems[kind],
            step - 1,
            self.rows.device_of(self.rows.ahead(step)),
        )

    def row_landed(self, kind, step):
        place = self.rows.behind(step)
        landed = self.spot(kind, place, self.pairs.place, self.sides.place)
        return send_to(
            landed, landed, self.row_sems[kind], step - 1, self.rows.device_of(place)
        )

    def pair_copy(self, kind, step, number):
        block = self.spot(kind, self.rows.behind(number), self.pairs.place, self.sides.place)
        return send_to(
            block if number else self.own_blocks[kind],
            block,
            self.pair_sems[kind],
            (step - 1) * self.row_count + number,
            self.pairs.device_of(self.pairs.ahead(step)),
        )

    def pair_landed(self, kind, step, number):
        place = self.pairs.behind(step)
        landed = self.spot(kind, self.rows.behind(number), place, self.sides.place)
        return send_to(
            landed,
            landed,
            self.pair_sems[kind],
            (step - 1) * self.row_count + number,
            self.pairs.device_of(place),
        )

    def side_copy(self, kind, step, number):
        place = self.pairs.behind(step)
        block = self.spot(kind, self.rows.behind(number), place, self.sides.place)
        return send_to(
            block if step or number else self.own_blocks[kind],
            block,
            self.side_sems[kind],
            step * self.row_count + number,
            self.sides.device_of(1 - self.sides.place),
        )

    def side_landed(self, kind, step, number):
        place = self.pairs.behind(step)
        landed = self.spot(kind, self.rows.behind(number), place, 1 - self.sides.place)
        return send_to(
            landed,
            landed,
            self.side_sems[kind],
            step * self.row_count + number,
            self.sides.device_of(1 - self.sides.place),
        )

    def start(self, kind):
        self.own_copy(kind).start()
        for step in range(1, self.row_count):
            self.row_copy(kind, step).start()
        for step in range(1, self.pair_count):
            self.pair_copy(kind, step, 0).start()
        self.side_copy(kind, 0, 0).start()

    def pass_rows(self, kind):
        for number in range(1, self.row_count):
            self.row_landed(kind, number).wait_recv()
            for step in range(1, self.pair_count):
                self.pair_copy(kind, step, number).start()
            self.side_copy(kind, 0, number).start()

    def pass_pairs(self, kind):
        for number in range(self.row_count):
            for step in range(1, self.pair_count):
                self.pair_landed(kind, step, number).wait_recv()
                self.side_copy(kind, step, number).start()

    def finish(self, kind):
        self.own_copy(kind).wait()
        for step in range(self.pair_count):
            for number in range(self.row_count):
                self.side_landed(kind, step, number).wait_recv()
        for step in range(1, self.row_count):
            self.row_copy(kind, step).wait_send()
        for number in range(self.row_count):
            for step in range(1, self.pair_count):
                self.pair_copy(kind, step, number).wait_send()
            for step in range(self.pair_count):
                self.side_copy(kind, step, number).wait_send()


def gathered_shapes(dims, blocks):
    row_count, pair_count = dims
    return tuple(
        jax.ShapeDtypeStruct(
            (row_count, 2 * pair_count * block.shape[0], block.shape[1]), block.dtype
        )
        for block in blocks
    )


def gather_dense_kernel(
    dims,
    copies,
    qkv_ref,
    out_ref,
    routes_ref,
    router_ref,
    shards_ref,
    qkv_full,
    out_full,
    routes_all,
    router_all,
    moved,
    *sems,
):
    gather = DenseGather(dims, (qkv_ref, out_ref), (qkv_full, out_full), sems[:13])
    small_send, small_recv, local_sems = sems[13:16]
    rows = gather.rows
    move = WeightMove(rows, copies, 0, shards_ref, moved, sems[16:])
    small = [
        Exchange(
            rows,
            small_send,
            small_recv,
            lambda place, chunk, ref=ref: ref,
            lambda place, step, chunk, full=full: full.at[place],
        )
        for ref, full in ((routes_ref, routes_all), (router_ref, router_all))
    ]
    greet(gather.groups())
    own_copies = [
        pltpu.make_async_copy(ref, full.at[rows.place], local_sems.at[number])
        for number, (ref, full) in enumerate(((routes_ref, routes_all), (router_ref, router_all)))
    ]
    for kind in range(2):
        gather.start(kind)
        own_copies[kind].start()
        small[kind].start(kind, None)
    move.start()
    for kind in range(2):
        gather.pass_rows(kind)
    for kind in range(2):
        gather.pass_pairs(kind)
    for kind in range(2):
        small[kind].wait_recv(kind, None)
        gather.finish(kind)
        own_copies[kind].wait()
        small[kind].wait_send(kind, None)
    move.wait_recv()
    move.wait_send()


def gather_dense(row_count, col_count, copies, qkv_block, out_block, routes, router, shards):
    dims = (row_count, col_count // 2)
    outside = pl.BlockSpec(memory_space=pl.ANY)
    return pl.pallas_call(
        functools.partial(gather_dense_kernel, dims, copies),
        out_shape=gathered_shapes(dims, (qkv_block, out_block))
        + tuple(jax.ShapeDtypeStruct((row_count, *x.shape), x.dtype) for x in (routes, router))
        + (moved_shape(row_count, shards),),
        in_specs=[outside] * 5,
        out_specs=(outside,) * 5,
        scratch_shapes=DenseGather.sems(dims, 2)
        + [
            *exchange_sems(2, row_count),
            pltpu.SemaphoreType.DMA((2,)),
            *WeightMove.sems(row_count),
        ],
        compiler_params=pltpu.CompilerParams(collective_id=4, has_side_effects=True),
        cost_estimate=no_cost,
        name="gather_dense",
    )(qkv_block, out_block, routes, router, shards)


def order_layer(layer, blocks, outputs, came, wide, in_sems, out_sems):
    block_count = len(blocks)
    row_index = lax.axis_index("row")
    count = 3 * block_count

    def load(number):
        return pltpu.make_async_copy(
            blocks[number // 3].at[number % 3], came.at[number % 4], in_sems.at[number % 4]
        )

    def store(number):
        expert = lax.rem(row_index + number // 3, block_count)
        return pltpu.make_async_copy(
            wide.at[number % 4], outputs[number % 3].at[layer, expert], out_sems.at[number % 4]
        )

    for number in range(min(3, count)):
        load(number).start()
    for number in range(count):
        if number + 3 < count:
            load(number + 3).start()
        load(number).wait()
        if number >= 4:
            store(number - 4).wait()
        wide[number % 4] = came[number % 4].astype(jnp.float32)
        store(number).start()
    for number in range(max(count - 4, 0), count):
        store(number).wait()


def order_grads_kernel(block_count, layers, early, *refs):
    blocks = [refs[block_count * n : block_count * (n + 1)] for n in range(len(layers))]
    refs = refs[block_count * len(layers) + (3 if early else 0) :]
    for layer, group in zip(layers, blocks):
        order_layer(layer, group, refs[:3], *refs[3:])


def order_grads(layer_count, groups, early):
    blocks = [block for _, group in groups for block in group]
    block_count = len(groups[0][1])
    outside = pl.BlockSpec(memory_space=pl.ANY)
    return pl.pallas_call(
        functools.partial(
            order_grads_kernel, block_count, tuple(layer for layer, _ in groups), bool(early)
        ),
        out_shape=ordered_shapes(layer_count, groups[0][1]),
        in_specs=[outside] * (len(blocks) + len(early)),
        out_specs=(outside,) * 3,
        scratch_shapes=order_scratch(*blocks[0].shape[1:]),
        input_output_aliases={len(blocks) + n: n for n in range(len(early))},
        compiler_params=pltpu.CompilerParams(vmem_limit_bytes=vmem_most),
        cost_estimate=no_cost,
        name="order_grads",
    )(*blocks, *early)


def pieces_nt(left, weights_ref):
    pieces, _, size = weights_ref.shape
    total = None
    for index in range(pieces):
        part = dot_nt(left[:, index * size : (index + 1) * size], weights_ref[index])
        total = part if total is None else total + part
    return total


def rotate(values, cosine, sine):
    return values * cosine + pltpu.roll(values, HEAD_SIZE // 2, 1) * sine


def head_lanes(head):
    return slice(2 * head * HEAD_SIZE, 2 * (head + 1) * HEAD_SIZE)


def key_lanes(head):
    return slice(2 * head * HEAD_SIZE, (2 * head + 1) * HEAD_SIZE)


def value_lanes(head):
    return slice((2 * head + 1) * HEAD_SIZE, 2 * (head + 1) * HEAD_SIZE)


def seen_keys(token_rows):
    position = lax.axis_index("col") * token_rows + iota((1, token_rows), 1)
    return (position // BLOCK + 1) * BLOCK


def attend_forward_kernel(
    dims,
    x_ref,
    gain_attn_ref,
    gain_moe_ref,
    cosine_ref,
    sine_ref,
    qkv_ref,
    out_w_ref,
    shards_ref,
    mid_ref,
    normed_ref,
    q_ref,
    kv_out,
    attended_ref,
    lse_ref,
    normed_moe_ref,
    moved,
    kv_all,
    value_t,
    proj,
    send_sem,
    recv_sem,
    local_sem,
    *move_sems,
):
    col_count, row_count, copies, layer, score_scale = dims
    token_rows = x_ref.shape[0]
    group = QUERY_HEADS // KEY_VALUE_HEADS
    kv_width = KEY_VALUE_HEADS * HEAD_SIZE
    cols = col_peers(col_count)

    def part(place):
        return pl.ds(pl.multiple_of(place * token_rows, token_rows), token_rows)

    share = Exchange(
        cols,
        send_sem,
        recv_sem,
        lambda place, chunk: kv_all.at[part(cols.place), chunk],
        lambda place, step, chunk: kv_all.at[part(place), chunk],
    )
    move = WeightMove(all_rows(row_count), copies, layer, shards_ref, moved, move_sems)
    greet((cols, move.rows))
    move.start()
    x = x_ref[...].astype(jnp.float32)
    inverse = lax.rsqrt(jnp.mean(x * x, axis=-1, keepdims=True) + eps_norm)
    normed_ref[...] = (x * inverse * gain_attn_ref[...]).astype(jnp.bfloat16)
    proj[...] = pieces_nt(normed_ref[...], qkv_ref)
    own = part(cols.place)
    for head in range(KEY_VALUE_HEADS):
        start = QUERY_FEATURES + head * HEAD_SIZE
        turned = rotate(proj[:, start : start + HEAD_SIZE], cosine_ref[...], sine_ref[...])
        kv_all[own, key_lanes(head)] = turned.astype(jnp.bfloat16)
        start = start + kv_width
        kv_all[own, value_lanes(head)] = proj[:, start : start + HEAD_SIZE].astype(jnp.bfloat16)
        share.start(head, head_lanes(head))
    for head in range(QUERY_HEADS):
        lanes = slice(head * HEAD_SIZE, (head + 1) * HEAD_SIZE)
        q_ref[:, lanes] = rotate(proj[:, lanes], cosine_ref[...], sine_ref[...]).astype(
            jnp.bfloat16
        )
    seen = seen_keys(token_rows)
    for kv_head in range(KEY_VALUE_HEADS):
        share.wait_recv(kv_head, head_lanes(kv_head))
        value_t[...] = kv_all[:, value_lanes(kv_head)].T

        def head_step(step, carry, kv_head=kv_head):
            index = kv_head * group + step
            lanes = pl.ds(pl.multiple_of(index * HEAD_SIZE, HEAD_SIZE), HEAD_SIZE)
            scores = dot_nt(kv_all[:, key_lanes(kv_head)], q_ref[:, lanes]) * score_scale
            scores = jnp.where(iota(scores.shape, 0) < seen, scores, masked_score)
            peak = jnp.max(scores, axis=0, keepdims=True)
            exponent = jnp.exp(scores - peak)
            total = jnp.sum(exponent, axis=0, keepdims=True)
            attended = dot_nn(value_t[...], exponent.astype(jnp.bfloat16)) / total
            attended_ref[:, lanes] = attended.T.astype(jnp.bfloat16)
            lse_ref[index] = peak + jnp.log(total)
            return carry

        lax.fori_loop(0, group, head_step, 0)
    keep = pltpu.make_async_copy(kv_all, kv_out, local_sem)
    keep.start()
    mid = x_ref[...].astype(jnp.float32) + pieces_nt(attended_ref[...], out_w_ref)
    mid_ref[...] = mid
    inverse = lax.rsqrt(jnp.mean(mid * mid, axis=-1, keepdims=True) + eps_norm)
    normed_moe_ref[...] = (mid * inverse * gain_moe_ref[...]).astype(jnp.bfloat16)
    for head in range(KEY_VALUE_HEADS):
        share.wait_send(head, head_lanes(head))
    keep.wait()
    move.wait_recv()
    move.wait_send()


def attend_forward(
    col_count,
    row_count,
    copies,
    layer,
    x,
    gain_attn,
    gain_moe,
    cosine,
    sine,
    qkv_full,
    out_full,
    shards,
):
    token_rows, model_width = x.shape
    seq_rows = col_count * token_rows
    kv_width = KEY_VALUE_HEADS * HEAD_SIZE
    vmem = pl.BlockSpec(memory_space=pltpu.VMEM)
    outside = pl.BlockSpec(memory_space=pl.ANY)
    rows_b = jax.ShapeDtypeStruct((token_rows, model_width), jnp.bfloat16)
    heads_b = jax.ShapeDtypeStruct((token_rows, QUERY_FEATURES), jnp.bfloat16)
    return pl.pallas_call(
        functools.partial(
            attend_forward_kernel, (col_count, row_count, copies, layer, HEAD_SIZE ** (-0.5))
        ),
        out_shape=(
            jax.ShapeDtypeStruct((token_rows, model_width), jnp.float32),
            rows_b,
            heads_b,
            jax.ShapeDtypeStruct((seq_rows, 2 * kv_width), jnp.bfloat16),
            heads_b,
            jax.ShapeDtypeStruct((QUERY_HEADS, 1, token_rows), jnp.float32),
            rows_b,
            moved_shape(row_count, shards),
        ),
        in_specs=[vmem] * 7 + [outside],
        out_specs=(vmem, vmem, vmem, outside, vmem, vmem, vmem, outside),
        scratch_shapes=[
            pltpu.VMEM((seq_rows, 2 * kv_width), jnp.bfloat16),
            pltpu.VMEM((HEAD_SIZE, seq_rows), jnp.bfloat16),
            pltpu.VMEM((token_rows, QUERY_FEATURES + 2 * kv_width), jnp.float32),
            *exchange_sems(KEY_VALUE_HEADS, col_count),
            pltpu.SemaphoreType.DMA,
            *WeightMove.sems(row_count),
        ],
        compiler_params=pltpu.CompilerParams(
            collective_id=5 + 5 * layer, has_side_effects=True, vmem_limit_bytes=vmem_most
        ),
        cost_estimate=no_cost,
        name="attend_forward",
    )(x, gain_attn, gain_moe, cosine, sine, qkv_full, out_full, shards)


def norm_backward(values, gain, incoming):
    inverse = lax.rsqrt(jnp.mean(values * values, axis=-1, keepdims=True) + eps_norm)
    scaled = incoming * gain
    inner_mean = jnp.mean(scaled * values, axis=-1, keepdims=True)
    grad = inverse * scaled - values * (inverse * inverse * inverse) * inner_mean
    return grad, jnp.sum(incoming * values * inverse, axis=0, keepdims=True)


def attend_backward_kernel(
    dims,
    incoming_ref,
    grad_moe_ref,
    mid_ref,
    x_ref,
    gain_attn_ref,
    gain_moe_ref,
    cosine_ref,
    sine_ref,
    qkv_ref,
    out_w_ref,
    q_ref,
    kv_ref,
    attended_ref,
    lse_ref,
    grad_x_ref,
    grad_mid_ref,
    grad_proj_ref,
    grad_gain_attn_ref,
    grad_gain_moe_ref,
    grad_attended,
    key_t,
    key_sum,
    value_sum,
    grad_kv,
    landed,
    send_sem,
    recv_sem,
):
    col_count, score_scale = dims
    token_rows = x_ref.shape[0]
    group = QUERY_HEADS // KEY_VALUE_HEADS
    kv_width = KEY_VALUE_HEADS * HEAD_SIZE
    cols = col_peers(col_count)

    def part(place):
        return pl.ds(pl.multiple_of(place * token_rows, token_rows), token_rows)

    share = Exchange(
        cols,
        send_sem,
        recv_sem,
        lambda place, chunk: grad_kv.at[part(place), chunk],
        lambda place, step, chunk: landed.at[step - 1, :, chunk],
    )
    greet((cols,))
    grad, gain_sum = norm_backward(mid_ref[...], gain_moe_ref[...], grad_moe_ref[...])
    grad_gain_moe_ref[...] = gain_sum
    grad_x_ref[...] = incoming_ref[...] + grad
    grad_mid_ref[...] = grad_x_ref[...].astype(jnp.bfloat16)
    pieces, _, size = out_w_ref.shape
    for index in range(pieces):
        lanes = slice(index * size, (index + 1) * size)
        grad_attended[:, lanes] = dot_nn(grad_mid_ref[...], out_w_ref[index]).astype(jnp.bfloat16)
    seen = seen_keys(token_rows)
    for kv_head in range(KEY_VALUE_HEADS):
        key_t[...] = kv_ref[:, key_lanes(kv_head)].T
        key_sum[...] = jnp.zeros_like(key_sum)
        value_sum[...] = jnp.zeros_like(value_sum)

        def head_step(step, carry, kv_head=kv_head):
            index = kv_head * group + step
            lanes = pl.ds(pl.multiple_of(index * HEAD_SIZE, HEAD_SIZE), HEAD_SIZE)
            query = q_ref[:, lanes]
            grad_out = grad_attended[:, lanes]
            product = grad_out.astype(jnp.float32) * attended_ref[:, lanes].astype(jnp.float32)
            inner = jnp.sum(product.T, axis=0, keepdims=True)
            scores = dot_nt(kv_ref[:, key_lanes(kv_head)], query) * score_scale
            soft = jnp.where(
                iota(scores.shape, 0) < seen, jnp.exp(scores - lse_ref[index]), 0.0
            )
            grad_soft = dot_nt(kv_ref[:, value_lanes(kv_head)], grad_out)
            grad_scores = (soft * (grad_soft - inner)).astype(jnp.bfloat16)
            value_sum[...] += dot_nn(soft.astype(jnp.bfloat16), grad_out)
            key_sum[...] += dot_nn(grad_scores, query)
            grad_q = (dot_nn(key_t[...], grad_scores) * score_scale).T
            grad_q = rotate(grad_q, cosine_ref[...], -sine_ref[...])
            grad_proj_ref[:, lanes] = grad_q.astype(jnp.bfloat16)
            return carry

        lax.fori_loop(0, group, head_step, 0)
        grad_kv[:, key_lanes(kv_head)] = (key_sum[...] * score_scale).astype(jnp.bfloat16)
        grad_kv[:, value_lanes(kv_head)] = value_sum[...].astype(jnp.bfloat16)
        share.start(kv_head, head_lanes(kv_head))
    for head in range(KEY_VALUE_HEADS):
        share.wait_recv(head, head_lanes(head))
        total = grad_kv[part(cols.place), head_lanes(head)].astype(jnp.float32)
        for step in range(1, col_count):
            total = total + landed[step - 1, :, head_lanes(head)].astype(jnp.float32)
        start = QUERY_FEATURES + head * HEAD_SIZE
        grad_key = rotate(total[:, :HEAD_SIZE], cosine_ref[...], -sine_ref[...])
        grad_proj_ref[:, start : start + HEAD_SIZE] = grad_key.astype(jnp.bfloat16)
        start = start + kv_width
        grad_proj_ref[:, start : start + HEAD_SIZE] = total[:, HEAD_SIZE:].astype(jnp.bfloat16)
    pieces = qkv_ref.shape[0]
    grad_normed = [dot_nn(grad_proj_ref[...], qkv_ref[index]) for index in range(pieces)]
    grad_normed = jnp.concatenate(grad_normed, axis=1) if pieces > 1 else grad_normed[0]
    grad, gain_sum = norm_backward(
        x_ref[...].astype(jnp.float32), gain_attn_ref[...], grad_normed
    )
    grad_gain_attn_ref[...] = gain_sum
    grad_x_ref[...] += grad
    for head in range(KEY_VALUE_HEADS):
        share.wait_send(head, head_lanes(head))


def attend_backward(
    col_count,
    incoming,
    grad_moe,
    mid,
    x,
    gain_attn,
    gain_moe,
    cosine,
    sine,
    qkv_full,
    out_full,
    queries,
    key_value,
    attended,
    log_sums,
):
    token_rows, model_width = x.shape
    seq_rows = col_count * token_rows
    kv_width = KEY_VALUE_HEADS * HEAD_SIZE
    vmem = pl.BlockSpec(memory_space=pltpu.VMEM)
    gain = jax.ShapeDtypeStruct((1, model_width), jnp.float32)
    return pl.pallas_call(
        functools.partial(attend_backward_kernel, (col_count, HEAD_SIZE ** (-0.5))),
        out_shape=(
            jax.ShapeDtypeStruct((token_rows, model_width), jnp.float32),
            jax.ShapeDtypeStruct((token_rows, model_width), jnp.bfloat16),
            jax.ShapeDtypeStruct((token_rows, QUERY_FEATURES + 2 * kv_width), jnp.bfloat16),
            gain,
            gain,
        ),
        in_specs=[vmem] * 14,
        out_specs=(vmem,) * 5,
        scratch_shapes=[
            pltpu.VMEM((token_rows, QUERY_FEATURES), jnp.bfloat16),
            pltpu.VMEM((HEAD_SIZE, seq_rows), jnp.bfloat16),
            pltpu.VMEM((seq_rows, HEAD_SIZE), jnp.float32),
            pltpu.VMEM((seq_rows, HEAD_SIZE), jnp.float32),
            pltpu.VMEM((seq_rows, 2 * kv_width), jnp.bfloat16),
            pltpu.VMEM((max(col_count - 1, 1), token_rows, 2 * kv_width), jnp.bfloat16),
            *exchange_sems(KEY_VALUE_HEADS, col_count),
        ],
        compiler_params=pltpu.CompilerParams(
            collective_id=6 if x.dtype == jnp.float32 else 14, has_side_effects=True, vmem_limit_bytes=vmem_most
        ),
        cost_estimate=no_cost,
        name="attend_backward",
    )(
        incoming,
        grad_moe,
        mid,
        x,
        gain_attn,
        gain_moe,
        cosine,
        sine,
        qkv_full,
        out_full,
        queries,
        key_value,
        attended,
        log_sums,
    )


def place_first(values, group_rows, expert_pick):
    rolled = jnp.roll(values.reshape(-1, group_rows, values.shape[1]), -expert_pick, axis=1)
    return rolled.transpose(1, 0, 2).reshape(values.shape)


def place_back(values, group_rows, expert_pick):
    rolled = values.reshape(group_rows, -1, values.shape[1]).transpose(1, 0, 2)
    return jnp.roll(rolled, expert_pick, axis=1).reshape(values.shape)


def body(
    hidden_in, routes, norm_attn, w_qkv, w_out, norm_moe, w_router, w_gate, w_up, w_down, cotangent
):
    row_count = lax.axis_size("row")
    col_count = lax.axis_size("col")
    device_count = row_count * col_count
    row_index = lax.axis_index("row")
    col_index = lax.axis_index("col")
    layer_count = w_qkv.shape[0]
    token_rows = hidden_in.shape[0]
    model_width = hidden_in.shape[1]
    local_experts = w_gate.shape[1]
    slice_width = w_gate.shape[3]
    copies = row_count // local_experts
    expert_pick = row_index // copies
    slot_rows = -(-local_experts * CAP // 16) * 16
    chunks = model_width // 384
    dims = (
        local_experts,
        col_count,
        copies,
        token_rows,
        slot_rows,
        chunks,
        model_width // chunks,
    )
    positions = col_index * token_rows + jnp.arange(token_rows, dtype=jnp.int32)
    cosine, sine = rope_angles(positions, HEAD_SIZE // 2)
    cosine = jnp.concatenate([cosine, cosine], axis=1)
    sine = jnp.concatenate([-sine, sine], axis=1)

    def move_grads(grads):
        blocks = [grads[0]]
        for step in range(1, row_count):
            pairs = [(index, (index - step) % row_count) for index in range(row_count)]
            blocks.append(lax.ppermute(grads[step], "row", pairs))
        return tuple(blocks)

    def own_grads(blocks):
        ordered = jnp.roll(jnp.stack(blocks), row_index, axis=0).astype(wide_type)
        return jnp.sum(ordered.reshape(local_experts, copies, *blocks[0].shape), axis=1)

    def pieced(full):
        if full.shape[2] % 128 == 0:
            return full
        return full.transpose(1, 0, 2).reshape(1, full.shape[1], -1)

    def packed(values):
        return jnp.pad(values.reshape(-1), (0, -values.size % 2048)).reshape(-1, 128)

    shards = (w_gate.transpose(0, 1, 3, 2), w_up.transpose(0, 1, 3, 2), w_down)
    experts = []
    route_lines = routes.transpose(0, 2, 1)
    router_lines = w_router.transpose(0, 2, 1)
    qkv_full, out_full, routes_all, router_all, moved_gate = gather_dense(
        row_count,
        col_count,
        copies,
        w_qkv[0].T,
        w_out[0].T,
        packed(route_lines),
        packed(router_lines),
        shards[0],
    )
    dense = [(pieced(qkv_full), pieced(out_full))]
    routes_all = routes_all.reshape(row_count, -1)[:, : route_lines.size]
    routes_all = routes_all.reshape(row_count, *route_lines.shape)
    if copies > 1:
        routes_all = jnp.take(
            routes_all, row_index % copies + copies * jnp.arange(local_experts), axis=0
        )
    router_all = router_all.reshape(row_count, -1)[:, : router_lines.size]
    router_all = router_all.reshape(row_count, *router_lines.shape)
    router_all = router_all.transpose(1, 2, 0, 3).reshape(layer_count, E, model_width)
    routers = [
        place_first(router_all[index], local_experts, expert_pick) for index in range(layer_count)
    ]
    gains_attn = norm_attn.astype(wide_type)[:, None, :]
    gains_moe = norm_moe.astype(wide_type)[:, None, :]
    hidden = hidden_in
    saved = []
    for layer_index in range(layer_count):
        early = 0 if layer_index else 1
        mid, normed, queries, key_value, attended, log_sums, normed_moe, moved = attend_forward(
            col_count,
            row_count,
            copies,
            layer_index,
            hidden,
            gains_attn[layer_index],
            gains_moe[layer_index],
            cosine,
            sine,
            *dense[layer_index],
            shards[early],
        )
        if layer_index == 0:
            weights, moving = [moved_gate, moved, shards[2]], (2,)
        else:
            weights, moving = [moved, shards[1], shards[2]], (1, 2)
        next_blocks = ()
        if layer_index + 1 < layer_count:
            next_blocks = (w_qkv[layer_index + 1].T, w_out[layer_index + 1].T)
        closing = layer_index + 1 == layer_count
        mixed, gates, slots, returned, *rest = moe_forward(
            dims,
            row_count,
            layer_index,
            normed_moe,
            routes_all[:, layer_index],
            routers[layer_index],
            weights,
            moving,
            next_blocks,
            closing,
            () if closing else (mid,),
        )
        if closing:
            left_sum = (mixed,)
        for kind, moved in zip(moving, rest):
            weights[kind] = moved
        experts.append(weights)
        if next_blocks:
            dense.append(tuple(pieced(full) for full in rest[len(moving) :]))
        saved.append(
            (hidden, mid, normed, queries, key_value, attended, log_sums, normed_moe)
            + (gates, slots, returned)
        )
        if not closing:
            hidden = mixed
    incoming = cotangent.astype(wide_type)
    dense_results = [None] * layer_count
    expert_results = [None] * layer_count
    part_sums = ()
    ordered = ()
    for layer_index in reversed(range(layer_count)):
        x, mid, normed, queries, key_value, attended, log_sums, normed_moe = saved[layer_index][:8]
        gates, slots, returned = saved[layer_index][8:]
        grad_moe, grad_router, *rest = moe_backward(
            dims,
            incoming.astype(narrow_type),
            routes_all[:, layer_index],
            routers[layer_index],
            gates,
            normed_moe,
            slots,
            returned,
            experts[layer_index],
            left_sum,
            part_sums,
        )
        if part_sums:
            dense_results[layer_index + 1] = rest[row_count : row_count + 3]
            del rest[row_count : row_count + 3]
        if left_sum:
            hidden = mid + rest.pop()
            left_sum = ()
        if layer_index + 1 < layer_count:
            grad_moe, expert_results[layer_index + 1] = lax.optimization_barrier(
                (grad_moe, expert_results[layer_index + 1])
            )
        expert_results[layer_index] = move_grads(rest)
        incoming, grad_mid, grad_projected, grad_gain_attn, grad_gain_moe = attend_backward(
            col_count,
            incoming,
            grad_moe,
            mid,
            x,
            gains_attn[layer_index],
            gains_moe[layer_index],
            cosine,
            sine,
            *dense[layer_index],
            queries,
            key_value,
            attended,
            log_sums,
        )
        small = jnp.concatenate(
            [
                place_back(grad_router, local_experts, expert_pick),
                grad_gain_attn,
                grad_gain_moe,
            ],
            axis=0,
        ).astype(narrow_type)
        small = small.reshape(E + 2, device_count, -1).transpose(1, 0, 2).reshape(device_count, -1)
        small_size = small.shape[1]
        small_rows = -(-small_size // 2048) * 16
        small = jnp.pad(small, ((0, 0), (0, small_rows * 128 - small_size)))
        small = small.reshape(row_count, col_count, small_rows, 128).transpose(1, 0, 2, 3)
        if layer_index == 0 and copies == 1 and layer_count > 1:
            groups = tuple((above, expert_results[above]) for above in range(1, layer_count))
            grad_mid, ordered = lax.optimization_barrier(
                (grad_mid, order_grads(layer_count, groups, ()))
            )
        part_sums = reduce_dense(
            row_count,
            col_count,
            normed,
            grad_projected,
            grad_mid,
            attended,
            small,
            layer_index == 0,
        )
        if layer_index > 0:
            incoming, part_sums = lax.optimization_barrier((incoming, part_sums))
        else:
            dense_results[0] = part_sums
    small_results = [
        small.reshape(-1)[:small_size].reshape(E + 2, -1).T for _, _, small in dense_results
    ]
    dense_results = [(qkv, out.T) for qkv, out, _ in dense_results]
    small = jnp.stack(small_results)
    if copies == 1:
        grad_gate, grad_up, grad_down = order_grads(
            layer_count, ((0, expert_results[0]),), ordered
        )
    else:
        ordered = jnp.stack([own_grads(blocks) for blocks in expert_results])
        grad_gate, grad_up, grad_down = (ordered[:, :, kind] for kind in range(3))
    grad_gate, grad_up = grad_gate.swapaxes(2, 3), grad_up.swapaxes(2, 3)
    return (
        hidden,
        incoming,
        small[:, :, E],
        jnp.stack([dense_results[index][0] for index in range(layer_count)]),
        jnp.stack([dense_results[index][1] for index in range(layer_count)]),
        small[:, :, E + 1],
        small[:, :, :E],
        grad_gate,
        grad_up,
        grad_down,
    )


def solution(mesh):
    in_specs = (
        P(("row", "col"), None),
        P(None, ("row", "col"), None),
        P(),
        P(None, "row", "col"),
        P(None, "row", "col"),
        P(),
        P(None, "row", None),
        P(None, "col", None, "row"),
        P(None, "col", None, "row"),
        P(None, "col", "row", None),
        P(("row", "col"), None),
    )
    out_specs = (
        P(("row", "col"), None),
        P(("row", "col"), None),
        P(None, ("row", "col")),
        P(None, "row", "col"),
        P(None, "row", "col"),
        P(None, ("row", "col")),
        P(None, ("row", "col"), None),
        P(None, "col", None, "row"),
        P(None, "col", None, "row"),
        P(None, "col", "row", None),
    )
    return jax.shard_map(body, mesh=mesh, in_specs=in_specs, out_specs=out_specs, check_vma=False)
```
